32 devices in a mesh: rep: 4 (over y, x), fsdp: 2 (over core), seq: 4 (over z).
Axes of the slice: x: 2, y: 2, z: 4, core: 2. Of those that a mesh axis runs over, the one named last changes fastest.
Arguments:
- hidden_in: bfloat16 [2, 8, 256, 1024], P(None, ('rep', 'fsdp'), 'seq'), may hold values from -6 to 6
- memory: bfloat16 [2, 8, 256, 1024], P(None, ('rep', 'fsdp'), 'seq'), may hold values from -6 to 6
- segment_ids: int32 [2, 8, 256], P(None, ('rep', 'fsdp')), may hold values from 0 to 2, never falling along the last dimension, each value on 1 to 128 neighbouring positions
- memory_ids: int32 [2, 8, 256], P(None, ('rep', 'fsdp')), may hold values from 0 to 2, never falling along the last dimension, each value on 1 to 128 neighbouring positions
- out_grad: bfloat16 [2, 8, 256, 1024], P(None, ('rep', 'fsdp'), 'seq'), may hold values from -6 to 6
- self_qkv: bfloat16 [1024, 3072], P('fsdp'), may hold values from -0.1875 to 0.1875
- self_out: bfloat16 [1024, 1024], P('fsdp'), may hold values from -0.75 to 0.75
- cross_query: bfloat16 [1024, 1024], P('fsdp'), may hold values from -0.1875 to 0.1875
- cross_kv: bfloat16 [1024, 2048], P('fsdp'), may hold values from -0.1875 to 0.1875
- cross_out: bfloat16 [1024, 1024], P('fsdp'), may hold values from -0.75 to 0.75
- fc_in: bfloat16 [1024, 8192], P(None, 'fsdp'), may hold values from -0.1875 to 0.1875
- fc_out: bfloat16 [8192, 1024], P('fsdp'), may hold values from -0.0625 to 0.0625
- biases: bfloat16 [1024, 7], P('fsdp'), may hold values from -2 to 2
- fc_in_bias: bfloat16 [8192], P('fsdp'), may hold values from -2 to 2
- norm_gains: bfloat16 [1024, 3], P('fsdp'), may hold values from 0.25 to 1.75
- norm_shifts: bfloat16 [1024, 3], P('fsdp'), may hold values from -2 to 2
Outputs:
- hidden_out: bfloat16 [2, 8, 256, 1024], P(None, ('rep', 'fsdp'), 'seq')
- hidden_grad: bfloat16 [2, 8, 256, 1024], P(None, ('rep', 'fsdp'), 'seq')
- memory_grad: bfloat16 [2, 8, 256, 1024], P(None, ('rep', 'fsdp'), 'seq')
- self_qkv_grad: float32 [1024, 3072], P('fsdp')
- self_out_grad: float32 [1024, 1024], P('fsdp')
- cross_query_grad: float32 [1024, 1024], P('fsdp')
- cross_kv_grad: float32 [1024, 2048], P('fsdp')
- cross_out_grad: float32 [1024, 1024], P('fsdp')
- fc_in_grad: float32 [1024, 8192], P(None, 'fsdp')
- fc_out_grad: float32 [8192, 1024], P('fsdp')
- biases_grad: float32 [1024, 7], P('fsdp')
- fc_in_bias_grad: float32 [8192], P('fsdp')
- norm_gains_grad: float32 [1024, 3], P('fsdp')
- norm_shifts_grad: float32 [1024, 3], P('fsdp')
The draws below stay inside these ranges and needn't reach their ends.
Inputs may be any that keep to these rules, and one draw needn't show every extreme that they name: `segment_ids`: within each sequence the ids never fall and each of 0 to 2 occurs. `memory_ids`: within each sequence the ids never fall and each of 0 to 2 occurs.
All inputs are finite; a program needn't handle non-finite values.
Results may differ from the reference program's by a relative error of at most 0.02.
Values may be sent and summed in bfloat16 or wider, within the bound.
A program may use at most 320 MiB of HBM per device.

```python
import math
import jax
import jax.numpy as jnp
import numpy as np
from jax import lax

D = 1024
HEAD = 64
FF = 8192
MICRO = 2
DOCS = 3
LEN = 256
MEM = 256
SEQS = 8


def strengthened(values, own_key, source, target, shards_of, factor):
    owner, partner = [(jnp.arange(values.shape[axis_at]) // (values.shape[axis_at] // shards_of)).reshape([-1 if axis == axis_at else 1 for axis in range(values.ndim)]) for axis_at in (source, target)]
    chosen = jax.random.permutation(own_key, shards_of)[partner]
    strong = (owner == chosen) | (owner == (partner + shards_of // 2) % shards_of)
    return jnp.where(strong, factor * values, values)


def block_scale(stream_key, dims, shards, low, top_value):
    gain, own = 1.0, jax.random.fold_in(stream_key, 6)
    for dim, parts in shards:
        steps = jnp.exp(jax.random.uniform(jax.random.fold_in(own, dim), (parts,), jnp.float32, low / len(shards), top_value / len(shards)))
        gain = gain * jnp.repeat(steps, dims[dim] // parts).reshape([-1 if axis == dim else 1 for axis in range(len(dims))])
    return gain


def split_up(number_of, total, most, slope):
    weights = [(1 << 20) // math.isqrt(grade ** slope) + 1 for grade in range(2, number_of + 1)]
    spare, given = total - most - (number_of - 1), [1] * (number_of - 1)
    while spare > 0:
        candidates = [i for i in range(number_of - 1) if given[i] < most]
        whole, remaining = sum([weights[i] for i in candidates]), spare
        for i in candidates:
            extra = min(most - given[i], max(1, remaining * weights[i] // whole), spare)
            given[i] = given[i] + extra
            spare = spare - extra
    return np.array([most] + given)


def ragged(own_key, count, total, bound, slope):
    if count == 2:
        one = jax.random.randint(own_key, (), max(1, total - bound), min(bound, total - 1) + 1)
        return jnp.stack([one, total - one])
    tallies = jnp.asarray(split_up(count, total, bound, slope), jnp.int32)
    pairs = (count - 1) // 2
    donor, sink = tallies[1:1 + 2 * pairs:2], tallies[2:2 + 2 * pairs:2]
    room = jnp.minimum(donor - 1, bound - sink)
    shifted = jax.random.randint(jax.random.fold_in(own_key, 1), (pairs,), 0, 1 << 20) % (room + 1)
    tallies = tallies.at[1:1 + 2 * pairs:2].set(donor - shifted).at[2:2 + 2 * pairs:2].set(sink + shifted)
    return tallies[jax.random.permutation(jax.random.fold_in(own_key, 2), count)]


def bell_draw(own_key, extent, width, reach, split=(), held_as=jnp.bfloat16):
    values = width * jax.random.normal(own_key, extent, jnp.float32)
    if split:
        values = values * block_scale(own_key, extent, split, -0.22, 0.18)
    return jnp.clip(values, -reach, reach).astype(held_as)


def noise_with(stream_key, shape, scale, reach, split, heavy, held_as=jnp.bfloat16):
    values = scale * jax.random.normal(stream_key, shape, jnp.float32)
    if split:
        values = values * block_scale(stream_key, shape, split, -0.22, 0.18)
    return jnp.clip(strengthened(values, jax.random.fold_in(stream_key, 3), *heavy), -reach, reach).astype(held_as)


def setup_inputs(seed: int = 0) -> dict:
    splits = jax.random.split(jax.random.key(seed), 17)
    return {
        "hidden_in": noise_with(splits[0], (MICRO, SEQS, LEN, D), 1.0, 6.0, ((1, 8), (2, 4)), (1, 3, 8, 2.0)),
        "memory": bell_draw(splits[1], (MICRO, SEQS, MEM, D), 1.0, 6.0, ((1, 8), (2, 4))),
        "segment_ids": jax.vmap(lambda own: jnp.searchsorted(jnp.cumsum(ragged(own, DOCS, LEN, LEN // 2, 1)), jnp.arange(LEN), side="right"))(jax.random.split(splits[2], MICRO * SEQS)).reshape((MICRO, SEQS, LEN)).astype(jnp.int32),
        "memory_ids": jax.vmap(lambda own: jnp.searchsorted(jnp.cumsum(ragged(own, DOCS, MEM, MEM // 2, 1)), jnp.arange(MEM), side="right"))(jax.random.split(splits[3], MICRO * SEQS)).reshape((MICRO, SEQS, MEM)).astype(jnp.int32),
        "out_grad": bell_draw(splits[4], (MICRO, SEQS, LEN, D), 1.0, 6.0, ((1, 8), (2, 4))),
        "self_qkv": bell_draw(splits[5], (D, 3 * D), D ** -0.5, 0.1875, ((0, 2),)),
        "self_out": bell_draw(splits[6], (D, D), (D // 16) ** -0.5, 0.75, ((0, 2),)),
        "cross_query": bell_draw(splits[7], (D, D), D ** -0.5, 0.1875, ((0, 2),)),
        "cross_kv": bell_draw(splits[8], (D, 2 * D), D ** -0.5, 0.1875, ((0, 2),)),
        "cross_out": bell_draw(splits[9], (D, D), (D // 16) ** -0.5, 0.75, ((0, 2),)),
        "fc_in": bell_draw(splits[10], (D, FF), D ** -0.5, 0.1875, ((1, 2),)),
        "fc_out": bell_draw(splits[11], (FF, D), FF ** -0.5, 0.0625, ((0, 2),)),
        "biases": bell_draw(splits[12], (D, 7), 0.3, 2.0, ((0, 2),)),
        "fc_in_bias": bell_draw(splits[13], (FF,), 0.3, 2.0, ((0, 2),)),
        "norm_gains": jnp.clip(1.0 + 0.15 * jax.random.normal(splits[14], (D, 3), jnp.float32), 0.25, 1.75).astype(jnp.bfloat16),
        "norm_shifts": bell_draw(splits[15], (D, 3), 0.3, 2.0, ((0, 2),)),
    }


@jax.custom_vjp
def low(v):
    return lax.optimization_barrier(v.astype(jnp.bfloat16)).astype(jnp.float32)

@jax.custom_vjp
def low_back(v):
    return v

def low_keep(v):
    return (low(v), None)

def low_pass(kept, grad):
    return (grad,)

def back_keep(v):
    return (v, None)

def back_low(kept, grad):
    return (low(grad),)
low.defvjp(low_keep, low_pass)
low_back.defvjp(back_keep, back_low)
NORM_EPSILON = 1e-05
MASKED_SCORE = -1e+30

def layer_norm(values, norm_gain, norm_shift):
    average = lax.optimization_barrier(jnp.mean(values, axis=-1, keepdims=True))
    centred = values - average
    variance = lax.optimization_barrier(jnp.mean(centred * centred, axis=-1, keepdims=True))
    return centred * lax.rsqrt(variance + NORM_EPSILON) * norm_gain + norm_shift

def project(rows, weight):
    return jnp.einsum('gtd,de->gte', rows, weight, precision=lax.Precision.HIGHEST)

def split_heads(values):
    return values.reshape(values.shape[:-1] + (values.shape[-1] // HEAD, HEAD))

def attend(queries, key_rows, value_rows, allowed):
    scores = jnp.einsum('gqhe,gkhe->ghqk', queries, key_rows, precision=lax.Precision.HIGHEST) * HEAD ** (-0.5)
    scores = low_back(jnp.where(allowed[:, None], scores, MASKED_SCORE))
    highest = lax.optimization_barrier(jnp.max(scores, axis=-1, keepdims=True))
    exponent = jnp.exp(scores - highest)
    weights = low(exponent / lax.optimization_barrier(jnp.sum(exponent, axis=-1, keepdims=True)))
    joined = jnp.einsum('ghqk,gkhe->gqhe', weights, value_rows, precision=lax.Precision.HIGHEST)
    return joined.reshape(joined.shape[:2] + (joined.shape[2] * joined.shape[3],))

def forward(params, hidden, source, token_ids, source_ids):
    self_qkv, self_out, cross_query, cross_kv, cross_out, fc_in, fc_out, biases, fc_in_bias, norm_gains, norm_shifts = params
    model_width = hidden.shape[-1]
    zero_row = jnp.zeros_like(biases[:, 0])
    positions = jnp.arange(hidden.shape[1])
    causal = positions[:, None] >= positions[None, :]
    self_allowed = causal[None] & (token_ids[:, :, None] == token_ids[:, None, :])
    cross_allowed = token_ids[:, :, None] == source_ids[:, None, :]
    normed_one = low(layer_norm(hidden, norm_gains[:, 0], norm_shifts[:, 0]))
    qkv_bias = jnp.concatenate([biases[:, 0], zero_row, biases[:, 1]])
    projected = low(low_back(project(normed_one, self_qkv) + qkv_bias))
    self_mixed = attend(split_heads(projected[..., :model_width]), split_heads(projected[..., model_width:2 * model_width]), split_heads(projected[..., 2 * model_width:]), self_allowed)
    self_mixed = low(low_back(self_mixed))
    after_self = hidden + low_back(project(self_mixed, self_out) + biases[:, 2])
    normed_two = low(layer_norm(after_self, norm_gains[:, 1], norm_shifts[:, 1]))
    cross_queries = low(low_back(project(normed_two, cross_query) + biases[:, 3]))
    memory_bias = jnp.concatenate([zero_row, biases[:, 4]])
    memory_kv = low(low_back(project(source, cross_kv) + memory_bias))
    cross_mixed = attend(split_heads(cross_queries), split_heads(memory_kv[..., :model_width]), split_heads(memory_kv[..., model_width:]), cross_allowed)
    cross_mixed = low(low_back(cross_mixed))
    after_cross = after_self + low_back(project(cross_mixed, cross_out) + biases[:, 5])
    normed_three = low(layer_norm(after_cross, norm_gains[:, 2], norm_shifts[:, 2]))
    pre_active = low_back(project(normed_three, fc_in) + fc_in_bias)
    active = low(jax.nn.gelu(pre_active, approximate=False))
    return after_cross + low_back(project(active, fc_out) + biases[:, 6])

def reference(hidden_in, memory, segment_ids, memory_ids, out_grad, self_qkv, self_out, cross_query, cross_kv, cross_out, fc_in, fc_out, biases, fc_in_bias, norm_gains, norm_shifts):
    params = tuple((weight.astype(jnp.float32) for weight in (self_qkv, self_out, cross_query, cross_kv, cross_out, fc_in, fc_out, biases, fc_in_bias, norm_gains, norm_shifts)))
    group_size = 4
    count = MICRO * SEQS

    def regroup(array):
        return array.reshape((count // group_size, group_size) + array.shape[2:])
    inputs = (regroup(hidden_in.astype(jnp.float32)), regroup(memory.astype(jnp.float32)), regroup(segment_ids), regroup(memory_ids), regroup(out_grad.astype(jnp.float32)))

    def group_step(totals, pieces):
        hidden, source, token_ids, source_ids, cotangent = pieces

        def apply_layer(weights, rows, memory_rows):
            return forward(weights, rows, memory_rows, token_ids, source_ids)
        result, pullback = jax.vjp(apply_layer, params, hidden, source)
        weight_grads, rows_grad, source_grad = pullback(cotangent)
        totals = jax.tree.map(jnp.add, totals, weight_grads)
        return (totals, (result.astype(jnp.bfloat16), rows_grad.astype(jnp.bfloat16), source_grad.astype(jnp.bfloat16)))
    initial = jax.tree.map(jnp.zeros_like, params)
    totals, stacked = lax.scan(group_step, initial, inputs)
    hidden_out = stacked[0].reshape(hidden_in.shape)
    hidden_grad = stacked[1].reshape(hidden_in.shape)
    memory_grad = stacked[2].reshape(memory.shape)
    grads = tuple((total.astype(jnp.float32) for total in totals))
    return (hidden_out, hidden_grad, memory_grad, grads[0], grads[1], grads[2], grads[3], grads[4], grads[5], grads[6], grads[7], grads[8], grads[9], grads[10])
```

```python
import functools
import math

import jax
import jax.numpy as jnp
from jax import lax
from jax.experimental import pallas as pl
from jax.experimental.pallas import tpu as pltpu
from jax.sharding import PartitionSpec as P

HEAD = 64


NORM_EPSILON = 1e-05
MASKED_SCORE = -1e30


def norm_forward(values, norm_gain, norm_shift):
    average = jnp.mean(values, axis=-1, keepdims=True)
    centred = values - average
    inverse = lax.rsqrt(jnp.mean(centred * centred, axis=-1, keepdims=True) + NORM_EPSILON)
    scaled = centred * inverse
    return (scaled * norm_gain + norm_shift, scaled, inverse)


def norm_backward(grad_normed, scaled, inverse, norm_gain):
    grad_scaled = grad_normed * norm_gain
    first_mean = jnp.mean(grad_scaled, axis=-1, keepdims=True)
    second_mean = jnp.mean(grad_scaled * scaled, axis=-1, keepdims=True)
    grad_values = (grad_scaled - first_mean - scaled * second_mean) * inverse
    gain_grad = jnp.sum(grad_normed * scaled, axis=(0, 1))
    shift_grad = jnp.sum(grad_normed, axis=(0, 1))
    return (grad_values, gain_grad, shift_grad)


def split_heads(values):
    return values.reshape(values.shape[:-1] + (values.shape[-1] // HEAD, HEAD))


def join_heads(values):
    return values.reshape(values.shape[:2] + (values.shape[2] * values.shape[3],))


def masked_scores(queries, key_rows, allowed):
    raw_scores = jnp.einsum(
        "mqhe,mkhe->mhqk", queries, key_rows, preferred_element_type=jnp.float32
    )
    return jnp.where(allowed[:, None], raw_scores * HEAD ** (-0.5), MASKED_SCORE)


def attend_forward(queries, key_rows, value_rows, allowed):
    scores = masked_scores(queries, key_rows, allowed)
    highest = jnp.max(scores, axis=-1, keepdims=True)
    exponent = jnp.exp(scores - highest)
    row_totals = jnp.sum(exponent, axis=-1, keepdims=True)
    weights = (exponent / row_totals).astype(jnp.bfloat16)
    joined = jnp.einsum("mhqk,mkhe->mqhe", weights, value_rows, preferred_element_type=jnp.float32)
    return (join_heads(joined).astype(jnp.bfloat16), highest + jnp.log(row_totals))


def attend_backward(queries, key_rows, value_rows, allowed, log_totals, grad_joined):
    scores = masked_scores(queries, key_rows, allowed)
    probability = jnp.exp(scores - log_totals)
    weights = probability.astype(jnp.bfloat16)
    grad_value_rows = jnp.einsum(
        "mhqk,mqhe->mkhe", weights, grad_joined, preferred_element_type=jnp.float32
    )
    grad_weights = jnp.einsum(
        "mqhe,mkhe->mhqk", grad_joined, value_rows, preferred_element_type=jnp.float32
    )
    grad_scores = probability * (
        grad_weights - jnp.sum(grad_weights * probability, axis=-1, keepdims=True)
    )
    grad_scores = grad_scores.astype(jnp.bfloat16)
    grad_queries = jnp.einsum(
        "mhqk,mkhe->mqhe", grad_scores, key_rows, preferred_element_type=jnp.float32
    ) * HEAD ** (-0.5)
    grad_key_rows = jnp.einsum(
        "mhqk,mqhe->mkhe", grad_scores, queries, preferred_element_type=jnp.float32
    ) * HEAD ** (-0.5)
    return (join_heads(grad_queries), join_heads(grad_key_rows), join_heads(grad_value_rows))


def gelu_slope(values):
    cumulative = 0.5 * (1.0 + lax.erf(values * 2.0 ** (-0.5)))
    density = jnp.exp(-0.5 * values * values) / math.sqrt(2.0 * math.pi)
    return cumulative + values * density


def feed_forward(rows, weight_in, bias_in, weight_out):
    pre_active = jnp.einsum(
        "mtd,df->mtf", rows, weight_in, preferred_element_type=jnp.float32
    ) + bias_in.astype(jnp.float32)
    active = jax.nn.gelu(pre_active, approximate=False).astype(jnp.bfloat16)
    partial_out = jnp.einsum("mtf,fd->mtd", active, weight_out, preferred_element_type=jnp.float32)
    return (pre_active, active, partial_out)


def feed_back(rows, grad_rows, pre_active, active, weight_in, weight_out):
    grad_active = jnp.einsum(
        "mtd,fd->mtf", grad_rows, weight_out, preferred_element_type=jnp.float32
    )
    grad_inner = (grad_active * gelu_slope(pre_active)).astype(jnp.bfloat16)
    grad_weight_out = jnp.einsum(
        "mtf,mtd->fd", active, grad_rows, preferred_element_type=jnp.float32
    )
    grad_weight_in = jnp.einsum("mtd,mtf->df", rows, grad_inner, preferred_element_type=jnp.float32)
    grad_bias_in = jnp.sum(grad_inner.astype(jnp.float32), axis=(0, 1))
    grad_rows_in = jnp.einsum(
        "mtf,df->mtd", grad_inner, weight_in, preferred_element_type=jnp.float32
    )
    return (grad_weight_in, grad_weight_out, grad_bias_in, grad_rows_in)


def project(rows, weight):
    return jnp.einsum("mtd,de->mte", rows, weight, preferred_element_type=jnp.float32)


def project_back(grad_rows, weight):
    return jnp.einsum("mte,de->mtd", grad_rows, weight, preferred_element_type=jnp.float32)


def weight_grad(rows, grad_rows):
    return jnp.einsum("mtd,mte->de", rows, grad_rows, preferred_element_type=jnp.float32)


def column_sums(grad_rows):
    return jnp.sum(grad_rows.astype(jnp.float32), axis=(0, 1))


def body(
    hidden_in,
    memory,
    segment_ids,
    memory_ids,
    out_grad,
    self_qkv,
    self_out,
    cross_query,
    cross_kv,
    cross_out,
    fc_in,
    fc_out,
    biases,
    fc_in_bias,
    norm_gains,
    norm_shifts,
):
    micro_count, single, tokens, model_width = hidden_in.shape
    seq_index = lax.axis_index("seq")
    zero_row = jnp.zeros((model_width,), jnp.float32)
    outputs_list = []
    grads_list = []
    memory_list = []
    attn_total = None
    mlp_total = None
    for micro in range(micro_count):
        full_qkv = lax.all_gather(self_qkv, "fsdp", axis=0, tiled=True)
        full_self_out = lax.all_gather(self_out, "fsdp", axis=0, tiled=True)
        full_query = lax.all_gather(cross_query, "fsdp", axis=0, tiled=True)
        full_memory_kv = lax.all_gather(cross_kv, "fsdp", axis=0, tiled=True)
        full_cross_out = lax.all_gather(cross_out, "fsdp", axis=0, tiled=True)
        full_biases = lax.all_gather(biases, "fsdp", axis=0, tiled=True)
        full_gains = lax.all_gather(norm_gains, "fsdp", axis=0, tiled=True)
        full_shifts = lax.all_gather(norm_shifts, "fsdp", axis=0, tiled=True)
        bias_float = full_biases.astype(jnp.float32)
        gain_float = full_gains.astype(jnp.float32)
        shift_float = full_shifts.astype(jnp.float32)
        hidden = hidden_in[micro : micro + 1][:, 0].astype(jnp.float32)
        memory_rows = memory[micro : micro + 1][:, 0]
        token_ids = segment_ids[micro : micro + 1][:, 0]
        source_ids = memory_ids[micro : micro + 1][:, 0]
        query_ids = lax.dynamic_slice_in_dim(token_ids, seq_index * tokens, tokens, 1)
        query_place = seq_index * tokens + jnp.arange(tokens, dtype=jnp.int32)
        key_place = jnp.arange(token_ids.shape[1], dtype=jnp.int32)
        self_allowed = (query_place[:, None] >= key_place[None, :])[None] & (
            query_ids[:, :, None] == token_ids[:, None, :]
        )
        cross_allowed = query_ids[:, :, None] == source_ids[:, None, :]
        normed_one, scaled_one, inverse_one = norm_forward(
            hidden, gain_float[:, 0], shift_float[:, 0]
        )
        normed_one = normed_one.astype(jnp.bfloat16)
        qkv_bias = jnp.concatenate([bias_float[:, 0], zero_row, bias_float[:, 1]])
        projected = (project(normed_one, full_qkv) + qkv_bias).astype(jnp.bfloat16)
        self_queries = split_heads(projected[..., :model_width])
        kv_all = lax.all_gather(projected[..., model_width:], "seq", axis=1, tiled=True)
        self_key_rows = split_heads(kv_all[..., :model_width])
        self_value_rows = split_heads(kv_all[..., model_width:])
        self_mixed, self_totals = attend_forward(
            self_queries, self_key_rows, self_value_rows, self_allowed
        )
        after_self = hidden + project(self_mixed, full_self_out) + bias_float[:, 2]
        normed_two, scaled_two, inverse_two = norm_forward(
            after_self, gain_float[:, 1], shift_float[:, 1]
        )
        normed_two = normed_two.astype(jnp.bfloat16)
        cross_queries = (project(normed_two, full_query) + bias_float[:, 3]).astype(jnp.bfloat16)
        memory_bias = jnp.concatenate([zero_row, bias_float[:, 4]])
        memory_kv = (project(memory_rows, full_memory_kv) + memory_bias).astype(jnp.bfloat16)
        memory_all = lax.all_gather(memory_kv, "seq", axis=1, tiled=True)
        memory_key_rows = split_heads(memory_all[..., :model_width])
        memory_value_rows = split_heads(memory_all[..., model_width:])
        cross_mixed, cross_totals = attend_forward(
            split_heads(cross_queries), memory_key_rows, memory_value_rows, cross_allowed
        )
        after_cross = after_self + project(cross_mixed, full_cross_out) + bias_float[:, 5]
        normed_three, scaled_three, inverse_three = norm_forward(
            after_cross, gain_float[:, 2], shift_float[:, 2]
        )
        normed_three = normed_three.astype(jnp.bfloat16)
        grad_out = out_grad[micro : micro + 1][:, 0]
        mlp_inputs = lax.all_gather(normed_three, "fsdp", axis=0, tiled=True)
        pre_active, active, partial_out = feed_forward(mlp_inputs, fc_in, fc_in_bias, fc_out)
        mlp_branch = lax.psum_scatter(
            partial_out.astype(jnp.bfloat16), "fsdp", scatter_dimension=0, tiled=True
        ).astype(jnp.float32)
        output = after_cross + mlp_branch + bias_float[:, 6]
        hidden_out = output.astype(jnp.bfloat16)[:, None]
        back_qkv = lax.all_gather(self_qkv, "fsdp", axis=0, tiled=True)
        back_self_out = lax.all_gather(self_out, "fsdp", axis=0, tiled=True)
        back_query = lax.all_gather(cross_query, "fsdp", axis=0, tiled=True)
        back_memory_kv = lax.all_gather(cross_kv, "fsdp", axis=0, tiled=True)
        back_cross_out = lax.all_gather(cross_out, "fsdp", axis=0, tiled=True)
        back_gains = lax.all_gather(norm_gains, "fsdp", axis=0, tiled=True)
        back_gain_float = back_gains.astype(jnp.float32)
        grad_gathered = lax.all_gather(grad_out, "fsdp", axis=0, tiled=True)
        one_grad_fc_in, one_grad_fc_out, one_grad_fc_bias, grad_partial = feed_back(
            mlp_inputs, grad_gathered, pre_active, active, fc_in, fc_out
        )
        grad_normed_three = lax.psum_scatter(
            grad_partial.astype(jnp.bfloat16), "fsdp", scatter_dimension=0, tiled=True
        ).astype(jnp.float32)
        grad_three, gain_three, shift_three = norm_backward(
            grad_normed_three, scaled_three, inverse_three, back_gain_float[:, 2]
        )
        grad_after_cross = grad_out.astype(jnp.float32) + grad_three
        grad_cross_branch = grad_after_cross.astype(jnp.bfloat16)
        grad_cross_out = weight_grad(cross_mixed, grad_cross_branch)
        grad_cross_mixed = project_back(grad_cross_branch, back_cross_out).astype(jnp.bfloat16)
        cross_grad_queries, memory_grad_keys, memory_grad_values = attend_backward(
            split_heads(cross_queries),
            memory_key_rows,
            memory_value_rows,
            cross_allowed,
            cross_totals,
            split_heads(grad_cross_mixed),
        )
        own_memory_keys = lax.psum_scatter(
            memory_grad_keys.astype(jnp.bfloat16), "seq", scatter_dimension=1, tiled=True
        )
        own_memory_values = lax.psum_scatter(
            memory_grad_values.astype(jnp.bfloat16), "seq", scatter_dimension=1, tiled=True
        )
        grad_memory_kv = jnp.concatenate([own_memory_keys, own_memory_values], axis=-1)
        grad_memory_weight = weight_grad(memory_rows, grad_memory_kv)
        memory_grad = project_back(grad_memory_kv, back_memory_kv).astype(jnp.bfloat16)[:, None]
        grad_cross_queries = cross_grad_queries.astype(jnp.bfloat16)
        grad_query_weight = weight_grad(normed_two, grad_cross_queries)
        grad_normed_two = project_back(grad_cross_queries, back_query)
        grad_two, gain_two, shift_two = norm_backward(
            grad_normed_two, scaled_two, inverse_two, back_gain_float[:, 1]
        )
        grad_after_self = grad_after_cross + grad_two
        grad_self_branch = grad_after_self.astype(jnp.bfloat16)
        grad_self_out = weight_grad(self_mixed, grad_self_branch)
        grad_self_mixed = project_back(grad_self_branch, back_self_out).astype(jnp.bfloat16)
        self_grad_queries, self_grad_keys, self_grad_values = attend_backward(
            self_queries,
            self_key_rows,
            self_value_rows,
            self_allowed,
            self_totals,
            split_heads(grad_self_mixed),
        )
        own_self_keys = lax.psum_scatter(
            self_grad_keys.astype(jnp.bfloat16), "seq", scatter_dimension=1, tiled=True
        )
        own_self_values = lax.psum_scatter(
            self_grad_values.astype(jnp.bfloat16), "seq", scatter_dimension=1, tiled=True
        )
        grad_projected = jnp.concatenate(
            [self_grad_queries.astype(jnp.bfloat16), own_self_keys, own_self_values], axis=-1
        )
        grad_qkv_weight = weight_grad(normed_one, grad_projected)
        grad_normed_one = project_back(grad_projected, back_qkv)
        grad_one, gain_one, shift_one = norm_backward(
            grad_normed_one, scaled_one, inverse_one, back_gain_float[:, 0]
        )
        hidden_grad = (grad_after_self + grad_one).astype(jnp.bfloat16)[:, None]
        grad_biases = jnp.stack(
            [
                column_sums(grad_projected[..., :model_width]),
                column_sums(grad_projected[..., 2 * model_width :]),
                column_sums(grad_self_branch),
                column_sums(grad_cross_queries),
                column_sums(grad_memory_kv[..., model_width:]),
                column_sums(grad_cross_branch),
                column_sums(grad_out),
            ],
            axis=1,
        )
        grad_gains = jnp.stack([gain_one, gain_two, gain_three], axis=1)
        grad_shifts = jnp.stack([shift_one, shift_two, shift_three], axis=1)
        attn_grads = (
            grad_qkv_weight,
            grad_self_out,
            grad_query_weight,
            grad_memory_weight,
            grad_cross_out,
            grad_biases,
            grad_gains,
            grad_shifts,
        )
        mlp_grads = (one_grad_fc_in, one_grad_fc_out, one_grad_fc_bias)
        hidden_out, hidden_grad, memory_grad, attn_grads, mlp_grads = (
            hidden_out,
            hidden_grad,
            memory_grad,
            attn_grads,
            mlp_grads,
        )
        outputs_list.append(hidden_out)
        grads_list.append(hidden_grad)
        memory_list.append(memory_grad)
        if attn_total is None:
            attn_total = attn_grads
            mlp_total = mlp_grads
        else:
            attn_total = jax.tree.map(jnp.add, attn_total, attn_grads)
            mlp_total = jax.tree.map(jnp.add, mlp_total, mlp_grads)
    grad_fc_in, grad_fc_out, grad_fc_bias = mlp_total
    (
        shard_qkv,
        shard_self_out,
        shard_query,
        shard_memory_kv,
        shard_cross_out,
        shard_biases,
        shard_gains,
        shard_shifts,
    ) = (
        lax.psum_scatter(
            attn_total[0].astype(jnp.bfloat16), "fsdp", scatter_dimension=0, tiled=True
        ).astype(jnp.float32),
        lax.psum_scatter(
            attn_total[1].astype(jnp.bfloat16), "fsdp", scatter_dimension=0, tiled=True
        ).astype(jnp.float32),
        lax.psum_scatter(
            attn_total[2].astype(jnp.bfloat16), "fsdp", scatter_dimension=0, tiled=True
        ).astype(jnp.float32),
        lax.psum_scatter(
            attn_total[3].astype(jnp.bfloat16), "fsdp", scatter_dimension=0, tiled=True
        ).astype(jnp.float32),
        lax.psum_scatter(
            attn_total[4].astype(jnp.bfloat16), "fsdp", scatter_dimension=0, tiled=True
        ).astype(jnp.float32),
        lax.psum_scatter(
            attn_total[5].astype(jnp.bfloat16), "fsdp", scatter_dimension=0, tiled=True
        ).astype(jnp.float32),
        lax.psum_scatter(
            attn_total[6].astype(jnp.bfloat16), "fsdp", scatter_dimension=0, tiled=True
        ).astype(jnp.float32),
        lax.psum_scatter(
            attn_total[7].astype(jnp.bfloat16), "fsdp", scatter_dimension=0, tiled=True
        ).astype(jnp.float32),
    )
    summed = (
        lax.psum(shard_qkv.astype(jnp.bfloat16), ("rep", "seq")).astype(jnp.float32),
        lax.psum(shard_self_out.astype(jnp.bfloat16), ("rep", "seq")).astype(jnp.float32),
        lax.psum(shard_query.astype(jnp.bfloat16), ("rep", "seq")).astype(jnp.float32),
        lax.psum(shard_memory_kv.astype(jnp.bfloat16), ("rep", "seq")).astype(jnp.float32),
        lax.psum(shard_cross_out.astype(jnp.bfloat16), ("rep", "seq")).astype(jnp.float32),
        lax.psum(grad_fc_in.astype(jnp.bfloat16), ("rep", "seq")).astype(jnp.float32),
        lax.psum(grad_fc_out.astype(jnp.bfloat16), ("rep", "seq")).astype(jnp.float32),
        lax.psum(shard_biases.astype(jnp.bfloat16), ("rep", "seq")).astype(jnp.float32),
        lax.psum(grad_fc_bias.astype(jnp.bfloat16), ("rep", "seq")).astype(jnp.float32),
        lax.psum(shard_gains.astype(jnp.bfloat16), ("rep", "seq")).astype(jnp.float32),
        lax.psum(shard_shifts.astype(jnp.bfloat16), ("rep", "seq")).astype(jnp.float32),
    )
    hidden_out = jnp.concatenate(outputs_list, axis=0)
    hidden_grad = jnp.concatenate(grads_list, axis=0)
    memory_grad = jnp.concatenate(memory_list, axis=0)
    return (
        hidden_out,
        hidden_grad,
        memory_grad,
        summed[0],
        summed[1],
        summed[2],
        summed[3],
        summed[4],
        summed[5],
        summed[6],
        summed[7],
        summed[8],
        summed[9],
        summed[10],
    )


def shift_rows(mine, other, core):
    low = jnp.where(core == 0, mine, other)
    high = jnp.where(core == 0, other, mine)
    return jnp.concatenate([low, high], axis=0)


def swap(values):
    return lax.ppermute(values, "fsdp", [(0, 1), (1, 0)])


def moves(turn):
    pairs = []
    for core in range(2):
        for place in range(4):
            odd = (place + turn) % 2
            pairs.append((core * 4 + place, (place // 2) * 4 + 2 * odd + core))
    return pairs


def bring(array, place):
    even = place % 2 == 0
    first = lax.ppermute(jnp.where(even, array[0], array[1]), ("fsdp", "seq"), moves(0))
    second = lax.ppermute(jnp.where(even, array[1], array[0]), ("fsdp", "seq"), moves(1))
    early = place < 2
    return jnp.concatenate(
        [jnp.where(early, first, second), jnp.where(early, second, first)], axis=0
    )


def send_back(rows, place):
    half = rows.shape[0] // 2
    early = place < 2
    even = place % 2 == 0
    one = jnp.where(early, rows[:half], rows[half:])
    two = jnp.where(early, rows[half:], rows[:half])
    back = [[(b, a) for a, b in moves(turn)] for turn in range(2)]
    one = lax.ppermute(one, ("fsdp", "seq"), back[0])
    two = lax.ppermute(two, ("fsdp", "seq"), back[1])
    return jnp.stack([jnp.where(even, one, two), jnp.where(even, two, one)], axis=0)


def mul(left, right):
    return jnp.dot(left, right, preferred_element_type=jnp.float32)


def mul_nt(left, right):
    return lax.dot_general(left, right, (((1,), (1,)), ((), ())), preferred_element_type=jnp.float32)


def mul_tn(left, right):
    return lax.dot_general(left, right, (((0,), (0,)), ((), ())), preferred_element_type=jnp.float32)


def half_of(values, core):
    width = values.shape[1] // 2
    return lax.dynamic_slice_in_dim(values, core * width, width, 1)


def gelu_pair(values):
    depth = 1.0 + (0.3275911 * 2.0**-0.5) * jnp.abs(values)
    inv = pltpu.reciprocal(depth, approx=True)
    inv = inv * (2.0 - depth * inv)
    bell = jnp.exp(-0.5 * values * values)
    series = 0.7107068705 + inv * (-0.7265760135 + inv * 0.5307027145)
    series = inv * (0.127414796 + inv * (-0.142248368 + inv * series))
    tail = series * bell
    cumulative = jnp.where(values >= 0.0, 1.0 - tail, tail)
    return values * cumulative, cumulative + values * (bell * (1.0 / math.sqrt(2.0 * math.pi)))


def ffn_kernel(
    step, rows_ref, grads_ref, in_ref, out_ref, bias_ref, din_ref, dout_ref, dbias_ref, flip, acc, us, das
):
    units = flip.shape[0]
    steps = rows_ref.shape[0] // step
    flip[...] = in_ref[...].T

    def front(turn):
        part = pl.ds(turn * step, step)
        us[turn % 2] = mul_nt(flip[...], rows_ref[part, :])
        das[turn % 2] = mul_nt(out_ref[...], grads_ref[part, :])

    front(0)
    bias = jnp.broadcast_to(bias_ref[...], (128, units)).T[:, :1]
    total = jnp.zeros((units, 128), jnp.float32)
    for turn in range(steps):
        if turn + 1 < steps:
            front(turn + 1)
        active, slope = gelu_pair(us[turn % 2] + bias)
        active = active.astype(jnp.bfloat16)
        inner = (das[turn % 2] * slope).astype(jnp.bfloat16)
        for lane in range(step // 128):
            total += inner[:, lane * 128 : (lane + 1) * 128].astype(jnp.float32)
        part = pl.ds(turn * step, step)
        if turn == 0:
            dout_ref[...] = mul(active, grads_ref[part, :])
            acc[...] = mul(inner, rows_ref[part, :])
        else:
            dout_ref[...] += mul(active, grads_ref[part, :])
            acc[...] += mul(inner, rows_ref[part, :])
    din_ref[...] = acc[...].T
    dbias_ref[...] = jnp.sum(total.T, axis=0, keepdims=True)


def ffn_grads(rows, grads, fc_in, fc_out, bias):
    count, width = rows.shape
    hidden = fc_in.shape[1]
    units, step = min(256, hidden), min(1024, count)
    whole = functools.partial(pl.BlockSpec, pipeline_mode=pl.Buffered(1))
    return pl.pallas_call(
        functools.partial(ffn_kernel, step),
        grid=(hidden // units,),
        in_specs=[
            whole((count, width), lambda at: (0, 0)),
            whole((count, width), lambda at: (0, 0)),
            pl.BlockSpec((width, units), lambda at: (0, at)),
            pl.BlockSpec((units, width), lambda at: (at, 0)),
            pl.BlockSpec((1, units), lambda at: (0, at)),
        ],
        out_specs=[
            pl.BlockSpec((width, units), lambda at: (0, at)),
            pl.BlockSpec((units, width), lambda at: (at, 0)),
            pl.BlockSpec((1, units), lambda at: (0, at)),
        ],
        out_shape=[
            jax.ShapeDtypeStruct((width, hidden), jnp.float32),
            jax.ShapeDtypeStruct((hidden, width), jnp.float32),
            jax.ShapeDtypeStruct((1, hidden), jnp.float32),
        ],
        scratch_shapes=[
            pltpu.VMEM((units, width), jnp.bfloat16),
            pltpu.VMEM((units, width), jnp.float32),
            pltpu.VMEM((2, units, step), jnp.float32),
            pltpu.VMEM((2, units, step), jnp.float32),
        ],
        compiler_params=pltpu.CompilerParams(vmem_limit_bytes=56 * 2**20),
        cost_estimate=pl.CostEstimate(
            flops=8 * count * width * hidden,
            bytes_accessed=4 * count * width + 12 * width * hidden,
            transcendentals=count * hidden,
        ),
    )(rows, grads, fc_in, fc_out, bias)


def fast_body(
    hidden_in,
    memory,
    segment_ids,
    memory_ids,
    out_grad,
    self_qkv,
    self_out,
    cross_query,
    cross_kv,
    cross_out,
    fc_in,
    fc_out,
    biases,
    fc_in_bias,
    norm_gains,
    norm_shifts,
):
    width = hidden_in.shape[-1]
    core = lax.axis_index("fsdp")
    place = lax.axis_index("seq")
    bf16, f32 = jnp.bfloat16, jnp.float32

    x_own = bring(hidden_in[:, 0], place)
    x_all = shift_rows(x_own, swap(x_own), core)
    memory_own = bring(memory[:, 0], place)
    memory_all = shift_rows(memory_own, swap(memory_own), core)
    grad_own = bring(out_grad[:, 0], place)
    grad_chip = shift_rows(grad_own, swap(grad_own), core)
    grad_every = lax.all_gather(grad_own, ("rep", "seq", "fsdp"), axis=0, tiled=True)

    micro, owner = place // 2, place % 2
    ids = jnp.stack([segment_ids[:, 0], memory_ids[:, 0]])
    ids_other = swap(ids)
    ids = jnp.where(owner == core, ids, ids_other)
    ids = lax.dynamic_index_in_dim(ids, micro, 1, keepdims=False)
    token_ids, source_ids = ids[0], ids[1]
    own_count = x_own.shape[0]
    query_place = core * own_count + jnp.arange(own_count, dtype=jnp.int32)
    key_place = jnp.arange(token_ids.shape[0], dtype=jnp.int32)
    query_ids = lax.dynamic_slice_in_dim(token_ids, core * own_count, own_count, 0)
    self_allowed = (query_place[:, None] >= key_place[None, :]) & (
        query_ids[:, None] == token_ids[None, :]
    )
    cross_allowed = query_ids[:, None] == source_ids[None, :]
    self_allowed, cross_allowed = self_allowed[None], cross_allowed[None]

    def whole(shard):
        return shift_rows(shard, swap(shard), core)

    qkv = whole(self_qkv)
    w_self_out = whole(self_out)
    w_query = whole(cross_query)
    w_memory_kv = whole(cross_kv)
    w_cross_out = whole(cross_out)
    small = whole(jnp.concatenate([biases, norm_gains, norm_shifts], axis=1)).astype(f32)
    bias = small[:, :7].T
    gain = small[:, 7:10].T
    shift = small[:, 10:13].T

    def lift(values):
        return split_heads(values)[None]

    normed_one_all, scaled_all, inverse_all = norm_forward(x_all.astype(f32), gain[0], shift[0])
    normed_one_all = normed_one_all.astype(bf16)

    def own_rows(values):
        return lax.dynamic_slice_in_dim(values, core * own_count, own_count, 0)

    normed_one = own_rows(normed_one_all)
    scaled_one, inverse_one = own_rows(scaled_all), own_rows(inverse_all)
    hidden = x_own.astype(f32)
    queries = (mul(normed_one, qkv[:, :width]) + bias[0]).astype(bf16)
    key_rows = mul(normed_one_all, qkv[:, width : 2 * width]).astype(bf16)
    value_rows = (mul(normed_one_all, qkv[:, 2 * width :]) + bias[1]).astype(bf16)
    queries, key_rows, value_rows = lift(queries), lift(key_rows), lift(value_rows)
    self_mixed, self_totals = attend_forward(queries, key_rows, value_rows, self_allowed)
    after_self = hidden + mul(self_mixed[0], w_self_out) + bias[2]
    normed_two, scaled_two, inverse_two = norm_forward(after_self, gain[1], shift[1])
    normed_two = normed_two.astype(bf16)
    cross_queries = lift((mul(normed_two, w_query) + bias[3]).astype(bf16))
    memory_kv = mul(memory_all, w_memory_kv)
    memory_keys = lift(memory_kv[:, :width].astype(bf16))
    memory_values = lift((memory_kv[:, width:] + bias[4]).astype(bf16))
    cross_mixed, cross_totals = attend_forward(
        cross_queries, memory_keys, memory_values, cross_allowed
    )
    after_cross = after_self + mul(cross_mixed[0], w_cross_out) + bias[5]
    normed_three, scaled_three, inverse_three = norm_forward(after_cross, gain[2], shift[2])
    normed_three = normed_three.astype(bf16)
    normed_chip = shift_rows(normed_three, swap(normed_three), core)
    normed_every = lax.all_gather(normed_three, ("rep", "seq", "fsdp"), axis=0, tiled=True)

    fc_bias = fc_in_bias.astype(f32)
    inner = mul(normed_chip, fc_in) + fc_bias
    active = jax.nn.gelu(inner, approximate=False).astype(bf16)
    grad_inner = (mul_nt(grad_chip, fc_out) * gelu_slope(inner)).astype(bf16)
    partial_out = mul(active, fc_out).astype(bf16)
    partial_grad = mul_nt(grad_inner, fc_in).astype(bf16)
    both = jnp.stack([partial_out, partial_grad])
    mine = lax.dynamic_slice_in_dim(both, core * own_count, own_count, 1)
    theirs = lax.dynamic_slice_in_dim(both, (1 - core) * own_count, own_count, 1)
    sums = mine.astype(f32) + swap(theirs).astype(f32)
    hidden_out = (after_cross + sums[0] + bias[6]).astype(bf16)

    def back_norm(grad_normed, scaled, inverse, row):
        grad, gain_grad, shift_grad = norm_backward(
            grad_normed[None], scaled[None], inverse[None], gain[row]
        )
        return grad[0], gain_grad, shift_grad

    grad_three, gain_three, shift_three = back_norm(sums[1], scaled_three, inverse_three, 2)
    grad_after_cross = grad_own.astype(f32) + grad_three
    cross_branch = grad_after_cross.astype(bf16)
    grad_cross_mixed = mul_nt(cross_branch, w_cross_out).astype(bf16)
    dq2, dk2, dv2 = attend_backward(
        cross_queries, memory_keys, memory_values, cross_allowed, cross_totals, lift(grad_cross_mixed)
    )
    dq2 = dq2[0].astype(bf16)
    dc2 = jnp.concatenate([dk2[0], dv2[0]], axis=1).astype(bf16)
    dc2 = (dc2.astype(f32) + swap(dc2).astype(f32)).astype(bf16)
    grad_two, gain_two, shift_two = back_norm(mul_nt(dq2, w_query), scaled_two, inverse_two, 1)
    grad_after_self = grad_after_cross + grad_two
    self_branch = grad_after_self.astype(bf16)
    grad_self_mixed = mul_nt(self_branch, w_self_out).astype(bf16)
    dq1, dk1, dv1 = attend_backward(
        queries, key_rows, value_rows, self_allowed, self_totals, lift(grad_self_mixed)
    )
    dq1 = dq1[0].astype(bf16)
    dkv1 = jnp.concatenate([dk1[0], dv1[0]], axis=1).astype(bf16)
    dkv1 = (dkv1.astype(f32) + swap(dkv1).astype(f32)).astype(bf16)
    grad_projected = jnp.concatenate([dq1, own_rows(dkv1)], axis=1)
    grad_one, gain_one, shift_one = back_norm(
        mul_nt(grad_projected, qkv), scaled_one, inverse_one, 0
    )
    hidden_grad = (grad_after_self + grad_one).astype(bf16)
    memory_grad = mul_nt(own_rows(dc2), w_memory_kv).astype(bf16)

    def chip_rows(values):
        return shift_rows(values, swap(values), core)

    def input_half(values):
        mine = half_of(values, core)
        theirs = half_of(values, 1 - core)
        return shift_rows(mine, swap(theirs), core)

    dq1_all = chip_rows(dq1)
    dp1_all = jnp.concatenate([dq1_all, dkv1], axis=1)
    self_all, dq2_all, cross_all = chip_rows(self_branch), chip_rows(dq2), chip_rows(cross_branch)
    grads = jnp.concatenate(
        [
            mul_tn(half_of(normed_one_all, core), dp1_all).astype(bf16),
            mul_tn(input_half(self_mixed[0]), self_all).astype(bf16),
            mul_tn(input_half(normed_two), dq2_all).astype(bf16),
            mul_tn(half_of(memory_all, core), dc2).astype(bf16),
            mul_tn(input_half(cross_mixed[0]), cross_all).astype(bf16),
        ],
        axis=1,
    )

    def sums_of(values):
        return jnp.sum(half_of(values, core).astype(f32), axis=0)

    gains = jnp.stack([gain_one, gain_two, gain_three, shift_one, shift_two, shift_three])
    gains = half_of(gains, core) + swap(half_of(gains, 1 - core))
    column = jnp.concatenate(
        [
            jnp.stack(
                [
                    sums_of(dq1_all),
                    sums_of(dkv1[:, width:]),
                    sums_of(self_all),
                    sums_of(dq2_all),
                    sums_of(dc2[:, width:]),
                    sums_of(cross_all),
                    sums_of(grad_chip),
                ]
            ),
            gains,
        ]
    )

    grad_fc_in, grad_fc_out, grad_fc_bias = ffn_grads(
        normed_every, grad_every, fc_in, fc_out, fc_bias[None]
    )
    column = jnp.pad(column.T, ((0, 0), (0, 128 - column.shape[0]))).astype(bf16)
    grads = jnp.concatenate([grads, column], axis=1)
    grads = lax.psum(grads, ("rep", "seq")).astype(f32)
    column = grads[:, 8 * width :]
    return (
        send_back(hidden_out, place)[:, None],
        send_back(hidden_grad, place)[:, None],
        send_back(memory_grad, place)[:, None],
        grads[:, : 3 * width],
        grads[:, 3 * width : 4 * width],
        grads[:, 4 * width : 5 * width],
        grads[:, 5 * width : 7 * width],
        grads[:, 7 * width : 8 * width],
        grad_fc_in,
        grad_fc_out,
        column[:, :7],
        grad_fc_bias[0],
        column[:, 7:10],
        column[:, 10:13],
    )


def solution(mesh):
    fits = mesh.shape["fsdp"] == 2 and mesh.shape["seq"] == 4
    chosen = fast_body if fits else body
    return jax.shard_map(
        chosen,
        mesh=mesh,
        in_specs=(
            P(None, ("rep", "fsdp"), "seq", None),
            P(None, ("rep", "fsdp"), "seq", None),
            P(None, ("rep", "fsdp"), None),
            P(None, ("rep", "fsdp"), None),
            P(None, ("rep", "fsdp"), "seq", None),
            P("fsdp", None),
            P("fsdp", None),
            P("fsdp", None),
            P("fsdp", None),
            P("fsdp", None),
            P(None, "fsdp"),
            P("fsdp", None),
            P("fsdp", None),
            P("fsdp"),
            P("fsdp", None),
            P("fsdp", None),
        ),
        out_specs=(
            P(None, ("rep", "fsdp"), "seq", None),
            P(None, ("rep", "fsdp"), "seq", None),
            P(None, ("rep", "fsdp"), "seq", None),
            P("fsdp", None),
            P("fsdp", None),
            P("fsdp", None),
            P("fsdp", None),
            P("fsdp", None),
            P(None, "fsdp"),
            P("fsdp", None),
            P("fsdp", None),
            P("fsdp"),
            P("fsdp", None),
            P("fsdp", None),
        ),
        check_vma=False,
    )
```

```python
import functools
import math

import jax
import jax.numpy as jnp
from jax import lax
from jax.experimental import pallas as pl
from jax.experimental.pallas import tpu as pltpu
from jax.sharding import PartitionSpec as P

HEAD = 64


NORM_EPSILON = 1e-05
MASKED_SCORE = -1e30


def norm_forward(values, norm_gain, norm_shift):
    average = jnp.mean(values, axis=-1, keepdims=True)
    centred = values - average
    inverse = lax.rsqrt(jnp.mean(centred * centred, axis=-1, keepdims=True) + NORM_EPSILON)
    scaled = centred * inverse
    return (scaled * norm_gain + norm_shift, scaled, inverse)


def norm_backward(grad_normed, scaled, inverse, norm_gain):
    grad_scaled = grad_normed * norm_gain
    first_mean = jnp.mean(grad_scaled, axis=-1, keepdims=True)
    second_mean = jnp.mean(grad_scaled * scaled, axis=-1, keepdims=True)
    grad_values = (grad_scaled - first_mean - scaled * second_mean) * inverse
    gain_grad = jnp.sum(grad_normed * scaled, axis=(0, 1))
    shift_grad = jnp.sum(grad_normed, axis=(0, 1))
    return (grad_values, gain_grad, shift_grad)


def split_heads(values):
    return values.reshape(values.shape[:-1] + (values.shape[-1] // HEAD, HEAD))


def join_heads(values):
    return values.reshape(values.shape[:2] + (values.shape[2] * values.shape[3],))


def masked_scores(queries, key_rows, allowed):
    raw_scores = jnp.einsum(
        "mqhe,mkhe->mhqk", queries, key_rows, preferred_element_type=jnp.float32
    )
    return jnp.where(allowed[:, None], raw_scores * HEAD ** (-0.5), MASKED_SCORE)


def attend_forward(queries, key_rows, value_rows, allowed):
    scores = masked_scores(queries, key_rows, allowed)
    highest = jnp.max(scores, axis=-1, keepdims=True)
    exponent = jnp.exp(scores - highest)
    row_totals = jnp.sum(exponent, axis=-1, keepdims=True)
    weights = (exponent / row_totals).astype(jnp.bfloat16)
    joined = jnp.einsum("mhqk,mkhe->mqhe", weights, value_rows, preferred_element_type=jnp.float32)
    return (join_heads(joined).astype(jnp.bfloat16), highest + jnp.log(row_totals))


def attend_backward(queries, key_rows, value_rows, allowed, log_totals, grad_joined):
    scores = masked_scores(queries, key_rows, allowed)
    probability = jnp.exp(scores - log_totals)
    weights = probability.astype(jnp.bfloat16)
    grad_value_rows = jnp.einsum(
        "mhqk,mqhe->mkhe", weights, grad_joined, preferred_element_type=jnp.float32
    )
    grad_weights = jnp.einsum(
        "mqhe,mkhe->mhqk", grad_joined, value_rows, preferred_element_type=jnp.float32
    )
    grad_scores = probability * (
        grad_weights - jnp.sum(grad_weights * probability, axis=-1, keepdims=True)
    )
    grad_scores = grad_scores.astype(jnp.bfloat16)
    grad_queries = jnp.einsum(
        "mhqk,mkhe->mqhe", grad_scores, key_rows, preferred_element_type=jnp.float32
    ) * HEAD ** (-0.5)
    grad_key_rows = jnp.einsum(
        "mhqk,mqhe->mkhe", grad_scores, queries, preferred_element_type=jnp.float32
    ) * HEAD ** (-0.5)
    return (join_heads(grad_queries), join_heads(grad_key_rows), join_heads(grad_value_rows))


def gelu_slope(values):
    cumulative = 0.5 * (1.0 + lax.erf(values * 2.0 ** (-0.5)))
    density = jnp.exp(-0.5 * values * values) / math.sqrt(2.0 * math.pi)
    return cumulative + values * density


def feed_forward(rows, weight_in, bias_in, weight_out):
    pre_active = jnp.einsum(
        "mtd,df->mtf", rows, weight_in, preferred_element_type=jnp.float32
    ) + bias_in.astype(jnp.float32)
    active = jax.nn.gelu(pre_active, approximate=False).astype(jnp.bfloat16)
    partial_out = jnp.einsum("mtf,fd->mtd", active, weight_out, preferred_element_type=jnp.float32)
    return (pre_active, active, partial_out)


def feed_back(rows, grad_rows, pre_active, active, weight_in, weight_out):
    grad_active = jnp.einsum(
        "mtd,fd->mtf", grad_rows, weight_out, preferred_element_type=jnp.float32
    )
    grad_inner = (grad_active * gelu_slope(pre_active)).astype(jnp.bfloat16)
    grad_weight_out = jnp.einsum(
        "mtf,mtd->fd", active, grad_rows, preferred_element_type=jnp.float32
    )
    grad_weight_in = jnp.einsum("mtd,mtf->df", rows, grad_inner, preferred_element_type=jnp.float32)
    grad_bias_in = jnp.sum(grad_inner.astype(jnp.float32), axis=(0, 1))
    grad_rows_in = jnp.einsum(
        "mtf,df->mtd", grad_inner, weight_in, preferred_element_type=jnp.float32
    )
    return (grad_weight_in, grad_weight_out, grad_bias_in, grad_rows_in)


def project(rows, weight):
    return jnp.einsum("mtd,de->mte", rows, weight, preferred_element_type=jnp.float32)


def project_back(grad_rows, weight):
    return jnp.einsum("mte,de->mtd", grad_rows, weight, preferred_element_type=jnp.float32)


def weight_grad(rows, grad_rows):
    return jnp.einsum("mtd,mte->de", rows, grad_rows, preferred_element_type=jnp.float32)


def column_sums(grad_rows):
    return jnp.sum(grad_rows.astype(jnp.float32), axis=(0, 1))


def body(
    hidden_in,
    memory,
    segment_ids,
    memory_ids,
    out_grad,
    self_qkv,
    self_out,
    cross_query,
    cross_kv,
    cross_out,
    fc_in,
    fc_out,
    biases,
    fc_in_bias,
    norm_gains,
    norm_shifts,
):
    micro_count, single, tokens, model_width = hidden_in.shape
    seq_index = lax.axis_index("seq")
    zero_row = jnp.zeros((model_width,), jnp.float32)
    outputs_list = []
    grads_list = []
    memory_list = []
    attn_total = None
    mlp_total = None
    for micro in range(micro_count):
        full_qkv = lax.all_gather(self_qkv, "fsdp", axis=0, tiled=True)
        full_self_out = lax.all_gather(self_out, "fsdp", axis=0, tiled=True)
        full_query = lax.all_gather(cross_query, "fsdp", axis=0, tiled=True)
        full_memory_kv = lax.all_gather(cross_kv, "fsdp", axis=0, tiled=True)
        full_cross_out = lax.all_gather(cross_out, "fsdp", axis=0, tiled=True)
        full_biases = lax.all_gather(biases, "fsdp", axis=0, tiled=True)
        full_gains = lax.all_gather(norm_gains, "fsdp", axis=0, tiled=True)
        full_shifts = lax.all_gather(norm_shifts, "fsdp", axis=0, tiled=True)
        bias_float = full_biases.astype(jnp.float32)
        gain_float = full_gains.astype(jnp.float32)
        shift_float = full_shifts.astype(jnp.float32)
        hidden = hidden_in[micro : micro + 1][:, 0].astype(jnp.float32)
        memory_rows = memory[micro : micro + 1][:, 0]
        token_ids = segment_ids[micro : micro + 1][:, 0]
        source_ids = memory_ids[micro : micro + 1][:, 0]
        query_ids = lax.dynamic_slice_in_dim(token_ids, seq_index * tokens, tokens, 1)
        query_place = seq_index * tokens + jnp.arange(tokens, dtype=jnp.int32)
        key_place = jnp.arange(token_ids.shape[1], dtype=jnp.int32)
        self_allowed = (query_place[:, None] >= key_place[None, :])[None] & (
            query_ids[:, :, None] == token_ids[:, None, :]
        )
        cross_allowed = query_ids[:, :, None] == source_ids[:, None, :]
        normed_one, scaled_one, inverse_one = norm_forward(
            hidden, gain_float[:, 0], shift_float[:, 0]
        )
        normed_one = normed_one.astype(jnp.bfloat16)
        qkv_bias = jnp.concatenate([bias_float[:, 0], zero_row, bias_float[:, 1]])
        projected = (project(normed_one, full_qkv) + qkv_bias).astype(jnp.bfloat16)
        self_queries = split_heads(projected[..., :model_width])
        kv_all = lax.all_gather(projected[..., model_width:], "seq", axis=1, tiled=True)
        self_key_rows = split_heads(kv_all[..., :model_width])
        self_value_rows = split_heads(kv_all[..., model_width:])
        self_mixed, self_totals = attend_forward(
            self_queries, self_key_rows, self_value_rows, self_allowed
        )
        after_self = hidden + project(self_mixed, full_self_out) + bias_float[:, 2]
        normed_two, scaled_two, inverse_two = norm_forward(
            after_self, gain_float[:, 1], shift_float[:, 1]
        )
        normed_two = normed_two.astype(jnp.bfloat16)
        cross_queries = (project(normed_two, full_query) + bias_float[:, 3]).astype(jnp.bfloat16)
        memory_bias = jnp.concatenate([zero_row, bias_float[:, 4]])
        memory_kv = (project(memory_rows, full_memory_kv) + memory_bias).astype(jnp.bfloat16)
        memory_all = lax.all_gather(memory_kv, "seq", axis=1, tiled=True)
        memory_key_rows = split_heads(memory_all[..., :model_width])
        memory_value_rows = split_heads(memory_all[..., model_width:])
        cross_mixed, cross_totals = attend_forward(
            split_heads(cross_queries), memory_key_rows, memory_value_rows, cross_allowed
        )
        after_cross = after_self + project(cross_mixed, full_cross_out) + bias_float[:, 5]
        normed_three, scaled_three, inverse_three = norm_forward(
            after_cross, gain_float[:, 2], shift_float[:, 2]
        )
        normed_three = normed_three.astype(jnp.bfloat16)
        grad_out = out_grad[micro : micro + 1][:, 0]
        mlp_inputs = lax.all_gather(normed_three, "fsdp", axis=0, tiled=True)
        pre_active, active, partial_out = feed_forward(mlp_inputs, fc_in, fc_in_bias, fc_out)
        mlp_branch = lax.psum_scatter(
            partial_out.astype(jnp.bfloat16), "fsdp", scatter_dimension=0, tiled=True
        ).astype(jnp.float32)
        output = after_cross + mlp_branch + bias_float[:, 6]
        hidden_out = output.astype(jnp.bfloat16)[:, None]
        back_qkv = lax.all_gather(self_qkv, "fsdp", axis=0, tiled=True)
        back_self_out = lax.all_gather(self_out, "fsdp", axis=0, tiled=True)
        back_query = lax.all_gather(cross_query, "fsdp", axis=0, tiled=True)
        back_memory_kv = lax.all_gather(cross_kv, "fsdp", axis=0, tiled=True)
        back_cross_out = lax.all_gather(cross_out, "fsdp", axis=0, tiled=True)
        back_gains = lax.all_gather(norm_gains, "fsdp", axis=0, tiled=True)
        back_gain_float = back_gains.astype(jnp.float32)
        grad_gathered = lax.all_gather(grad_out, "fsdp", axis=0, tiled=True)
        one_grad_fc_in, one_grad_fc_out, one_grad_fc_bias, grad_partial = feed_back(
            mlp_inputs, grad_gathered, pre_active, active, fc_in, fc_out
        )
        grad_normed_three = lax.psum_scatter(
            grad_partial.astype(jnp.bfloat16), "fsdp", scatter_dimension=0, tiled=True
        ).astype(jnp.float32)
        grad_three, gain_three, shift_three = norm_backward(
            grad_normed_three, scaled_three, inverse_three, back_gain_float[:, 2]
        )
        grad_after_cross = grad_out.astype(jnp.float32) + grad_three
        grad_cross_branch = grad_after_cross.astype(jnp.bfloat16)
        grad_cross_out = weight_grad(cross_mixed, grad_cross_branch)
        grad_cross_mixed = project_back(grad_cross_branch, back_cross_out).astype(jnp.bfloat16)
        cross_grad_queries, memory_grad_keys, memory_grad_values = attend_backward(
            split_heads(cross_queries),
            memory_key_rows,
            memory_value_rows,
            cross_allowed,
            cross_totals,
            split_heads(grad_cross_mixed),
        )
        own_memory_keys = lax.psum_scatter(
            memory_grad_keys.astype(jnp.bfloat16), "seq", scatter_dimension=1, tiled=True
        )
        own_memory_values = lax.psum_scatter(
            memory_grad_values.astype(jnp.bfloat16), "seq", scatter_dimension=1, tiled=True
        )
        grad_memory_kv = jnp.concatenate([own_memory_keys, own_memory_values], axis=-1)
        grad_memory_weight = weight_grad(memory_rows, grad_memory_kv)
        memory_grad = project_back(grad_memory_kv, back_memory_kv).astype(jnp.bfloat16)[:, None]
        grad_cross_queries = cross_grad_queries.astype(jnp.bfloat16)
        grad_query_weight = weight_grad(normed_two, grad_cross_queries)
        grad_normed_two = project_back(grad_cross_queries, back_query)
        grad_two, gain_two, shift_two = norm_backward(
            grad_normed_two, scaled_two, inverse_two, back_gain_float[:, 1]
        )
        grad_after_self = grad_after_cross + grad_two
        grad_self_branch = grad_after_self.astype(jnp.bfloat16)
        grad_self_out = weight_grad(self_mixed, grad_self_branch)
        grad_self_mixed = project_back(grad_self_branch, back_self_out).astype(jnp.bfloat16)
        self_grad_queries, self_grad_keys, self_grad_values = attend_backward(
            self_queries,
            self_key_rows,
            self_value_rows,
            self_allowed,
            self_totals,
            split_heads(grad_self_mixed),
        )
        own_self_keys = lax.psum_scatter(
            self_grad_keys.astype(jnp.bfloat16), "seq", scatter_dimension=1, tiled=True
        )
        own_self_values = lax.psum_scatter(
            self_grad_values.astype(jnp.bfloat16), "seq", scatter_dimension=1, tiled=True
        )
        grad_projected = jnp.concatenate(
            [self_grad_queries.astype(jnp.bfloat16), own_self_keys, own_self_values], axis=-1
        )
        grad_qkv_weight = weight_grad(normed_one, grad_projected)
        grad_normed_one = project_back(grad_projected, back_qkv)
        grad_one, gain_one, shift_one = norm_backward(
            grad_normed_one, scaled_one, inverse_one, back_gain_float[:, 0]
        )
        hidden_grad = (grad_after_self + grad_one).astype(jnp.bfloat16)[:, None]
        grad_biases = jnp.stack(
            [
                column_sums(grad_projected[..., :model_width]),
                column_sums(grad_projected[..., 2 * model_width :]),
                column_sums(grad_self_branch),
                column_sums(grad_cross_queries),
                column_sums(grad_memory_kv[..., model_width:]),
                column_sums(grad_cross_branch),
                column_sums(grad_out),
            ],
            axis=1,
        )
        grad_gains = jnp.stack([gain_one, gain_two, gain_three], axis=1)
        grad_shifts = jnp.stack([shift_one, shift_two, shift_three], axis=1)
        attn_grads = (
            grad_qkv_weight,
            grad_self_out,
            grad_query_weight,
            grad_memory_weight,
            grad_cross_out,
            grad_biases,
            grad_gains,
            grad_shifts,
        )
        mlp_grads = (one_grad_fc_in, one_grad_fc_out, one_grad_fc_bias)
        hidden_out, hidden_grad, memory_grad, attn_grads, mlp_grads = (
            hidden_out,
            hidden_grad,
            memory_grad,
            attn_grads,
            mlp_grads,
        )
        outputs_list.append(hidden_out)
        grads_list.append(hidden_grad)
        memory_list.append(memory_grad)
        if attn_total is None:
            attn_total = attn_grads
            mlp_total = mlp_grads
        else:
            attn_total = jax.tree.map(jnp.add, attn_total, attn_grads)
            mlp_total = jax.tree.map(jnp.add, mlp_total, mlp_grads)
    grad_fc_in, grad_fc_out, grad_fc_bias = mlp_total
    (
        shard_qkv,
        shard_self_out,
        shard_query,
        shard_memory_kv,
        shard_cross_out,
        shard_biases,
        shard_gains,
        shard_shifts,
    ) = (
        lax.psum_scatter(
            attn_total[0].astype(jnp.bfloat16), "fsdp", scatter_dimension=0, tiled=True
        ).astype(jnp.float32),
        lax.psum_scatter(
            attn_total[1].astype(jnp.bfloat16), "fsdp", scatter_dimension=0, tiled=True
        ).astype(jnp.float32),
        lax.psum_scatter(
            attn_total[2].astype(jnp.bfloat16), "fsdp", scatter_dimension=0, tiled=True
        ).astype(jnp.float32),
        lax.psum_scatter(
            attn_total[3].astype(jnp.bfloat16), "fsdp", scatter_dimension=0, tiled=True
        ).astype(jnp.float32),
        lax.psum_scatter(
            attn_total[4].astype(jnp.bfloat16), "fsdp", scatter_dimension=0, tiled=True
        ).astype(jnp.float32),
        lax.psum_scatter(
            attn_total[5].astype(jnp.bfloat16), "fsdp", scatter_dimension=0, tiled=True
        ).astype(jnp.float32),
        lax.psum_scatter(
            attn_total[6].astype(jnp.bfloat16), "fsdp", scatter_dimension=0, tiled=True
        ).astype(jnp.float32),
        lax.psum_scatter(
            attn_total[7].astype(jnp.bfloat16), "fsdp", scatter_dimension=0, tiled=True
        ).astype(jnp.float32),
    )
    summed = (
        lax.psum(shard_qkv.astype(jnp.bfloat16), ("rep", "seq")).astype(jnp.float32),
        lax.psum(shard_self_out.astype(jnp.bfloat16), ("rep", "seq")).astype(jnp.float32),
        lax.psum(shard_query.astype(jnp.bfloat16), ("rep", "seq")).astype(jnp.float32),
        lax.psum(shard_memory_kv.astype(jnp.bfloat16), ("rep", "seq")).astype(jnp.float32),
        lax.psum(shard_cross_out.astype(jnp.bfloat16), ("rep", "seq")).astype(jnp.float32),
        lax.psum(grad_fc_in.astype(jnp.bfloat16), ("rep", "seq")).astype(jnp.float32),
        lax.psum(grad_fc_out.astype(jnp.bfloat16), ("rep", "seq")).astype(jnp.float32),
        lax.psum(shard_biases.astype(jnp.bfloat16), ("rep", "seq")).astype(jnp.float32),
        lax.psum(grad_fc_bias.astype(jnp.bfloat16), ("rep", "seq")).astype(jnp.float32),
        lax.psum(shard_gains.astype(jnp.bfloat16), ("rep", "seq")).astype(jnp.float32),
        lax.psum(shard_shifts.astype(jnp.bfloat16), ("rep", "seq")).astype(jnp.float32),
    )
    hidden_out = jnp.concatenate(outputs_list, axis=0)
    hidden_grad = jnp.concatenate(grads_list, axis=0)
    memory_grad = jnp.concatenate(memory_list, axis=0)
    return (
        hidden_out,
        hidden_grad,
        memory_grad,
        summed[0],
        summed[1],
        summed[2],
        summed[3],
        summed[4],
        summed[5],
        summed[6],
        summed[7],
        summed[8],
        summed[9],
        summed[10],
    )


def shift_rows(mine, other, core):
    low = jnp.where(core == 0, mine, other)
    high = jnp.where(core == 0, other, mine)
    return jnp.concatenate([low, high], axis=0)


def swap(values):
    return lax.ppermute(values, "fsdp", [(0, 1), (1, 0)])


def moves(turn):
    pairs = []
    for core in range(2):
        for place in range(4):
            odd = (place + turn) % 2
            pairs.append((core * 4 + place, (place // 2) * 4 + 2 * odd + core))
    return pairs


def bring(array, place):
    even = place % 2 == 0
    first = lax.ppermute(jnp.where(even, array[0], array[1]), ("fsdp", "seq"), moves(0))
    second = lax.ppermute(jnp.where(even, array[1], array[0]), ("fsdp", "seq"), moves(1))
    early = place < 2
    return jnp.concatenate(
        [jnp.where(early, first, second), jnp.where(early, second, first)], axis=0
    )


def send_back(rows, place):
    half = rows.shape[0] // 2
    early = place < 2
    even = place % 2 == 0
    one = jnp.where(early, rows[:half], rows[half:])
    two = jnp.where(early, rows[half:], rows[:half])
    back = [[(b, a) for a, b in moves(turn)] for turn in range(2)]
    one = lax.ppermute(one, ("fsdp", "seq"), back[0])
    two = lax.ppermute(two, ("fsdp", "seq"), back[1])
    return jnp.stack([jnp.where(even, one, two), jnp.where(even, two, one)], axis=0)


def mul(left, right):
    return jnp.dot(left, right, preferred_element_type=jnp.float32)


def mul_nt(left, right):
    return lax.dot_general(left, right, (((1,), (1,)), ((), ())), preferred_element_type=jnp.float32)


def mul_tn(left, right):
    return lax.dot_general(left, right, (((0,), (0,)), ((), ())), preferred_element_type=jnp.float32)


def half_of(values, core):
    width = values.shape[1] // 2
    return lax.dynamic_slice_in_dim(values, core * width, width, 1)


MESH = pl.DeviceIdType.MESH


def gelu_pair(values):
    depth = 1.0 + (0.3275911 * 2.0**-0.5) * jnp.abs(values)
    inv = pltpu.reciprocal(depth, approx=True)
    inv = inv * (2.0 - depth * inv)
    bell = jnp.exp(-0.5 * values * values)
    series = 0.7107068705 + inv * (-0.7265760135 + inv * 0.5307027145)
    series = inv * (0.127414796 + inv * (-0.142248368 + inv * series))
    tail = series * bell
    cumulative = jnp.where(values >= 0.0, 1.0 - tail, tail)
    return values * cumulative, cumulative + values * (bell * (1.0 / math.sqrt(2.0 * math.pi)))


def position():
    rep, core, deep = lax.axis_index("rep"), lax.axis_index("fsdp"), lax.axis_index("seq")
    return rep % 2, rep // 2, core, deep


def device(across, up, core, deep):
    return (up * 2 + across, core, deep)


def greet(partners):
    barrier = pltpu.get_barrier_semaphore()
    for partner in partners:
        pl.semaphore_signal(barrier, inc=1, device_id=partner, device_id_type=MESH)
    pl.semaphore_wait(barrier, len(partners))


class ChunkSum:
    def __init__(self, turned, column, width, own_ref, sum_ref, held, first, second, third, done, send, recv, local):
        across, up, core, deep = position()
        self.side, self.next = (up, across) if turned else (across, up)
        one = device(1 - across, up, core, deep)
        two = device(across, 1 - up, core, deep)
        self.one, self.two = (two, one) if turned else (one, two)
        self.deep = deep
        self.others = [(deep + step) % 4 for step in (1, 2, 3)]
        self.third_ids = [device(across, up, core, other) for other in self.others]
        self.columns = pl.ds(column, width)
        self.own, self.sum = own_ref, sum_ref
        self.held, self.first, self.second, self.third, self.done = held, first, second, third, done
        self.send, self.recv, self.local = send, recv, local
        self.quarter = pl.multiple_of(self.next * 128, 128)
        self.start_row = self.side * 256

    def remote(self, index, src, dst, target):
        return pltpu.make_async_remote_copy(
            src_ref=src,
            dst_ref=dst,
            send_sem=self.send.at[index],
            recv_sem=self.recv.at[index],
            device_id=target,
            device_id_type=MESH,
        )

    def rows(self, ref, start, count):
        return ref.at[pl.ds(pl.multiple_of(start, 32), count), self.columns]

    def copy_a(self):
        return self.remote(0, self.rows(self.own, (1 - self.side) * 256, 256), self.first, self.one)

    def load(self):
        return pltpu.make_async_copy(self.rows(self.own, self.start_row, 256), self.held, self.local.at[0])

    def copy_b(self):
        away = pl.multiple_of((1 - self.next) * 128, 128)
        return self.remote(1, self.held.at[pl.ds(away, 128)], self.second, self.two)

    def copy_c(self, turn):
        start = pl.multiple_of(self.quarter + self.others[turn] * 32, 32)
        return self.remote(2 + turn, self.held.at[pl.ds(start, 32)], self.third.at[turn], self.third_ids[turn])

    def place(self):
        return self.rows(self.sum, self.start_row + self.quarter + self.deep * 32, 32)

    def copy_d(self, turn):
        return self.remote(5 + turn, self.done, self.place(), self.third_ids[turn])

    def store(self):
        return pltpu.make_async_copy(self.done, self.place(), self.local.at[1])

    def copy_e(self):
        part = self.rows(self.sum, self.start_row + self.quarter, 128)
        return self.remote(8, part, part, self.two)

    def copy_f(self):
        part = self.rows(self.sum, self.start_row, 256)
        return self.remote(9, part, part, self.one)

    def stage(self, number):
        if number == 0:
            self.copy_a().start()
            self.load().start()
        elif number == 1:
            self.load().wait()
            self.copy_a().wait_recv()
            self.held[...] = self.held[...] + self.first[...]
            self.copy_b().start()
        elif number == 2:
            self.copy_b().wait_recv()
            self.copy_b().wait_send()
            mine = pl.ds(self.quarter, 128)
            self.held[mine] = self.held[mine] + self.second[...]
            for turn in range(3):
                self.copy_c(turn).start()
        elif number == 3:
            for turn in range(3):
                self.copy_c(turn).wait_recv()
            start = pl.multiple_of(self.quarter + self.deep * 32, 32)
            total = self.held[pl.ds(start, 32)].astype(jnp.float32)
            for turn in range(3):
                total += self.third[turn].astype(jnp.float32)
            self.done[...] = total.astype(self.done.dtype)
            self.store().start()
            for turn in range(3):
                self.copy_d(turn).start()
        elif number == 4:
            self.store().wait()
            for turn in range(3):
                self.copy_d(turn).wait_recv()
            self.copy_e().start()
        elif number == 5:
            self.copy_e().wait_recv()
            self.copy_f().start()
        elif number == 6:
            self.copy_f().wait_recv()
            self.copy_a().wait_send()
            for turn in range(3):
                self.copy_c(turn).wait_send()
                self.copy_d(turn).wait_send()
            self.copy_e().wait_send()
            self.copy_f().wait_send()


AFTER = (0, 5, 8, 12, 16, 19, 24)


def ffn_kernel(
    step, plan, rows_ref, grads_ref, in_ref, out_ref, bias_ref, own_ref,
    din_ref, dout_ref, dbias_ref, sum_ref, flip, acc, us, das, *rest
):
    units = flip.shape[0]
    steps = rows_ref.shape[0] // step
    at = pl.program_id(0)
    send, recv, local = rest[-3:]
    buffers = rest[:-3]
    chunks = []
    for index, (turned, column, width, begin) in enumerate(plan):
        held, first, second, third, done = buffers[5 * index : 5 * index + 5]
        chunks.append(
            ChunkSum(turned, column, width, own_ref, sum_ref, held, first, second, third, done,
                     send.at[index], recv.at[index], local.at[index])
        )

    @pl.when(at == 0)
    def _():
        across, up, core, deep = position()
        greet(
            [device(1 - across, up, core, deep), device(across, 1 - up, core, deep)]
            + [device(across, up, core, (deep + turn) % 4) for turn in (1, 2, 3)]
        )

    def traffic(turn):
        work = {}
        for chunk, (_, _, _, begin) in zip(chunks, plan):
            for number, after in enumerate(AFTER):
                slot = begin + after
                if slot % steps == turn:
                    work.setdefault(slot // steps, []).append((chunk, number))
        for when, jobs in sorted(work.items()):
            @pl.when(at == when)
            def _():
                for chunk, number in jobs:
                    chunk.stage(number)

    flip[...] = in_ref[...].T

    def front(turn):
        part = pl.ds(turn * step, step)
        us[turn % 2] = mul_nt(flip[...], rows_ref[part, :])
        das[turn % 2] = mul_nt(out_ref[...], grads_ref[part, :])

    traffic(0)
    front(0)
    bias = jnp.broadcast_to(bias_ref[...], (128, units)).T[:, :1]
    total = jnp.zeros((units, 128), jnp.float32)
    for turn in range(steps):
        if turn:
            traffic(turn)
        if turn + 1 < steps:
            front(turn + 1)
        active, slope = gelu_pair(us[turn % 2] + bias)
        active = active.astype(jnp.bfloat16)
        inner = (das[turn % 2] * slope).astype(jnp.bfloat16)
        for lane in range(step // 128):
            total += inner[:, lane * 128 : (lane + 1) * 128].astype(jnp.float32)
        part = pl.ds(turn * step, step)
        if turn == 0:
            dout_ref[...] = mul(active, grads_ref[part, :])
            acc[...] = mul(inner, rows_ref[part, :])
        else:
            dout_ref[...] += mul(active, grads_ref[part, :])
            acc[...] += mul(inner, rows_ref[part, :])
    din_ref[...] = acc[...].T
    dbias_ref[...] = jnp.sum(total.T, axis=0, keepdims=True)


def ffn_grads(rows, grads, fc_in, fc_out, bias, own):
    count, width = rows.shape
    hidden = fc_in.shape[1]
    units, step = 256, 1024
    plan = [(False, 8 * width, 128, 0)]
    for pair in range(4):
        plan.append((False, pair * width, width, 1 + 10 * pair))
        plan.append((True, (4 + pair) * width, width, 1 + 10 * pair))
    buffers = []
    for _, _, columns, _ in plan:
        buffers += [
            pltpu.VMEM((256, columns), jnp.bfloat16),
            pltpu.VMEM((256, columns), jnp.bfloat16),
            pltpu.VMEM((128, columns), jnp.bfloat16),
            pltpu.VMEM((3, 32, columns), jnp.bfloat16),
            pltpu.VMEM((32, columns), jnp.bfloat16),
        ]
    whole = functools.partial(pl.BlockSpec, pipeline_mode=pl.Buffered(1))
    return pl.pallas_call(
        functools.partial(ffn_kernel, step, plan),
        grid=(hidden // units,),
        in_specs=[
            whole((count, width), lambda at: (0, 0)),
            whole((count, width), lambda at: (0, 0)),
            pl.BlockSpec((width, units), lambda at: (0, at)),
            pl.BlockSpec((units, width), lambda at: (at, 0)),
            pl.BlockSpec((1, units), lambda at: (0, at)),
            pl.BlockSpec(memory_space=pl.ANY),
        ],
        out_specs=[
            pl.BlockSpec((width, units), lambda at: (0, at)),
            pl.BlockSpec((units, width), lambda at: (at, 0)),
            pl.BlockSpec((1, units), lambda at: (0, at)),
            pl.BlockSpec(memory_space=pl.ANY),
        ],
        out_shape=[
            jax.ShapeDtypeStruct((width, hidden), jnp.float32),
            jax.ShapeDtypeStruct((hidden, width), jnp.float32),
            jax.ShapeDtypeStruct((1, hidden), jnp.float32),
            jax.ShapeDtypeStruct(own.shape, own.dtype),
        ],
        scratch_shapes=[
            pltpu.VMEM((units, width), jnp.bfloat16),
            pltpu.VMEM((units, width), jnp.float32),
            pltpu.VMEM((2, units, step), jnp.float32),
            pltpu.VMEM((2, units, step), jnp.float32),
            *buffers,
            pltpu.SemaphoreType.DMA((len(plan), 10)),
            pltpu.SemaphoreType.DMA((len(plan), 10)),
            pltpu.SemaphoreType.DMA((len(plan), 2)),
        ],
        compiler_params=pltpu.CompilerParams(
            vmem_limit_bytes=58 * 2**20, collective_id=0, has_side_effects=True
        ),
        cost_estimate=pl.CostEstimate(
            flops=8 * count * width * hidden,
            bytes_accessed=4 * count * width + 12 * width * hidden,
            transcendentals=count * hidden,
        ),
    )(rows, grads, fc_in, fc_out, bias, own)


def fast_body(
    hidden_in,
    memory,
    segment_ids,
    memory_ids,
    out_grad,
    self_qkv,
    self_out,
    cross_query,
    cross_kv,
    cross_out,
    fc_in,
    fc_out,
    biases,
    fc_in_bias,
    norm_gains,
    norm_shifts,
):
    width = hidden_in.shape[-1]
    core = lax.axis_index("fsdp")
    place = lax.axis_index("seq")
    bf16, f32 = jnp.bfloat16, jnp.float32

    x_own = bring(hidden_in[:, 0], place)
    x_all = shift_rows(x_own, swap(x_own), core)
    memory_own = bring(memory[:, 0], place)
    memory_all = shift_rows(memory_own, swap(memory_own), core)
    grad_own = bring(out_grad[:, 0], place)
    grad_chip = shift_rows(grad_own, swap(grad_own), core)
    grad_every = lax.all_gather(grad_own, ("rep", "seq", "fsdp"), axis=0, tiled=True)

    micro, owner = place // 2, place % 2
    ids = jnp.stack([segment_ids[:, 0], memory_ids[:, 0]])
    ids_other = swap(ids)
    ids = jnp.where(owner == core, ids, ids_other)
    ids = lax.dynamic_index_in_dim(ids, micro, 1, keepdims=False)
    token_ids, source_ids = ids[0], ids[1]
    own_count = x_own.shape[0]
    query_place = core * own_count + jnp.arange(own_count, dtype=jnp.int32)
    key_place = jnp.arange(token_ids.shape[0], dtype=jnp.int32)
    query_ids = lax.dynamic_slice_in_dim(token_ids, core * own_count, own_count, 0)
    self_allowed = (query_place[:, None] >= key_place[None, :]) & (
        query_ids[:, None] == token_ids[None, :]
    )
    cross_allowed = query_ids[:, None] == source_ids[None, :]
    self_allowed, cross_allowed = self_allowed[None], cross_allowed[None]

    def whole(shard):
        return shift_rows(shard, swap(shard), core)

    qkv = whole(self_qkv)
    w_self_out = whole(self_out)
    w_query = whole(cross_query)
    w_memory_kv = whole(cross_kv)
    w_cross_out = whole(cross_out)
    small = whole(jnp.concatenate([biases, norm_gains, norm_shifts], axis=1)).astype(f32)
    bias = small[:, :7].T
    gain = small[:, 7:10].T
    shift = small[:, 10:13].T

    def lift(values):
        return split_heads(values)[None]

    normed_one_all, scaled_all, inverse_all = norm_forward(x_all.astype(f32), gain[0], shift[0])
    normed_one_all = normed_one_all.astype(bf16)

    def own_rows(values):
        return lax.dynamic_slice_in_dim(values, core * own_count, own_count, 0)

    normed_one = own_rows(normed_one_all)
    scaled_one, inverse_one = own_rows(scaled_all), own_rows(inverse_all)
    hidden = x_own.astype(f32)
    queries = (mul(normed_one, qkv[:, :width]) + bias[0]).astype(bf16)
    key_rows = mul(normed_one_all, qkv[:, width : 2 * width]).astype(bf16)
    value_rows = (mul(normed_one_all, qkv[:, 2 * width :]) + bias[1]).astype(bf16)
    queries, key_rows, value_rows = lift(queries), lift(key_rows), lift(value_rows)
    self_mixed, self_totals = attend_forward(queries, key_rows, value_rows, self_allowed)
    after_self = hidden + mul(self_mixed[0], w_self_out) + bias[2]
    normed_two, scaled_two, inverse_two = norm_forward(after_self, gain[1], shift[1])
    normed_two = normed_two.astype(bf16)
    cross_queries = lift((mul(normed_two, w_query) + bias[3]).astype(bf16))
    memory_kv = mul(memory_all, w_memory_kv)
    memory_keys = lift(memory_kv[:, :width].astype(bf16))
    memory_values = lift((memory_kv[:, width:] + bias[4]).astype(bf16))
    cross_mixed, cross_totals = attend_forward(
        cross_queries, memory_keys, memory_values, cross_allowed
    )
    after_cross = after_self + mul(cross_mixed[0], w_cross_out) + bias[5]
    normed_three, scaled_three, inverse_three = norm_forward(after_cross, gain[2], shift[2])
    normed_three = normed_three.astype(bf16)
    normed_chip = shift_rows(normed_three, swap(normed_three), core)
    normed_every = lax.all_gather(normed_three, ("rep", "seq", "fsdp"), axis=0, tiled=True)

    fc_bias = fc_in_bias.astype(f32)
    inner = mul(normed_chip, fc_in) + fc_bias
    active = jax.nn.gelu(inner, approximate=False).astype(bf16)
    grad_inner = (mul_nt(grad_chip, fc_out) * gelu_slope(inner)).astype(bf16)
    partial_out = mul(active, fc_out).astype(bf16)
    partial_grad = mul_nt(grad_inner, fc_in).astype(bf16)
    both = jnp.stack([partial_out, partial_grad])
    mine = lax.dynamic_slice_in_dim(both, core * own_count, own_count, 1)
    theirs = lax.dynamic_slice_in_dim(both, (1 - core) * own_count, own_count, 1)
    sums = mine.astype(f32) + swap(theirs).astype(f32)
    hidden_out = (after_cross + sums[0] + bias[6]).astype(bf16)

    def back_norm(grad_normed, scaled, inverse, row):
        grad, gain_grad, shift_grad = norm_backward(
            grad_normed[None], scaled[None], inverse[None], gain[row]
        )
        return grad[0], gain_grad, shift_grad

    grad_three, gain_three, shift_three = back_norm(sums[1], scaled_three, inverse_three, 2)
    grad_after_cross = grad_own.astype(f32) + grad_three
    cross_branch = grad_after_cross.astype(bf16)
    grad_cross_mixed = mul_nt(cross_branch, w_cross_out).astype(bf16)
    dq2, dk2, dv2 = attend_backward(
        cross_queries, memory_keys, memory_values, cross_allowed, cross_totals, lift(grad_cross_mixed)
    )
    dq2 = dq2[0].astype(bf16)
    dc2 = jnp.concatenate([dk2[0], dv2[0]], axis=1).astype(bf16)
    dc2 = (dc2.astype(f32) + swap(dc2).astype(f32)).astype(bf16)
    grad_two, gain_two, shift_two = back_norm(mul_nt(dq2, w_query), scaled_two, inverse_two, 1)
    grad_after_self = grad_after_cross + grad_two
    self_branch = grad_after_self.astype(bf16)
    grad_self_mixed = mul_nt(self_branch, w_self_out).astype(bf16)
    dq1, dk1, dv1 = attend_backward(
        queries, key_rows, value_rows, self_allowed, self_totals, lift(grad_self_mixed)
    )
    dq1 = dq1[0].astype(bf16)
    dkv1 = jnp.concatenate([dk1[0], dv1[0]], axis=1).astype(bf16)
    dkv1 = (dkv1.astype(f32) + swap(dkv1).astype(f32)).astype(bf16)
    grad_projected = jnp.concatenate([dq1, own_rows(dkv1)], axis=1)
    grad_one, gain_one, shift_one = back_norm(
        mul_nt(grad_projected, qkv), scaled_one, inverse_one, 0
    )
    hidden_grad = (grad_after_self + grad_one).astype(bf16)
    memory_grad = mul_nt(own_rows(dc2), w_memory_kv).astype(bf16)

    def chip_rows(values):
        return shift_rows(values, swap(values), core)

    def input_half(values):
        mine = half_of(values, core)
        theirs = half_of(values, 1 - core)
        return shift_rows(mine, swap(theirs), core)

    dq1_all = chip_rows(dq1)
    dp1_all = jnp.concatenate([dq1_all, dkv1], axis=1)
    self_all, dq2_all, cross_all = chip_rows(self_branch), chip_rows(dq2), chip_rows(cross_branch)
    grads = jnp.concatenate(
        [
            mul_tn(half_of(normed_one_all, core), dp1_all).astype(bf16),
            mul_tn(input_half(self_mixed[0]), self_all).astype(bf16),
            mul_tn(input_half(normed_two), dq2_all).astype(bf16),
            mul_tn(half_of(memory_all, core), dc2).astype(bf16),
            mul_tn(input_half(cross_mixed[0]), cross_all).astype(bf16),
        ],
        axis=1,
    )

    def sums_of(values):
        return jnp.sum(half_of(values, core).astype(f32), axis=0)

    gains = jnp.stack([gain_one, gain_two, gain_three, shift_one, shift_two, shift_three])
    gains = half_of(gains, core) + swap(half_of(gains, 1 - core))
    column = jnp.concatenate(
        [
            jnp.stack(
                [
                    sums_of(dq1_all),
                    sums_of(dkv1[:, width:]),
                    sums_of(self_all),
                    sums_of(dq2_all),
                    sums_of(dc2[:, width:]),
                    sums_of(cross_all),
                    sums_of(grad_chip),
                ]
            ),
            gains,
        ]
    )

    column = jnp.pad(column.T, ((0, 0), (0, 128 - column.shape[0]))).astype(bf16)
    grads = jnp.concatenate([grads, column], axis=1)
    grad_fc_in, grad_fc_out, grad_fc_bias, grads = ffn_grads(
        normed_every, grad_every, fc_in, fc_out, fc_bias[None], grads
    )
    grads = grads.astype(f32)
    column = grads[:, 8 * width :]
    return (
        send_back(hidden_out, place)[:, None],
        send_back(hidden_grad, place)[:, None],
        send_back(memory_grad, place)[:, None],
        grads[:, : 3 * width],
        grads[:, 3 * width : 4 * width],
        grads[:, 4 * width : 5 * width],
        grads[:, 5 * width : 7 * width],
        grads[:, 7 * width : 8 * width],
        grad_fc_in,
        grad_fc_out,
        column[:, :7],
        grad_fc_bias[0],
        column[:, 7:10],
        column[:, 10:13],
    )


def solution(mesh):
    fits = mesh.shape["fsdp"] == 2 and mesh.shape["seq"] == 4
    chosen = fast_body if fits else body
    return jax.shard_map(
        chosen,
        mesh=mesh,
        in_specs=(
            P(None, ("rep", "fsdp"), "seq", None),
            P(None, ("rep", "fsdp"), "seq", None),
            P(None, ("rep", "fsdp"), None),
            P(None, ("rep", "fsdp"), None),
            P(None, ("rep", "fsdp"), "seq", None),
            P("fsdp", None),
            P("fsdp", None),
            P("fsdp", None),
            P("fsdp", None),
            P("fsdp", None),
            P(None, "fsdp"),
            P("fsdp", None),
            P("fsdp", None),
            P("fsdp"),
            P("fsdp", None),
            P("fsdp", None),
        ),
        out_specs=(
            P(None, ("rep", "fsdp"), "seq", None),
            P(None, ("rep", "fsdp"), "seq", None),
            P(None, ("rep", "fsdp"), "seq", None),
            P("fsdp", None),
            P("fsdp", None),
            P("fsdp", None),
            P("fsdp", None),
            P("fsdp", None),
            P(None, "fsdp"),
            P("fsdp", None),
            P("fsdp", None),
            P("fsdp"),
            P("fsdp", None),
            P("fsdp", None),
        ),
        check_vma=False,
    )
```

```python
import functools
import math

import jax
import jax.numpy as jnp
from jax import lax
from jax.experimental import pallas as pl
from jax.experimental.pallas import tpu as pltpu
from jax.sharding import PartitionSpec as P

HEAD = 64


NORM_EPSILON = 1e-05
MASKED_SCORE = -1e30


def norm_forward(values, norm_gain, norm_shift):
    average = jnp.mean(values, axis=-1, keepdims=True)
    centred = values - average
    inverse = lax.rsqrt(jnp.mean(centred * centred, axis=-1, keepdims=True) + NORM_EPSILON)
    scaled = centred * inverse
    return (scaled * norm_gain + norm_shift, scaled, inverse)


def norm_backward(grad_normed, scaled, inverse, norm_gain):
    grad_scaled = grad_normed * norm_gain
    first_mean = jnp.mean(grad_scaled, axis=-1, keepdims=True)
    second_mean = jnp.mean(grad_scaled * scaled, axis=-1, keepdims=True)
    grad_values = (grad_scaled - first_mean - scaled * second_mean) * inverse
    gain_grad = jnp.sum(grad_normed * scaled, axis=(0, 1))
    shift_grad = jnp.sum(grad_normed, axis=(0, 1))
    return (grad_values, gain_grad, shift_grad)


def split_heads(values):
    return values.reshape(values.shape[:-1] + (values.shape[-1] // HEAD, HEAD))


def join_heads(values):
    return values.reshape(values.shape[:2] + (values.shape[2] * values.shape[3],))


def masked_scores(queries, key_rows, allowed):
    raw_scores = jnp.einsum(
        "mqhe,mkhe->mhqk", queries, key_rows, preferred_element_type=jnp.float32
    )
    return jnp.where(allowed[:, None], raw_scores * HEAD ** (-0.5), MASKED_SCORE)


def attend_forward(queries, key_rows, value_rows, allowed):
    scores = masked_scores(queries, key_rows, allowed)
    highest = jnp.max(scores, axis=-1, keepdims=True)
    exponent = jnp.exp(scores - highest)
    row_totals = jnp.sum(exponent, axis=-1, keepdims=True)
    weights = (exponent / row_totals).astype(jnp.bfloat16)
    joined = jnp.einsum("mhqk,mkhe->mqhe", weights, value_rows, preferred_element_type=jnp.float32)
    return (join_heads(joined).astype(jnp.bfloat16), highest + jnp.log(row_totals))


def attend_backward(queries, key_rows, value_rows, allowed, log_totals, grad_joined):
    scores = masked_scores(queries, key_rows, allowed)
    probability = jnp.exp(scores - log_totals)
    weights = probability.astype(jnp.bfloat16)
    grad_value_rows = jnp.einsum(
        "mhqk,mqhe->mkhe", weights, grad_joined, preferred_element_type=jnp.float32
    )
    grad_weights = jnp.einsum(
        "mqhe,mkhe->mhqk", grad_joined, value_rows, preferred_element_type=jnp.float32
    )
    grad_scores = probability * (
        grad_weights - jnp.sum(grad_weights * probability, axis=-1, keepdims=True)
    )
    grad_scores = grad_scores.astype(jnp.bfloat16)
    grad_queries = jnp.einsum(
        "mhqk,mkhe->mqhe", grad_scores, key_rows, preferred_element_type=jnp.float32
    ) * HEAD ** (-0.5)
    grad_key_rows = jnp.einsum(
        "mhqk,mqhe->mkhe", grad_scores, queries, preferred_element_type=jnp.float32
    ) * HEAD ** (-0.5)
    return (join_heads(grad_queries), join_heads(grad_key_rows), join_heads(grad_value_rows))


def gelu_slope(values):
    cumulative = 0.5 * (1.0 + lax.erf(values * 2.0 ** (-0.5)))
    density = jnp.exp(-0.5 * values * values) / math.sqrt(2.0 * math.pi)
    return cumulative + values * density


def feed_forward(rows, weight_in, bias_in, weight_out):
    pre_active = jnp.einsum(
        "mtd,df->mtf", rows, weight_in, preferred_element_type=jnp.float32
    ) + bias_in.astype(jnp.float32)
    active = jax.nn.gelu(pre_active, approximate=False).astype(jnp.bfloat16)
    partial_out = jnp.einsum("mtf,fd->mtd", active, weight_out, preferred_element_type=jnp.float32)
    return (pre_active, active, partial_out)


def feed_back(rows, grad_rows, pre_active, active, weight_in, weight_out):
    grad_active = jnp.einsum(
        "mtd,fd->mtf", grad_rows, weight_out, preferred_element_type=jnp.float32
    )
    grad_inner = (grad_active * gelu_slope(pre_active)).astype(jnp.bfloat16)
    grad_weight_out = jnp.einsum(
        "mtf,mtd->fd", active, grad_rows, preferred_element_type=jnp.float32
    )
    grad_weight_in = jnp.einsum("mtd,mtf->df", rows, grad_inner, preferred_element_type=jnp.float32)
    grad_bias_in = jnp.sum(grad_inner.astype(jnp.float32), axis=(0, 1))
    grad_rows_in = jnp.einsum(
        "mtf,df->mtd", grad_inner, weight_in, preferred_element_type=jnp.float32
    )
    return (grad_weight_in, grad_weight_out, grad_bias_in, grad_rows_in)


def project(rows, weight):
    return jnp.einsum("mtd,de->mte", rows, weight, preferred_element_type=jnp.float32)


def project_back(grad_rows, weight):
    return jnp.einsum("mte,de->mtd", grad_rows, weight, preferred_element_type=jnp.float32)


def weight_grad(rows, grad_rows):
    return jnp.einsum("mtd,mte->de", rows, grad_rows, preferred_element_type=jnp.float32)


def column_sums(grad_rows):
    return jnp.sum(grad_rows.astype(jnp.float32), axis=(0, 1))


def body(
    hidden_in,
    memory,
    segment_ids,
    memory_ids,
    out_grad,
    self_qkv,
    self_out,
    cross_query,
    cross_kv,
    cross_out,
    fc_in,
    fc_out,
    biases,
    fc_in_bias,
    norm_gains,
    norm_shifts,
):
    micro_count, single, tokens, model_width = hidden_in.shape
    seq_index = lax.axis_index("seq")
    zero_row = jnp.zeros((model_width,), jnp.float32)
    outputs_list = []
    grads_list = []
    memory_list = []
    attn_total = None
    mlp_total = None
    for micro in range(micro_count):
        full_qkv = lax.all_gather(self_qkv, "fsdp", axis=0, tiled=True)
        full_self_out = lax.all_gather(self_out, "fsdp", axis=0, tiled=True)
        full_query = lax.all_gather(cross_query, "fsdp", axis=0, tiled=True)
        full_memory_kv = lax.all_gather(cross_kv, "fsdp", axis=0, tiled=True)
        full_cross_out = lax.all_gather(cross_out, "fsdp", axis=0, tiled=True)
        full_biases = lax.all_gather(biases, "fsdp", axis=0, tiled=True)
        full_gains = lax.all_gather(norm_gains, "fsdp", axis=0, tiled=True)
        full_shifts = lax.all_gather(norm_shifts, "fsdp", axis=0, tiled=True)
        bias_float = full_biases.astype(jnp.float32)
        gain_float = full_gains.astype(jnp.float32)
        shift_float = full_shifts.astype(jnp.float32)
        hidden = hidden_in[micro : micro + 1][:, 0].astype(jnp.float32)
        memory_rows = memory[micro : micro + 1][:, 0]
        token_ids = segment_ids[micro : micro + 1][:, 0]
        source_ids = memory_ids[micro : micro + 1][:, 0]
        query_ids = lax.dynamic_slice_in_dim(token_ids, seq_index * tokens, tokens, 1)
        query_place = seq_index * tokens + jnp.arange(tokens, dtype=jnp.int32)
        key_place = jnp.arange(token_ids.shape[1], dtype=jnp.int32)
        self_allowed = (query_place[:, None] >= key_place[None, :])[None] & (
            query_ids[:, :, None] == token_ids[:, None, :]
        )
        cross_allowed = query_ids[:, :, None] == source_ids[:, None, :]
        normed_one, scaled_one, inverse_one = norm_forward(
            hidden, gain_float[:, 0], shift_float[:, 0]
        )
        normed_one = normed_one.astype(jnp.bfloat16)
        qkv_bias = jnp.concatenate([bias_float[:, 0], zero_row, bias_float[:, 1]])
        projected = (project(normed_one, full_qkv) + qkv_bias).astype(jnp.bfloat16)
        self_queries = split_heads(projected[..., :model_width])
        kv_all = lax.all_gather(projected[..., model_width:], "seq", axis=1, tiled=True)
        self_key_rows = split_heads(kv_all[..., :model_width])
        self_value_rows = split_heads(kv_all[..., model_width:])
        self_mixed, self_totals = attend_forward(
            self_queries, self_key_rows, self_value_rows, self_allowed
        )
        after_self = hidden + project(self_mixed, full_self_out) + bias_float[:, 2]
        normed_two, scaled_two, inverse_two = norm_forward(
            after_self, gain_float[:, 1], shift_float[:, 1]
        )
        normed_two = normed_two.astype(jnp.bfloat16)
        cross_queries = (project(normed_two, full_query) + bias_float[:, 3]).astype(jnp.bfloat16)
        memory_bias = jnp.concatenate([zero_row, bias_float[:, 4]])
        memory_kv = (project(memory_rows, full_memory_kv) + memory_bias).astype(jnp.bfloat16)
        memory_all = lax.all_gather(memory_kv, "seq", axis=1, tiled=True)
        memory_key_rows = split_heads(memory_all[..., :model_width])
        memory_value_rows = split_heads(memory_all[..., model_width:])
        cross_mixed, cross_totals = attend_forward(
            split_heads(cross_queries), memory_key_rows, memory_value_rows, cross_allowed
        )
        after_cross = after_self + project(cross_mixed, full_cross_out) + bias_float[:, 5]
        normed_three, scaled_three, inverse_three = norm_forward(
            after_cross, gain_float[:, 2], shift_float[:, 2]
        )
        normed_three = normed_three.astype(jnp.bfloat16)
        grad_out = out_grad[micro : micro + 1][:, 0]
        mlp_inputs = lax.all_gather(normed_three, "fsdp", axis=0, tiled=True)
        pre_active, active, partial_out = feed_forward(mlp_inputs, fc_in, fc_in_bias, fc_out)
        mlp_branch = lax.psum_scatter(
            partial_out.astype(jnp.bfloat16), "fsdp", scatter_dimension=0, tiled=True
        ).astype(jnp.float32)
        output = after_cross + mlp_branch + bias_float[:, 6]
        hidden_out = output.astype(jnp.bfloat16)[:, None]
        back_qkv = lax.all_gather(self_qkv, "fsdp", axis=0, tiled=True)
        back_self_out = lax.all_gather(self_out, "fsdp", axis=0, tiled=True)
        back_query = lax.all_gather(cross_query, "fsdp", axis=0, tiled=True)
        back_memory_kv = lax.all_gather(cross_kv, "fsdp", axis=0, tiled=True)
        back_cross_out = lax.all_gather(cross_out, "fsdp", axis=0, tiled=True)
        back_gains = lax.all_gather(norm_gains, "fsdp", axis=0, tiled=True)
        back_gain_float = back_gains.astype(jnp.float32)
        grad_gathered = lax.all_gather(grad_out, "fsdp", axis=0, tiled=True)
        one_grad_fc_in, one_grad_fc_out, one_grad_fc_bias, grad_partial = feed_back(
            mlp_inputs, grad_gathered, pre_active, active, fc_in, fc_out
        )
        grad_normed_three = lax.psum_scatter(
            grad_partial.astype(jnp.bfloat16), "fsdp", scatter_dimension=0, tiled=True
        ).astype(jnp.float32)
        grad_three, gain_three, shift_three = norm_backward(
            grad_normed_three, scaled_three, inverse_three, back_gain_float[:, 2]
        )
        grad_after_cross = grad_out.astype(jnp.float32) + grad_three
        grad_cross_branch = grad_after_cross.astype(jnp.bfloat16)
        grad_cross_out = weight_grad(cross_mixed, grad_cross_branch)
        grad_cross_mixed = project_back(grad_cross_branch, back_cross_out).astype(jnp.bfloat16)
        cross_grad_queries, memory_grad_keys, memory_grad_values = attend_backward(
            split_heads(cross_queries),
            memory_key_rows,
            memory_value_rows,
            cross_allowed,
            cross_totals,
            split_heads(grad_cross_mixed),
        )
        own_memory_keys = lax.psum_scatter(
            memory_grad_keys.astype(jnp.bfloat16), "seq", scatter_dimension=1, tiled=True
        )
        own_memory_values = lax.psum_scatter(
            memory_grad_values.astype(jnp.bfloat16), "seq", scatter_dimension=1, tiled=True
        )
        grad_memory_kv = jnp.concatenate([own_memory_keys, own_memory_values], axis=-1)
        grad_memory_weight = weight_grad(memory_rows, grad_memory_kv)
        memory_grad = project_back(grad_memory_kv, back_memory_kv).astype(jnp.bfloat16)[:, None]
        grad_cross_queries = cross_grad_queries.astype(jnp.bfloat16)
        grad_query_weight = weight_grad(normed_two, grad_cross_queries)
        grad_normed_two = project_back(grad_cross_queries, back_query)
        grad_two, gain_two, shift_two = norm_backward(
            grad_normed_two, scaled_two, inverse_two, back_gain_float[:, 1]
        )
        grad_after_self = grad_after_cross + grad_two
        grad_self_branch = grad_after_self.astype(jnp.bfloat16)
        grad_self_out = weight_grad(self_mixed, grad_self_branch)
        grad_self_mixed = project_back(grad_self_branch, back_self_out).astype(jnp.bfloat16)
        self_grad_queries, self_grad_keys, self_grad_values = attend_backward(
            self_queries,
            self_key_rows,
            self_value_rows,
            self_allowed,
            self_totals,
            split_heads(grad_self_mixed),
        )
        own_self_keys = lax.psum_scatter(
            self_grad_keys.astype(jnp.bfloat16), "seq", scatter_dimension=1, tiled=True
        )
        own_self_values = lax.psum_scatter(
            self_grad_values.astype(jnp.bfloat16), "seq", scatter_dimension=1, tiled=True
        )
        grad_projected = jnp.concatenate(
            [self_grad_queries.astype(jnp.bfloat16), own_self_keys, own_self_values], axis=-1
        )
        grad_qkv_weight = weight_grad(normed_one, grad_projected)
        grad_normed_one = project_back(grad_projected, back_qkv)
        grad_one, gain_one, shift_one = norm_backward(
            grad_normed_one, scaled_one, inverse_one, back_gain_float[:, 0]
        )
        hidden_grad = (grad_after_self + grad_one).astype(jnp.bfloat16)[:, None]
        grad_biases = jnp.stack(
            [
                column_sums(grad_projected[..., :model_width]),
                column_sums(grad_projected[..., 2 * model_width :]),
                column_sums(grad_self_branch),
                column_sums(grad_cross_queries),
                column_sums(grad_memory_kv[..., model_width:]),
                column_sums(grad_cross_branch),
                column_sums(grad_out),
            ],
            axis=1,
        )
        grad_gains = jnp.stack([gain_one, gain_two, gain_three], axis=1)
        grad_shifts = jnp.stack([shift_one, shift_two, shift_three], axis=1)
        attn_grads = (
            grad_qkv_weight,
            grad_self_out,
            grad_query_weight,
            grad_memory_weight,
            grad_cross_out,
            grad_biases,
            grad_gains,
            grad_shifts,
        )
        mlp_grads = (one_grad_fc_in, one_grad_fc_out, one_grad_fc_bias)
        hidden_out, hidden_grad, memory_grad, attn_grads, mlp_grads = (
            hidden_out,
            hidden_grad,
            memory_grad,
            attn_grads,
            mlp_grads,
        )
        outputs_list.append(hidden_out)
        grads_list.append(hidden_grad)
        memory_list.append(memory_grad)
        if attn_total is None:
            attn_total = attn_grads
            mlp_total = mlp_grads
        else:
            attn_total = jax.tree.map(jnp.add, attn_total, attn_grads)
            mlp_total = jax.tree.map(jnp.add, mlp_total, mlp_grads)
    grad_fc_in, grad_fc_out, grad_fc_bias = mlp_total
    (
        shard_qkv,
        shard_self_out,
        shard_query,
        shard_memory_kv,
        shard_cross_out,
        shard_biases,
        shard_gains,
        shard_shifts,
    ) = (
        lax.psum_scatter(
            attn_total[0].astype(jnp.bfloat16), "fsdp", scatter_dimension=0, tiled=True
        ).astype(jnp.float32),
        lax.psum_scatter(
            attn_total[1].astype(jnp.bfloat16), "fsdp", scatter_dimension=0, tiled=True
        ).astype(jnp.float32),
        lax.psum_scatter(
            attn_total[2].astype(jnp.bfloat16), "fsdp", scatter_dimension=0, tiled=True
        ).astype(jnp.float32),
        lax.psum_scatter(
            attn_total[3].astype(jnp.bfloat16), "fsdp", scatter_dimension=0, tiled=True
        ).astype(jnp.float32),
        lax.psum_scatter(
            attn_total[4].astype(jnp.bfloat16), "fsdp", scatter_dimension=0, tiled=True
        ).astype(jnp.float32),
        lax.psum_scatter(
            attn_total[5].astype(jnp.bfloat16), "fsdp", scatter_dimension=0, tiled=True
        ).astype(jnp.float32),
        lax.psum_scatter(
            attn_total[6].astype(jnp.bfloat16), "fsdp", scatter_dimension=0, tiled=True
        ).astype(jnp.float32),
        lax.psum_scatter(
            attn_total[7].astype(jnp.bfloat16), "fsdp", scatter_dimension=0, tiled=True
        ).astype(jnp.float32),
    )
    summed = (
        lax.psum(shard_qkv.astype(jnp.bfloat16), ("rep", "seq")).astype(jnp.float32),
        lax.psum(shard_self_out.astype(jnp.bfloat16), ("rep", "seq")).astype(jnp.float32),
        lax.psum(shard_query.astype(jnp.bfloat16), ("rep", "seq")).astype(jnp.float32),
        lax.psum(shard_memory_kv.astype(jnp.bfloat16), ("rep", "seq")).astype(jnp.float32),
        lax.psum(shard_cross_out.astype(jnp.bfloat16), ("rep", "seq")).astype(jnp.float32),
        lax.psum(grad_fc_in.astype(jnp.bfloat16), ("rep", "seq")).astype(jnp.float32),
        lax.psum(grad_fc_out.astype(jnp.bfloat16), ("rep", "seq")).astype(jnp.float32),
        lax.psum(shard_biases.astype(jnp.bfloat16), ("rep", "seq")).astype(jnp.float32),
        lax.psum(grad_fc_bias.astype(jnp.bfloat16), ("rep", "seq")).astype(jnp.float32),
        lax.psum(shard_gains.astype(jnp.bfloat16), ("rep", "seq")).astype(jnp.float32),
        lax.psum(shard_shifts.astype(jnp.bfloat16), ("rep", "seq")).astype(jnp.float32),
    )
    hidden_out = jnp.concatenate(outputs_list, axis=0)
    hidden_grad = jnp.concatenate(grads_list, axis=0)
    memory_grad = jnp.concatenate(memory_list, axis=0)
    return (
        hidden_out,
        hidden_grad,
        memory_grad,
        summed[0],
        summed[1],
        summed[2],
        summed[3],
        summed[4],
        summed[5],
        summed[6],
        summed[7],
        summed[8],
        summed[9],
        summed[10],
    )


def shift_rows(mine, other, core):
    low = jnp.where(core == 0, mine, other)
    high = jnp.where(core == 0, other, mine)
    return jnp.concatenate([low, high], axis=0)


def swap(values):
    return lax.ppermute(values, "fsdp", [(0, 1), (1, 0)])


def moves(turn):
    pairs = []
    for core in range(2):
        for place in range(4):
            odd = (place + turn) % 2
            pairs.append((core * 4 + place, (place // 2) * 4 + 2 * odd + core))
    return pairs


def bring(array, place):
    even = place % 2 == 0
    first = lax.ppermute(jnp.where(even, array[0], array[1]), ("fsdp", "seq"), moves(0))
    second = lax.ppermute(jnp.where(even, array[1], array[0]), ("fsdp", "seq"), moves(1))
    early = place < 2
    return jnp.concatenate(
        [jnp.where(early, first, second), jnp.where(early, second, first)], axis=0
    )


def send_back(rows, place):
    half = rows.shape[0] // 2
    early = place < 2
    even = place % 2 == 0
    one = jnp.where(early, rows[:half], rows[half:])
    two = jnp.where(early, rows[half:], rows[:half])
    back = [[(b, a) for a, b in moves(turn)] for turn in range(2)]
    one = lax.ppermute(one, ("fsdp", "seq"), back[0])
    two = lax.ppermute(two, ("fsdp", "seq"), back[1])
    return jnp.stack([jnp.where(even, one, two), jnp.where(even, two, one)], axis=0)


def mul(left, right):
    return jnp.dot(left, right, preferred_element_type=jnp.float32)


def mul_nt(left, right):
    return lax.dot_general(left, right, (((1,), (1,)), ((), ())), preferred_element_type=jnp.float32)


def mul_tn(left, right):
    return lax.dot_general(left, right, (((0,), (0,)), ((), ())), preferred_element_type=jnp.float32)


def half_of(values, core):
    width = values.shape[1] // 2
    return lax.dynamic_slice_in_dim(values, core * width, width, 1)


MESH = pl.DeviceIdType.MESH


def gelu_pair(values):
    depth = 1.0 + (0.3275911 * 2.0**-0.5) * jnp.abs(values)
    inv = pltpu.reciprocal(depth, approx=True)
    inv = inv * (2.0 - depth * inv)
    bell = jnp.exp(-0.5 * values * values)
    series = 0.7107068705 + inv * (-0.7265760135 + inv * 0.5307027145)
    series = inv * (0.127414796 + inv * (-0.142248368 + inv * series))
    tail = series * bell
    cumulative = jnp.where(values >= 0.0, 1.0 - tail, tail)
    return values * cumulative, cumulative + values * (bell * (1.0 / math.sqrt(2.0 * math.pi)))


def position():
    rep, core, deep = lax.axis_index("rep"), lax.axis_index("fsdp"), lax.axis_index("seq")
    return rep % 2, rep // 2, core, deep


def device(across, up, core, deep):
    return (up * 2 + across, core, deep)


def greet(partners):
    barrier = pltpu.get_barrier_semaphore()
    for partner in partners:
        pl.semaphore_signal(barrier, inc=1, device_id=partner, device_id_type=MESH)
    pl.semaphore_wait(barrier, len(partners))


class ChunkSum:
    def __init__(self, turned, column, width, own_ref, sum_ref, held, first, second, third, done, send, recv, local):
        across, up, core, deep = position()
        self.side, self.next = (up, across) if turned else (across, up)
        one = device(1 - across, up, core, deep)
        two = device(across, 1 - up, core, deep)
        self.one, self.two = (two, one) if turned else (one, two)
        self.deep = deep
        self.others = [(deep + step) % 4 for step in (1, 2, 3)]
        self.third_ids = [device(across, up, core, other) for other in self.others]
        self.columns = pl.ds(column, width)
        self.own, self.sum = own_ref, sum_ref
        self.held, self.first, self.second, self.third, self.done = held, first, second, third, done
        self.send, self.recv, self.local = send, recv, local
        self.quarter = pl.multiple_of(self.next * 128, 128)
        self.start_row = self.side * 256

    def remote(self, index, src, dst, target):
        return pltpu.make_async_remote_copy(
            src_ref=src,
            dst_ref=dst,
            send_sem=self.send.at[index],
            recv_sem=self.recv.at[index],
            device_id=target,
            device_id_type=MESH,
        )

    def rows(self, ref, start, count):
        return ref.at[pl.ds(pl.multiple_of(start, 32), count), self.columns]

    def copy_a(self):
        return self.remote(0, self.rows(self.own, (1 - self.side) * 256, 256), self.first, self.one)

    def load(self):
        return pltpu.make_async_copy(self.rows(self.own, self.start_row, 256), self.held, self.local.at[0])

    def copy_b(self):
        away = pl.multiple_of((1 - self.next) * 128, 128)
        return self.remote(1, self.held.at[pl.ds(away, 128)], self.second, self.two)

    def copy_c(self, turn):
        start = pl.multiple_of(self.quarter + self.others[turn] * 32, 32)
        return self.remote(2 + turn, self.held.at[pl.ds(start, 32)], self.third.at[turn], self.third_ids[turn])

    def place(self):
        return self.rows(self.sum, self.start_row + self.quarter + self.deep * 32, 32)

    def copy_d(self, turn):
        return self.remote(5 + turn, self.done, self.place(), self.third_ids[turn])

    def store(self):
        return pltpu.make_async_copy(self.done, self.place(), self.local.at[1])

    def copy_e(self):
        part = self.rows(self.sum, self.start_row + self.quarter, 128)
        return self.remote(8, part, part, self.two)

    def copy_f(self):
        part = self.rows(self.sum, self.start_row, 256)
        return self.remote(9, part, part, self.one)

    def stage(self, number):
        if number == 0:
            self.copy_a().start()
            self.load().start()
        elif number == 1:
            self.load().wait()
            self.copy_a().wait_recv()
            self.held[...] = self.held[...] + self.first[...]
            self.copy_b().start()
        elif number == 2:
            self.copy_b().wait_recv()
            self.copy_b().wait_send()
            mine = pl.ds(self.quarter, 128)
            self.held[mine] = self.held[mine] + self.second[...]
            for turn in range(3):
                self.copy_c(turn).start()
        elif number == 3:
            for turn in range(3):
                self.copy_c(turn).wait_recv()
            start = pl.multiple_of(self.quarter + self.deep * 32, 32)
            total = self.held[pl.ds(start, 32)].astype(jnp.float32)
            for turn in range(3):
                total += self.third[turn].astype(jnp.float32)
            self.done[...] = total.astype(self.done.dtype)
            self.store().start()
            for turn in range(3):
                self.copy_d(turn).start()
        elif number == 4:
            self.store().wait()
            for turn in range(3):
                self.copy_d(turn).wait_recv()
            self.copy_e().start()
        elif number == 5:
            self.copy_e().wait_recv()
            self.copy_f().start()
        elif number == 6:
            self.copy_f().wait_recv()
            self.copy_a().wait_send()
            for turn in range(3):
                self.copy_c(turn).wait_send()
                self.copy_d(turn).wait_send()
            self.copy_e().wait_send()
            self.copy_f().wait_send()


AFTER = (0, 5, 8, 12, 16, 19, 24)


def ffn_kernel(
    step, plan, rows_ref, grads_ref, in_ref, out_ref, bias_ref, own_ref,
    din_ref, dout_ref, dbias_ref, sum_ref, flip, acc, us, das, *rest
):
    units = flip.shape[0]
    steps = rows_ref.shape[0] // step
    at = pl.program_id(0)
    send, recv, local = rest[-3:]
    buffers = rest[:-3]
    chunks = []
    for index, (turned, column, width, begin) in enumerate(plan):
        held, first, second, third, done = buffers[5 * index : 5 * index + 5]
        chunks.append(
            ChunkSum(turned, column, width, own_ref, sum_ref, held, first, second, third, done,
                     send.at[index], recv.at[index], local.at[index])
        )

    @pl.when(at == 0)
    def _():
        across, up, core, deep = position()
        greet(
            [device(1 - across, up, core, deep), device(across, 1 - up, core, deep)]
            + [device(across, up, core, (deep + turn) % 4) for turn in (1, 2, 3)]
        )

    def traffic(turn):
        work = {}
        for chunk, (_, _, _, begin) in zip(chunks, plan):
            for number, after in enumerate(AFTER):
                slot = begin + after
                if slot % steps == turn:
                    work.setdefault(slot // steps, []).append((chunk, number))
        for when, jobs in sorted(work.items()):
            @pl.when(at == when)
            def _():
                for chunk, number in jobs:
                    chunk.stage(number)

    flip[...] = in_ref[...].T

    def front(turn):
        part = pl.ds(turn * step, step)
        us[turn % 2] = mul_nt(flip[...], rows_ref[part, :])
        das[turn % 2] = mul_nt(out_ref[...], grads_ref[part, :])

    traffic(0)
    front(0)
    bias = jnp.broadcast_to(bias_ref[...], (128, units)).T[:, :1]
    total = jnp.zeros((units, 128), jnp.float32)
    for turn in range(steps):
        if turn:
            traffic(turn)
        if turn + 1 < steps:
            front(turn + 1)
        active, slope = gelu_pair(us[turn % 2] + bias)
        active = active.astype(jnp.bfloat16)
        inner = (das[turn % 2] * slope).astype(jnp.bfloat16)
        for lane in range(step // 128):
            total += inner[:, lane * 128 : (lane + 1) * 128].astype(jnp.float32)
        part = pl.ds(turn * step, step)
        if turn == 0:
            dout_ref[...] = mul(active, grads_ref[part, :])
            acc[...] = mul(inner, rows_ref[part, :])
        else:
            dout_ref[...] += mul(active, grads_ref[part, :])
            acc[...] += mul(inner, rows_ref[part, :])
    din_ref[...] = acc[...].T
    dbias_ref[...] = jnp.sum(total.T, axis=0, keepdims=True)


def ffn_grads(rows, grads, fc_in, fc_out, bias, own):
    count, width = rows.shape
    hidden = fc_in.shape[1]
    units, step = 256, 1024
    plan = [(False, 8 * width, 128, 0)]
    for pair in range(4):
        plan.append((False, pair * width, width, 1 + 10 * pair))
        plan.append((True, (4 + pair) * width, width, 1 + 10 * pair))
    buffers = []
    for _, _, columns, _ in plan:
        buffers += [
            pltpu.VMEM((256, columns), jnp.bfloat16),
            pltpu.VMEM((256, columns), jnp.bfloat16),
            pltpu.VMEM((128, columns), jnp.bfloat16),
            pltpu.VMEM((3, 32, columns), jnp.bfloat16),
            pltpu.VMEM((32, columns), jnp.bfloat16),
        ]
    whole = functools.partial(pl.BlockSpec, pipeline_mode=pl.Buffered(1))
    return pl.pallas_call(
        functools.partial(ffn_kernel, step, plan),
        grid=(hidden // units,),
        in_specs=[
            whole((count, width), lambda at: (0, 0)),
            whole((count, width), lambda at: (0, 0)),
            pl.BlockSpec((width, units), lambda at: (0, at)),
            pl.BlockSpec((units, width), lambda at: (at, 0)),
            pl.BlockSpec((1, units), lambda at: (0, at)),
            pl.BlockSpec(memory_space=pl.ANY),
        ],
        out_specs=[
            pl.BlockSpec((width, units), lambda at: (0, at)),
            pl.BlockSpec((units, width), lambda at: (at, 0)),
            pl.BlockSpec((1, units), lambda at: (0, at)),
            pl.BlockSpec(memory_space=pl.ANY),
        ],
        out_shape=[
            jax.ShapeDtypeStruct((width, hidden), jnp.float32),
            jax.ShapeDtypeStruct((hidden, width), jnp.float32),
            jax.ShapeDtypeStruct((1, hidden), jnp.float32),
            jax.ShapeDtypeStruct(own.shape, own.dtype),
        ],
        scratch_shapes=[
            pltpu.VMEM((units, width), jnp.bfloat16),
            pltpu.VMEM((units, width), jnp.float32),
            pltpu.VMEM((2, units, step), jnp.float32),
            pltpu.VMEM((2, units, step), jnp.float32),
            *buffers,
            pltpu.SemaphoreType.DMA((len(plan), 10)),
            pltpu.SemaphoreType.DMA((len(plan), 10)),
            pltpu.SemaphoreType.DMA((len(plan), 2)),
        ],
        compiler_params=pltpu.CompilerParams(
            vmem_limit_bytes=58 * 2**20, collective_id=0, has_side_effects=True
        ),
        cost_estimate=pl.CostEstimate(
            flops=8 * count * width * hidden,
            bytes_accessed=4 * count * width + 12 * width * hidden,
            transcendentals=count * hidden,
        ),
    )(rows, grads, fc_in, fc_out, bias, own)


def norm_parts(values):
    centred = values - jnp.mean(values, axis=-1, keepdims=True)
    inverse = lax.rsqrt(jnp.mean(centred * centred, axis=-1, keepdims=True) + NORM_EPSILON)
    return centred * inverse, inverse


def normed(values, vectors, which):
    scaled, _ = norm_parts(values)
    return (scaled * vectors[7 + which : 8 + which] + vectors[10 + which : 11 + which]).astype(jnp.bfloat16)


class Partner:
    def __init__(self, send, recv):
        across, up, core, deep = position()
        self.core = core
        self.id = device(across, up, 1 - core, deep)
        self.send, self.recv = send, recv
        self.copies = []

    def push(self, src, dst):
        index = len(self.copies)
        copy = pltpu.make_async_remote_copy(
            src_ref=src,
            dst_ref=dst,
            send_sem=self.send.at[index],
            recv_sem=self.recv.at[index],
            device_id=self.id,
            device_id_type=MESH,
        )
        copy.start()
        self.copies.append(copy)
        return copy

    def finish(self):
        for copy in self.copies:
            copy.wait_send()


class Weights:
    def __init__(self, partner, shard, whole, local):
        half = shard.shape[0]
        mine = whole.at[pl.ds(pl.multiple_of(partner.core * half, half), half)]
        self.remote = partner.push(shard, mine)
        self.near = pltpu.make_async_copy(shard, mine, local)
        self.near.start()
        self.whole = whole

    def get(self):
        self.near.wait()
        self.remote.wait_recv()
        return self.whole


def two_heads(values, lane):
    zero = jnp.zeros_like(values)
    return jnp.concatenate([jnp.where(lane, values, zero), jnp.where(lane, zero, values)], axis=0)


def lane_of():
    return lax.broadcasted_iota(jnp.int32, (1, 2 * HEAD), 1) < HEAD


def attend(q_ref, k_ref, v_ref, p_ref, o_ref, allowed):
    lane = lane_of()
    count = q_ref.shape[0]
    for pair in range(q_ref.shape[1] // (2 * HEAD)):
        columns = pl.ds(pair * 2 * HEAD, 2 * HEAD)
        scores = mul_nt(two_heads(q_ref[:, columns], lane), k_ref[:, columns])
        scores = jnp.where(allowed, scores * HEAD ** (-0.5), MASKED_SCORE)
        exponent = jnp.exp(scores - jnp.max(scores, axis=-1, keepdims=True))
        weights = (exponent / jnp.sum(exponent, axis=-1, keepdims=True)).astype(jnp.bfloat16)
        p_ref[pair] = weights
        mixed = mul(weights, v_ref[:, columns])
        o_ref[:, columns] = jnp.where(lane, mixed[:count], mixed[count:]).astype(jnp.bfloat16)


def attend_back(q_ref, k_ref, v_ref, p_ref, go_ref, dq_ref, dk_ref, dv_ref):
    lane = lane_of()
    count = q_ref.shape[0]
    for pair in range(q_ref.shape[1] // (2 * HEAD)):
        columns = pl.ds(pair * 2 * HEAD, 2 * HEAD)
        grads = two_heads(go_ref[:, columns], lane)
        weights = p_ref[pair]
        dv_ref[:, columns] = mul_tn(weights, grads).astype(jnp.bfloat16)
        grad_weights = mul_nt(grads, v_ref[:, columns])
        exact = weights.astype(jnp.float32)
        inner = jnp.sum(grad_weights * exact, axis=-1, keepdims=True)
        scores = (exact * (grad_weights - inner)).astype(jnp.bfloat16)
        queries = mul(scores, k_ref[:, columns]) * HEAD ** (-0.5)
        dq_ref[:, columns] = jnp.where(lane, queries[:count], queries[count:]).astype(jnp.bfloat16)
        keys = mul_tn(scores, two_heads(q_ref[:, columns], lane)) * HEAD ** (-0.5)
        dk_ref[:, columns] = keys.astype(jnp.bfloat16)


def forward_kernel(
    x_ref, m_ref, vec_ref, qid_ref, tid_ref, sid_ref, qkv_hbm, so_hbm, cq_hbm, ckv_hbm, co_hbm,
    n1_ref, q1_ref, k1_ref, v1_ref, p1_ref, o1_ref, h1_ref, n2_ref, q2_ref, k2_ref, v2_ref, p2_ref,
    o2_ref, h2_ref, n3_ref,
    qkv_w, so_w, cq_w, ckv_w, co_w, send, recv, local,
):
    across, up, core, deep = position()
    greet([device(across, up, 1 - core, deep)])
    partner = Partner(send, recv)
    qkv = Weights(partner, qkv_hbm, qkv_w, local.at[0])
    ckv = Weights(partner, ckv_hbm, ckv_w, local.at[1])
    so = Weights(partner, so_hbm, so_w, local.at[2])
    cq = Weights(partner, cq_hbm, cq_w, local.at[3])
    co = Weights(partner, co_hbm, co_w, local.at[4])
    count, width = q1_ref.shape
    mine = pl.ds(pl.multiple_of(core * count, count), count)
    vectors = vec_ref[...]
    n1_ref[...] = normed(x_ref[...].astype(jnp.float32), vectors, 0)
    place = core * count + lax.broadcasted_iota(jnp.int32, (count, 1), 0)
    keys = lax.broadcasted_iota(jnp.int32, (1, tid_ref.shape[1]), 1)
    allowed = (place >= keys) & (qid_ref[...] == tid_ref[...])
    allowed = jnp.concatenate([allowed, allowed], axis=0)
    w = qkv.get()
    q1_ref[...] = (mul(n1_ref[mine, :], w[:, :width]) + vectors[0:1]).astype(jnp.bfloat16)
    k1_ref[...] = mul(n1_ref[...], w[:, width : 2 * width]).astype(jnp.bfloat16)
    v1_ref[...] = (mul(n1_ref[...], w[:, 2 * width :]) + vectors[1:2]).astype(jnp.bfloat16)
    attend(q1_ref, k1_ref, v1_ref, p1_ref, o1_ref, allowed)
    w = ckv.get()
    k2_ref[...] = mul(m_ref[...], w[:, :width]).astype(jnp.bfloat16)
    v2_ref[...] = (mul(m_ref[...], w[:, width:]) + vectors[4:5]).astype(jnp.bfloat16)
    w = so.get()
    h1_ref[...] = x_ref[mine, :].astype(jnp.float32) + mul(o1_ref[...], w[...]) + vectors[2:3]
    n2_ref[...] = normed(h1_ref[...], vectors, 1)
    w = cq.get()
    q2_ref[...] = (mul(n2_ref[...], w[...]) + vectors[3:4]).astype(jnp.bfloat16)
    allowed = qid_ref[...] == sid_ref[...]
    allowed = jnp.concatenate([allowed, allowed], axis=0)
    attend(q2_ref, k2_ref, v2_ref, p2_ref, o2_ref, allowed)
    w = co.get()
    h2_ref[...] = h1_ref[...] + mul(o2_ref[...], w[...]) + vectors[5:6]
    n3_ref[...] = normed(h2_ref[...], vectors, 2)
    partner.finish()


def attention_forward(x, memory, vectors, query_ids, token_ids, source_ids, weights):
    rows, width = x.shape
    count = rows // 2
    bf16, f32 = jnp.bfloat16, jnp.float32
    scores = (width // (2 * HEAD), rows, rows)
    shapes = [
        ((rows, width), bf16), ((count, width), bf16), ((rows, width), bf16), ((rows, width), bf16),
        (scores, bf16), ((count, width), bf16), ((count, width), f32), ((count, width), bf16),
        ((count, width), bf16), ((rows, width), bf16), ((rows, width), bf16), (scores, bf16),
        ((count, width), bf16), ((count, width), f32), ((count, width), bf16),
    ]
    vmem = pl.BlockSpec(memory_space=pltpu.VMEM)
    return pl.pallas_call(
        forward_kernel,
        in_specs=[vmem] * 6 + [pl.BlockSpec(memory_space=pl.ANY)] * 5,
        out_specs=[vmem] * len(shapes),
        out_shape=[jax.ShapeDtypeStruct(*shape) for shape in shapes],
        scratch_shapes=[
            *[pltpu.VMEM((2 * w.shape[0], w.shape[1]), bf16) for w in weights],
            pltpu.SemaphoreType.DMA((5,)),
            pltpu.SemaphoreType.DMA((5,)),
            pltpu.SemaphoreType.DMA((5,)),
        ],
        compiler_params=pltpu.CompilerParams(
            vmem_limit_bytes=48 * 2**20, collective_id=1, has_side_effects=True
        ),
        cost_estimate=pl.CostEstimate(flops=60 * 10**9, bytes_accessed=32 * 2**20, transcendentals=0),
    )(x, memory, vectors, query_ids, token_ids, source_ids, *weights)


def norm_back(grads, values, gain, sums_ref, row):
    scaled, inverse = norm_parts(values)
    sums_ref[row : row + 1, :] = jnp.sum(grads * scaled, axis=0, keepdims=True)
    sums_ref[row + 3 : row + 4, :] = jnp.sum(grads, axis=0, keepdims=True)
    inner = grads * gain
    first = jnp.mean(inner, axis=-1, keepdims=True)
    second = jnp.mean(inner * scaled, axis=-1, keepdims=True)
    return (inner - first - scaled * second) * inverse


def backward_kernel(
    x_ref, m_ref, g_ref, vec_ref, fcb_ref,
    n1_ref, q1_ref, k1_ref, v1_ref, p1_ref, o1_ref, h1_ref, n2_ref, q2_ref, k2_ref, v2_ref, p2_ref,
    o2_ref, h2_ref, n3_ref,
    qkv_hbm, so_hbm, cq_hbm, ckv_hbm, co_hbm, in_hbm, out_hbm,
    y_ref, dx_ref, dm_ref, grads_ref,
    qkv_w, so_w, cq_w, ckv_w, co_w, in_w, out_w, chip_n, acc_y, acc_n, part, got, go_ref,
    dkv2, dkv2_got, dkv1, dkv1_got, dq1, dq2, e1, e2, n2_half, o1_half, o2_half, dh_ref, sums, sums_got,
    stage, send, recv, local, tiles, stores,
):
    across, up, core, deep = position()
    greet([device(across, up, 1 - core, deep)])
    partner = Partner(send, recv)
    bf16, f32 = jnp.bfloat16, jnp.float32
    count, width = q1_ref.shape
    units = in_w.shape[2]
    mine = pl.ds(pl.multiple_of(core * count, count), count)
    theirs = pl.ds(pl.multiple_of((1 - core) * count, count), count)
    half = width // 2
    my_half = pl.ds(pl.multiple_of(core * half, half), half)
    their_half = pl.ds(pl.multiple_of((1 - core) * half, half), half)
    rows_sent = partner.push(n3_ref, chip_n.at[mine])
    chip_n[mine, :] = n3_ref[...]

    def tile_copies(index):
        slot = index % 2
        where = pl.ds(index * units, units)
        return (
            pltpu.make_async_copy(in_hbm.at[:, where], in_w.at[slot], tiles.at[slot, 0]),
            pltpu.make_async_copy(out_hbm.at[where], out_w.at[slot], tiles.at[slot, 1]),
        )

    steps = in_hbm.shape[1] // units
    for copy in tile_copies(0):
        copy.start()
    co = Weights(partner, co_hbm, co_w, local.at[4])
    cq = Weights(partner, cq_hbm, cq_w, local.at[3])
    so = Weights(partner, so_hbm, so_w, local.at[2])
    ckv = Weights(partner, ckv_hbm, ckv_w, local.at[1])
    qkv = Weights(partner, qkv_hbm, qkv_w, local.at[0])
    halves = [
        partner.push(n2_ref.at[:, their_half], n2_half.at[mine]),
        partner.push(o1_ref.at[:, their_half], o1_half.at[mine]),
        partner.push(o2_ref.at[:, their_half], o2_half.at[mine]),
    ]
    n2_half[mine, :] = n2_ref[:, my_half]
    o1_half[mine, :] = o1_ref[:, my_half]
    o2_half[mine, :] = o2_ref[:, my_half]
    vectors = vec_ref[...]
    rows_sent.wait_recv()
    for index in range(steps):
        if index + 1 < steps:
            for copy in tile_copies(index + 1):
                copy.start()
        for copy in tile_copies(index):
            copy.wait()
        slot = index % 2
        inner = mul(chip_n[...], in_w[slot]) + fcb_ref[:, index * units : (index + 1) * units]
        active, slope = gelu_pair(inner)
        back = (mul_nt(g_ref[...], out_w[slot]) * slope).astype(bf16)
        if index == 0:
            acc_y[...] = mul(active.astype(bf16), out_w[slot])
            acc_n[...] = mul_nt(back, in_w[slot])
        else:
            acc_y[...] += mul(active.astype(bf16), out_w[slot])
            acc_n[...] += mul_nt(back, in_w[slot])
    part[0] = acc_n[theirs, :].astype(bf16)
    sent_n = partner.push(part.at[0], got.at[0])
    part[1] = acc_y[theirs, :].astype(bf16)
    sent_y = partner.push(part.at[1], got.at[1])

    sent_n.wait_recv()
    grad = acc_n[mine, :] + got[0].astype(f32)
    grad = norm_back(grad, h2_ref[...], vectors[9:10], sums, 2) + g_ref[mine, :].astype(f32)
    dh_ref[...] = grad
    e2[mine, :] = grad.astype(bf16)
    sent_e2 = partner.push(e2.at[mine], e2.at[mine])
    go_ref[...] = mul_nt(e2[mine, :], co.get()[...]).astype(bf16)
    attend_back(q2_ref, k2_ref, v2_ref, p2_ref, go_ref, dq2.at[mine], dkv2.at[:, :width], dkv2.at[:, width:])
    sent_dkv2 = partner.push(dkv2, dkv2_got)
    sent_dq2 = partner.push(dq2.at[mine], dq2.at[mine])
    grad = mul_nt(dq2[mine, :], cq.get()[...])
    grad = norm_back(grad, h1_ref[...], vectors[8:9], sums, 1) + dh_ref[...]
    dh_ref[...] = grad
    e1[mine, :] = grad.astype(bf16)
    sent_e1 = partner.push(e1.at[mine], e1.at[mine])
    go_ref[...] = mul_nt(e1[mine, :], so.get()[...]).astype(bf16)
    attend_back(q1_ref, k1_ref, v1_ref, p1_ref, go_ref, dq1.at[mine], dkv1.at[:, :width], dkv1.at[:, width:])
    sent_dkv1 = partner.push(dkv1, dkv1_got)
    sent_dq1 = partner.push(dq1.at[mine], dq1.at[mine])

    sent_y.wait_recv()
    y = h2_ref[...] + (acc_y[mine, :] + got[1].astype(f32) + vectors[6:7])
    y_ref[...] = y.astype(bf16)
    sent_dkv2.wait_recv()
    dkv2_got[...] = (dkv2[...].astype(f32) + dkv2_got[...].astype(f32)).astype(bf16)
    dm_ref[...] = mul_nt(dkv2_got[mine, :], ckv.get()[...]).astype(bf16)

    sent = []

    def weight_grad_of(left, right, column):
        index = len(sent)
        slot = index % 2
        if index >= 2:
            sent[index - 2].wait()
        stage[slot] = mul_tn(left, right).astype(bf16)
        copy = pltpu.make_async_copy(
            stage.at[slot], grads_ref.at[:, pl.ds(column, width)], stores.at[index]
        )
        copy.start()
        sent.append(copy)

    for copy in halves:
        copy.wait_recv()
    sent_e2.wait_recv()
    weight_grad_of(o2_half[...], e2[...], 7 * width)
    weight_grad_of(m_ref[:, my_half], dkv2_got[:, :width], 5 * width)
    weight_grad_of(m_ref[:, my_half], dkv2_got[:, width:], 6 * width)
    sent_dq2.wait_recv()
    weight_grad_of(n2_half[...], dq2[...], 4 * width)
    sent_e1.wait_recv()
    weight_grad_of(o1_half[...], e1[...], 3 * width)
    sent_dkv1.wait_recv()
    dkv1_got[...] = (dkv1[...].astype(f32) + dkv1_got[...].astype(f32)).astype(bf16)
    w = qkv.get()
    grad = mul_nt(dq1[mine, :], w[:, :width])
    grad += mul_nt(dkv1_got[mine, :width], w[:, width : 2 * width])
    grad += mul_nt(dkv1_got[mine, width:], w[:, 2 * width :])
    dx = norm_back(grad, x_ref[mine, :].astype(f32), vectors[7:8], sums, 0) + dh_ref[...]
    dx_ref[...] = dx.astype(bf16)
    sent_sums = partner.push(sums, sums_got)
    weight_grad_of(n1_ref[:, my_half], dkv1_got[:, :width], width)
    weight_grad_of(n1_ref[:, my_half], dkv1_got[:, width:], 2 * width)
    sent_dq1.wait_recv()
    weight_grad_of(n1_ref[:, my_half], dq1[...], 0)

    def columns(values):
        return jnp.sum(values.astype(f32), axis=0, keepdims=True)

    value_half = pl.ds(pl.multiple_of(width + core * half, half), half)
    sent_sums.wait_recv()
    lines = [
        columns(dq1[:, my_half]),
        columns(dkv1_got[:, value_half]),
        columns(e1[:, my_half]),
        columns(dq2[:, my_half]),
        columns(dkv2_got[:, value_half]),
        columns(e2[:, my_half]),
        columns(g_ref[:, my_half]),
        sums[0:6, my_half] + sums_got[0:6, my_half],
    ]
    lines = jnp.concatenate(lines + [jnp.zeros((128 - 13, half), f32)], axis=0).T
    sent[-1].wait()
    sent[-2].wait()
    stage[0, :, :128] = lines.astype(bf16)
    last = pltpu.make_async_copy(
        stage.at[0, :, pl.ds(0, 128)], grads_ref.at[:, pl.ds(8 * width, 128)], stores.at[8]
    )
    last.start()
    last.wait()
    partner.finish()


def attention_backward(x, memory, grads, vectors, fc_bias, kept, weights, fc_in, fc_out):
    rows, width = x.shape
    count = rows // 2
    units = 512
    bf16, f32 = jnp.bfloat16, jnp.float32
    half = width // 2
    vmem = pl.BlockSpec(memory_space=pltpu.VMEM)
    hbm = pl.BlockSpec(memory_space=pl.ANY)
    own = jax.ShapeDtypeStruct((count, width), bf16)
    return pl.pallas_call(
        backward_kernel,
        in_specs=[vmem] * (5 + len(kept)) + [hbm] * 7,
        out_specs=[vmem] * 3 + [hbm],
        out_shape=[own, own, own, jax.ShapeDtypeStruct((half, 8 * width + 128), bf16)],
        scratch_shapes=[
            *[pltpu.VMEM((2 * w.shape[0], w.shape[1]), bf16) for w in weights],
            pltpu.VMEM((2, width, units), bf16),
            pltpu.VMEM((2, units, width), bf16),
            pltpu.VMEM((rows, width), bf16),
            pltpu.VMEM((rows, width), f32),
            pltpu.VMEM((rows, width), f32),
            pltpu.VMEM((2, count, width), bf16),
            pltpu.VMEM((2, count, width), bf16),
            pltpu.VMEM((count, width), bf16),
            *[pltpu.VMEM((rows, 2 * width), bf16)] * 4,
            *[pltpu.VMEM((rows, width), bf16)] * 4,
            *[pltpu.VMEM((rows, half), bf16)] * 3,
            pltpu.VMEM((count, width), f32),
            pltpu.VMEM((8, width), f32),
            pltpu.VMEM((8, width), f32),
            pltpu.VMEM((2, half, width), bf16),
            pltpu.SemaphoreType.DMA((24,)),
            pltpu.SemaphoreType.DMA((24,)),
            pltpu.SemaphoreType.DMA((5,)),
            pltpu.SemaphoreType.DMA((2, 2)),
            pltpu.SemaphoreType.DMA((9,)),
        ],
        compiler_params=pltpu.CompilerParams(
            vmem_limit_bytes=58 * 2**20, collective_id=2, has_side_effects=True
        ),
        cost_estimate=pl.CostEstimate(flops=80 * 10**9, bytes_accessed=64 * 2**20, transcendentals=0),
    )(x, memory, grads, vectors, fc_bias, *kept, *weights, fc_in, fc_out)


def fast_body(
    hidden_in,
    memory,
    segment_ids,
    memory_ids,
    out_grad,
    self_qkv,
    self_out,
    cross_query,
    cross_kv,
    cross_out,
    fc_in,
    fc_out,
    biases,
    fc_in_bias,
    norm_gains,
    norm_shifts,
):
    width = hidden_in.shape[-1]
    core = lax.axis_index("fsdp")
    place = lax.axis_index("seq")
    bf16, f32 = jnp.bfloat16, jnp.float32

    x_own = bring(hidden_in[:, 0], place)
    x_all = shift_rows(x_own, swap(x_own), core)
    memory_own = bring(memory[:, 0], place)
    memory_all = shift_rows(memory_own, swap(memory_own), core)
    grad_own = bring(out_grad[:, 0], place)
    grad_chip = shift_rows(grad_own, swap(grad_own), core)
    grad_every = lax.all_gather(grad_own, ("rep", "seq", "fsdp"), axis=0, tiled=True)

    micro, owner = place // 2, place % 2
    ids = jnp.stack([segment_ids[:, 0], memory_ids[:, 0]])
    ids_other = swap(ids)
    ids = jnp.where(owner == core, ids, ids_other)
    ids = lax.dynamic_index_in_dim(ids, micro, 1, keepdims=False)
    token_ids, source_ids = ids[0], ids[1]
    own_count = x_own.shape[0]
    query_ids = lax.dynamic_slice_in_dim(token_ids, core * own_count, own_count, 0)

    small = jnp.concatenate([biases, norm_gains, norm_shifts], axis=1)
    vectors = shift_rows(small, swap(small), core).astype(f32).T
    vectors = jnp.pad(vectors, ((0, 16 - vectors.shape[0]), (0, 0)))
    weights = (self_qkv, self_out, cross_query, cross_kv, cross_out)
    fc_bias = fc_in_bias.astype(f32)[None]
    kept = attention_forward(
        x_all, memory_all, vectors, query_ids[:, None], token_ids[None], source_ids[None], weights
    )
    normed_every = lax.all_gather(kept[-1], ("rep", "seq", "fsdp"), axis=0, tiled=True)
    hidden_out, hidden_grad, memory_grad, grads = attention_backward(
        x_all, memory_all, grad_chip, vectors, fc_bias, kept, weights, fc_in, fc_out
    )
    grad_fc_in, grad_fc_out, grad_fc_bias, grads = ffn_grads(
        normed_every, grad_every, fc_in, fc_out, fc_bias, grads
    )
    grads = grads.astype(f32)
    column = grads[:, 8 * width :]
    return (
        send_back(hidden_out, place)[:, None],
        send_back(hidden_grad, place)[:, None],
        send_back(memory_grad, place)[:, None],
        grads[:, : 3 * width],
        grads[:, 3 * width : 4 * width],
        grads[:, 4 * width : 5 * width],
        grads[:, 5 * width : 7 * width],
        grads[:, 7 * width : 8 * width],
        grad_fc_in,
        grad_fc_out,
        column[:, :7],
        grad_fc_bias[0],
        column[:, 7:10],
        column[:, 10:13],
    )


def solution(mesh):
    fits = mesh.shape["fsdp"] == 2 and mesh.shape["seq"] == 4
    chosen = fast_body if fits else body
    return jax.shard_map(
        chosen,
        mesh=mesh,
        in_specs=(
            P(None, ("rep", "fsdp"), "seq", None),
            P(None, ("rep", "fsdp"), "seq", None),
            P(None, ("rep", "fsdp"), None),
            P(None, ("rep", "fsdp"), None),
            P(None, ("rep", "fsdp"), "seq", None),
            P("fsdp", None),
            P("fsdp", None),
            P("fsdp", None),
            P("fsdp", None),
            P("fsdp", None),
            P(None, "fsdp"),
            P("fsdp", None),
            P("fsdp", None),
            P("fsdp"),
            P("fsdp", None),
            P("fsdp", None),
        ),
        out_specs=(
            P(None, ("rep", "fsdp"), "seq", None),
            P(None, ("rep", "fsdp"), "seq", None),
            P(None, ("rep", "fsdp"), "seq", None),
            P("fsdp", None),
            P("fsdp", None),
            P("fsdp", None),
            P("fsdp", None),
            P("fsdp", None),
            P(None, "fsdp"),
            P("fsdp", None),
            P("fsdp", None),
            P("fsdp"),
            P("fsdp", None),
            P("fsdp", None),
        ),
        check_vma=False,
    )
```

```python
import functools
import math

import jax
import jax.numpy as jnp
from jax import lax
from jax.experimental import pallas as pl
from jax.experimental.pallas import tpu as pltpu
from jax.sharding import PartitionSpec as P

HEAD = 64


NORM_EPSILON = 1e-05
MASKED_SCORE = -1e30


def norm_forward(values, norm_gain, norm_shift):
    average = jnp.mean(values, axis=-1, keepdims=True)
    centred = values - average
    inverse = lax.rsqrt(jnp.mean(centred * centred, axis=-1, keepdims=True) + NORM_EPSILON)
    scaled = centred * inverse
    return (scaled * norm_gain + norm_shift, scaled, inverse)


def norm_backward(grad_normed, scaled, inverse, norm_gain):
    grad_scaled = grad_normed * norm_gain
    first_mean = jnp.mean(grad_scaled, axis=-1, keepdims=True)
    second_mean = jnp.mean(grad_scaled * scaled, axis=-1, keepdims=True)
    grad_values = (grad_scaled - first_mean - scaled * second_mean) * inverse
    gain_grad = jnp.sum(grad_normed * scaled, axis=(0, 1))
    shift_grad = jnp.sum(grad_normed, axis=(0, 1))
    return (grad_values, gain_grad, shift_grad)


def split_heads(values):
    return values.reshape(values.shape[:-1] + (values.shape[-1] // HEAD, HEAD))


def join_heads(values):
    return values.reshape(values.shape[:2] + (values.shape[2] * values.shape[3],))


def masked_scores(queries, key_rows, allowed):
    raw_scores = jnp.einsum(
        "mqhe,mkhe->mhqk", queries, key_rows, preferred_element_type=jnp.float32
    )
    return jnp.where(allowed[:, None], raw_scores * HEAD ** (-0.5), MASKED_SCORE)


def attend_forward(queries, key_rows, value_rows, allowed):
    scores = masked_scores(queries, key_rows, allowed)
    highest = jnp.max(scores, axis=-1, keepdims=True)
    exponent = jnp.exp(scores - highest)
    row_totals = jnp.sum(exponent, axis=-1, keepdims=True)
    weights = (exponent / row_totals).astype(jnp.bfloat16)
    joined = jnp.einsum("mhqk,mkhe->mqhe", weights, value_rows, preferred_element_type=jnp.float32)
    return (join_heads(joined).astype(jnp.bfloat16), highest + jnp.log(row_totals))


def attend_backward(queries, key_rows, value_rows, allowed, log_totals, grad_joined):
    scores = masked_scores(queries, key_rows, allowed)
    probability = jnp.exp(scores - log_totals)
    weights = probability.astype(jnp.bfloat16)
    grad_value_rows = jnp.einsum(
        "mhqk,mqhe->mkhe", weights, grad_joined, preferred_element_type=jnp.float32
    )
    grad_weights = jnp.einsum(
        "mqhe,mkhe->mhqk", grad_joined, value_rows, preferred_element_type=jnp.float32
    )
    grad_scores = probability * (
        grad_weights - jnp.sum(grad_weights * probability, axis=-1, keepdims=True)
    )
    grad_scores = grad_scores.astype(jnp.bfloat16)
    grad_queries = jnp.einsum(
        "mhqk,mkhe->mqhe", grad_scores, key_rows, preferred_element_type=jnp.float32
    ) * HEAD ** (-0.5)
    grad_key_rows = jnp.einsum(
        "mhqk,mqhe->mkhe", grad_scores, queries, preferred_element_type=jnp.float32
    ) * HEAD ** (-0.5)
    return (join_heads(grad_queries), join_heads(grad_key_rows), join_heads(grad_value_rows))


def gelu_slope(values):
    cumulative = 0.5 * (1.0 + lax.erf(values * 2.0 ** (-0.5)))
    density = jnp.exp(-0.5 * values * values) / math.sqrt(2.0 * math.pi)
    return cumulative + values * density


def feed_forward(rows, weight_in, bias_in, weight_out):
    pre_active = jnp.einsum(
        "mtd,df->mtf", rows, weight_in, preferred_element_type=jnp.float32
    ) + bias_in.astype(jnp.float32)
    active = jax.nn.gelu(pre_active, approximate=False).astype(jnp.bfloat16)
    partial_out = jnp.einsum("mtf,fd->mtd", active, weight_out, preferred_element_type=jnp.float32)
    return (pre_active, active, partial_out)


def feed_back(rows, grad_rows, pre_active, active, weight_in, weight_out):
    grad_active = jnp.einsum(
        "mtd,fd->mtf", grad_rows, weight_out, preferred_element_type=jnp.float32
    )
    grad_inner = (grad_active * gelu_slope(pre_active)).astype(jnp.bfloat16)
    grad_weight_out = jnp.einsum(
        "mtf,mtd->fd", active, grad_rows, preferred_element_type=jnp.float32
    )
    grad_weight_in = jnp.einsum("mtd,mtf->df", rows, grad_inner, preferred_element_type=jnp.float32)
    grad_bias_in = jnp.sum(grad_inner.astype(jnp.float32), axis=(0, 1))
    grad_rows_in = jnp.einsum(
        "mtf,df->mtd", grad_inner, weight_in, preferred_element_type=jnp.float32
    )
    return (grad_weight_in, grad_weight_out, grad_bias_in, grad_rows_in)


def project(rows, weight):
    return jnp.einsum("mtd,de->mte", rows, weight, preferred_element_type=jnp.float32)


def project_back(grad_rows, weight):
    return jnp.einsum("mte,de->mtd", grad_rows, weight, preferred_element_type=jnp.float32)


def weight_grad(rows, grad_rows):
    return jnp.einsum("mtd,mte->de", rows, grad_rows, preferred_element_type=jnp.float32)


def column_sums(grad_rows):
    return jnp.sum(grad_rows.astype(jnp.float32), axis=(0, 1))


def body(
    hidden_in,
    memory,
    segment_ids,
    memory_ids,
    out_grad,
    self_qkv,
    self_out,
    cross_query,
    cross_kv,
    cross_out,
    fc_in,
    fc_out,
    biases,
    fc_in_bias,
    norm_gains,
    norm_shifts,
):
    micro_count, single, tokens, model_width = hidden_in.shape
    seq_index = lax.axis_index("seq")
    zero_row = jnp.zeros((model_width,), jnp.float32)
    outputs_list = []
    grads_list = []
    memory_list = []
    attn_total = None
    mlp_total = None
    for micro in range(micro_count):
        full_qkv = lax.all_gather(self_qkv, "fsdp", axis=0, tiled=True)
        full_self_out = lax.all_gather(self_out, "fsdp", axis=0, tiled=True)
        full_query = lax.all_gather(cross_query, "fsdp", axis=0, tiled=True)
        full_memory_kv = lax.all_gather(cross_kv, "fsdp", axis=0, tiled=True)
        full_cross_out = lax.all_gather(cross_out, "fsdp", axis=0, tiled=True)
        full_biases = lax.all_gather(biases, "fsdp", axis=0, tiled=True)
        full_gains = lax.all_gather(norm_gains, "fsdp", axis=0, tiled=True)
        full_shifts = lax.all_gather(norm_shifts, "fsdp", axis=0, tiled=True)
        bias_float = full_biases.astype(jnp.float32)
        gain_float = full_gains.astype(jnp.float32)
        shift_float = full_shifts.astype(jnp.float32)
        hidden = hidden_in[micro : micro + 1][:, 0].astype(jnp.float32)
        memory_rows = memory[micro : micro + 1][:, 0]
        token_ids = segment_ids[micro : micro + 1][:, 0]
        source_ids = memory_ids[micro : micro + 1][:, 0]
        query_ids = lax.dynamic_slice_in_dim(token_ids, seq_index * tokens, tokens, 1)
        query_place = seq_index * tokens + jnp.arange(tokens, dtype=jnp.int32)
        key_place = jnp.arange(token_ids.shape[1], dtype=jnp.int32)
        self_allowed = (query_place[:, None] >= key_place[None, :])[None] & (
            query_ids[:, :, None] == token_ids[:, None, :]
        )
        cross_allowed = query_ids[:, :, None] == source_ids[:, None, :]
        normed_one, scaled_one, inverse_one = norm_forward(
            hidden, gain_float[:, 0], shift_float[:, 0]
        )
        normed_one = normed_one.astype(jnp.bfloat16)
        qkv_bias = jnp.concatenate([bias_float[:, 0], zero_row, bias_float[:, 1]])
        projected = (project(normed_one, full_qkv) + qkv_bias).astype(jnp.bfloat16)
        self_queries = split_heads(projected[..., :model_width])
        kv_all = lax.all_gather(projected[..., model_width:], "seq", axis=1, tiled=True)
        self_key_rows = split_heads(kv_all[..., :model_width])
        self_value_rows = split_heads(kv_all[..., model_width:])
        self_mixed, self_totals = attend_forward(
            self_queries, self_key_rows, self_value_rows, self_allowed
        )
        after_self = hidden + project(self_mixed, full_self_out) + bias_float[:, 2]
        normed_two, scaled_two, inverse_two = norm_forward(
            after_self, gain_float[:, 1], shift_float[:, 1]
        )
        normed_two = normed_two.astype(jnp.bfloat16)
        cross_queries = (project(normed_two, full_query) + bias_float[:, 3]).astype(jnp.bfloat16)
        memory_bias = jnp.concatenate([zero_row, bias_float[:, 4]])
        memory_kv = (project(memory_rows, full_memory_kv) + memory_bias).astype(jnp.bfloat16)
        memory_all = lax.all_gather(memory_kv, "seq", axis=1, tiled=True)
        memory_key_rows = split_heads(memory_all[..., :model_width])
        memory_value_rows = split_heads(memory_all[..., model_width:])
        cross_mixed, cross_totals = attend_forward(
            split_heads(cross_queries), memory_key_rows, memory_value_rows, cross_allowed
        )
        after_cross = after_self + project(cross_mixed, full_cross_out) + bias_float[:, 5]
        normed_three, scaled_three, inverse_three = norm_forward(
            after_cross, gain_float[:, 2], shift_float[:, 2]
        )
        normed_three = normed_three.astype(jnp.bfloat16)
        grad_out = out_grad[micro : micro + 1][:, 0]
        mlp_inputs = lax.all_gather(normed_three, "fsdp", axis=0, tiled=True)
        pre_active, active, partial_out = feed_forward(mlp_inputs, fc_in, fc_in_bias, fc_out)
        mlp_branch = lax.psum_scatter(
            partial_out.astype(jnp.bfloat16), "fsdp", scatter_dimension=0, tiled=True
        ).astype(jnp.float32)
        output = after_cross + mlp_branch + bias_float[:, 6]
        hidden_out = output.astype(jnp.bfloat16)[:, None]
        back_qkv = lax.all_gather(self_qkv, "fsdp", axis=0, tiled=True)
        back_self_out = lax.all_gather(self_out, "fsdp", axis=0, tiled=True)
        back_query = lax.all_gather(cross_query, "fsdp", axis=0, tiled=True)
        back_memory_kv = lax.all_gather(cross_kv, "fsdp", axis=0, tiled=True)
        back_cross_out = lax.all_gather(cross_out, "fsdp", axis=0, tiled=True)
        back_gains = lax.all_gather(norm_gains, "fsdp", axis=0, tiled=True)
        back_gain_float = back_gains.astype(jnp.float32)
        grad_gathered = lax.all_gather(grad_out, "fsdp", axis=0, tiled=True)
        one_grad_fc_in, one_grad_fc_out, one_grad_fc_bias, grad_partial = feed_back(
            mlp_inputs, grad_gathered, pre_active, active, fc_in, fc_out
        )
        grad_normed_three = lax.psum_scatter(
            grad_partial.astype(jnp.bfloat16), "fsdp", scatter_dimension=0, tiled=True
        ).astype(jnp.float32)
        grad_three, gain_three, shift_three = norm_backward(
            grad_normed_three, scaled_three, inverse_three, back_gain_float[:, 2]
        )
        grad_after_cross = grad_out.astype(jnp.float32) + grad_three
        grad_cross_branch = grad_after_cross.astype(jnp.bfloat16)
        grad_cross_out = weight_grad(cross_mixed, grad_cross_branch)
        grad_cross_mixed = project_back(grad_cross_branch, back_cross_out).astype(jnp.bfloat16)
        cross_grad_queries, memory_grad_keys, memory_grad_values = attend_backward(
            split_heads(cross_queries),
            memory_key_rows,
            memory_value_rows,
            cross_allowed,
            cross_totals,
            split_heads(grad_cross_mixed),
        )
        own_memory_keys = lax.psum_scatter(
            memory_grad_keys.astype(jnp.bfloat16), "seq", scatter_dimension=1, tiled=True
        )
        own_memory_values = lax.psum_scatter(
            memory_grad_values.astype(jnp.bfloat16), "seq", scatter_dimension=1, tiled=True
        )
        grad_memory_kv = jnp.concatenate([own_memory_keys, own_memory_values], axis=-1)
        grad_memory_weight = weight_grad(memory_rows, grad_memory_kv)
        memory_grad = project_back(grad_memory_kv, back_memory_kv).astype(jnp.bfloat16)[:, None]
        grad_cross_queries = cross_grad_queries.astype(jnp.bfloat16)
        grad_query_weight = weight_grad(normed_two, grad_cross_queries)
        grad_normed_two = project_back(grad_cross_queries, back_query)
        grad_two, gain_two, shift_two = norm_backward(
            grad_normed_two, scaled_two, inverse_two, back_gain_float[:, 1]
        )
        grad_after_self = grad_after_cross + grad_two
        grad_self_branch = grad_after_self.astype(jnp.bfloat16)
        grad_self_out = weight_grad(self_mixed, grad_self_branch)
        grad_self_mixed = project_back(grad_self_branch, back_self_out).astype(jnp.bfloat16)
        self_grad_queries, self_grad_keys, self_grad_values = attend_backward(
            self_queries,
            self_key_rows,
            self_value_rows,
            self_allowed,
            self_totals,
            split_heads(grad_self_mixed),
        )
        own_self_keys = lax.psum_scatter(
            self_grad_keys.astype(jnp.bfloat16), "seq", scatter_dimension=1, tiled=True
        )
        own_self_values = lax.psum_scatter(
            self_grad_values.astype(jnp.bfloat16), "seq", scatter_dimension=1, tiled=True
        )
        grad_projected = jnp.concatenate(
            [self_grad_queries.astype(jnp.bfloat16), own_self_keys, own_self_values], axis=-1
        )
        grad_qkv_weight = weight_grad(normed_one, grad_projected)
        grad_normed_one = project_back(grad_projected, back_qkv)
        grad_one, gain_one, shift_one = norm_backward(
            grad_normed_one, scaled_one, inverse_one, back_gain_float[:, 0]
        )
        hidden_grad = (grad_after_self + grad_one).astype(jnp.bfloat16)[:, None]
        grad_biases = jnp.stack(
            [
                column_sums(grad_projected[..., :model_width]),
                column_sums(grad_projected[..., 2 * model_width :]),
                column_sums(grad_self_branch),
                column_sums(grad_cross_queries),
                column_sums(grad_memory_kv[..., model_width:]),
                column_sums(grad_cross_branch),
                column_sums(grad_out),
            ],
            axis=1,
        )
        grad_gains = jnp.stack([gain_one, gain_two, gain_three], axis=1)
        grad_shifts = jnp.stack([shift_one, shift_two, shift_three], axis=1)
        attn_grads = (
            grad_qkv_weight,
            grad_self_out,
            grad_query_weight,
            grad_memory_weight,
            grad_cross_out,
            grad_biases,
            grad_gains,
            grad_shifts,
        )
        mlp_grads = (one_grad_fc_in, one_grad_fc_out, one_grad_fc_bias)
        hidden_out, hidden_grad, memory_grad, attn_grads, mlp_grads = (
            hidden_out,
            hidden_grad,
            memory_grad,
            attn_grads,
            mlp_grads,
        )
        outputs_list.append(hidden_out)
        grads_list.append(hidden_grad)
        memory_list.append(memory_grad)
        if attn_total is None:
            attn_total = attn_grads
            mlp_total = mlp_grads
        else:
            attn_total = jax.tree.map(jnp.add, attn_total, attn_grads)
            mlp_total = jax.tree.map(jnp.add, mlp_total, mlp_grads)
    grad_fc_in, grad_fc_out, grad_fc_bias = mlp_total
    (
        shard_qkv,
        shard_self_out,
        shard_query,
        shard_memory_kv,
        shard_cross_out,
        shard_biases,
        shard_gains,
        shard_shifts,
    ) = (
        lax.psum_scatter(
            attn_total[0].astype(jnp.bfloat16), "fsdp", scatter_dimension=0, tiled=True
        ).astype(jnp.float32),
        lax.psum_scatter(
            attn_total[1].astype(jnp.bfloat16), "fsdp", scatter_dimension=0, tiled=True
        ).astype(jnp.float32),
        lax.psum_scatter(
            attn_total[2].astype(jnp.bfloat16), "fsdp", scatter_dimension=0, tiled=True
        ).astype(jnp.float32),
        lax.psum_scatter(
            attn_total[3].astype(jnp.bfloat16), "fsdp", scatter_dimension=0, tiled=True
        ).astype(jnp.float32),
        lax.psum_scatter(
            attn_total[4].astype(jnp.bfloat16), "fsdp", scatter_dimension=0, tiled=True
        ).astype(jnp.float32),
        lax.psum_scatter(
            attn_total[5].astype(jnp.bfloat16), "fsdp", scatter_dimension=0, tiled=True
        ).astype(jnp.float32),
        lax.psum_scatter(
            attn_total[6].astype(jnp.bfloat16), "fsdp", scatter_dimension=0, tiled=True
        ).astype(jnp.float32),
        lax.psum_scatter(
            attn_total[7].astype(jnp.bfloat16), "fsdp", scatter_dimension=0, tiled=True
        ).astype(jnp.float32),
    )
    summed = (
        lax.psum(shard_qkv.astype(jnp.bfloat16), ("rep", "seq")).astype(jnp.float32),
        lax.psum(shard_self_out.astype(jnp.bfloat16), ("rep", "seq")).astype(jnp.float32),
        lax.psum(shard_query.astype(jnp.bfloat16), ("rep", "seq")).astype(jnp.float32),
        lax.psum(shard_memory_kv.astype(jnp.bfloat16), ("rep", "seq")).astype(jnp.float32),
        lax.psum(shard_cross_out.astype(jnp.bfloat16), ("rep", "seq")).astype(jnp.float32),
        lax.psum(grad_fc_in.astype(jnp.bfloat16), ("rep", "seq")).astype(jnp.float32),
        lax.psum(grad_fc_out.astype(jnp.bfloat16), ("rep", "seq")).astype(jnp.float32),
        lax.psum(shard_biases.astype(jnp.bfloat16), ("rep", "seq")).astype(jnp.float32),
        lax.psum(grad_fc_bias.astype(jnp.bfloat16), ("rep", "seq")).astype(jnp.float32),
        lax.psum(shard_gains.astype(jnp.bfloat16), ("rep", "seq")).astype(jnp.float32),
        lax.psum(shard_shifts.astype(jnp.bfloat16), ("rep", "seq")).astype(jnp.float32),
    )
    hidden_out = jnp.concatenate(outputs_list, axis=0)
    hidden_grad = jnp.concatenate(grads_list, axis=0)
    memory_grad = jnp.concatenate(memory_list, axis=0)
    return (
        hidden_out,
        hidden_grad,
        memory_grad,
        summed[0],
        summed[1],
        summed[2],
        summed[3],
        summed[4],
        summed[5],
        summed[6],
        summed[7],
        summed[8],
        summed[9],
        summed[10],
    )


def mul(left, right):
    return jnp.dot(left, right, preferred_element_type=jnp.float32)


def mul_nt(left, right):
    return lax.dot_general(left, right, (((1,), (1,)), ((), ())), preferred_element_type=jnp.float32)


def mul_tn(left, right):
    return lax.dot_general(left, right, (((0,), (0,)), ((), ())), preferred_element_type=jnp.float32)


MESH = pl.DeviceIdType.MESH


def gelu_pair(values):
    depth = 1.0 + (0.3275911 * 2.0**-0.5) * jnp.abs(values)
    inv = pltpu.reciprocal(depth, approx=True)
    inv = inv * (2.0 - depth * inv)
    bell = jnp.exp(-0.5 * values * values)
    series = 0.7107068705 + inv * (-0.7265760135 + inv * 0.5307027145)
    series = inv * (0.127414796 + inv * (-0.142248368 + inv * series))
    tail = series * bell
    cumulative = jnp.where(values >= 0.0, 1.0 - tail, tail)
    return values * cumulative, cumulative + values * (bell * (1.0 / math.sqrt(2.0 * math.pi)))


def position():
    rep, core, deep = lax.axis_index("rep"), lax.axis_index("fsdp"), lax.axis_index("seq")
    return rep % 2, rep // 2, core, deep


def device(across, up, core, deep):
    return (up * 2 + across, core, deep)


def greet(partners):
    barrier = pltpu.get_barrier_semaphore()
    for partner in partners:
        pl.semaphore_signal(barrier, inc=1, device_id=partner, device_id_type=MESH)
    pl.semaphore_wait(barrier, len(partners))


class ChunkSum:
    def __init__(self, turned, column, width, own_ref, sum_ref, held, first, second, third, done, send, recv, local):
        across, up, core, deep = position()
        self.side, self.next = (up, across) if turned else (across, up)
        one = device(1 - across, up, core, deep)
        two = device(across, 1 - up, core, deep)
        self.one, self.two = (two, one) if turned else (one, two)
        self.deep = deep
        self.others = [(deep + step) % 4 for step in (1, 2, 3)]
        self.third_ids = [device(across, up, core, other) for other in self.others]
        self.columns = pl.ds(column, width)
        self.own, self.sum = own_ref, sum_ref
        self.held, self.first, self.second, self.third, self.done = held, first, second, third, done
        self.send, self.recv, self.local = send, recv, local
        self.quarter = pl.multiple_of(self.next * 128, 128)
        self.start_row = self.side * 256

    def remote(self, index, src, dst, target):
        return pltpu.make_async_remote_copy(
            src_ref=src,
            dst_ref=dst,
            send_sem=self.send.at[index],
            recv_sem=self.recv.at[index],
            device_id=target,
            device_id_type=MESH,
        )

    def rows(self, ref, start, count):
        return ref.at[pl.ds(pl.multiple_of(start, 32), count), self.columns]

    def copy_a(self):
        return self.remote(0, self.rows(self.own, (1 - self.side) * 256, 256), self.first, self.one)

    def load(self):
        return pltpu.make_async_copy(self.rows(self.own, self.start_row, 256), self.held, self.local.at[0])

    def copy_b(self):
        away = pl.multiple_of((1 - self.next) * 128, 128)
        return self.remote(1, self.held.at[pl.ds(away, 128)], self.second, self.two)

    def copy_c(self, turn):
        start = pl.multiple_of(self.quarter + self.others[turn] * 32, 32)
        return self.remote(2 + turn, self.held.at[pl.ds(start, 32)], self.third.at[turn], self.third_ids[turn])

    def place(self):
        return self.rows(self.sum, self.start_row + self.quarter + self.deep * 32, 32)

    def copy_d(self, turn):
        return self.remote(5 + turn, self.done, self.place(), self.third_ids[turn])

    def store(self):
        return pltpu.make_async_copy(self.done, self.place(), self.local.at[1])

    def copy_e(self):
        part = self.rows(self.sum, self.start_row + self.quarter, 128)
        return self.remote(8, part, part, self.two)

    def copy_f(self):
        part = self.rows(self.sum, self.start_row, 256)
        return self.remote(9, part, part, self.one)

    def stage(self, number):
        if number == 0:
            self.copy_a().start()
            self.load().start()
        elif number == 1:
            self.load().wait()
            self.copy_a().wait_recv()
            self.held[...] = self.held[...] + self.first[...]
            self.copy_b().start()
        elif number == 2:
            self.copy_b().wait_recv()
            self.copy_b().wait_send()
            mine = pl.ds(self.quarter, 128)
            self.held[mine] = self.held[mine] + self.second[...]
            for turn in range(3):
                self.copy_c(turn).start()
        elif number == 3:
            for turn in range(3):
                self.copy_c(turn).wait_recv()
            start = pl.multiple_of(self.quarter + self.deep * 32, 32)
            total = self.held[pl.ds(start, 32)].astype(jnp.float32)
            for turn in range(3):
                total += self.third[turn].astype(jnp.float32)
            self.done[...] = total.astype(self.done.dtype)
            self.store().start()
            for turn in range(3):
                self.copy_d(turn).start()
        elif number == 4:
            self.store().wait()
            for turn in range(3):
                self.copy_d(turn).wait_recv()
            self.copy_e().start()
        elif number == 5:
            self.copy_e().wait_recv()
            self.copy_f().start()
        elif number == 6:
            self.copy_f().wait_recv()
            self.copy_a().wait_send()
            for turn in range(3):
                self.copy_c(turn).wait_send()
                self.copy_d(turn).wait_send()
            self.copy_e().wait_send()
            self.copy_f().wait_send()


AFTER = (0, 5, 8, 12, 16, 19, 24)


def ffn_kernel(
    step, plan, rows_ref, grads_ref, in_ref, out_ref, bias_ref, own_ref,
    din_ref, dout_ref, dbias_ref, sum_ref, flip, acc, us, das, *rest
):
    units = flip.shape[0]
    steps = rows_ref.shape[0] // step
    at = pl.program_id(0)
    send, recv, local = rest[-3:]
    buffers = rest[:-3]
    chunks = []
    for index, (turned, column, width, begin) in enumerate(plan):
        held, first, second, third, done = buffers[5 * index : 5 * index + 5]
        chunks.append(
            ChunkSum(turned, column, width, own_ref, sum_ref, held, first, second, third, done,
                     send.at[index], recv.at[index], local.at[index])
        )

    @pl.when(at == 0)
    def _():
        across, up, core, deep = position()
        greet(
            [device(1 - across, up, core, deep), device(across, 1 - up, core, deep)]
            + [device(across, up, core, (deep + turn) % 4) for turn in (1, 2, 3)]
        )

    def traffic(turn):
        work = {}
        for chunk, (_, _, _, begin) in zip(chunks, plan):
            for number, after in enumerate(AFTER):
                slot = begin + after
                if slot % steps == turn:
                    work.setdefault(slot // steps, []).append((chunk, number))
        for when, jobs in sorted(work.items()):
            @pl.when(at == when)
            def _():
                for chunk, number in jobs:
                    chunk.stage(number)

    flip[...] = in_ref[...].T

    def front(turn):
        part = pl.ds(turn * step, step)
        us[turn % 2] = mul_nt(flip[...], rows_ref[part, :])
        das[turn % 2] = mul_nt(out_ref[...], grads_ref[part, :])

    traffic(0)
    front(0)
    bias = jnp.broadcast_to(bias_ref[...], (128, units)).T[:, :1]
    total = jnp.zeros((units, 128), jnp.float32)
    for turn in range(steps):
        if turn:
            traffic(turn)
        if turn + 1 < steps:
            front(turn + 1)
        active, slope = gelu_pair(us[turn % 2] + bias)
        active = active.astype(jnp.bfloat16)
        inner = (das[turn % 2] * slope).astype(jnp.bfloat16)
        for lane in range(step // 128):
            total += inner[:, lane * 128 : (lane + 1) * 128].astype(jnp.float32)
        part = pl.ds(turn * step, step)
        if turn == 0:
            dout_ref[...] = mul(active, grads_ref[part, :])
            acc[...] = mul(inner, rows_ref[part, :])
        else:
            dout_ref[...] += mul(active, grads_ref[part, :])
            acc[...] += mul(inner, rows_ref[part, :])
    din_ref[...] = acc[...].T
    dbias_ref[...] = jnp.sum(total.T, axis=0, keepdims=True)


def ffn_grads(rows, grads, fc_in, fc_out, bias, own):
    count, width = rows.shape
    hidden = fc_in.shape[1]
    units, step = 256, 1024
    plan = [(False, 8 * width, 128, 0)]
    for pair in range(4):
        plan.append((False, pair * width, width, 1 + 10 * pair))
        plan.append((True, (4 + pair) * width, width, 1 + 10 * pair))
    buffers = []
    for _, _, columns, _ in plan:
        buffers += [
            pltpu.VMEM((256, columns), jnp.bfloat16),
            pltpu.VMEM((256, columns), jnp.bfloat16),
            pltpu.VMEM((128, columns), jnp.bfloat16),
            pltpu.VMEM((3, 32, columns), jnp.bfloat16),
            pltpu.VMEM((32, columns), jnp.bfloat16),
        ]
    whole = functools.partial(pl.BlockSpec, pipeline_mode=pl.Buffered(1))
    return pl.pallas_call(
        functools.partial(ffn_kernel, step, plan),
        grid=(hidden // units,),
        in_specs=[
            whole((count, width), lambda at: (0, 0)),
            whole((count, width), lambda at: (0, 0)),
            pl.BlockSpec((width, units), lambda at: (0, at)),
            pl.BlockSpec((units, width), lambda at: (at, 0)),
            pl.BlockSpec((1, units), lambda at: (0, at)),
            pl.BlockSpec(memory_space=pl.ANY),
        ],
        out_specs=[
            pl.BlockSpec((width, units), lambda at: (0, at)),
            pl.BlockSpec((units, width), lambda at: (at, 0)),
            pl.BlockSpec((1, units), lambda at: (0, at)),
            pl.BlockSpec(memory_space=pl.ANY),
        ],
        out_shape=[
            jax.ShapeDtypeStruct((width, hidden), jnp.float32),
            jax.ShapeDtypeStruct((hidden, width), jnp.float32),
            jax.ShapeDtypeStruct((1, hidden), jnp.float32),
            jax.ShapeDtypeStruct(own.shape, own.dtype),
        ],
        scratch_shapes=[
            pltpu.VMEM((units, width), jnp.bfloat16),
            pltpu.VMEM((units, width), jnp.float32),
            pltpu.VMEM((2, units, step), jnp.float32),
            pltpu.VMEM((2, units, step), jnp.float32),
            *buffers,
            pltpu.SemaphoreType.DMA((len(plan), 10)),
            pltpu.SemaphoreType.DMA((len(plan), 10)),
            pltpu.SemaphoreType.DMA((len(plan), 2)),
        ],
        compiler_params=pltpu.CompilerParams(
            vmem_limit_bytes=58 * 2**20, collective_id=0, has_side_effects=True
        ),
        cost_estimate=pl.CostEstimate(
            flops=8 * count * width * hidden,
            bytes_accessed=4 * count * width + 12 * width * hidden,
            transcendentals=count * hidden,
        ),
    )(rows, grads, fc_in, fc_out, bias, own)


def norm_parts(values):
    centred = values - jnp.mean(values, axis=-1, keepdims=True)
    inverse = lax.rsqrt(jnp.mean(centred * centred, axis=-1, keepdims=True) + NORM_EPSILON)
    return centred * inverse, inverse


def normed(values, vectors, which):
    scaled, _ = norm_parts(values)
    return (scaled * vectors[7 + which : 8 + which] + vectors[10 + which : 11 + which]).astype(jnp.bfloat16)


class Partner:
    def __init__(self, send, recv):
        across, up, core, deep = position()
        self.core = core
        self.id = device(across, up, 1 - core, deep)
        self.send, self.recv = send, recv
        self.copies = []

    def push(self, src, dst):
        index = len(self.copies)
        copy = pltpu.make_async_remote_copy(
            src_ref=src,
            dst_ref=dst,
            send_sem=self.send.at[index],
            recv_sem=self.recv.at[index],
            device_id=self.id,
            device_id_type=MESH,
        )
        copy.start()
        self.copies.append(copy)
        return copy

    def finish(self):
        for copy in self.copies:
            copy.wait_send()


class Weights:
    def __init__(self, partner, shard, whole, local):
        half = shard.shape[0]
        mine = whole.at[pl.ds(pl.multiple_of(partner.core * half, half), half)]
        self.remote = partner.push(shard, mine)
        self.near = pltpu.make_async_copy(shard, mine, local)
        self.near.start()
        self.whole = whole

    def get(self):
        self.near.wait()
        self.remote.wait_recv()
        return self.whole


def two_heads(values, lane):
    zero = jnp.zeros_like(values)
    return jnp.concatenate([jnp.where(lane, values, zero), jnp.where(lane, zero, values)], axis=0)


def lane_of():
    return lax.broadcasted_iota(jnp.int32, (1, 2 * HEAD), 1) < HEAD


def attend(q_ref, k_ref, v_ref, p_ref, o_ref, allowed):
    lane = lane_of()
    count = q_ref.shape[0]
    for pair in range(q_ref.shape[1] // (2 * HEAD)):
        columns = pl.ds(pair * 2 * HEAD, 2 * HEAD)
        scores = mul_nt(two_heads(q_ref[:, columns], lane), k_ref[:, columns])
        scores = jnp.where(allowed, scores * HEAD ** (-0.5), MASKED_SCORE)
        exponent = jnp.exp(scores - jnp.max(scores, axis=-1, keepdims=True))
        weights = (exponent / jnp.sum(exponent, axis=-1, keepdims=True)).astype(jnp.bfloat16)
        p_ref[pair] = weights
        mixed = mul(weights, v_ref[:, columns])
        o_ref[:, columns] = jnp.where(lane, mixed[:count], mixed[count:]).astype(jnp.bfloat16)


def attend_back(q_ref, k_ref, v_ref, p_ref, go_ref, dq_ref, dk_ref, dv_ref):
    lane = lane_of()
    count = q_ref.shape[0]
    for pair in range(q_ref.shape[1] // (2 * HEAD)):
        columns = pl.ds(pair * 2 * HEAD, 2 * HEAD)
        grads = two_heads(go_ref[:, columns], lane)
        weights = p_ref[pair]
        dv_ref[:, columns] = mul_tn(weights, grads).astype(jnp.bfloat16)
        grad_weights = mul_nt(grads, v_ref[:, columns])
        exact = weights.astype(jnp.float32)
        inner = jnp.sum(grad_weights * exact, axis=-1, keepdims=True)
        scores = (exact * (grad_weights - inner)).astype(jnp.bfloat16)
        queries = mul(scores, k_ref[:, columns]) * HEAD ** (-0.5)
        dq_ref[:, columns] = jnp.where(lane, queries[:count], queries[count:]).astype(jnp.bfloat16)
        keys = mul_tn(scores, two_heads(q_ref[:, columns], lane)) * HEAD ** (-0.5)
        dk_ref[:, columns] = keys.astype(jnp.bfloat16)


def norm_back(grads, values, gain, sums_ref, row):
    scaled, inverse = norm_parts(values)
    sums_ref[row : row + 1, :] = jnp.sum(grads * scaled, axis=0, keepdims=True)
    sums_ref[row + 3 : row + 4, :] = jnp.sum(grads, axis=0, keepdims=True)
    inner = grads * gain
    first = jnp.mean(inner, axis=-1, keepdims=True)
    second = jnp.mean(inner * scaled, axis=-1, keepdims=True)
    return (inner - first - scaled * second) * inverse


class Bring:
    def __init__(self, src, dst, send, recv, local):
        across, up, core, deep = position()
        self.core, self.deep = core, deep
        self.src, self.dst = src, dst
        self.send, self.recv, self.local = send, recv, local
        self.across, self.up = across, up

    def stays(self, micro):
        return (self.deep // 2 == self.core) & (2 * micro + self.core == self.deep)

    def far(self, micro, index):
        block = self.src.shape[1]
        return pltpu.make_async_remote_copy(
            src_ref=self.src.at[micro],
            dst_ref=self.dst.at[pl.ds(pl.multiple_of(self.deep * block, block), block)],
            send_sem=self.send.at[micro],
            recv_sem=self.recv.at[index],
            device_id=device(self.across, self.up, self.deep // 2, 2 * micro + self.core),
            device_id_type=MESH,
        )

    def near(self, micro):
        block = self.src.shape[1]
        return pltpu.make_async_copy(
            self.src.at[micro],
            self.dst.at[pl.ds(pl.multiple_of(self.deep * block, block), block)],
            self.local,
        )

    def start(self):
        for micro in range(2):
            @pl.when(self.stays(micro))
            def _():
                self.near(micro).start()

            @pl.when(jnp.logical_not(self.stays(micro)))
            def _():
                self.far(micro, self.deep % 2).start()

    def wait(self):
        for block in range(2):
            here = (self.deep % 2 == self.core) & (2 * self.core + block == self.deep)

            @pl.when(here)
            def _():
                self.near(block).wait()

            @pl.when(jnp.logical_not(here))
            def _():
                self.far(block, block).wait_recv()

    def finish(self):
        for micro in range(2):
            @pl.when(jnp.logical_not(self.stays(micro)))
            def _():
                self.far(micro, self.deep % 2).wait_send()


class SendBack:
    def __init__(self, src, dst, send, recv, local):
        self.src, self.dst = src, dst
        self.send, self.recv, self.local = send, recv, local
        self.across, self.up, self.core, self.deep = position()

    def stays(self, block):
        return (self.deep % 2 == self.core) & (2 * self.core + block == self.deep)

    def far(self, block, index):
        count = self.dst.shape[1]
        return pltpu.make_async_remote_copy(
            src_ref=self.src.at[pl.ds(block * count, count)],
            dst_ref=self.dst.at[self.deep // 2],
            send_sem=self.send.at[block],
            recv_sem=self.recv.at[index],
            device_id=device(self.across, self.up, self.deep % 2, 2 * self.core + block),
            device_id_type=MESH,
        )

    def near(self, block):
        count = self.dst.shape[1]
        return pltpu.make_async_copy(
            self.src.at[pl.ds(block * count, count)], self.dst.at[self.deep // 2], self.local
        )

    def start(self):
        for block in range(2):
            @pl.when(self.stays(block))
            def _():
                self.near(block).start()

            @pl.when(jnp.logical_not(self.stays(block)))
            def _():
                self.far(block, self.deep // 2).start()

    def finish(self):
        for micro in range(2):
            here = (self.deep // 2 == self.core) & (2 * micro + self.core == self.deep)

            @pl.when(here)
            def _():
                self.near(micro).wait()

            @pl.when(jnp.logical_not(here))
            def _():
                self.far(micro, micro).wait_recv()
        for block in range(2):
            @pl.when(jnp.logical_not(self.stays(block)))
            def _():
                self.far(block, self.deep // 2).wait_send()


class Spread:
    def __init__(self, own, every, send, recv, local):
        self.own, self.every = own, every
        self.send, self.recv, self.local = send, recv, local
        self.across, self.up, self.core, self.deep = position()
        self.count = own.shape[0]
        self.right = device(1 - self.across, self.up, self.core, self.deep)
        self.above = device(self.across, 1 - self.up, self.core, self.deep)
        self.twin = device(self.across, self.up, 1 - self.core, self.deep)

    def item(self, flip_x, flip_y, step, half=None):
        across = 1 - self.across if flip_x else self.across
        up = 1 - self.up if flip_y else self.up
        slot = ((up * 2 + across) * 4 + (self.deep + step) % 4) * 2 + self.core
        start = slot * self.count
        if half is None:
            return self.every.at[pl.ds(pl.multiple_of(start, self.count), self.count)]
        part = self.count // 2
        return self.every.at[pl.ds(pl.multiple_of(start + half * part, part), part)]

    def copy(self, index, src, dst, target):
        return pltpu.make_async_remote_copy(
            src_ref=src,
            dst_ref=dst,
            send_sem=self.send.at[index],
            recv_sem=self.recv.at[index],
            device_id=target,
            device_id_type=MESH,
        )

    def along(self, step):
        target = device(self.across, self.up, self.core, (self.deep + step) % 4)
        return self.copy(step - 1, self.own, self.item(False, False, 0), target)

    def column(self, step, index, target):
        place = self.item(False, False, step)
        return self.copy(index + step, self.own if step == 0 else place, place, target)

    def passed(self, step, index, flip_x, flip_y, target, half=None):
        place = self.item(flip_x, flip_y, step, half)
        return self.copy(index + step, place, place, target)

    def store(self):
        return pltpu.make_async_copy(self.own, self.item(False, False, 0), self.local)

    def fan(self, step):
        self.column(step, 3, self.right).start()
        self.column(step, 7, self.above).start()
        self.column(step, 19, self.twin).start()

    def begin(self):
        self.fan(0)
        for step in (1, 3, 2):
            self.along(step).start()
        self.store().start()

    def relay(self, step):
        self.along(4 - step).wait_recv()
        self.fan(step)

    def corner(self, step):
        self.column(step, 3, self.right).wait_recv()
        self.passed(step, 15, True, False, self.above, 0).start()
        self.passed(step, 23, True, False, self.twin).start()
        self.column(step, 7, self.above).wait_recv()
        self.passed(step, 11, False, True, self.right, 1).start()
        self.passed(step, 27, False, True, self.twin).start()

    def last(self, step):
        self.passed(step, 15, True, False, self.above, 0).wait_recv()
        self.passed(step, 11, False, True, self.right, 1).wait_recv()
        self.passed(step, 31, True, True, self.twin).start()

    def finish(self):
        self.store().wait()
        for step in range(4):
            arrivals = [
                self.column(step, 19, self.twin),
                self.passed(step, 23, True, False, self.twin),
                self.passed(step, 27, False, True, self.twin),
                self.passed(step, 31, True, True, self.twin),
            ]
            for copy in arrivals:
                copy.wait_recv()
                copy.wait_send()
            self.column(step, 3, self.right).wait_send()
            self.column(step, 7, self.above).wait_send()
            self.passed(step, 15, True, False, self.above, 0).wait_send()
            self.passed(step, 11, False, True, self.right, 1).wait_send()
            if step:
                self.along(step).wait_send()


def layer_kernel(
    vec_half_ref, ids_ref, fcb_ref, x_hbm, m_hbm, g_hbm,
    qkv_hbm, so_hbm, cq_hbm, ckv_hbm, co_hbm, in_hbm, out_hbm,
    y_out, dx_out, dm_out, grads_ref, every_n, every_g,
    x_ref, m_ref, g_ref, vec_ref, ids_got, ids_all, id_rows,
    n1_ref, q1_ref, k1_ref, v1_ref, p1_ref, o1_ref, h1_ref, n2_ref, q2_ref, k2_ref, v2_ref, p2_ref,
    o2_ref, h2_ref, n3_ref, y_ref, dx_ref, dm_ref,
    qkv_w, so_w, cq_w, ckv_w, co_w, in_w, out_w, chip_n, acc_y, acc_n, part, got, go_ref,
    dkv2, dkv2_got, dkv1, dkv1_got, dq1, dq2, e1, e2, n2_half, o1_half, o2_half, dh_ref, sums, sums_got,
    stage, send, recv, local, tiles, stores, move_send, move_recv, move_local,
    spread_send, spread_recv, spread_local,
):
    across, up, core, deep = position()
    column = [device(across, up, 1 - core, deep)]
    for turn in (1, 2, 3):
        for other in (0, 1):
            column.append(device(across, up, other, (deep + turn) % 4))
    greet(column + [device(1 - across, up, core, deep), device(across, 1 - up, core, deep)])
    partner = Partner(send, recv)
    bf16, f32 = jnp.bfloat16, jnp.float32
    count, width = q1_ref.shape
    units = in_w.shape[2]
    half = width // 2
    mine = pl.ds(pl.multiple_of(core * count, count), count)
    theirs = pl.ds(pl.multiple_of((1 - core) * count, count), count)
    my_half = pl.ds(pl.multiple_of(core * half, half), half)
    their_half = pl.ds(pl.multiple_of((1 - core) * half, half), half)

    def bring(index, src, dst):
        return Bring(src, dst, move_send.at[index], move_recv.at[index], move_local.at[index])

    def give(index, src, dst):
        return SendBack(src, dst, move_send.at[index], move_recv.at[index], move_local.at[index])

    bring_x = bring(0, x_hbm, x_ref)
    bring_x.start()
    sent_ids = partner.push(ids_ref, ids_got)
    sent_vec = partner.push(vec_half_ref, vec_ref.at[:, my_half])
    vec_ref[:, my_half] = vec_half_ref[...]
    qkv = Weights(partner, qkv_hbm, qkv_w, local.at[0])
    bring_x.wait()
    sent_x = partner.push(x_ref.at[mine], x_ref.at[mine])
    bring_g, bring_m = bring(1, g_hbm, g_ref), bring(2, m_hbm, m_ref)
    bring_m.start()
    bring_g.start()
    so = Weights(partner, so_hbm, so_w, local.at[2])
    ckv = Weights(partner, ckv_hbm, ckv_w, local.at[1])
    cq = Weights(partner, cq_hbm, cq_w, local.at[3])
    co = Weights(partner, co_hbm, co_w, local.at[4])

    sent_ids.wait_recv()
    ids = jnp.where(deep % 2 == core, ids_ref[...], ids_got[...])
    ids_all[...] = ids
    micro = deep // 2
    token_row = jnp.where(micro == 0, ids[0:1], ids[1:2])
    source_row = jnp.where(micro == 0, ids[2:3], ids[3:4])
    id_rows[...] = jnp.broadcast_to(token_row, (128, token_row.shape[1])).T
    query_ids = id_rows[mine, :][:, :1]
    sent_vec.wait_recv()
    vectors = vec_ref[...]
    sent_x.wait_recv()
    n1_ref[...] = normed(x_ref[...].astype(f32), vectors, 0)
    place = core * count + lax.broadcasted_iota(jnp.int32, (count, 1), 0)
    keys = lax.broadcasted_iota(jnp.int32, (1, token_row.shape[1]), 1)
    allowed = (place >= keys) & (query_ids == token_row)
    allowed = jnp.concatenate([allowed, allowed], axis=0)
    w = qkv.get()
    q1_ref[...] = (mul(n1_ref[mine, :], w[:, :width]) + vectors[0:1]).astype(bf16)
    k1_ref[...] = mul(n1_ref[...], w[:, width : 2 * width]).astype(bf16)
    v1_ref[...] = (mul(n1_ref[...], w[:, 2 * width :]) + vectors[1:2]).astype(bf16)
    attend(q1_ref, k1_ref, v1_ref, p1_ref, o1_ref, allowed)
    bring_m.wait()
    sent_m = partner.push(m_ref.at[mine], m_ref.at[mine])
    bring_g.wait()
    sent_g = partner.push(g_ref.at[mine], g_ref.at[mine])
    spread_g = Spread(g_ref.at[mine], every_g, spread_send.at[0], spread_recv.at[0], spread_local.at[0])
    spread_g.begin()
    w = so.get()
    h1_ref[...] = x_ref[mine, :].astype(f32) + mul(o1_ref[...], w[...]) + vectors[2:3]
    n2_ref[...] = normed(h1_ref[...], vectors, 1)
    w = ckv.get()
    sent_m.wait_recv()
    k2_ref[...] = mul(m_ref[...], w[:, :width]).astype(bf16)
    v2_ref[...] = (mul(m_ref[...], w[:, width:]) + vectors[4:5]).astype(bf16)
    w = cq.get()
    q2_ref[...] = (mul(n2_ref[...], w[...]) + vectors[3:4]).astype(bf16)
    allowed = query_ids == source_row
    allowed = jnp.concatenate([allowed, allowed], axis=0)
    attend(q2_ref, k2_ref, v2_ref, p2_ref, o2_ref, allowed)
    w = co.get()
    h2_ref[...] = h1_ref[...] + mul(o2_ref[...], w[...]) + vectors[5:6]
    n3_ref[...] = normed(h2_ref[...], vectors, 2)
    rows_sent = partner.push(n3_ref, chip_n.at[mine])
    chip_n[mine, :] = n3_ref[...]
    spread_g.relay(1)
    spread_g.relay(3)
    spread_n = Spread(n3_ref, every_n, spread_send.at[1], spread_recv.at[1], spread_local.at[1])
    spread_n.begin()

    def tile_copies(index):
        slot = index % 2
        where = pl.ds(index * units, units)
        return (
            pltpu.make_async_copy(in_hbm.at[:, where], in_w.at[slot], tiles.at[slot, 0]),
            pltpu.make_async_copy(out_hbm.at[where], out_w.at[slot], tiles.at[slot, 1]),
        )

    steps = in_hbm.shape[1] // units
    for copy in tile_copies(0):
        copy.start()
    halves = [
        partner.push(n2_ref.at[:, their_half], n2_half.at[mine]),
        partner.push(o1_ref.at[:, their_half], o1_half.at[mine]),
        partner.push(o2_ref.at[:, their_half], o2_half.at[mine]),
    ]
    n2_half[mine, :] = n2_ref[:, my_half]
    o1_half[mine, :] = o1_ref[:, my_half]
    o2_half[mine, :] = o2_ref[:, my_half]
    sent_g.wait_recv()
    rows_sent.wait_recv()
    for index in range(steps):
        if index + 1 < steps:
            for copy in tile_copies(index + 1):
                copy.start()
        for copy in tile_copies(index):
            copy.wait()
        slot = index % 2
        inner = mul(chip_n[...], in_w[slot]) + fcb_ref[:, index * units : (index + 1) * units]
        active, slope = gelu_pair(inner)
        back = (mul_nt(g_ref[...], out_w[slot]) * slope).astype(bf16)
        if index == 0:
            acc_y[...] = mul(active.astype(bf16), out_w[slot])
            acc_n[...] = mul_nt(back, in_w[slot])
        else:
            acc_y[...] += mul(active.astype(bf16), out_w[slot])
            acc_n[...] += mul_nt(back, in_w[slot])
        if index == 2 * steps // 8:
            spread_g.relay(2)
            spread_g.corner(0)
        if index == 6 * steps // 8:
            spread_g.corner(1)
            spread_g.corner(3)
    part[0] = acc_n[theirs, :].astype(bf16)
    sent_n = partner.push(part.at[0], got.at[0])
    part[1] = acc_y[theirs, :].astype(bf16)
    sent_y = partner.push(part.at[1], got.at[1])
    spread_n.relay(1)
    spread_n.relay(3)

    sent_n.wait_recv()
    grad = acc_n[mine, :] + got[0].astype(f32)
    grad = norm_back(grad, h2_ref[...], vectors[9:10], sums, 2) + g_ref[mine, :].astype(f32)
    dh_ref[...] = grad
    e2[mine, :] = grad.astype(bf16)
    sent_e2 = partner.push(e2.at[mine], e2.at[mine])
    sent_y.wait_recv()
    y = h2_ref[...] + (acc_y[mine, :] + got[1].astype(f32) + vectors[6:7])
    y_ref[...] = y.astype(bf16)
    give_y = give(3, y_ref, y_out)
    give_y.start()
    go_ref[...] = mul_nt(e2[mine, :], co_w[...]).astype(bf16)
    attend_back(q2_ref, k2_ref, v2_ref, p2_ref, go_ref, dq2.at[mine], dkv2.at[:, :width], dkv2.at[:, width:])
    sent_dkv2 = partner.push(dkv2, dkv2_got)
    sent_dq2 = partner.push(dq2.at[mine], dq2.at[mine])
    spread_g.corner(2)
    spread_g.last(0)
    spread_n.relay(2)
    spread_n.corner(0)
    grad = mul_nt(dq2[mine, :], cq_w[...])
    grad = norm_back(grad, h1_ref[...], vectors[8:9], sums, 1) + dh_ref[...]
    dh_ref[...] = grad
    e1[mine, :] = grad.astype(bf16)
    sent_e1 = partner.push(e1.at[mine], e1.at[mine])
    go_ref[...] = mul_nt(e1[mine, :], so_w[...]).astype(bf16)
    attend_back(q1_ref, k1_ref, v1_ref, p1_ref, go_ref, dq1.at[mine], dkv1.at[:, :width], dkv1.at[:, width:])
    sent_dkv1 = partner.push(dkv1, dkv1_got)
    sent_dq1 = partner.push(dq1.at[mine], dq1.at[mine])
    spread_g.last(1)
    spread_g.last(3)
    spread_n.corner(1)
    spread_n.corner(3)

    sent_dkv2.wait_recv()
    dkv2_got[...] = (dkv2[...].astype(f32) + dkv2_got[...].astype(f32)).astype(bf16)
    dm_ref[...] = mul_nt(dkv2_got[mine, :], ckv_w[...]).astype(bf16)
    give_dm = give(4, dm_ref, dm_out)
    give_dm.start()

    sent = []

    def weight_grad_of(left, right, column):
        index = len(sent)
        slot = index % 2
        if index >= 2:
            sent[index - 2].wait()
        stage[slot] = mul_tn(left, right).astype(bf16)
        copy = pltpu.make_async_copy(
            stage.at[slot], grads_ref.at[:, pl.ds(column, width)], stores.at[index]
        )
        copy.start()
        sent.append(copy)

    for copy in halves:
        copy.wait_recv()
    sent_e2.wait_recv()
    weight_grad_of(o2_half[...], e2[...], 7 * width)
    weight_grad_of(m_ref[:, my_half], dkv2_got[:, :width], 5 * width)
    weight_grad_of(m_ref[:, my_half], dkv2_got[:, width:], 6 * width)
    spread_g.last(2)
    spread_n.corner(2)
    sent_dq2.wait_recv()
    weight_grad_of(n2_half[...], dq2[...], 4 * width)
    sent_e1.wait_recv()
    weight_grad_of(o1_half[...], e1[...], 3 * width)
    sent_dkv1.wait_recv()
    dkv1_got[...] = (dkv1[...].astype(f32) + dkv1_got[...].astype(f32)).astype(bf16)
    grad = mul_nt(dq1[mine, :], qkv_w[:, :width])
    grad += mul_nt(dkv1_got[mine, :width], qkv_w[:, width : 2 * width])
    grad += mul_nt(dkv1_got[mine, width:], qkv_w[:, 2 * width :])
    dx = norm_back(grad, x_ref[mine, :].astype(f32), vectors[7:8], sums, 0) + dh_ref[...]
    dx_ref[...] = dx.astype(bf16)
    give_dx = give(5, dx_ref, dx_out)
    give_dx.start()
    sent_sums = partner.push(sums, sums_got)
    weight_grad_of(n1_ref[:, my_half], dkv1_got[:, :width], width)
    weight_grad_of(n1_ref[:, my_half], dkv1_got[:, width:], 2 * width)
    sent_dq1.wait_recv()
    weight_grad_of(n1_ref[:, my_half], dq1[...], 0)

    def columns(values):
        return jnp.sum(values.astype(f32), axis=0, keepdims=True)

    value_half = pl.ds(pl.multiple_of(width + core * half, half), half)
    sent_sums.wait_recv()
    lines = [
        columns(dq1[:, my_half]),
        columns(dkv1_got[:, value_half]),
        columns(e1[:, my_half]),
        columns(dq2[:, my_half]),
        columns(dkv2_got[:, value_half]),
        columns(e2[:, my_half]),
        columns(g_ref[:, my_half]),
        sums[0:6, my_half] + sums_got[0:6, my_half],
    ]
    lines = jnp.concatenate(lines + [jnp.zeros((128 - 13, half), f32)], axis=0).T
    sent[-1].wait()
    sent[-2].wait()
    stage[0, :, :128] = lines.astype(bf16)
    final = pltpu.make_async_copy(
        stage.at[0, :, pl.ds(0, 128)], grads_ref.at[:, pl.ds(8 * width, 128)], stores.at[8]
    )
    final.start()
    for step in (0, 1, 3, 2):
        spread_n.last(step)
    final.wait()
    partner.finish()
    for move in (bring_x, bring_m, bring_g, give_y, give_dm, give_dx):
        move.finish()
    spread_g.finish()
    spread_n.finish()


def layer(x, memory, grads, vectors, ids, fc_bias, weights, fc_in, fc_out, devices):
    block, width = x.shape[1:]
    rows = ids.shape[1]
    count = rows // 2
    units = 512
    bf16, f32 = jnp.bfloat16, jnp.float32
    half = width // 2
    vmem = pl.BlockSpec(memory_space=pltpu.VMEM)
    hbm = pl.BlockSpec(memory_space=pl.ANY)
    every = jax.ShapeDtypeStruct((devices * count, width), bf16)
    moved = jax.ShapeDtypeStruct(x.shape, bf16)
    scores = (width // (2 * HEAD), rows, rows)
    kept = [
        ((rows, width), bf16), ((count, width), bf16), ((rows, width), bf16), ((rows, width), bf16),
        (scores, bf16), ((count, width), bf16), ((count, width), f32), ((count, width), bf16),
        ((count, width), bf16), ((rows, width), bf16), ((rows, width), bf16), (scores, bf16),
        ((count, width), bf16), ((count, width), f32), ((count, width), bf16),
    ]
    return pl.pallas_call(
        layer_kernel,
        in_specs=[vmem] * 3 + [hbm] * 10,
        out_specs=[hbm] * 6,
        out_shape=[
            moved, moved, moved, jax.ShapeDtypeStruct((half, 8 * width + 128), bf16), every, every
        ],
        scratch_shapes=[
            *[pltpu.VMEM((rows, width), bf16)] * 3,
            pltpu.VMEM((16, width), f32),
            pltpu.VMEM(ids.shape, jnp.int32),
            pltpu.VMEM(ids.shape, jnp.int32),
            pltpu.VMEM((rows, 128), jnp.int32),
            *[pltpu.VMEM(*shape) for shape in kept],
            *[pltpu.VMEM((count, width), bf16)] * 3,
            *[pltpu.VMEM((2 * w.shape[0], w.shape[1]), bf16) for w in weights],
            pltpu.VMEM((2, width, units), bf16),
            pltpu.VMEM((2, units, width), bf16),
            pltpu.VMEM((rows, width), bf16),
            pltpu.VMEM((rows, width), f32),
            pltpu.VMEM((rows, width), f32),
            pltpu.VMEM((2, count, width), bf16),
            pltpu.VMEM((2, count, width), bf16),
            pltpu.VMEM((count, width), bf16),
            *[pltpu.VMEM((rows, 2 * width), bf16)] * 4,
            *[pltpu.VMEM((rows, width), bf16)] * 4,
            *[pltpu.VMEM((rows, half), bf16)] * 3,
            pltpu.VMEM((count, width), f32),
            pltpu.VMEM((8, width), f32),
            pltpu.VMEM((8, width), f32),
            pltpu.VMEM((2, half, width), bf16),
            pltpu.SemaphoreType.DMA((32,)),
            pltpu.SemaphoreType.DMA((32,)),
            pltpu.SemaphoreType.DMA((5,)),
            pltpu.SemaphoreType.DMA((2, 2)),
            pltpu.SemaphoreType.DMA((9,)),
            pltpu.SemaphoreType.DMA((6, 2)),
            pltpu.SemaphoreType.DMA((6, 2)),
            pltpu.SemaphoreType.DMA((6,)),
            pltpu.SemaphoreType.DMA((2, 35)),
            pltpu.SemaphoreType.DMA((2, 35)),
            pltpu.SemaphoreType.DMA((2,)),
        ],
        compiler_params=pltpu.CompilerParams(
            vmem_limit_bytes=60 * 2**20, collective_id=1, has_side_effects=True
        ),
        cost_estimate=pl.CostEstimate(flops=80 * 10**9, bytes_accessed=64 * 2**20, transcendentals=0),
    )(vectors, ids, fc_bias, x, memory, grads, *weights, fc_in, fc_out)


def fast_body(
    hidden_in,
    memory,
    segment_ids,
    memory_ids,
    out_grad,
    self_qkv,
    self_out,
    cross_query,
    cross_kv,
    cross_out,
    fc_in,
    fc_out,
    biases,
    fc_in_bias,
    norm_gains,
    norm_shifts,
):
    width = hidden_in.shape[-1]
    f32 = jnp.float32
    ids = jnp.concatenate([segment_ids[:, 0], memory_ids[:, 0]], axis=0)
    vectors = jnp.concatenate([biases, norm_gains, norm_shifts], axis=1).astype(f32).T
    vectors = jnp.pad(vectors, ((0, 16 - vectors.shape[0]), (0, 0)))
    fc_bias = fc_in_bias.astype(f32)[None]
    devices = lax.axis_size("rep") * lax.axis_size("fsdp") * lax.axis_size("seq")
    weights = (self_qkv, self_out, cross_query, cross_kv, cross_out)
    hidden_out, hidden_grad, memory_grad, grads, normed_every, grad_every = layer(
        hidden_in[:, 0], memory[:, 0], out_grad[:, 0], vectors, ids, fc_bias, weights, fc_in, fc_out, devices
    )
    grad_fc_in, grad_fc_out, grad_fc_bias, grads = ffn_grads(
        normed_every, grad_every, fc_in, fc_out, fc_bias, grads
    )
    grads = grads.astype(f32)
    column = grads[:, 8 * width :]
    return (
        hidden_out[:, None],
        hidden_grad[:, None],
        memory_grad[:, None],
        grads[:, : 3 * width],
        grads[:, 3 * width : 4 * width],
        grads[:, 4 * width : 5 * width],
        grads[:, 5 * width : 7 * width],
        grads[:, 7 * width : 8 * width],
        grad_fc_in,
        grad_fc_out,
        column[:, :7],
        grad_fc_bias[0],
        column[:, 7:10],
        column[:, 10:13],
    )


def solution(mesh):
    fits = mesh.shape["fsdp"] == 2 and mesh.shape["seq"] == 4
    chosen = fast_body if fits else body
    return jax.shard_map(
        chosen,
        mesh=mesh,
        in_specs=(
            P(None, ("rep", "fsdp"), "seq", None),
            P(None, ("rep", "fsdp"), "seq", None),
            P(None, ("rep", "fsdp"), None),
            P(None, ("rep", "fsdp"), None),
            P(None, ("rep", "fsdp"), "seq", None),
            P("fsdp", None),
            P("fsdp", None),
            P("fsdp", None),
            P("fsdp", None),
            P("fsdp", None),
            P(None, "fsdp"),
            P("fsdp", None),
            P("fsdp", None),
            P("fsdp"),
            P("fsdp", None),
            P("fsdp", None),
        ),
        out_specs=(
            P(None, ("rep", "fsdp"), "seq", None),
            P(None, ("rep", "fsdp"), "seq", None),
            P(None, ("rep", "fsdp"), "seq", None),
            P("fsdp", None),
            P("fsdp", None),
            P("fsdp", None),
            P("fsdp", None),
            P("fsdp", None),
            P(None, "fsdp"),
            P("fsdp", None),
            P("fsdp", None),
            P("fsdp"),
            P("fsdp", None),
            P("fsdp", None),
        ),
        check_vma=False,
    )
```

```python
import functools
import math

import jax
import jax.numpy as jnp
from jax import lax
from jax.experimental import pallas as pl
from jax.experimental.pallas import tpu as pltpu
from jax.sharding import PartitionSpec as P

HEAD = 64


NORM_EPSILON = 1e-05
MASKED_SCORE = -1e30


def norm_forward(values, norm_gain, norm_shift):
    average = jnp.mean(values, axis=-1, keepdims=True)
    centred = values - average
    inverse = lax.rsqrt(jnp.mean(centred * centred, axis=-1, keepdims=True) + NORM_EPSILON)
    scaled = centred * inverse
    return (scaled * norm_gain + norm_shift, scaled, inverse)


def norm_backward(grad_normed, scaled, inverse, norm_gain):
    grad_scaled = grad_normed * norm_gain
    first_mean = jnp.mean(grad_scaled, axis=-1, keepdims=True)
    second_mean = jnp.mean(grad_scaled * scaled, axis=-1, keepdims=True)
    grad_values = (grad_scaled - first_mean - scaled * second_mean) * inverse
    gain_grad = jnp.sum(grad_normed * scaled, axis=(0, 1))
    shift_grad = jnp.sum(grad_normed, axis=(0, 1))
    return (grad_values, gain_grad, shift_grad)


def split_heads(values):
    return values.reshape(values.shape[:-1] + (values.shape[-1] // HEAD, HEAD))


def join_heads(values):
    return values.reshape(values.shape[:2] + (values.shape[2] * values.shape[3],))


def masked_scores(queries, key_rows, allowed):
    raw_scores = jnp.einsum(
        "mqhe,mkhe->mhqk", queries, key_rows, preferred_element_type=jnp.float32
    )
    return jnp.where(allowed[:, None], raw_scores * HEAD ** (-0.5), MASKED_SCORE)


def attend_forward(queries, key_rows, value_rows, allowed):
    scores = masked_scores(queries, key_rows, allowed)
    highest = jnp.max(scores, axis=-1, keepdims=True)
    exponent = jnp.exp(scores - highest)
    row_totals = jnp.sum(exponent, axis=-1, keepdims=True)
    weights = (exponent / row_totals).astype(jnp.bfloat16)
    joined = jnp.einsum("mhqk,mkhe->mqhe", weights, value_rows, preferred_element_type=jnp.float32)
    return (join_heads(joined).astype(jnp.bfloat16), highest + jnp.log(row_totals))


def attend_backward(queries, key_rows, value_rows, allowed, log_totals, grad_joined):
    scores = masked_scores(queries, key_rows, allowed)
    probability = jnp.exp(scores - log_totals)
    weights = probability.astype(jnp.bfloat16)
    grad_value_rows = jnp.einsum(
        "mhqk,mqhe->mkhe", weights, grad_joined, preferred_element_type=jnp.float32
    )
    grad_weights = jnp.einsum(
        "mqhe,mkhe->mhqk", grad_joined, value_rows, preferred_element_type=jnp.float32
    )
    grad_scores = probability * (
        grad_weights - jnp.sum(grad_weights * probability, axis=-1, keepdims=True)
    )
    grad_scores = grad_scores.astype(jnp.bfloat16)
    grad_queries = jnp.einsum(
        "mhqk,mkhe->mqhe", grad_scores, key_rows, preferred_element_type=jnp.float32
    ) * HEAD ** (-0.5)
    grad_key_rows = jnp.einsum(
        "mhqk,mqhe->mkhe", grad_scores, queries, preferred_element_type=jnp.float32
    ) * HEAD ** (-0.5)
    return (join_heads(grad_queries), join_heads(grad_key_rows), join_heads(grad_value_rows))


def gelu_slope(values):
    cumulative = 0.5 * (1.0 + lax.erf(values * 2.0 ** (-0.5)))
    density = jnp.exp(-0.5 * values * values) / math.sqrt(2.0 * math.pi)
    return cumulative + values * density


def feed_forward(rows, weight_in, bias_in, weight_out):
    pre_active = jnp.einsum(
        "mtd,df->mtf", rows, weight_in, preferred_element_type=jnp.float32
    ) + bias_in.astype(jnp.float32)
    active = jax.nn.gelu(pre_active, approximate=False).astype(jnp.bfloat16)
    partial_out = jnp.einsum("mtf,fd->mtd", active, weight_out, preferred_element_type=jnp.float32)
    return (pre_active, active, partial_out)


def feed_back(rows, grad_rows, pre_active, active, weight_in, weight_out):
    grad_active = jnp.einsum(
        "mtd,fd->mtf", grad_rows, weight_out, preferred_element_type=jnp.float32
    )
    grad_inner = (grad_active * gelu_slope(pre_active)).astype(jnp.bfloat16)
    grad_weight_out = jnp.einsum(
        "mtf,mtd->fd", active, grad_rows, preferred_element_type=jnp.float32
    )
    grad_weight_in = jnp.einsum("mtd,mtf->df", rows, grad_inner, preferred_element_type=jnp.float32)
    grad_bias_in = jnp.sum(grad_inner.astype(jnp.float32), axis=(0, 1))
    grad_rows_in = jnp.einsum(
        "mtf,df->mtd", grad_inner, weight_in, preferred_element_type=jnp.float32
    )
    return (grad_weight_in, grad_weight_out, grad_bias_in, grad_rows_in)


def project(rows, weight):
    return jnp.einsum("mtd,de->mte", rows, weight, preferred_element_type=jnp.float32)


def project_back(grad_rows, weight):
    return jnp.einsum("mte,de->mtd", grad_rows, weight, preferred_element_type=jnp.float32)


def weight_grad(rows, grad_rows):
    return jnp.einsum("mtd,mte->de", rows, grad_rows, preferred_element_type=jnp.float32)


def column_sums(grad_rows):
    return jnp.sum(grad_rows.astype(jnp.float32), axis=(0, 1))


def body(
    hidden_in,
    memory,
    segment_ids,
    memory_ids,
    out_grad,
    self_qkv,
    self_out,
    cross_query,
    cross_kv,
    cross_out,
    fc_in,
    fc_out,
    biases,
    fc_in_bias,
    norm_gains,
    norm_shifts,
):
    micro_count, single, tokens, model_width = hidden_in.shape
    seq_index = lax.axis_index("seq")
    zero_row = jnp.zeros((model_width,), jnp.float32)
    outputs_list = []
    grads_list = []
    memory_list = []
    attn_total = None
    mlp_total = None
    for micro in range(micro_count):
        full_qkv = lax.all_gather(self_qkv, "fsdp", axis=0, tiled=True)
        full_self_out = lax.all_gather(self_out, "fsdp", axis=0, tiled=True)
        full_query = lax.all_gather(cross_query, "fsdp", axis=0, tiled=True)
        full_memory_kv = lax.all_gather(cross_kv, "fsdp", axis=0, tiled=True)
        full_cross_out = lax.all_gather(cross_out, "fsdp", axis=0, tiled=True)
        full_biases = lax.all_gather(biases, "fsdp", axis=0, tiled=True)
        full_gains = lax.all_gather(norm_gains, "fsdp", axis=0, tiled=True)
        full_shifts = lax.all_gather(norm_shifts, "fsdp", axis=0, tiled=True)
        bias_float = full_biases.astype(jnp.float32)
        gain_float = full_gains.astype(jnp.float32)
        shift_float = full_shifts.astype(jnp.float32)
        hidden = hidden_in[micro : micro + 1][:, 0].astype(jnp.float32)
        memory_rows = memory[micro : micro + 1][:, 0]
        token_ids = segment_ids[micro : micro + 1][:, 0]
        source_ids = memory_ids[micro : micro + 1][:, 0]
        query_ids = lax.dynamic_slice_in_dim(token_ids, seq_index * tokens, tokens, 1)
        query_place = seq_index * tokens + jnp.arange(tokens, dtype=jnp.int32)
        key_place = jnp.arange(token_ids.shape[1], dtype=jnp.int32)
        self_allowed = (query_place[:, None] >= key_place[None, :])[None] & (
            query_ids[:, :, None] == token_ids[:, None, :]
        )
        cross_allowed = query_ids[:, :, None] == source_ids[:, None, :]
        normed_one, scaled_one, inverse_one = norm_forward(
            hidden, gain_float[:, 0], shift_float[:, 0]
        )
        normed_one = normed_one.astype(jnp.bfloat16)
        qkv_bias = jnp.concatenate([bias_float[:, 0], zero_row, bias_float[:, 1]])
        projected = (project(normed_one, full_qkv) + qkv_bias).astype(jnp.bfloat16)
        self_queries = split_heads(projected[..., :model_width])
        kv_all = lax.all_gather(projected[..., model_width:], "seq", axis=1, tiled=True)
        self_key_rows = split_heads(kv_all[..., :model_width])
        self_value_rows = split_heads(kv_all[..., model_width:])
        self_mixed, self_totals = attend_forward(
            self_queries, self_key_rows, self_value_rows, self_allowed
        )
        after_self = hidden + project(self_mixed, full_self_out) + bias_float[:, 2]
        normed_two, scaled_two, inverse_two = norm_forward(
            after_self, gain_float[:, 1], shift_float[:, 1]
        )
        normed_two = normed_two.astype(jnp.bfloat16)
        cross_queries = (project(normed_two, full_query) + bias_float[:, 3]).astype(jnp.bfloat16)
        memory_bias = jnp.concatenate([zero_row, bias_float[:, 4]])
        memory_kv = (project(memory_rows, full_memory_kv) + memory_bias).astype(jnp.bfloat16)
        memory_all = lax.all_gather(memory_kv, "seq", axis=1, tiled=True)
        memory_key_rows = split_heads(memory_all[..., :model_width])
        memory_value_rows = split_heads(memory_all[..., model_width:])
        cross_mixed, cross_totals = attend_forward(
            split_heads(cross_queries), memory_key_rows, memory_value_rows, cross_allowed
        )
        after_cross = after_self + project(cross_mixed, full_cross_out) + bias_float[:, 5]
        normed_three, scaled_three, inverse_three = norm_forward(
            after_cross, gain_float[:, 2], shift_float[:, 2]
        )
        normed_three = normed_three.astype(jnp.bfloat16)
        grad_out = out_grad[micro : micro + 1][:, 0]
        mlp_inputs = lax.all_gather(normed_three, "fsdp", axis=0, tiled=True)
        pre_active, active, partial_out = feed_forward(mlp_inputs, fc_in, fc_in_bias, fc_out)
        mlp_branch = lax.psum_scatter(
            partial_out.astype(jnp.bfloat16), "fsdp", scatter_dimension=0, tiled=True
        ).astype(jnp.float32)
        output = after_cross + mlp_branch + bias_float[:, 6]
        hidden_out = output.astype(jnp.bfloat16)[:, None]
        back_qkv = lax.all_gather(self_qkv, "fsdp", axis=0, tiled=True)
        back_self_out = lax.all_gather(self_out, "fsdp", axis=0, tiled=True)
        back_query = lax.all_gather(cross_query, "fsdp", axis=0, tiled=True)
        back_memory_kv = lax.all_gather(cross_kv, "fsdp", axis=0, tiled=True)
        back_cross_out = lax.all_gather(cross_out, "fsdp", axis=0, tiled=True)
        back_gains = lax.all_gather(norm_gains, "fsdp", axis=0, tiled=True)
        back_gain_float = back_gains.astype(jnp.float32)
        grad_gathered = lax.all_gather(grad_out, "fsdp", axis=0, tiled=True)
        one_grad_fc_in, one_grad_fc_out, one_grad_fc_bias, grad_partial = feed_back(
            mlp_inputs, grad_gathered, pre_active, active, fc_in, fc_out
        )
        grad_normed_three = lax.psum_scatter(
            grad_partial.astype(jnp.bfloat16), "fsdp", scatter_dimension=0, tiled=True
        ).astype(jnp.float32)
        grad_three, gain_three, shift_three = norm_backward(
            grad_normed_three, scaled_three, inverse_three, back_gain_float[:, 2]
        )
        grad_after_cross = grad_out.astype(jnp.float32) + grad_three
        grad_cross_branch = grad_after_cross.astype(jnp.bfloat16)
        grad_cross_out = weight_grad(cross_mixed, grad_cross_branch)
        grad_cross_mixed = project_back(grad_cross_branch, back_cross_out).astype(jnp.bfloat16)
        cross_grad_queries, memory_grad_keys, memory_grad_values = attend_backward(
            split_heads(cross_queries),
            memory_key_rows,
            memory_value_rows,
            cross_allowed,
            cross_totals,
            split_heads(grad_cross_mixed),
        )
        own_memory_keys = lax.psum_scatter(
            memory_grad_keys.astype(jnp.bfloat16), "seq", scatter_dimension=1, tiled=True
        )
        own_memory_values = lax.psum_scatter(
            memory_grad_values.astype(jnp.bfloat16), "seq", scatter_dimension=1, tiled=True
        )
        grad_memory_kv = jnp.concatenate([own_memory_keys, own_memory_values], axis=-1)
        grad_memory_weight = weight_grad(memory_rows, grad_memory_kv)
        memory_grad = project_back(grad_memory_kv, back_memory_kv).astype(jnp.bfloat16)[:, None]
        grad_cross_queries = cross_grad_queries.astype(jnp.bfloat16)
        grad_query_weight = weight_grad(normed_two, grad_cross_queries)
        grad_normed_two = project_back(grad_cross_queries, back_query)
        grad_two, gain_two, shift_two = norm_backward(
            grad_normed_two, scaled_two, inverse_two, back_gain_float[:, 1]
        )
        grad_after_self = grad_after_cross + grad_two
        grad_self_branch = grad_after_self.astype(jnp.bfloat16)
        grad_self_out = weight_grad(self_mixed, grad_self_branch)
        grad_self_mixed = project_back(grad_self_branch, back_self_out).astype(jnp.bfloat16)
        self_grad_queries, self_grad_keys, self_grad_values = attend_backward(
            self_queries,
            self_key_rows,
            self_value_rows,
            self_allowed,
            self_totals,
            split_heads(grad_self_mixed),
        )
        own_self_keys = lax.psum_scatter(
            self_grad_keys.astype(jnp.bfloat16), "seq", scatter_dimension=1, tiled=True
        )
        own_self_values = lax.psum_scatter(
            self_grad_values.astype(jnp.bfloat16), "seq", scatter_dimension=1, tiled=True
        )
        grad_projected = jnp.concatenate(
            [self_grad_queries.astype(jnp.bfloat16), own_self_keys, own_self_values], axis=-1
        )
        grad_qkv_weight = weight_grad(normed_one, grad_projected)
        grad_normed_one = project_back(grad_projected, back_qkv)
        grad_one, gain_one, shift_one = norm_backward(
            grad_normed_one, scaled_one, inverse_one, back_gain_float[:, 0]
        )
        hidden_grad = (grad_after_self + grad_one).astype(jnp.bfloat16)[:, None]
        grad_biases = jnp.stack(
            [
                column_sums(grad_projected[..., :model_width]),
                column_sums(grad_projected[..., 2 * model_width :]),
                column_sums(grad_self_branch),
                column_sums(grad_cross_queries),
                column_sums(grad_memory_kv[..., model_width:]),
                column_sums(grad_cross_branch),
                column_sums(grad_out),
            ],
            axis=1,
        )
        grad_gains = jnp.stack([gain_one, gain_two, gain_three], axis=1)
        grad_shifts = jnp.stack([shift_one, shift_two, shift_three], axis=1)
        attn_grads = (
            grad_qkv_weight,
            grad_self_out,
            grad_query_weight,
            grad_memory_weight,
            grad_cross_out,
            grad_biases,
            grad_gains,
            grad_shifts,
        )
        mlp_grads = (one_grad_fc_in, one_grad_fc_out, one_grad_fc_bias)
        hidden_out, hidden_grad, memory_grad, attn_grads, mlp_grads = (
            hidden_out,
            hidden_grad,
            memory_grad,
            attn_grads,
            mlp_grads,
        )
        outputs_list.append(hidden_out)
        grads_list.append(hidden_grad)
        memory_list.append(memory_grad)
        if attn_total is None:
            attn_total = attn_grads
            mlp_total = mlp_grads
        else:
            attn_total = jax.tree.map(jnp.add, attn_total, attn_grads)
            mlp_total = jax.tree.map(jnp.add, mlp_total, mlp_grads)
    grad_fc_in, grad_fc_out, grad_fc_bias = mlp_total
    (
        shard_qkv,
        shard_self_out,
        shard_query,
        shard_memory_kv,
        shard_cross_out,
        shard_biases,
        shard_gains,
        shard_shifts,
    ) = (
        lax.psum_scatter(
            attn_total[0].astype(jnp.bfloat16), "fsdp", scatter_dimension=0, tiled=True
        ).astype(jnp.float32),
        lax.psum_scatter(
            attn_total[1].astype(jnp.bfloat16), "fsdp", scatter_dimension=0, tiled=True
        ).astype(jnp.float32),
        lax.psum_scatter(
            attn_total[2].astype(jnp.bfloat16), "fsdp", scatter_dimension=0, tiled=True
        ).astype(jnp.float32),
        lax.psum_scatter(
            attn_total[3].astype(jnp.bfloat16), "fsdp", scatter_dimension=0, tiled=True
        ).astype(jnp.float32),
        lax.psum_scatter(
            attn_total[4].astype(jnp.bfloat16), "fsdp", scatter_dimension=0, tiled=True
        ).astype(jnp.float32),
        lax.psum_scatter(
            attn_total[5].astype(jnp.bfloat16), "fsdp", scatter_dimension=0, tiled=True
        ).astype(jnp.float32),
        lax.psum_scatter(
            attn_total[6].astype(jnp.bfloat16), "fsdp", scatter_dimension=0, tiled=True
        ).astype(jnp.float32),
        lax.psum_scatter(
            attn_total[7].astype(jnp.bfloat16), "fsdp", scatter_dimension=0, tiled=True
        ).astype(jnp.float32),
    )
    summed = (
        lax.psum(shard_qkv.astype(jnp.bfloat16), ("rep", "seq")).astype(jnp.float32),
        lax.psum(shard_self_out.astype(jnp.bfloat16), ("rep", "seq")).astype(jnp.float32),
        lax.psum(shard_query.astype(jnp.bfloat16), ("rep", "seq")).astype(jnp.float32),
        lax.psum(shard_memory_kv.astype(jnp.bfloat16), ("rep", "seq")).astype(jnp.float32),
        lax.psum(shard_cross_out.astype(jnp.bfloat16), ("rep", "seq")).astype(jnp.float32),
        lax.psum(grad_fc_in.astype(jnp.bfloat16), ("rep", "seq")).astype(jnp.float32),
        lax.psum(grad_fc_out.astype(jnp.bfloat16), ("rep", "seq")).astype(jnp.float32),
        lax.psum(shard_biases.astype(jnp.bfloat16), ("rep", "seq")).astype(jnp.float32),
        lax.psum(grad_fc_bias.astype(jnp.bfloat16), ("rep", "seq")).astype(jnp.float32),
        lax.psum(shard_gains.astype(jnp.bfloat16), ("rep", "seq")).astype(jnp.float32),
        lax.psum(shard_shifts.astype(jnp.bfloat16), ("rep", "seq")).astype(jnp.float32),
    )
    hidden_out = jnp.concatenate(outputs_list, axis=0)
    hidden_grad = jnp.concatenate(grads_list, axis=0)
    memory_grad = jnp.concatenate(memory_list, axis=0)
    return (
        hidden_out,
        hidden_grad,
        memory_grad,
        summed[0],
        summed[1],
        summed[2],
        summed[3],
        summed[4],
        summed[5],
        summed[6],
        summed[7],
        summed[8],
        summed[9],
        summed[10],
    )


def mul(left, right):
    return jnp.dot(left, right, preferred_element_type=jnp.float32)


def mul_nt(left, right):
    return lax.dot_general(left, right, (((1,), (1,)), ((), ())), preferred_element_type=jnp.float32)


def mul_tn(left, right):
    return lax.dot_general(left, right, (((0,), (0,)), ((), ())), preferred_element_type=jnp.float32)


MESH = pl.DeviceIdType.MESH


def gelu_pair(values, refine=False):
    depth = 1.0 + (0.3275911 * 2.0**-0.5) * jnp.abs(values)
    inv = pltpu.reciprocal(depth, approx=True)
    if refine:
        inv = inv * (2.0 - depth * inv)
    bell = jnp.exp(-0.5 * values * values)
    series = 0.7107068705 + inv * (-0.7265760135 + inv * 0.5307027145)
    series = inv * (0.127414796 + inv * (-0.142248368 + inv * series))
    tail = series * bell
    cumulative = jnp.where(values >= 0.0, 1.0 - tail, tail)
    return values * cumulative, cumulative + values * (bell * (1.0 / math.sqrt(2.0 * math.pi)))


def position():
    rep, core, deep = lax.axis_index("rep"), lax.axis_index("fsdp"), lax.axis_index("seq")
    return rep % 2, rep // 2, core, deep


def device(across, up, core, deep):
    return (up * 2 + across, core, deep)


def greet(partners):
    barrier = pltpu.get_barrier_semaphore()
    for partner in partners:
        pl.semaphore_signal(barrier, inc=1, device_id=partner, device_id_type=MESH)
    pl.semaphore_wait(barrier, len(partners))


class ChunkSum:
    def __init__(self, turned, column, width, own_ref, sum_ref, held, first, second, third, done, send, recv, local):
        across, up, core, deep = position()
        self.side, self.next = (up, across) if turned else (across, up)
        one = device(1 - across, up, core, deep)
        two = device(across, 1 - up, core, deep)
        self.one, self.two = (two, one) if turned else (one, two)
        self.deep = deep
        self.others = [(deep + step) % 4 for step in (1, 2, 3)]
        self.third_ids = [device(across, up, core, other) for other in self.others]
        self.columns = pl.ds(column, width)
        self.own, self.sum = own_ref, sum_ref
        self.held, self.first, self.second, self.third, self.done = held, first, second, third, done
        self.send, self.recv, self.local = send, recv, local
        self.quarter = pl.multiple_of(self.next * 128, 128)
        self.start_row = self.side * 256

    def remote(self, index, src, dst, target):
        return pltpu.make_async_remote_copy(
            src_ref=src,
            dst_ref=dst,
            send_sem=self.send.at[index],
            recv_sem=self.recv.at[index],
            device_id=target,
            device_id_type=MESH,
        )

    def rows(self, ref, start, count):
        return ref.at[pl.ds(pl.multiple_of(start, 32), count), self.columns]

    def copy_a(self):
        return self.remote(0, self.rows(self.own, (1 - self.side) * 256, 256), self.first, self.one)

    def load(self):
        return pltpu.make_async_copy(self.rows(self.own, self.start_row, 256), self.held, self.local.at[0])

    def copy_b(self):
        away = pl.multiple_of((1 - self.next) * 128, 128)
        return self.remote(1, self.held.at[pl.ds(away, 128)], self.second, self.two)

    def copy_c(self, turn):
        start = pl.multiple_of(self.quarter + self.others[turn] * 32, 32)
        return self.remote(2 + turn, self.held.at[pl.ds(start, 32)], self.third.at[turn], self.third_ids[turn])

    def place(self):
        return self.rows(self.sum, self.start_row + self.quarter + self.deep * 32, 32)

    def copy_d(self, turn):
        return self.remote(5 + turn, self.done, self.place(), self.third_ids[turn])

    def store(self):
        return pltpu.make_async_copy(self.done, self.place(), self.local.at[1])

    def copy_e(self):
        part = self.rows(self.sum, self.start_row + self.quarter, 128)
        return self.remote(8, part, part, self.two)

    def copy_f(self):
        part = self.rows(self.sum, self.start_row, 256)
        return self.remote(9, part, part, self.one)

    def stage(self, number):
        if number == 0:
            self.copy_a().start()
            self.load().start()
        elif number == 1:
            self.load().wait()
            self.copy_a().wait_recv()
            self.held[...] = self.held[...] + self.first[...]
            self.copy_b().start()
        elif number == 2:
            self.copy_b().wait_recv()
            self.copy_b().wait_send()
            mine = pl.ds(self.quarter, 128)
            self.held[mine] = self.held[mine] + self.second[...]
            for turn in range(3):
                self.copy_c(turn).start()
        elif number == 3:
            for turn in range(3):
                self.copy_c(turn).wait_recv()
            start = pl.multiple_of(self.quarter + self.deep * 32, 32)
            total = self.held[pl.ds(start, 32)].astype(jnp.float32)
            for turn in range(3):
                total += self.third[turn].astype(jnp.float32)
            self.done[...] = total.astype(self.done.dtype)
            self.store().start()
            for turn in range(3):
                self.copy_d(turn).start()
        elif number == 4:
            self.store().wait()
            for turn in range(3):
                self.copy_d(turn).wait_recv()
            self.copy_e().start()
        elif number == 5:
            self.copy_e().wait_recv()
            self.copy_f().start()
        elif number == 6:
            self.copy_f().wait_recv()
            self.copy_a().wait_send()
            for turn in range(3):
                self.copy_c(turn).wait_send()
                self.copy_d(turn).wait_send()
            self.copy_e().wait_send()
            self.copy_f().wait_send()


BEGIN = (0, 3, 6, 9)
AFTER = (0, 2, 3, 4, 5, 6, 8)


def ffn_kernel(
    step, tiles, plan, rows_ref, grads_ref, in_ref, out_ref, bias_ref, own_ref,
    din_ref, dout_ref, dbias_ref, sum_ref, flip, acc_in, acc_out, us, das, actives, inners, sums, *rest
):
    units = flip.shape[0]
    steps = rows_ref.shape[0] // step
    at = pl.program_id(0)
    send, recv, local = rest[-3:]
    buffers = rest[:-3]
    chunks = []
    for index, (turned, column, width, _) in enumerate(plan):
        held, first, second, third, done = buffers[5 * index : 5 * index + 5]
        chunks.append(
            ChunkSum(turned, column, width, own_ref, sum_ref, held, first, second, third, done,
                     send.at[index], recv.at[index], local.at[index])
        )

    @pl.when(at == 0)
    def _():
        across, up, core, deep = position()
        greet(
            [device(1 - across, up, core, deep), device(across, 1 - up, core, deep)]
            + [device(across, up, core, (deep + turn) % 4) for turn in (1, 2, 3)]
        )

    work = {}
    for chunk, (_, _, _, slots) in zip(chunks, plan):
        for number, slot in enumerate(slots):
            work.setdefault(min(slot, tiles), []).append((slot, number, chunk))

    def traffic(slot):
        for _, number, chunk in sorted(work.get(slot, []), key=lambda job: job[:2]):
            chunk.stage(number)

    for slot in range(tiles):
        if slot in work:
            pl.when(at == slot)(functools.partial(traffic, slot))

    flip[...] = in_ref[...].T

    def front(turn):
        part = pl.ds(turn * step, step)
        us[turn % 2] = mul_nt(flip[...], rows_ref[part, :])
        das[turn % 2] = mul_nt(out_ref[...], grads_ref[part, :])

    bias = jnp.broadcast_to(bias_ref[...], (128, units)).T[:, :1]

    def middle(turn):
        active, slope = gelu_pair(us[turn % 2] + bias)
        inner = (das[turn % 2] * slope).astype(jnp.bfloat16)
        actives[turn % 2] = active.astype(jnp.bfloat16)
        inners[turn % 2] = inner
        total = inner[:, :128].astype(jnp.float32)
        for lane in range(1, step // 128):
            total += inner[:, lane * 128 : (lane + 1) * 128].astype(jnp.float32)
        sums[...] = total if turn == 0 else sums[...] + total

    def back(turn):
        part = pl.ds(turn * step, step)
        out_part = mul(actives[turn % 2], grads_ref[part, :])
        in_part = mul(inners[turn % 2], rows_ref[part, :])
        if turn:
            out_part += acc_out[...]
            in_part += acc_in[...]
        if turn < steps - 1:
            acc_out[...] = out_part
            acc_in[...] = in_part
        else:
            dout_ref[...] = out_part.astype(jnp.bfloat16)
            din_ref[...] = in_part.astype(jnp.bfloat16).T

    front(0)
    for turn in range(steps + 1):
        if turn:
            back(turn - 1)
        if turn + 1 < steps:
            front(turn + 1)
        if turn < steps:
            middle(turn)
    dbias_ref[...] = jnp.sum(sums[...].T, axis=0, keepdims=True)
    pl.when(at == tiles - 1)(functools.partial(traffic, tiles))


def ffn_grads(rows, grads, fc_in, fc_out, bias, own):
    count, width = rows.shape
    hidden = fc_in.shape[1]
    units, step = 256, count // 4
    tiles = hidden // units
    plan = [(False, 8 * width, 128, (0, 1, 2, 3, 4, 5, 6))]
    for pair, begin in enumerate(BEGIN):
        slots = [begin + after for after in AFTER]
        plan.append((False, pair * width, width, slots))
        plan.append((True, (len(BEGIN) + pair) * width, width, slots))
    buffers = []
    for _, _, columns, _ in plan:
        buffers += [
            pltpu.VMEM((256, columns), jnp.bfloat16),
            pltpu.VMEM((256, columns), jnp.bfloat16),
            pltpu.VMEM((128, columns), jnp.bfloat16),
            pltpu.VMEM((3, 32, columns), jnp.bfloat16),
            pltpu.VMEM((32, columns), jnp.bfloat16),
        ]
    whole = functools.partial(pl.BlockSpec, pipeline_mode=pl.Buffered(1))
    return pl.pallas_call(
        functools.partial(ffn_kernel, step, tiles, plan),
        grid=(tiles,),
        in_specs=[
            whole((count, width), lambda at: (0, 0)),
            whole((count, width), lambda at: (0, 0)),
            pl.BlockSpec((width, units), lambda at: (0, at)),
            pl.BlockSpec((units, width), lambda at: (at, 0)),
            pl.BlockSpec((1, units), lambda at: (0, at)),
            pl.BlockSpec(memory_space=pl.ANY),
        ],
        out_specs=[
            pl.BlockSpec((width, units), lambda at: (0, at)),
            pl.BlockSpec((units, width), lambda at: (at, 0)),
            pl.BlockSpec((1, units), lambda at: (0, at)),
            pl.BlockSpec(memory_space=pl.ANY),
        ],
        out_shape=[
            jax.ShapeDtypeStruct((width, hidden), jnp.bfloat16),
            jax.ShapeDtypeStruct((hidden, width), jnp.bfloat16),
            jax.ShapeDtypeStruct((1, hidden), jnp.float32),
            jax.ShapeDtypeStruct(own.shape, own.dtype),
        ],
        scratch_shapes=[
            pltpu.VMEM((units, width), jnp.bfloat16),
            pltpu.VMEM((units, width), jnp.float32),
            pltpu.VMEM((units, width), jnp.float32),
            pltpu.VMEM((2, units, step), jnp.float32),
            pltpu.VMEM((2, units, step), jnp.float32),
            pltpu.VMEM((2, units, step), jnp.bfloat16),
            pltpu.VMEM((2, units, step), jnp.bfloat16),
            pltpu.VMEM((units, 128), jnp.float32),
            *buffers,
            pltpu.SemaphoreType.DMA((len(plan), 10)),
            pltpu.SemaphoreType.DMA((len(plan), 10)),
            pltpu.SemaphoreType.DMA((len(plan), 2)),
        ],
        compiler_params=pltpu.CompilerParams(
            vmem_limit_bytes=58 * 2**20, collective_id=0, has_side_effects=True
        ),
        cost_estimate=pl.CostEstimate(
            flops=8 * count * width * hidden,
            bytes_accessed=4 * count * width + 12 * width * hidden,
            transcendentals=count * hidden,
        ),
    )(rows, grads, fc_in, fc_out, bias, own)


def norm_parts(values):
    centred = values - jnp.mean(values, axis=-1, keepdims=True)
    inverse = lax.rsqrt(jnp.mean(centred * centred, axis=-1, keepdims=True) + NORM_EPSILON)
    return centred * inverse, inverse


def normed(values, vectors, which):
    scaled, _ = norm_parts(values)
    return (scaled * vectors[7 + which : 8 + which] + vectors[10 + which : 11 + which]).astype(jnp.bfloat16)


class Partner:
    def __init__(self, send, recv):
        across, up, core, deep = position()
        self.core = core
        self.id = device(across, up, 1 - core, deep)
        self.send, self.recv = send, recv
        self.copies = []

    def push(self, src, dst):
        index = len(self.copies)
        copy = pltpu.make_async_remote_copy(
            src_ref=src,
            dst_ref=dst,
            send_sem=self.send.at[index],
            recv_sem=self.recv.at[index],
            device_id=self.id,
            device_id_type=MESH,
        )
        copy.start()
        self.copies.append(copy)
        return copy

    def finish(self):
        for copy in self.copies:
            copy.wait_send()


class Weights:
    def __init__(self, partner, shard, whole, local):
        half = shard.shape[0]
        mine = whole.at[pl.ds(pl.multiple_of(partner.core * half, half), half)]
        self.remote = partner.push(shard, mine)
        self.near = pltpu.make_async_copy(shard, mine, local)
        self.near.start()
        self.whole = whole

    def get(self):
        self.near.wait()
        self.remote.wait_recv()
        return self.whole


def two_heads(values, lane):
    zero = jnp.zeros_like(values)
    return jnp.concatenate([jnp.where(lane, values, zero), jnp.where(lane, zero, values)], axis=0)


def lane_of():
    return lax.broadcasted_iota(jnp.int32, (1, 2 * HEAD), 1) < HEAD


def attend(q_ref, k_ref, v_ref, p_ref, o_ref, allowed):
    lane = lane_of()
    count = q_ref.shape[0]
    for pair in range(q_ref.shape[1] // (2 * HEAD)):
        columns = pl.ds(pair * 2 * HEAD, 2 * HEAD)
        scores = mul_nt(two_heads(q_ref[:, columns], lane), k_ref[:, columns])
        scores = jnp.where(allowed, scores * HEAD ** (-0.5), MASKED_SCORE)
        exponent = jnp.exp(scores - jnp.max(scores, axis=-1, keepdims=True))
        weights = (exponent / jnp.sum(exponent, axis=-1, keepdims=True)).astype(jnp.bfloat16)
        p_ref[pair] = weights
        mixed = mul(weights, v_ref[:, columns])
        o_ref[:, columns] = jnp.where(lane, mixed[:count], mixed[count:]).astype(jnp.bfloat16)


def attend_back(q_ref, k_ref, v_ref, p_ref, go_ref, dq_ref, dk_ref, dv_ref):
    lane = lane_of()
    count = q_ref.shape[0]
    for pair in range(q_ref.shape[1] // (2 * HEAD)):
        columns = pl.ds(pair * 2 * HEAD, 2 * HEAD)
        grads = two_heads(go_ref[:, columns], lane)
        weights = p_ref[pair]
        dv_ref[:, columns] = mul_tn(weights, grads).astype(jnp.bfloat16)
        grad_weights = mul_nt(grads, v_ref[:, columns])
        exact = weights.astype(jnp.float32)
        inner = jnp.sum(grad_weights * exact, axis=-1, keepdims=True)
        scores = (exact * (grad_weights - inner)).astype(jnp.bfloat16)
        queries = mul(scores, k_ref[:, columns]) * HEAD ** (-0.5)
        dq_ref[:, columns] = jnp.where(lane, queries[:count], queries[count:]).astype(jnp.bfloat16)
        keys = mul_tn(scores, two_heads(q_ref[:, columns], lane)) * HEAD ** (-0.5)
        dk_ref[:, columns] = keys.astype(jnp.bfloat16)


def norm_back(grads, values, gain, sums_ref, row):
    scaled, inverse = norm_parts(values)
    sums_ref[row : row + 1, :] = jnp.sum(grads * scaled, axis=0, keepdims=True)
    sums_ref[row + 3 : row + 4, :] = jnp.sum(grads, axis=0, keepdims=True)
    inner = grads * gain
    first = jnp.mean(inner, axis=-1, keepdims=True)
    second = jnp.mean(inner * scaled, axis=-1, keepdims=True)
    return (inner - first - scaled * second) * inverse


class Bring:
    def __init__(self, src, dst, send, recv, local):
        across, up, core, deep = position()
        self.core, self.deep = core, deep
        self.src, self.dst = src, dst
        self.send, self.recv, self.local = send, recv, local
        self.across, self.up = across, up

    def stays(self, micro):
        return (self.deep // 2 == self.core) & (2 * micro + self.core == self.deep)

    def far(self, micro, index):
        block = self.src.shape[1]
        return pltpu.make_async_remote_copy(
            src_ref=self.src.at[micro],
            dst_ref=self.dst.at[pl.ds(pl.multiple_of(self.deep * block, block), block)],
            send_sem=self.send.at[micro],
            recv_sem=self.recv.at[index],
            device_id=device(self.across, self.up, self.deep // 2, 2 * micro + self.core),
            device_id_type=MESH,
        )

    def near(self, micro):
        block = self.src.shape[1]
        return pltpu.make_async_copy(
            self.src.at[micro],
            self.dst.at[pl.ds(pl.multiple_of(self.deep * block, block), block)],
            self.local,
        )

    def start(self):
        for micro in range(2):
            @pl.when(self.stays(micro))
            def _():
                self.near(micro).start()

            @pl.when(jnp.logical_not(self.stays(micro)))
            def _():
                self.far(micro, self.deep % 2).start()

    def wait(self):
        for block in range(2):
            here = (self.deep % 2 == self.core) & (2 * self.core + block == self.deep)

            @pl.when(here)
            def _():
                self.near(block).wait()

            @pl.when(jnp.logical_not(here))
            def _():
                self.far(block, block).wait_recv()

    def finish(self):
        for micro in range(2):
            @pl.when(jnp.logical_not(self.stays(micro)))
            def _():
                self.far(micro, self.deep % 2).wait_send()


class SendBack:
    def __init__(self, src, dst, send, recv, local):
        self.src, self.dst = src, dst
        self.send, self.recv, self.local = send, recv, local
        self.across, self.up, self.core, self.deep = position()

    def stays(self, block):
        return (self.deep % 2 == self.core) & (2 * self.core + block == self.deep)

    def far(self, block, index):
        count = self.dst.shape[1]
        return pltpu.make_async_remote_copy(
            src_ref=self.src.at[pl.ds(block * count, count)],
            dst_ref=self.dst.at[self.deep // 2],
            send_sem=self.send.at[block],
            recv_sem=self.recv.at[index],
            device_id=device(self.across, self.up, self.deep % 2, 2 * self.core + block),
            device_id_type=MESH,
        )

    def near(self, block):
        count = self.dst.shape[1]
        return pltpu.make_async_copy(
            self.src.at[pl.ds(block * count, count)], self.dst.at[self.deep // 2], self.local
        )

    def start(self):
        for block in range(2):
            @pl.when(self.stays(block))
            def _():
                self.near(block).start()

            @pl.when(jnp.logical_not(self.stays(block)))
            def _():
                self.far(block, self.deep // 2).start()

    def finish(self):
        for micro in range(2):
            here = (self.deep // 2 == self.core) & (2 * micro + self.core == self.deep)

            @pl.when(here)
            def _():
                self.near(micro).wait()

            @pl.when(jnp.logical_not(here))
            def _():
                self.far(micro, micro).wait_recv()
        for block in range(2):
            @pl.when(jnp.logical_not(self.stays(block)))
            def _():
                self.far(block, self.deep // 2).wait_send()


class Spread:
    def __init__(self, own, every, send, recv, local):
        self.own, self.every = own, every
        self.send, self.recv, self.local = send, recv, local
        self.across, self.up, self.core, self.deep = position()
        self.count = own.shape[0]
        self.right = device(1 - self.across, self.up, self.core, self.deep)
        self.above = device(self.across, 1 - self.up, self.core, self.deep)
        self.twin = device(self.across, self.up, 1 - self.core, self.deep)

    def item(self, flip_x, flip_y, step, half=None):
        column = (2 if flip_y else 0) + (1 if flip_x else 0)
        slot = (column * 4 + (self.deep + step) % 4) * 2 + self.core
        start = slot * self.count
        if half is None:
            return self.every.at[pl.ds(pl.multiple_of(start, self.count), self.count)]
        part = self.count // 2
        return self.every.at[pl.ds(pl.multiple_of(start + half * part, part), part)]

    def copy(self, index, src, dst, target):
        return pltpu.make_async_remote_copy(
            src_ref=src,
            dst_ref=dst,
            send_sem=self.send.at[index],
            recv_sem=self.recv.at[index],
            device_id=target,
            device_id_type=MESH,
        )

    def along(self, step):
        target = device(self.across, self.up, self.core, (self.deep + step) % 4)
        return self.copy(step - 1, self.own, self.item(False, False, 0), target)

    def column(self, step, index, target):
        src = self.own if step == 0 else self.item(False, False, step)
        dst = self.item(index == 3, index == 7, step)
        return self.copy(index + step, src, dst, target)

    def passed(self, step, index, flip_x, flip_y, target, half=None):
        src = self.item(flip_x, flip_y, step, half)
        dst = src if half is None else self.item(True, True, step, half)
        return self.copy(index + step, src, dst, target)

    def store(self):
        return pltpu.make_async_copy(self.own, self.item(False, False, 0), self.local)

    def fan(self, step):
        self.column(step, 3, self.right).start()
        self.column(step, 7, self.above).start()
        self.column(step, 19, self.twin).start()

    def begin(self):
        self.fan(0)
        for step in (1, 3, 2):
            self.along(step).start()
        self.store().start()

    def relay(self, step):
        self.along(4 - step).wait_recv()
        self.fan(step)

    def corner(self, step):
        self.column(step, 3, self.right).wait_recv()
        self.passed(step, 15, True, False, self.above, 0).start()
        self.passed(step, 23, True, False, self.twin).start()
        self.column(step, 7, self.above).wait_recv()
        self.passed(step, 11, False, True, self.right, 1).start()
        self.passed(step, 27, False, True, self.twin).start()

    def last(self, step):
        self.passed(step, 15, True, False, self.above, 0).wait_recv()
        self.passed(step, 11, False, True, self.right, 1).wait_recv()
        self.passed(step, 31, True, True, self.twin).start()

    def finish(self):
        self.store().wait()
        for step in range(4):
            arrivals = [
                self.column(step, 19, self.twin),
                self.passed(step, 23, True, False, self.twin),
                self.passed(step, 27, False, True, self.twin),
                self.passed(step, 31, True, True, self.twin),
            ]
            for copy in arrivals:
                copy.wait_recv()
                copy.wait_send()
            self.column(step, 3, self.right).wait_send()
            self.column(step, 7, self.above).wait_send()
            self.passed(step, 15, True, False, self.above, 0).wait_send()
            self.passed(step, 11, False, True, self.right, 1).wait_send()
            if step:
                self.along(step).wait_send()


def layer_kernel(
    vec_half_ref, ids_ref, fcb_ref, x_hbm, m_hbm, g_hbm,
    qkv_hbm, so_hbm, cq_hbm, ckv_hbm, co_hbm, in_hbm, out_hbm,
    y_out, dx_out, dm_out, grads_ref, every_n, every_g,
    x_ref, m_ref, g_ref, vec_ref, ids_got, ids_all, id_rows,
    n1_ref, q1_ref, k1_ref, v1_ref, p1_ref, o1_ref, h1_ref, n2_ref, q2_ref, k2_ref, v2_ref, p2_ref,
    o2_ref, h2_ref, n3_ref, y_ref, dx_ref, dm_ref,
    qkv_w, so_w, cq_w, ckv_w, co_w, in_w, out_w, chip_n, acc_y, acc_n, part, got, go_ref,
    dkv2, dkv2_got, dkv1, dkv1_got, dq1, dq2, e1, e2, n2_half, o1_half, o2_half, dh_ref, sums, sums_got,
    stage, send, recv, local, tiles, stores, move_send, move_recv, move_local,
    spread_send, spread_recv, spread_local,
):
    across, up, core, deep = position()
    column = [device(across, up, 1 - core, deep)]
    for turn in (1, 2, 3):
        for other in (0, 1):
            column.append(device(across, up, other, (deep + turn) % 4))
    greet(column + [device(1 - across, up, core, deep), device(across, 1 - up, core, deep)])
    partner = Partner(send, recv)
    bf16, f32 = jnp.bfloat16, jnp.float32
    count, width = q1_ref.shape
    units = in_w.shape[2]
    half = width // 2
    mine = pl.ds(pl.multiple_of(core * count, count), count)
    theirs = pl.ds(pl.multiple_of((1 - core) * count, count), count)
    my_half = pl.ds(pl.multiple_of(core * half, half), half)
    their_half = pl.ds(pl.multiple_of((1 - core) * half, half), half)

    def bring(index, src, dst):
        return Bring(src, dst, move_send.at[index], move_recv.at[index], move_local.at[index])

    def give(index, src, dst):
        return SendBack(src, dst, move_send.at[index], move_recv.at[index], move_local.at[index])

    bring_x = bring(0, x_hbm, x_ref)
    bring_x.start()
    sent_ids = partner.push(ids_ref, ids_got)
    sent_vec = partner.push(vec_half_ref, vec_ref.at[:, my_half])
    vec_ref[:, my_half] = vec_half_ref[...]
    qkv = Weights(partner, qkv_hbm, qkv_w, local.at[0])
    bring_x.wait()
    sent_x = partner.push(x_ref.at[mine], x_ref.at[mine])
    bring_g, bring_m = bring(1, g_hbm, g_ref), bring(2, m_hbm, m_ref)
    bring_m.start()
    bring_g.start()
    so = Weights(partner, so_hbm, so_w, local.at[2])
    ckv = Weights(partner, ckv_hbm, ckv_w, local.at[1])
    cq = Weights(partner, cq_hbm, cq_w, local.at[3])
    co = Weights(partner, co_hbm, co_w, local.at[4])

    sent_ids.wait_recv()
    ids = jnp.where(deep % 2 == core, ids_ref[...], ids_got[...])
    ids_all[...] = ids
    micro = deep // 2
    token_row = jnp.where(micro == 0, ids[0:1], ids[1:2])
    source_row = jnp.where(micro == 0, ids[2:3], ids[3:4])
    id_rows[...] = jnp.broadcast_to(token_row, (128, token_row.shape[1])).T
    query_ids = id_rows[mine, :][:, :1]
    sent_vec.wait_recv()
    vectors = vec_ref[...]
    sent_x.wait_recv()
    n1_ref[...] = normed(x_ref[...].astype(f32), vectors, 0)
    place = core * count + lax.broadcasted_iota(jnp.int32, (count, 1), 0)
    keys = lax.broadcasted_iota(jnp.int32, (1, token_row.shape[1]), 1)
    allowed = (place >= keys) & (query_ids == token_row)
    allowed = jnp.concatenate([allowed, allowed], axis=0)
    w = qkv.get()
    q1_ref[...] = (mul(n1_ref[mine, :], w[:, :width]) + vectors[0:1]).astype(bf16)
    k1_ref[...] = mul(n1_ref[...], w[:, width : 2 * width]).astype(bf16)
    v1_ref[...] = (mul(n1_ref[...], w[:, 2 * width :]) + vectors[1:2]).astype(bf16)
    attend(q1_ref, k1_ref, v1_ref, p1_ref, o1_ref, allowed)
    bring_m.wait()
    sent_m = partner.push(m_ref.at[mine], m_ref.at[mine])
    bring_g.wait()
    sent_g = partner.push(g_ref.at[mine], g_ref.at[mine])
    spread_g = Spread(g_ref.at[mine], every_g, spread_send.at[0], spread_recv.at[0], spread_local.at[0])
    spread_g.begin()
    w = so.get()
    h1_ref[...] = x_ref[mine, :].astype(f32) + mul(o1_ref[...], w[...]) + vectors[2:3]
    n2_ref[...] = normed(h1_ref[...], vectors, 1)
    w = ckv.get()
    sent_m.wait_recv()
    k2_ref[...] = mul(m_ref[...], w[:, :width]).astype(bf16)
    v2_ref[...] = (mul(m_ref[...], w[:, width:]) + vectors[4:5]).astype(bf16)
    w = cq.get()
    q2_ref[...] = (mul(n2_ref[...], w[...]) + vectors[3:4]).astype(bf16)
    allowed = query_ids == source_row
    allowed = jnp.concatenate([allowed, allowed], axis=0)
    attend(q2_ref, k2_ref, v2_ref, p2_ref, o2_ref, allowed)
    w = co.get()
    h2_ref[...] = h1_ref[...] + mul(o2_ref[...], w[...]) + vectors[5:6]
    n3_ref[...] = normed(h2_ref[...], vectors, 2)
    rows_sent = partner.push(n3_ref, chip_n.at[mine])
    chip_n[mine, :] = n3_ref[...]
    spread_g.relay(1)
    spread_g.relay(3)
    spread_n = Spread(n3_ref, every_n, spread_send.at[1], spread_recv.at[1], spread_local.at[1])
    spread_n.begin()

    def tile_copies(index):
        slot = index % 2
        where = pl.ds(index * units, units)
        return (
            pltpu.make_async_copy(in_hbm.at[:, where], in_w.at[slot], tiles.at[slot, 0]),
            pltpu.make_async_copy(out_hbm.at[where], out_w.at[slot], tiles.at[slot, 1]),
        )

    steps = in_hbm.shape[1] // units
    for copy in tile_copies(0):
        copy.start()
    halves = [
        partner.push(n2_ref.at[:, their_half], n2_half.at[mine]),
        partner.push(o1_ref.at[:, their_half], o1_half.at[mine]),
        partner.push(o2_ref.at[:, their_half], o2_half.at[mine]),
    ]
    n2_half[mine, :] = n2_ref[:, my_half]
    o1_half[mine, :] = o1_ref[:, my_half]
    o2_half[mine, :] = o2_ref[:, my_half]
    sent_g.wait_recv()
    rows_sent.wait_recv()
    for index in range(steps):
        if index + 1 < steps:
            for copy in tile_copies(index + 1):
                copy.start()
        for copy in tile_copies(index):
            copy.wait()
        slot = index % 2
        inner = mul(chip_n[...], in_w[slot]) + fcb_ref[:, index * units : (index + 1) * units]
        active, slope = gelu_pair(inner, refine=True)
        back = (mul_nt(g_ref[...], out_w[slot]) * slope).astype(bf16)
        if index == 0:
            acc_y[...] = mul(active.astype(bf16), out_w[slot])
            acc_n[...] = mul_nt(back, in_w[slot])
        else:
            acc_y[...] += mul(active.astype(bf16), out_w[slot])
            acc_n[...] += mul_nt(back, in_w[slot])
        if index == 2 * steps // 8:
            spread_g.relay(2)
            spread_g.corner(0)
        if index == 6 * steps // 8:
            spread_g.corner(1)
            spread_g.corner(3)
    part[0] = acc_n[theirs, :].astype(bf16)
    sent_n = partner.push(part.at[0], got.at[0])
    part[1] = acc_y[theirs, :].astype(bf16)
    sent_y = partner.push(part.at[1], got.at[1])
    spread_n.relay(1)
    spread_n.relay(3)

    sent_n.wait_recv()
    grad = acc_n[mine, :] + got[0].astype(f32)
    grad = norm_back(grad, h2_ref[...], vectors[9:10], sums, 2) + g_ref[mine, :].astype(f32)
    dh_ref[...] = grad
    e2[mine, :] = grad.astype(bf16)
    sent_e2 = partner.push(e2.at[mine], e2.at[mine])
    sent_y.wait_recv()
    y = h2_ref[...] + (acc_y[mine, :] + got[1].astype(f32) + vectors[6:7])
    y_ref[...] = y.astype(bf16)
    give_y = give(3, y_ref, y_out)
    give_y.start()
    go_ref[...] = mul_nt(e2[mine, :], co_w[...]).astype(bf16)
    attend_back(q2_ref, k2_ref, v2_ref, p2_ref, go_ref, dq2.at[mine], dkv2.at[:, :width], dkv2.at[:, width:])
    sent_dkv2 = partner.push(dkv2, dkv2_got)
    sent_dq2 = partner.push(dq2.at[mine], dq2.at[mine])
    spread_g.corner(2)
    spread_g.last(0)
    spread_n.relay(2)
    spread_n.corner(0)
    grad = mul_nt(dq2[mine, :], cq_w[...])
    grad = norm_back(grad, h1_ref[...], vectors[8:9], sums, 1) + dh_ref[...]
    dh_ref[...] = grad
    e1[mine, :] = grad.astype(bf16)
    sent_e1 = partner.push(e1.at[mine], e1.at[mine])
    go_ref[...] = mul_nt(e1[mine, :], so_w[...]).astype(bf16)
    attend_back(q1_ref, k1_ref, v1_ref, p1_ref, go_ref, dq1.at[mine], dkv1.at[:, :width], dkv1.at[:, width:])
    sent_dkv1 = partner.push(dkv1, dkv1_got)
    sent_dq1 = partner.push(dq1.at[mine], dq1.at[mine])
    spread_g.last(1)
    spread_g.last(3)
    spread_n.corner(1)
    spread_n.corner(3)

    sent_dkv2.wait_recv()
    dkv2_got[...] = (dkv2[...].astype(f32) + dkv2_got[...].astype(f32)).astype(bf16)
    dm_ref[...] = mul_nt(dkv2_got[mine, :], ckv_w[...]).astype(bf16)
    give_dm = give(4, dm_ref, dm_out)
    give_dm.start()

    sent = []

    def weight_grad_of(left, right, column):
        index = len(sent)
        slot = index % 2
        if index >= 2:
            sent[index - 2].wait()
        stage[slot] = mul_tn(left, right).astype(bf16)
        copy = pltpu.make_async_copy(
            stage.at[slot], grads_ref.at[:, pl.ds(column, width)], stores.at[index]
        )
        copy.start()
        sent.append(copy)

    for copy in halves:
        copy.wait_recv()
    sent_e2.wait_recv()
    weight_grad_of(o2_half[...], e2[...], 7 * width)
    weight_grad_of(m_ref[:, my_half], dkv2_got[:, :width], 5 * width)
    weight_grad_of(m_ref[:, my_half], dkv2_got[:, width:], 6 * width)
    spread_g.last(2)
    spread_n.corner(2)
    sent_dq2.wait_recv()
    weight_grad_of(n2_half[...], dq2[...], 4 * width)
    sent_e1.wait_recv()
    weight_grad_of(o1_half[...], e1[...], 3 * width)
    sent_dkv1.wait_recv()
    dkv1_got[...] = (dkv1[...].astype(f32) + dkv1_got[...].astype(f32)).astype(bf16)
    grad = mul_nt(dq1[mine, :], qkv_w[:, :width])
    grad += mul_nt(dkv1_got[mine, :width], qkv_w[:, width : 2 * width])
    grad += mul_nt(dkv1_got[mine, width:], qkv_w[:, 2 * width :])
    dx = norm_back(grad, x_ref[mine, :].astype(f32), vectors[7:8], sums, 0) + dh_ref[...]
    dx_ref[...] = dx.astype(bf16)
    give_dx = give(5, dx_ref, dx_out)
    give_dx.start()
    sent_sums = partner.push(sums, sums_got)
    weight_grad_of(n1_ref[:, my_half], dkv1_got[:, :width], width)
    weight_grad_of(n1_ref[:, my_half], dkv1_got[:, width:], 2 * width)
    sent_dq1.wait_recv()
    weight_grad_of(n1_ref[:, my_half], dq1[...], 0)

    def columns(values):
        return jnp.sum(values.astype(f32), axis=0, keepdims=True)

    value_half = pl.ds(pl.multiple_of(width + core * half, half), half)
    sent_sums.wait_recv()
    lines = [
        columns(dq1[:, my_half]),
        columns(dkv1_got[:, value_half]),
        columns(e1[:, my_half]),
        columns(dq2[:, my_half]),
        columns(dkv2_got[:, value_half]),
        columns(e2[:, my_half]),
        columns(g_ref[:, my_half]),
        sums[0:6, my_half] + sums_got[0:6, my_half],
    ]
    lines = jnp.concatenate(lines + [jnp.zeros((128 - 13, half), f32)], axis=0).T
    sent[-1].wait()
    sent[-2].wait()
    stage[0, :, :128] = lines.astype(bf16)
    final = pltpu.make_async_copy(
        stage.at[0, :, pl.ds(0, 128)], grads_ref.at[:, pl.ds(8 * width, 128)], stores.at[8]
    )
    final.start()
    for step in (0, 1, 3, 2):
        spread_n.last(step)
    final.wait()
    partner.finish()
    for move in (bring_x, bring_m, bring_g, give_y, give_dm, give_dx):
        move.finish()
    spread_g.finish()
    spread_n.finish()


def layer(x, memory, grads, vectors, ids, fc_bias, weights, fc_in, fc_out, devices):
    block, width = x.shape[1:]
    rows = ids.shape[1]
    count = rows // 2
    units = 512
    bf16, f32 = jnp.bfloat16, jnp.float32
    half = width // 2
    vmem = pl.BlockSpec(memory_space=pltpu.VMEM)
    hbm = pl.BlockSpec(memory_space=pl.ANY)
    every = jax.ShapeDtypeStruct((devices * count, width), bf16)
    moved = jax.ShapeDtypeStruct(x.shape, bf16)
    scores = (width // (2 * HEAD), rows, rows)
    kept = [
        ((rows, width), bf16), ((count, width), bf16), ((rows, width), bf16), ((rows, width), bf16),
        (scores, bf16), ((count, width), bf16), ((count, width), f32), ((count, width), bf16),
        ((count, width), bf16), ((rows, width), bf16), ((rows, width), bf16), (scores, bf16),
        ((count, width), bf16), ((count, width), f32), ((count, width), bf16),
    ]
    return pl.pallas_call(
        layer_kernel,
        in_specs=[vmem] * 3 + [hbm] * 10,
        out_specs=[hbm] * 6,
        out_shape=[
            moved, moved, moved, jax.ShapeDtypeStruct((half, 8 * width + 128), bf16), every, every
        ],
        scratch_shapes=[
            *[pltpu.VMEM((rows, width), bf16)] * 3,
            pltpu.VMEM((16, width), f32),
            pltpu.VMEM(ids.shape, jnp.int32),
            pltpu.VMEM(ids.shape, jnp.int32),
            pltpu.VMEM((rows, 128), jnp.int32),
            *[pltpu.VMEM(*shape) for shape in kept],
            *[pltpu.VMEM((count, width), bf16)] * 3,
            *[pltpu.VMEM((2 * w.shape[0], w.shape[1]), bf16) for w in weights],
            pltpu.VMEM((2, width, units), bf16),
            pltpu.VMEM((2, units, width), bf16),
            pltpu.VMEM((rows, width), bf16),
            pltpu.VMEM((rows, width), f32),
            pltpu.VMEM((rows, width), f32),
            pltpu.VMEM((2, count, width), bf16),
            pltpu.VMEM((2, count, width), bf16),
            pltpu.VMEM((count, width), bf16),
            *[pltpu.VMEM((rows, 2 * width), bf16)] * 4,
            *[pltpu.VMEM((rows, width), bf16)] * 4,
            *[pltpu.VMEM((rows, half), bf16)] * 3,
            pltpu.VMEM((count, width), f32),
            pltpu.VMEM((8, width), f32),
            pltpu.VMEM((8, width), f32),
            pltpu.VMEM((2, half, width), bf16),
            pltpu.SemaphoreType.DMA((32,)),
            pltpu.SemaphoreType.DMA((32,)),
            pltpu.SemaphoreType.DMA((5,)),
            pltpu.SemaphoreType.DMA((2, 2)),
            pltpu.SemaphoreType.DMA((9,)),
            pltpu.SemaphoreType.DMA((6, 2)),
            pltpu.SemaphoreType.DMA((6, 2)),
            pltpu.SemaphoreType.DMA((6,)),
            pltpu.SemaphoreType.DMA((2, 35)),
            pltpu.SemaphoreType.DMA((2, 35)),
            pltpu.SemaphoreType.DMA((2,)),
        ],
        compiler_params=pltpu.CompilerParams(
            vmem_limit_bytes=60 * 2**20, collective_id=1, has_side_effects=True
        ),
        cost_estimate=pl.CostEstimate(flops=80 * 10**9, bytes_accessed=64 * 2**20, transcendentals=0),
    )(vectors, ids, fc_bias, x, memory, grads, *weights, fc_in, fc_out)


def widen_kernel(*refs):
    din_part, dout_part, sum_ref, din_ref, dout_ref = refs[:5]
    din_ref[...] = din_part[...].astype(jnp.float32)
    dout_ref[...] = dout_part[...].astype(jnp.float32)
    column = 0
    for shard_ref in refs[5:]:
        shard_ref[...] = sum_ref[:, column : column + shard_ref.shape[1]].astype(jnp.float32)
        column += shard_ref.shape[1]


def widen(din, dout, total, widths):
    width, hidden = din.shape
    steps = 8
    units, height = hidden // steps, total.shape[0] // steps
    wide = pl.BlockSpec((width // steps, hidden), lambda at: (at, 0))
    tall = pl.BlockSpec((units, width), lambda at: (at, 0))
    f32 = jnp.float32
    return pl.pallas_call(
        widen_kernel,
        grid=(steps,),
        in_specs=[wide, tall, pl.BlockSpec((height, total.shape[1]), lambda at: (at, 0))],
        out_specs=[wide, tall] + [pl.BlockSpec((height, w), lambda at: (at, 0)) for w in widths],
        out_shape=[jax.ShapeDtypeStruct(din.shape, f32), jax.ShapeDtypeStruct(dout.shape, f32)]
        + [jax.ShapeDtypeStruct((total.shape[0], w), f32) for w in widths],
        compiler_params=pltpu.CompilerParams(vmem_limit_bytes=56 * 2**20),
        cost_estimate=pl.CostEstimate(flops=0, bytes_accessed=18 * width * hidden, transcendentals=0),
    )(din, dout, total)


def fast_body(
    hidden_in,
    memory,
    segment_ids,
    memory_ids,
    out_grad,
    self_qkv,
    self_out,
    cross_query,
    cross_kv,
    cross_out,
    fc_in,
    fc_out,
    biases,
    fc_in_bias,
    norm_gains,
    norm_shifts,
):
    width = hidden_in.shape[-1]
    f32 = jnp.float32
    ids = jnp.concatenate([segment_ids[:, 0], memory_ids[:, 0]], axis=0)
    vectors = jnp.concatenate([biases, norm_gains, norm_shifts], axis=1).astype(f32).T
    vectors = jnp.pad(vectors, ((0, 16 - vectors.shape[0]), (0, 0)))
    fc_bias = fc_in_bias.astype(f32)[None]
    devices = lax.axis_size("rep") * lax.axis_size("fsdp") * lax.axis_size("seq")
    weights = (self_qkv, self_out, cross_query, cross_kv, cross_out)
    hidden_out, hidden_grad, memory_grad, grads, normed_every, grad_every = layer(
        hidden_in[:, 0], memory[:, 0], out_grad[:, 0], vectors, ids, fc_bias, weights, fc_in, fc_out, devices
    )
    din, dout, grad_fc_bias, total = ffn_grads(
        normed_every, grad_every, fc_in, fc_out, fc_bias, grads
    )
    widths = [weight.shape[1] for weight in weights]
    grad_fc_in, grad_fc_out, *shards = widen(din, dout, total, widths)
    column = total[:, 8 * width :].astype(f32)
    return (
        hidden_out[:, None],
        hidden_grad[:, None],
        memory_grad[:, None],
        *shards,
        grad_fc_in,
        grad_fc_out,
        column[:, :7],
        grad_fc_bias[0],
        column[:, 7:10],
        column[:, 10:13],
    )


def solution(mesh):
    fits = mesh.shape["rep"] == 4 and mesh.shape["fsdp"] == 2 and mesh.shape["seq"] == 4
    chosen = fast_body if fits else body
    return jax.shard_map(
        chosen,
        mesh=mesh,
        in_specs=(
            P(None, ("rep", "fsdp"), "seq", None),
            P(None, ("rep", "fsdp"), "seq", None),
            P(None, ("rep", "fsdp"), None),
            P(None, ("rep", "fsdp"), None),
            P(None, ("rep", "fsdp"), "seq", None),
            P("fsdp", None),
            P("fsdp", None),
            P("fsdp", None),
            P("fsdp", None),
            P("fsdp", None),
            P(None, "fsdp"),
            P("fsdp", None),
            P("fsdp", None),
            P("fsdp"),
            P("fsdp", None),
            P("fsdp", None),
        ),
        out_specs=(
            P(None, ("rep", "fsdp"), "seq", None),
            P(None, ("rep", "fsdp"), "seq", None),
            P(None, ("rep", "fsdp"), "seq", None),
            P("fsdp", None),
            P("fsdp", None),
            P("fsdp", None),
            P("fsdp", None),
            P("fsdp", None),
            P(None, "fsdp"),
            P("fsdp", None),
            P("fsdp", None),
            P("fsdp"),
            P("fsdp", None),
            P("fsdp", None),
        ),
        check_vma=False,
    )
```

```python
import functools
import math

import jax
import jax.numpy as jnp
from jax import lax
from jax.experimental import pallas as pl
from jax.experimental.pallas import tpu as pltpu
from jax.sharding import PartitionSpec as P

HEAD = 64


NORM_EPSILON = 1e-05
MASKED_SCORE = -1e30


def norm_forward(values, norm_gain, norm_shift):
    average = jnp.mean(values, axis=-1, keepdims=True)
    centred = values - average
    inverse = lax.rsqrt(jnp.mean(centred * centred, axis=-1, keepdims=True) + NORM_EPSILON)
    scaled = centred * inverse
    return (scaled * norm_gain + norm_shift, scaled, inverse)


def norm_backward(grad_normed, scaled, inverse, norm_gain):
    grad_scaled = grad_normed * norm_gain
    first_mean = jnp.mean(grad_scaled, axis=-1, keepdims=True)
    second_mean = jnp.mean(grad_scaled * scaled, axis=-1, keepdims=True)
    grad_values = (grad_scaled - first_mean - scaled * second_mean) * inverse
    gain_grad = jnp.sum(grad_normed * scaled, axis=(0, 1))
    shift_grad = jnp.sum(grad_normed, axis=(0, 1))
    return (grad_values, gain_grad, shift_grad)


def split_heads(values):
    return values.reshape(values.shape[:-1] + (values.shape[-1] // HEAD, HEAD))


def join_heads(values):
    return values.reshape(values.shape[:2] + (values.shape[2] * values.shape[3],))


def masked_scores(queries, key_rows, allowed):
    raw_scores = jnp.einsum(
        "mqhe,mkhe->mhqk", queries, key_rows, preferred_element_type=jnp.float32
    )
    return jnp.where(allowed[:, None], raw_scores * HEAD ** (-0.5), MASKED_SCORE)


def attend_forward(queries, key_rows, value_rows, allowed):
    scores = masked_scores(queries, key_rows, allowed)
    highest = jnp.max(scores, axis=-1, keepdims=True)
    exponent = jnp.exp(scores - highest)
    row_totals = jnp.sum(exponent, axis=-1, keepdims=True)
    weights = (exponent / row_totals).astype(jnp.bfloat16)
    joined = jnp.einsum("mhqk,mkhe->mqhe", weights, value_rows, preferred_element_type=jnp.float32)
    return (join_heads(joined).astype(jnp.bfloat16), highest + jnp.log(row_totals))


def attend_backward(queries, key_rows, value_rows, allowed, log_totals, grad_joined):
    scores = masked_scores(queries, key_rows, allowed)
    probability = jnp.exp(scores - log_totals)
    weights = probability.astype(jnp.bfloat16)
    grad_value_rows = jnp.einsum(
        "mhqk,mqhe->mkhe", weights, grad_joined, preferred_element_type=jnp.float32
    )
    grad_weights = jnp.einsum(
        "mqhe,mkhe->mhqk", grad_joined, value_rows, preferred_element_type=jnp.float32
    )
    grad_scores = probability * (
        grad_weights - jnp.sum(grad_weights * probability, axis=-1, keepdims=True)
    )
    grad_scores = grad_scores.astype(jnp.bfloat16)
    grad_queries = jnp.einsum(
        "mhqk,mkhe->mqhe", grad_scores, key_rows, preferred_element_type=jnp.float32
    ) * HEAD ** (-0.5)
    grad_key_rows = jnp.einsum(
        "mhqk,mqhe->mkhe", grad_scores, queries, preferred_element_type=jnp.float32
    ) * HEAD ** (-0.5)
    return (join_heads(grad_queries), join_heads(grad_key_rows), join_heads(grad_value_rows))


def gelu_slope(values):
    cumulative = 0.5 * (1.0 + lax.erf(values * 2.0 ** (-0.5)))
    density = jnp.exp(-0.5 * values * values) / math.sqrt(2.0 * math.pi)
    return cumulative + values * density


def feed_forward(rows, weight_in, bias_in, weight_out):
    pre_active = jnp.einsum(
        "mtd,df->mtf", rows, weight_in, preferred_element_type=jnp.float32
    ) + bias_in.astype(jnp.float32)
    active = jax.nn.gelu(pre_active, approximate=False).astype(jnp.bfloat16)
    partial_out = jnp.einsum("mtf,fd->mtd", active, weight_out, preferred_element_type=jnp.float32)
    return (pre_active, active, partial_out)


def feed_back(rows, grad_rows, pre_active, active, weight_in, weight_out):
    grad_active = jnp.einsum(
        "mtd,fd->mtf", grad_rows, weight_out, preferred_element_type=jnp.float32
    )
    grad_inner = (grad_active * gelu_slope(pre_active)).astype(jnp.bfloat16)
    grad_weight_out = jnp.einsum(
        "mtf,mtd->fd", active, grad_rows, preferred_element_type=jnp.float32
    )
    grad_weight_in = jnp.einsum("mtd,mtf->df", rows, grad_inner, preferred_element_type=jnp.float32)
    grad_bias_in = jnp.sum(grad_inner.astype(jnp.float32), axis=(0, 1))
    grad_rows_in = jnp.einsum(
        "mtf,df->mtd", grad_inner, weight_in, preferred_element_type=jnp.float32
    )
    return (grad_weight_in, grad_weight_out, grad_bias_in, grad_rows_in)


def project(rows, weight):
    return jnp.einsum("mtd,de->mte", rows, weight, preferred_element_type=jnp.float32)


def project_back(grad_rows, weight):
    return jnp.einsum("mte,de->mtd", grad_rows, weight, preferred_element_type=jnp.float32)


def weight_grad(rows, grad_rows):
    return jnp.einsum("mtd,mte->de", rows, grad_rows, preferred_element_type=jnp.float32)


def column_sums(grad_rows):
    return jnp.sum(grad_rows.astype(jnp.float32), axis=(0, 1))


def body(
    hidden_in,
    memory,
    segment_ids,
    memory_ids,
    out_grad,
    self_qkv,
    self_out,
    cross_query,
    cross_kv,
    cross_out,
    fc_in,
    fc_out,
    biases,
    fc_in_bias,
    norm_gains,
    norm_shifts,
):
    micro_count, single, tokens, model_width = hidden_in.shape
    seq_index = lax.axis_index("seq")
    zero_row = jnp.zeros((model_width,), jnp.float32)
    outputs_list = []
    grads_list = []
    memory_list = []
    attn_total = None
    mlp_total = None
    for micro in range(micro_count):
        full_qkv = lax.all_gather(self_qkv, "fsdp", axis=0, tiled=True)
        full_self_out = lax.all_gather(self_out, "fsdp", axis=0, tiled=True)
        full_query = lax.all_gather(cross_query, "fsdp", axis=0, tiled=True)
        full_memory_kv = lax.all_gather(cross_kv, "fsdp", axis=0, tiled=True)
        full_cross_out = lax.all_gather(cross_out, "fsdp", axis=0, tiled=True)
        full_biases = lax.all_gather(biases, "fsdp", axis=0, tiled=True)
        full_gains = lax.all_gather(norm_gains, "fsdp", axis=0, tiled=True)
        full_shifts = lax.all_gather(norm_shifts, "fsdp", axis=0, tiled=True)
        bias_float = full_biases.astype(jnp.float32)
        gain_float = full_gains.astype(jnp.float32)
        shift_float = full_shifts.astype(jnp.float32)
        hidden = hidden_in[micro : micro + 1][:, 0].astype(jnp.float32)
        memory_rows = memory[micro : micro + 1][:, 0]
        token_ids = segment_ids[micro : micro + 1][:, 0]
        source_ids = memory_ids[micro : micro + 1][:, 0]
        query_ids = lax.dynamic_slice_in_dim(token_ids, seq_index * tokens, tokens, 1)
        query_place = seq_index * tokens + jnp.arange(tokens, dtype=jnp.int32)
        key_place = jnp.arange(token_ids.shape[1], dtype=jnp.int32)
        self_allowed = (query_place[:, None] >= key_place[None, :])[None] & (
            query_ids[:, :, None] == token_ids[:, None, :]
        )
        cross_allowed = query_ids[:, :, None] == source_ids[:, None, :]
        normed_one, scaled_one, inverse_one = norm_forward(
            hidden, gain_float[:, 0], shift_float[:, 0]
        )
        normed_one = normed_one.astype(jnp.bfloat16)
        qkv_bias = jnp.concatenate([bias_float[:, 0], zero_row, bias_float[:, 1]])
        projected = (project(normed_one, full_qkv) + qkv_bias).astype(jnp.bfloat16)
        self_queries = split_heads(projected[..., :model_width])
        kv_all = lax.all_gather(projected[..., model_width:], "seq", axis=1, tiled=True)
        self_key_rows = split_heads(kv_all[..., :model_width])
        self_value_rows = split_heads(kv_all[..., model_width:])
        self_mixed, self_totals = attend_forward(
            self_queries, self_key_rows, self_value_rows, self_allowed
        )
        after_self = hidden + project(self_mixed, full_self_out) + bias_float[:, 2]
        normed_two, scaled_two, inverse_two = norm_forward(
            after_self, gain_float[:, 1], shift_float[:, 1]
        )
        normed_two = normed_two.astype(jnp.bfloat16)
        cross_queries = (project(normed_two, full_query) + bias_float[:, 3]).astype(jnp.bfloat16)
        memory_bias = jnp.concatenate([zero_row, bias_float[:, 4]])
        memory_kv = (project(memory_rows, full_memory_kv) + memory_bias).astype(jnp.bfloat16)
        memory_all = lax.all_gather(memory_kv, "seq", axis=1, tiled=True)
        memory_key_rows = split_heads(memory_all[..., :model_width])
        memory_value_rows = split_heads(memory_all[..., model_width:])
        cross_mixed, cross_totals = attend_forward(
            split_heads(cross_queries), memory_key_rows, memory_value_rows, cross_allowed
        )
        after_cross = after_self + project(cross_mixed, full_cross_out) + bias_float[:, 5]
        normed_three, scaled_three, inverse_three = norm_forward(
            after_cross, gain_float[:, 2], shift_float[:, 2]
        )
        normed_three = normed_three.astype(jnp.bfloat16)
        grad_out = out_grad[micro : micro + 1][:, 0]
        mlp_inputs = lax.all_gather(normed_three, "fsdp", axis=0, tiled=True)
        pre_active, active, partial_out = feed_forward(mlp_inputs, fc_in, fc_in_bias, fc_out)
        mlp_branch = lax.psum_scatter(
            partial_out.astype(jnp.bfloat16), "fsdp", scatter_dimension=0, tiled=True
        ).astype(jnp.float32)
        output = after_cross + mlp_branch + bias_float[:, 6]
        hidden_out = output.astype(jnp.bfloat16)[:, None]
        back_qkv = lax.all_gather(self_qkv, "fsdp", axis=0, tiled=True)
        back_self_out = lax.all_gather(self_out, "fsdp", axis=0, tiled=True)
        back_query = lax.all_gather(cross_query, "fsdp", axis=0, tiled=True)
        back_memory_kv = lax.all_gather(cross_kv, "fsdp", axis=0, tiled=True)
        back_cross_out = lax.all_gather(cross_out, "fsdp", axis=0, tiled=True)
        back_gains = lax.all_gather(norm_gains, "fsdp", axis=0, tiled=True)
        back_gain_float = back_gains.astype(jnp.float32)
        grad_gathered = lax.all_gather(grad_out, "fsdp", axis=0, tiled=True)
        one_grad_fc_in, one_grad_fc_out, one_grad_fc_bias, grad_partial = feed_back(
            mlp_inputs, grad_gathered, pre_active, active, fc_in, fc_out
        )
        grad_normed_three = lax.psum_scatter(
            grad_partial.astype(jnp.bfloat16), "fsdp", scatter_dimension=0, tiled=True
        ).astype(jnp.float32)
        grad_three, gain_three, shift_three = norm_backward(
            grad_normed_three, scaled_three, inverse_three, back_gain_float[:, 2]
        )
        grad_after_cross = grad_out.astype(jnp.float32) + grad_three
        grad_cross_branch = grad_after_cross.astype(jnp.bfloat16)
        grad_cross_out = weight_grad(cross_mixed, grad_cross_branch)
        grad_cross_mixed = project_back(grad_cross_branch, back_cross_out).astype(jnp.bfloat16)
        cross_grad_queries, memory_grad_keys, memory_grad_values = attend_backward(
            split_heads(cross_queries),
            memory_key_rows,
            memory_value_rows,
            cross_allowed,
            cross_totals,
            split_heads(grad_cross_mixed),
        )
        own_memory_keys = lax.psum_scatter(
            memory_grad_keys.astype(jnp.bfloat16), "seq", scatter_dimension=1, tiled=True
        )
        own_memory_values = lax.psum_scatter(
            memory_grad_values.astype(jnp.bfloat16), "seq", scatter_dimension=1, tiled=True
        )
        grad_memory_kv = jnp.concatenate([own_memory_keys, own_memory_values], axis=-1)
        grad_memory_weight = weight_grad(memory_rows, grad_memory_kv)
        memory_grad = project_back(grad_memory_kv, back_memory_kv).astype(jnp.bfloat16)[:, None]
        grad_cross_queries = cross_grad_queries.astype(jnp.bfloat16)
        grad_query_weight = weight_grad(normed_two, grad_cross_queries)
        grad_normed_two = project_back(grad_cross_queries, back_query)
        grad_two, gain_two, shift_two = norm_backward(
            grad_normed_two, scaled_two, inverse_two, back_gain_float[:, 1]
        )
        grad_after_self = grad_after_cross + grad_two
        grad_self_branch = grad_after_self.astype(jnp.bfloat16)
        grad_self_out = weight_grad(self_mixed, grad_self_branch)
        grad_self_mixed = project_back(grad_self_branch, back_self_out).astype(jnp.bfloat16)
        self_grad_queries, self_grad_keys, self_grad_values = attend_backward(
            self_queries,
            self_key_rows,
            self_value_rows,
            self_allowed,
            self_totals,
            split_heads(grad_self_mixed),
        )
        own_self_keys = lax.psum_scatter(
            self_grad_keys.astype(jnp.bfloat16), "seq", scatter_dimension=1, tiled=True
        )
        own_self_values = lax.psum_scatter(
            self_grad_values.astype(jnp.bfloat16), "seq", scatter_dimension=1, tiled=True
        )
        grad_projected = jnp.concatenate(
            [self_grad_queries.astype(jnp.bfloat16), own_self_keys, own_self_values], axis=-1
        )
        grad_qkv_weight = weight_grad(normed_one, grad_projected)
        grad_normed_one = project_back(grad_projected, back_qkv)
        grad_one, gain_one, shift_one = norm_backward(
            grad_normed_one, scaled_one, inverse_one, back_gain_float[:, 0]
        )
        hidden_grad = (grad_after_self + grad_one).astype(jnp.bfloat16)[:, None]
        grad_biases = jnp.stack(
            [
                column_sums(grad_projected[..., :model_width]),
                column_sums(grad_projected[..., 2 * model_width :]),
                column_sums(grad_self_branch),
                column_sums(grad_cross_queries),
                column_sums(grad_memory_kv[..., model_width:]),
                column_sums(grad_cross_branch),
                column_sums(grad_out),
            ],
            axis=1,
        )
        grad_gains = jnp.stack([gain_one, gain_two, gain_three], axis=1)
        grad_shifts = jnp.stack([shift_one, shift_two, shift_three], axis=1)
        attn_grads = (
            grad_qkv_weight,
            grad_self_out,
            grad_query_weight,
            grad_memory_weight,
            grad_cross_out,
            grad_biases,
            grad_gains,
            grad_shifts,
        )
        mlp_grads = (one_grad_fc_in, one_grad_fc_out, one_grad_fc_bias)
        hidden_out, hidden_grad, memory_grad, attn_grads, mlp_grads = (
            hidden_out,
            hidden_grad,
            memory_grad,
            attn_grads,
            mlp_grads,
        )
        outputs_list.append(hidden_out)
        grads_list.append(hidden_grad)
        memory_list.append(memory_grad)
        if attn_total is None:
            attn_total = attn_grads
            mlp_total = mlp_grads
        else:
            attn_total = jax.tree.map(jnp.add, attn_total, attn_grads)
            mlp_total = jax.tree.map(jnp.add, mlp_total, mlp_grads)
    grad_fc_in, grad_fc_out, grad_fc_bias = mlp_total
    (
        shard_qkv,
        shard_self_out,
        shard_query,
        shard_memory_kv,
        shard_cross_out,
        shard_biases,
        shard_gains,
        shard_shifts,
    ) = (
        lax.psum_scatter(
            attn_total[0].astype(jnp.bfloat16), "fsdp", scatter_dimension=0, tiled=True
        ).astype(jnp.float32),
        lax.psum_scatter(
            attn_total[1].astype(jnp.bfloat16), "fsdp", scatter_dimension=0, tiled=True
        ).astype(jnp.float32),
        lax.psum_scatter(
            attn_total[2].astype(jnp.bfloat16), "fsdp", scatter_dimension=0, tiled=True
        ).astype(jnp.float32),
        lax.psum_scatter(
            attn_total[3].astype(jnp.bfloat16), "fsdp", scatter_dimension=0, tiled=True
        ).astype(jnp.float32),
        lax.psum_scatter(
            attn_total[4].astype(jnp.bfloat16), "fsdp", scatter_dimension=0, tiled=True
        ).astype(jnp.float32),
        lax.psum_scatter(
            attn_total[5].astype(jnp.bfloat16), "fsdp", scatter_dimension=0, tiled=True
        ).astype(jnp.float32),
        lax.psum_scatter(
            attn_total[6].astype(jnp.bfloat16), "fsdp", scatter_dimension=0, tiled=True
        ).astype(jnp.float32),
        lax.psum_scatter(
            attn_total[7].astype(jnp.bfloat16), "fsdp", scatter_dimension=0, tiled=True
        ).astype(jnp.float32),
    )
    summed = (
        lax.psum(shard_qkv.astype(jnp.bfloat16), ("rep", "seq")).astype(jnp.float32),
        lax.psum(shard_self_out.astype(jnp.bfloat16), ("rep", "seq")).astype(jnp.float32),
        lax.psum(shard_query.astype(jnp.bfloat16), ("rep", "seq")).astype(jnp.float32),
        lax.psum(shard_memory_kv.astype(jnp.bfloat16), ("rep", "seq")).astype(jnp.float32),
        lax.psum(shard_cross_out.astype(jnp.bfloat16), ("rep", "seq")).astype(jnp.float32),
        lax.psum(grad_fc_in.astype(jnp.bfloat16), ("rep", "seq")).astype(jnp.float32),
        lax.psum(grad_fc_out.astype(jnp.bfloat16), ("rep", "seq")).astype(jnp.float32),
        lax.psum(shard_biases.astype(jnp.bfloat16), ("rep", "seq")).astype(jnp.float32),
        lax.psum(grad_fc_bias.astype(jnp.bfloat16), ("rep", "seq")).astype(jnp.float32),
        lax.psum(shard_gains.astype(jnp.bfloat16), ("rep", "seq")).astype(jnp.float32),
        lax.psum(shard_shifts.astype(jnp.bfloat16), ("rep", "seq")).astype(jnp.float32),
    )
    hidden_out = jnp.concatenate(outputs_list, axis=0)
    hidden_grad = jnp.concatenate(grads_list, axis=0)
    memory_grad = jnp.concatenate(memory_list, axis=0)
    return (
        hidden_out,
        hidden_grad,
        memory_grad,
        summed[0],
        summed[1],
        summed[2],
        summed[3],
        summed[4],
        summed[5],
        summed[6],
        summed[7],
        summed[8],
        summed[9],
        summed[10],
    )


def mul(left, right):
    return jnp.dot(left, right, preferred_element_type=jnp.float32)


def mul_nt(left, right):
    return lax.dot_general(left, right, (((1,), (1,)), ((), ())), preferred_element_type=jnp.float32)


def mul_tn(left, right):
    return lax.dot_general(left, right, (((0,), (0,)), ((), ())), preferred_element_type=jnp.float32)


MESH = pl.DeviceIdType.MESH


def gelu_pair(values, refine=False):
    depth = 1.0 + (0.3275911 * 2.0**-0.5) * jnp.abs(values)
    inv = pltpu.reciprocal(depth, approx=True)
    if refine:
        inv = inv * (2.0 - depth * inv)
    bell = jnp.exp(-0.5 * values * values)
    series = 0.7107068705 + inv * (-0.7265760135 + inv * 0.5307027145)
    series = inv * (0.127414796 + inv * (-0.142248368 + inv * series))
    tail = series * bell
    cumulative = jnp.where(values >= 0.0, 1.0 - tail, tail)
    return values * cumulative, cumulative + values * (bell * (1.0 / math.sqrt(2.0 * math.pi)))


def position():
    rep, core, deep = lax.axis_index("rep"), lax.axis_index("fsdp"), lax.axis_index("seq")
    return rep % 2, rep // 2, core, deep


def device(across, up, core, deep):
    return (up * 2 + across, core, deep)


def greet(partners):
    barrier = pltpu.get_barrier_semaphore()
    for partner in partners:
        pl.semaphore_signal(barrier, inc=1, device_id=partner, device_id_type=MESH)
    pl.semaphore_wait(barrier, len(partners))


class ChunkSum:
    def __init__(self, turned, column, width, own_ref, sum_ref, held, first, second, third, done, send, recv, local):
        across, up, core, deep = position()
        self.side, self.next = (up, across) if turned else (across, up)
        one = device(1 - across, up, core, deep)
        two = device(across, 1 - up, core, deep)
        self.one, self.two = (two, one) if turned else (one, two)
        self.deep = deep
        self.others = [(deep + step) % 4 for step in (1, 2, 3)]
        self.third_ids = [device(across, up, core, other) for other in self.others]
        self.columns = pl.ds(column, width)
        self.own, self.sum = own_ref, sum_ref
        self.held, self.first, self.second, self.third, self.done = held, first, second, third, done
        self.send, self.recv, self.local = send, recv, local
        self.quarter = pl.multiple_of(self.next * 128, 128)
        self.start_row = self.side * 256

    def remote(self, index, src, dst, target):
        return pltpu.make_async_remote_copy(
            src_ref=src,
            dst_ref=dst,
            send_sem=self.send.at[index],
            recv_sem=self.recv.at[index],
            device_id=target,
            device_id_type=MESH,
        )

    def rows(self, ref, start, count):
        return ref.at[pl.ds(pl.multiple_of(start, 32), count), self.columns]

    def copy_a(self):
        return self.remote(0, self.rows(self.own, (1 - self.side) * 256, 256), self.first, self.one)

    def load(self):
        return pltpu.make_async_copy(self.rows(self.own, self.start_row, 256), self.held, self.local.at[0])

    def copy_b(self):
        away = pl.multiple_of((1 - self.next) * 128, 128)
        return self.remote(1, self.held.at[pl.ds(away, 128)], self.second, self.two)

    def copy_c(self, turn):
        start = pl.multiple_of(self.quarter + self.others[turn] * 32, 32)
        return self.remote(2 + turn, self.held.at[pl.ds(start, 32)], self.third.at[turn], self.third_ids[turn])

    def place(self):
        return self.rows(self.sum, self.start_row + self.quarter + self.deep * 32, 32)

    def copy_d(self, turn):
        return self.remote(5 + turn, self.done, self.place(), self.third_ids[turn])

    def store(self):
        return pltpu.make_async_copy(self.done, self.place(), self.local.at[1])

    def copy_e(self):
        part = self.rows(self.sum, self.start_row + self.quarter, 128)
        return self.remote(8, part, part, self.two)

    def copy_f(self):
        part = self.rows(self.sum, self.start_row, 256)
        return self.remote(9, part, part, self.one)

    def stage(self, number):
        if number == 0:
            self.copy_a().start()
            self.load().start()
        elif number == 1:
            self.load().wait()
            self.copy_a().wait_recv()
            self.held[...] = self.held[...] + self.first[...]
            self.copy_b().start()
        elif number == 2:
            self.copy_b().wait_recv()
            self.copy_b().wait_send()
            mine = pl.ds(self.quarter, 128)
            self.held[mine] = self.held[mine] + self.second[...]
            for turn in range(3):
                self.copy_c(turn).start()
        elif number == 3:
            for turn in range(3):
                self.copy_c(turn).wait_recv()
            start = pl.multiple_of(self.quarter + self.deep * 32, 32)
            total = self.held[pl.ds(start, 32)].astype(jnp.float32)
            for turn in range(3):
                total += self.third[turn].astype(jnp.float32)
            self.done[...] = total.astype(self.done.dtype)
            self.store().start()
            for turn in range(3):
                self.copy_d(turn).start()
        elif number == 4:
            self.store().wait()
            for turn in range(3):
                self.copy_d(turn).wait_recv()
            self.copy_e().start()
        elif number == 5:
            self.copy_e().wait_recv()
            self.copy_f().start()
        elif number == 6:
            self.copy_f().wait_recv()
            self.copy_a().wait_send()
            for turn in range(3):
                self.copy_c(turn).wait_send()
                self.copy_d(turn).wait_send()
            self.copy_e().wait_send()
            self.copy_f().wait_send()


BEGIN = (0, 3, 6, 9)
AFTER = (0, 2, 3, 4, 5, 6, 8)


def ffn_kernel(
    step, tiles, plan, rows_ref, grads_ref, in_ref, out_ref, bias_ref, own_ref,
    din_ref, dout_ref, dbias_ref, sum_ref, flip, acc_in, acc_out, us, das, actives, inners, sums, *rest
):
    units = flip.shape[0]
    steps = rows_ref.shape[0] // step
    at = pl.program_id(0)
    send, recv, local = rest[-3:]
    buffers = rest[:-3]
    chunks = []
    for index, (turned, column, width, _) in enumerate(plan):
        held, first, second, third, done = buffers[5 * index : 5 * index + 5]
        chunks.append(
            ChunkSum(turned, column, width, own_ref, sum_ref, held, first, second, third, done,
                     send.at[index], recv.at[index], local.at[index])
        )

    @pl.when(at == 0)
    def _():
        across, up, core, deep = position()
        greet(
            [device(1 - across, up, core, deep), device(across, 1 - up, core, deep)]
            + [device(across, up, core, (deep + turn) % 4) for turn in (1, 2, 3)]
        )

    work = {}
    for chunk, (_, _, _, slots) in zip(chunks, plan):
        for number, slot in enumerate(slots):
            work.setdefault(min(slot, tiles), []).append((slot, number, chunk))

    def traffic(slot):
        for _, number, chunk in sorted(work.get(slot, []), key=lambda job: job[:2]):
            chunk.stage(number)

    for slot in range(tiles):
        if slot in work:
            pl.when(at == slot)(functools.partial(traffic, slot))

    flip[...] = in_ref[...].T

    def front(turn):
        part = pl.ds(turn * step, step)
        us[turn % 2] = mul_nt(flip[...], rows_ref[part, :])
        das[turn % 2] = mul_nt(out_ref[...], grads_ref[part, :])

    bias = jnp.broadcast_to(bias_ref[...], (128, units)).T[:, :1]

    def middle(turn):
        active, slope = gelu_pair(us[turn % 2] + bias)
        inner = (das[turn % 2] * slope).astype(jnp.bfloat16)
        actives[turn % 2] = active.astype(jnp.bfloat16)
        inners[turn % 2] = inner
        total = inner[:, :128].astype(jnp.float32)
        for lane in range(1, step // 128):
            total += inner[:, lane * 128 : (lane + 1) * 128].astype(jnp.float32)
        sums[...] = total if turn == 0 else sums[...] + total

    def back(turn):
        part = pl.ds(turn * step, step)
        out_part = mul(actives[turn % 2], grads_ref[part, :])
        in_part = mul(inners[turn % 2], rows_ref[part, :])
        if turn:
            out_part += acc_out[...]
            in_part += acc_in[...]
        if turn < steps - 1:
            acc_out[...] = out_part
            acc_in[...] = in_part
        else:
            dout_ref[...] = out_part.astype(jnp.bfloat16)
            din_ref[...] = in_part.astype(jnp.bfloat16).T

    front(0)
    for turn in range(steps + 1):
        if turn:
            back(turn - 1)
        if turn + 1 < steps:
            front(turn + 1)
        if turn < steps:
            middle(turn)
    dbias_ref[...] = jnp.sum(sums[...].T, axis=0, keepdims=True)
    pl.when(at == tiles - 1)(functools.partial(traffic, tiles))


def ffn_grads(rows, grads, fc_in, fc_out, bias, own):
    count, width = rows.shape
    hidden = fc_in.shape[1]
    units, step = 256, count // 4
    tiles = hidden // units
    plan = [(False, 8 * width, 128, (0, 1, 2, 3, 4, 5, 6))]
    for pair, begin in enumerate(BEGIN):
        slots = [begin + after for after in AFTER]
        plan.append((False, pair * width, width, slots))
        plan.append((True, (len(BEGIN) + pair) * width, width, slots))
    buffers = []
    for _, _, columns, _ in plan:
        buffers += [
            pltpu.VMEM((256, columns), jnp.bfloat16),
            pltpu.VMEM((256, columns), jnp.bfloat16),
            pltpu.VMEM((128, columns), jnp.bfloat16),
            pltpu.VMEM((3, 32, columns), jnp.bfloat16),
            pltpu.VMEM((32, columns), jnp.bfloat16),
        ]
    whole = functools.partial(pl.BlockSpec, pipeline_mode=pl.Buffered(1))
    return pl.pallas_call(
        functools.partial(ffn_kernel, step, tiles, plan),
        grid=(tiles,),
        in_specs=[
            whole((count, width), lambda at: (0, 0)),
            whole((count, width), lambda at: (0, 0)),
            pl.BlockSpec((width, units), lambda at: (0, at)),
            pl.BlockSpec((units, width), lambda at: (at, 0)),
            pl.BlockSpec((1, units), lambda at: (0, at)),
            pl.BlockSpec(memory_space=pl.ANY),
        ],
        out_specs=[
            pl.BlockSpec((width, units), lambda at: (0, at)),
            pl.BlockSpec((units, width), lambda at: (at, 0)),
            pl.BlockSpec((1, units), lambda at: (0, at)),
            pl.BlockSpec(memory_space=pl.ANY),
        ],
        out_shape=[
            jax.ShapeDtypeStruct((width, hidden), jnp.bfloat16),
            jax.ShapeDtypeStruct((hidden, width), jnp.bfloat16),
            jax.ShapeDtypeStruct((1, hidden), jnp.float32),
            jax.ShapeDtypeStruct(own.shape, own.dtype),
        ],
        scratch_shapes=[
            pltpu.VMEM((units, width), jnp.bfloat16),
            pltpu.VMEM((units, width), jnp.float32),
            pltpu.VMEM((units, width), jnp.float32),
            pltpu.VMEM((2, units, step), jnp.float32),
            pltpu.VMEM((2, units, step), jnp.float32),
            pltpu.VMEM((2, units, step), jnp.bfloat16),
            pltpu.VMEM((2, units, step), jnp.bfloat16),
            pltpu.VMEM((units, 128), jnp.float32),
            *buffers,
            pltpu.SemaphoreType.DMA((len(plan), 10)),
            pltpu.SemaphoreType.DMA((len(plan), 10)),
            pltpu.SemaphoreType.DMA((len(plan), 2)),
        ],
        compiler_params=pltpu.CompilerParams(
            vmem_limit_bytes=58 * 2**20, collective_id=0, has_side_effects=True
        ),
        cost_estimate=pl.CostEstimate(
            flops=8 * count * width * hidden,
            bytes_accessed=4 * count * width + 12 * width * hidden,
            transcendentals=count * hidden,
        ),
    )(rows, grads, fc_in, fc_out, bias, own)


def norm_parts(values):
    centred = values - jnp.mean(values, axis=-1, keepdims=True)
    inverse = lax.rsqrt(jnp.mean(centred * centred, axis=-1, keepdims=True) + NORM_EPSILON)
    return centred * inverse, inverse


def normed(values, vectors, which):
    scaled, _ = norm_parts(values)
    return (scaled * vectors[7 + which : 8 + which] + vectors[10 + which : 11 + which]).astype(jnp.bfloat16)


class Partner:
    def __init__(self, send, recv):
        across, up, core, deep = position()
        self.core = core
        self.id = device(across, up, 1 - core, deep)
        self.send, self.recv = send, recv
        self.copies = []

    def push(self, src, dst):
        index = len(self.copies)
        copy = pltpu.make_async_remote_copy(
            src_ref=src,
            dst_ref=dst,
            send_sem=self.send.at[index],
            recv_sem=self.recv.at[index],
            device_id=self.id,
            device_id_type=MESH,
        )
        copy.start()
        self.copies.append(copy)
        return copy

    def finish(self):
        for copy in self.copies:
            copy.wait_send()


class Weights:
    def __init__(self, partner, shard, whole, local):
        half = shard.shape[0]
        mine = whole.at[pl.ds(pl.multiple_of(partner.core * half, half), half)]
        self.remote = partner.push(shard, mine)
        self.near = pltpu.make_async_copy(shard, mine, local)
        self.near.start()
        self.whole = whole

    def get(self):
        self.near.wait()
        self.remote.wait_recv()
        return self.whole


def two_heads(values, lane):
    zero = jnp.zeros_like(values)
    return jnp.concatenate([jnp.where(lane, values, zero), jnp.where(lane, zero, values)], axis=0)


def lane_of():
    return lax.broadcasted_iota(jnp.int32, (1, 2 * HEAD), 1) < HEAD


def attend(q_ref, k_ref, v_ref, p_ref, o_ref, allowed):
    lane = lane_of()
    count = q_ref.shape[0]
    for pair in range(q_ref.shape[1] // (2 * HEAD)):
        columns = pl.ds(pair * 2 * HEAD, 2 * HEAD)
        scores = mul_nt(two_heads(q_ref[:, columns], lane), k_ref[:, columns])
        scores = jnp.where(allowed, scores * HEAD ** (-0.5), MASKED_SCORE)
        exponent = jnp.exp(scores - jnp.max(scores, axis=-1, keepdims=True))
        weights = (exponent / jnp.sum(exponent, axis=-1, keepdims=True)).astype(jnp.bfloat16)
        p_ref[pair] = weights
        mixed = mul(weights, v_ref[:, columns])
        o_ref[:, columns] = jnp.where(lane, mixed[:count], mixed[count:]).astype(jnp.bfloat16)


def attend_back(q_ref, k_ref, v_ref, p_ref, go_ref, dq_ref, dk_ref, dv_ref):
    lane = lane_of()
    count = q_ref.shape[0]
    for pair in range(q_ref.shape[1] // (2 * HEAD)):
        columns = pl.ds(pair * 2 * HEAD, 2 * HEAD)
        grads = two_heads(go_ref[:, columns], lane)
        weights = p_ref[pair]
        dv_ref[:, columns] = mul_tn(weights, grads).astype(jnp.bfloat16)
        grad_weights = mul_nt(grads, v_ref[:, columns])
        exact = weights.astype(jnp.float32)
        inner = jnp.sum(grad_weights * exact, axis=-1, keepdims=True)
        scores = (exact * (grad_weights - inner)).astype(jnp.bfloat16)
        queries = mul(scores, k_ref[:, columns]) * HEAD ** (-0.5)
        dq_ref[:, columns] = jnp.where(lane, queries[:count], queries[count:]).astype(jnp.bfloat16)
        keys = mul_tn(scores, two_heads(q_ref[:, columns], lane)) * HEAD ** (-0.5)
        dk_ref[:, columns] = keys.astype(jnp.bfloat16)


def norm_back(grads, values, gain, sums_ref, row):
    scaled, inverse = norm_parts(values)
    sums_ref[row : row + 1, :] = jnp.sum(grads * scaled, axis=0, keepdims=True)
    sums_ref[row + 3 : row + 4, :] = jnp.sum(grads, axis=0, keepdims=True)
    inner = grads * gain
    first = jnp.mean(inner, axis=-1, keepdims=True)
    second = jnp.mean(inner * scaled, axis=-1, keepdims=True)
    return (inner - first - scaled * second) * inverse


class Bring:
    def __init__(self, src, dst, send, recv, local):
        across, up, core, deep = position()
        self.core, self.deep = core, deep
        self.src, self.dst = src, dst
        self.send, self.recv, self.local = send, recv, local
        self.across, self.up = across, up

    def stays(self, micro):
        return (self.deep // 2 == self.core) & (2 * micro + self.core == self.deep)

    def far(self, micro, index):
        block = self.src.shape[1]
        return pltpu.make_async_remote_copy(
            src_ref=self.src.at[micro],
            dst_ref=self.dst.at[pl.ds(pl.multiple_of(self.deep * block, block), block)],
            send_sem=self.send.at[micro],
            recv_sem=self.recv.at[index],
            device_id=device(self.across, self.up, self.deep // 2, 2 * micro + self.core),
            device_id_type=MESH,
        )

    def near(self, micro):
        block = self.src.shape[1]
        return pltpu.make_async_copy(
            self.src.at[micro],
            self.dst.at[pl.ds(pl.multiple_of(self.deep * block, block), block)],
            self.local,
        )

    def start(self):
        for micro in range(2):
            @pl.when(self.stays(micro))
            def _():
                self.near(micro).start()

            @pl.when(jnp.logical_not(self.stays(micro)))
            def _():
                self.far(micro, self.deep % 2).start()

    def wait(self):
        for block in range(2):
            here = (self.deep % 2 == self.core) & (2 * self.core + block == self.deep)

            @pl.when(here)
            def _():
                self.near(block).wait()

            @pl.when(jnp.logical_not(here))
            def _():
                self.far(block, block).wait_recv()

    def finish(self):
        for micro in range(2):
            @pl.when(jnp.logical_not(self.stays(micro)))
            def _():
                self.far(micro, self.deep % 2).wait_send()


class SendBack:
    def __init__(self, src, dst, send, recv, local):
        self.src, self.dst = src, dst
        self.send, self.recv, self.local = send, recv, local
        self.across, self.up, self.core, self.deep = position()

    def stays(self, block):
        return (self.deep % 2 == self.core) & (2 * self.core + block == self.deep)

    def far(self, block, index):
        count = self.dst.shape[1]
        return pltpu.make_async_remote_copy(
            src_ref=self.src.at[pl.ds(block * count, count)],
            dst_ref=self.dst.at[self.deep // 2],
            send_sem=self.send.at[block],
            recv_sem=self.recv.at[index],
            device_id=device(self.across, self.up, self.deep % 2, 2 * self.core + block),
            device_id_type=MESH,
        )

    def near(self, block):
        count = self.dst.shape[1]
        return pltpu.make_async_copy(
            self.src.at[pl.ds(block * count, count)], self.dst.at[self.deep // 2], self.local
        )

    def start(self):
        for block in range(2):
            @pl.when(self.stays(block))
            def _():
                self.near(block).start()

            @pl.when(jnp.logical_not(self.stays(block)))
            def _():
                self.far(block, self.deep // 2).start()

    def finish(self):
        for micro in range(2):
            here = (self.deep // 2 == self.core) & (2 * micro + self.core == self.deep)

            @pl.when(here)
            def _():
                self.near(micro).wait()

            @pl.when(jnp.logical_not(here))
            def _():
                self.far(micro, micro).wait_recv()
        for block in range(2):
            @pl.when(jnp.logical_not(self.stays(block)))
            def _():
                self.far(block, self.deep // 2).wait_send()


class Spread:
    def __init__(self, own, every, send, recv, local):
        self.own, self.every = own, every
        self.send, self.recv, self.local = send, recv, local
        self.across, self.up, self.core, self.deep = position()
        self.count = own.shape[0]
        self.right = device(1 - self.across, self.up, self.core, self.deep)
        self.above = device(self.across, 1 - self.up, self.core, self.deep)
        self.twin = device(self.across, self.up, 1 - self.core, self.deep)

    def item(self, flip_x, flip_y, step, half=None):
        column = (2 if flip_y else 0) + (1 if flip_x else 0)
        slot = (column * 4 + (self.deep + step) % 4) * 2 + self.core
        start = slot * self.count
        if half is None:
            return self.every.at[pl.ds(pl.multiple_of(start, self.count), self.count)]
        part = self.count // 2
        return self.every.at[pl.ds(pl.multiple_of(start + half * part, part), part)]

    def copy(self, index, src, dst, target):
        return pltpu.make_async_remote_copy(
            src_ref=src,
            dst_ref=dst,
            send_sem=self.send.at[index],
            recv_sem=self.recv.at[index],
            device_id=target,
            device_id_type=MESH,
        )

    def hop(self, step, up):
        there = (step - 1) % 4 if up else (step + 1) % 4
        place = self.item(False, False, step)
        target = device(self.across, self.up, self.core, (self.deep + (1 if up else 3)) % 4)
        return pltpu.make_async_remote_copy(
            src_ref=self.own if step == 0 else place,
            dst_ref=place,
            send_sem=self.send.at[(35 if up else 39) + step],
            recv_sem=self.recv.at[there - 1],
            device_id=target,
            device_id_type=MESH,
        )

    def arrived(self, step):
        place = self.item(False, False, step)
        return pltpu.make_async_remote_copy(
            src_ref=place,
            dst_ref=place,
            send_sem=self.send.at[35],
            recv_sem=self.recv.at[step - 1],
            device_id=self.twin,
            device_id_type=MESH,
        )

    def column(self, step, index, target):
        src = self.own if step == 0 else self.item(False, False, step)
        dst = self.item(index == 3, index == 7, step)
        return self.copy(index + step, src, dst, target)

    def passed(self, step, index, flip_x, flip_y, target, half=None):
        src = self.item(flip_x, flip_y, step, half)
        dst = src if half is None else self.item(True, True, step, half)
        return self.copy(index + step, src, dst, target)

    def store(self):
        return pltpu.make_async_copy(self.own, self.item(False, False, 0), self.local)

    def fan(self, step):
        self.column(step, 3, self.right).start()
        self.column(step, 7, self.above).start()
        self.column(step, 19, self.twin).start()

    def begin(self):
        self.fan(0)
        pl.when(self.deep < 3)(lambda: self.hop(0, True).start())
        pl.when(self.deep > 0)(lambda: self.hop(0, False).start())
        self.store().start()

    def relay(self, step, up):
        self.arrived(step).wait_recv()
        if up and step > 1:
            pl.when(self.deep < 3)(lambda: self.hop(step, True).start())
        if not up and step < 3:
            pl.when(self.deep > 0)(lambda: self.hop(step, False).start())
        self.fan(step)

    def near(self):
        pl.when(self.deep > 0)(lambda: self.relay(3, True))
        pl.when(self.deep < 3)(lambda: self.relay(1, False))

    def middle(self):
        pl.when(self.deep > 1)(lambda: self.relay(2, True))
        pl.when(self.deep < 2)(lambda: self.relay(2, False))

    def far(self):
        pl.when(self.deep == 3)(lambda: self.relay(1, True))
        pl.when(self.deep == 0)(lambda: self.relay(3, False))

    def corner(self, step):
        self.column(step, 3, self.right).wait_recv()
        self.passed(step, 15, True, False, self.above, 0).start()
        self.passed(step, 23, True, False, self.twin).start()
        self.column(step, 7, self.above).wait_recv()
        self.passed(step, 11, False, True, self.right, 1).start()
        self.passed(step, 27, False, True, self.twin).start()

    def last(self, step):
        self.passed(step, 15, True, False, self.above, 0).wait_recv()
        self.passed(step, 11, False, True, self.right, 1).wait_recv()
        self.passed(step, 31, True, True, self.twin).start()

    def finish(self):
        self.store().wait()
        for step in range(4):
            arrivals = [
                self.column(step, 19, self.twin),
                self.passed(step, 23, True, False, self.twin),
                self.passed(step, 27, False, True, self.twin),
                self.passed(step, 31, True, True, self.twin),
            ]
            for copy in arrivals:
                copy.wait_recv()
                copy.wait_send()
            self.column(step, 3, self.right).wait_send()
            self.column(step, 7, self.above).wait_send()
            self.passed(step, 15, True, False, self.above, 0).wait_send()
            self.passed(step, 11, False, True, self.right, 1).wait_send()
        pl.when(self.deep < 3)(lambda: self.hop(0, True).wait_send())
        pl.when((self.deep < 3) & (self.deep > 0))(lambda: self.hop(3, True).wait_send())
        pl.when(self.deep == 2)(lambda: self.hop(2, True).wait_send())
        pl.when(self.deep > 0)(lambda: self.hop(0, False).wait_send())
        pl.when((self.deep < 3) & (self.deep > 0))(lambda: self.hop(1, False).wait_send())
        pl.when(self.deep == 1)(lambda: self.hop(2, False).wait_send())


def layer_kernel(
    vec_half_ref, ids_ref, fcb_ref, x_hbm, m_hbm, g_hbm,
    qkv_hbm, so_hbm, cq_hbm, ckv_hbm, co_hbm, in_hbm, out_hbm,
    y_out, dx_out, dm_out, grads_ref, every_n, every_g,
    x_ref, m_ref, g_ref, vec_ref, ids_got, ids_all, id_rows,
    n1_ref, q1_ref, k1_ref, v1_ref, p1_ref, o1_ref, h1_ref, n2_ref, q2_ref, k2_ref, v2_ref, p2_ref,
    o2_ref, h2_ref, n3_ref, y_ref, dx_ref, dm_ref,
    qkv_w, so_w, cq_w, ckv_w, co_w, in_w, out_w, chip_n, acc_y, acc_n, part, got, go_ref,
    dkv2, dkv2_got, dkv1, dkv1_got, dq1, dq2, e1, e2, n2_half, o1_half, o2_half, dh_ref, sums, sums_got,
    stage, send, recv, local, tiles, stores, move_send, move_recv, move_local,
    spread_send, spread_recv, spread_local,
):
    across, up, core, deep = position()
    column = [device(across, up, 1 - core, deep)]
    for turn in (1, 2, 3):
        for other in (0, 1):
            column.append(device(across, up, other, (deep + turn) % 4))
    greet(column + [device(1 - across, up, core, deep), device(across, 1 - up, core, deep)])
    partner = Partner(send, recv)
    bf16, f32 = jnp.bfloat16, jnp.float32
    count, width = q1_ref.shape
    units = in_w.shape[2]
    half = width // 2
    mine = pl.ds(pl.multiple_of(core * count, count), count)
    theirs = pl.ds(pl.multiple_of((1 - core) * count, count), count)
    my_half = pl.ds(pl.multiple_of(core * half, half), half)
    their_half = pl.ds(pl.multiple_of((1 - core) * half, half), half)

    def bring(index, src, dst):
        return Bring(src, dst, move_send.at[index], move_recv.at[index], move_local.at[index])

    def give(index, src, dst):
        return SendBack(src, dst, move_send.at[index], move_recv.at[index], move_local.at[index])

    bring_x = bring(0, x_hbm, x_ref)
    bring_x.start()
    sent_ids = partner.push(ids_ref, ids_got)
    sent_vec = partner.push(vec_half_ref, vec_ref.at[:, my_half])
    vec_ref[:, my_half] = vec_half_ref[...]
    qkv = Weights(partner, qkv_hbm, qkv_w, local.at[0])
    bring_x.wait()
    sent_x = partner.push(x_ref.at[mine], x_ref.at[mine])
    bring_g, bring_m = bring(1, g_hbm, g_ref), bring(2, m_hbm, m_ref)
    bring_m.start()
    bring_g.start()
    so = Weights(partner, so_hbm, so_w, local.at[2])
    ckv = Weights(partner, ckv_hbm, ckv_w, local.at[1])
    cq = Weights(partner, cq_hbm, cq_w, local.at[3])
    co = Weights(partner, co_hbm, co_w, local.at[4])

    sent_ids.wait_recv()
    ids = jnp.where(deep % 2 == core, ids_ref[...], ids_got[...])
    ids_all[...] = ids
    micro = deep // 2
    token_row = jnp.where(micro == 0, ids[0:1], ids[1:2])
    source_row = jnp.where(micro == 0, ids[2:3], ids[3:4])
    id_rows[...] = jnp.broadcast_to(token_row, (128, token_row.shape[1])).T
    query_ids = id_rows[mine, :][:, :1]
    sent_vec.wait_recv()
    vectors = vec_ref[...]
    sent_x.wait_recv()
    n1_ref[...] = normed(x_ref[...].astype(f32), vectors, 0)
    place = core * count + lax.broadcasted_iota(jnp.int32, (count, 1), 0)
    keys = lax.broadcasted_iota(jnp.int32, (1, token_row.shape[1]), 1)
    allowed = (place >= keys) & (query_ids == token_row)
    allowed = jnp.concatenate([allowed, allowed], axis=0)
    w = qkv.get()
    q1_ref[...] = (mul(n1_ref[mine, :], w[:, :width]) + vectors[0:1]).astype(bf16)
    k1_ref[...] = mul(n1_ref[...], w[:, width : 2 * width]).astype(bf16)
    v1_ref[...] = (mul(n1_ref[...], w[:, 2 * width :]) + vectors[1:2]).astype(bf16)
    attend(q1_ref, k1_ref, v1_ref, p1_ref, o1_ref, allowed)
    bring_m.wait()
    sent_m = partner.push(m_ref.at[mine], m_ref.at[mine])
    bring_g.wait()
    sent_g = partner.push(g_ref.at[mine], g_ref.at[mine])
    spread_g = Spread(g_ref.at[mine], every_g, spread_send.at[0], spread_recv.at[0], spread_local.at[0])
    spread_g.begin()
    w = so.get()
    h1_ref[...] = x_ref[mine, :].astype(f32) + mul(o1_ref[...], w[...]) + vectors[2:3]
    n2_ref[...] = normed(h1_ref[...], vectors, 1)
    w = ckv.get()
    sent_m.wait_recv()
    k2_ref[...] = mul(m_ref[...], w[:, :width]).astype(bf16)
    v2_ref[...] = (mul(m_ref[...], w[:, width:]) + vectors[4:5]).astype(bf16)
    w = cq.get()
    q2_ref[...] = (mul(n2_ref[...], w[...]) + vectors[3:4]).astype(bf16)
    spread_g.near()
    allowed = query_ids == source_row
    allowed = jnp.concatenate([allowed, allowed], axis=0)
    attend(q2_ref, k2_ref, v2_ref, p2_ref, o2_ref, allowed)
    w = co.get()
    h2_ref[...] = h1_ref[...] + mul(o2_ref[...], w[...]) + vectors[5:6]
    n3_ref[...] = normed(h2_ref[...], vectors, 2)
    rows_sent = partner.push(n3_ref, chip_n.at[mine])
    chip_n[mine, :] = n3_ref[...]
    spread_g.middle()
    spread_n = Spread(n3_ref, every_n, spread_send.at[1], spread_recv.at[1], spread_local.at[1])
    spread_n.begin()

    def tile_copies(index):
        slot = index % 2
        where = pl.ds(index * units, units)
        return (
            pltpu.make_async_copy(in_hbm.at[:, where], in_w.at[slot], tiles.at[slot, 0]),
            pltpu.make_async_copy(out_hbm.at[where], out_w.at[slot], tiles.at[slot, 1]),
        )

    steps = in_hbm.shape[1] // units
    for copy in tile_copies(0):
        copy.start()
    halves = [
        partner.push(n2_ref.at[:, their_half], n2_half.at[mine]),
        partner.push(o1_ref.at[:, their_half], o1_half.at[mine]),
        partner.push(o2_ref.at[:, their_half], o2_half.at[mine]),
    ]
    n2_half[mine, :] = n2_ref[:, my_half]
    o1_half[mine, :] = o1_ref[:, my_half]
    o2_half[mine, :] = o2_ref[:, my_half]
    sent_g.wait_recv()
    rows_sent.wait_recv()
    for index in range(steps):
        if index + 1 < steps:
            for copy in tile_copies(index + 1):
                copy.start()
        for copy in tile_copies(index):
            copy.wait()
        slot = index % 2
        inner = mul(chip_n[...], in_w[slot]) + fcb_ref[:, index * units : (index + 1) * units]
        active, slope = gelu_pair(inner, refine=True)
        back = (mul_nt(g_ref[...], out_w[slot]) * slope).astype(bf16)
        if index == 0:
            acc_y[...] = mul(active.astype(bf16), out_w[slot])
            acc_n[...] = mul_nt(back, in_w[slot])
        else:
            acc_y[...] += mul(active.astype(bf16), out_w[slot])
            acc_n[...] += mul_nt(back, in_w[slot])
        if index == 2 * steps // 8:
            spread_g.far()
            spread_g.corner(0)
        if index == 6 * steps // 8:
            spread_n.near()
            spread_g.corner(2)
    part[0] = acc_n[theirs, :].astype(bf16)
    sent_n = partner.push(part.at[0], got.at[0])
    part[1] = acc_y[theirs, :].astype(bf16)
    sent_y = partner.push(part.at[1], got.at[1])
    spread_g.corner(1)
    spread_g.corner(3)
    sent_n.wait_recv()
    grad = acc_n[mine, :] + got[0].astype(f32)
    grad = norm_back(grad, h2_ref[...], vectors[9:10], sums, 2) + g_ref[mine, :].astype(f32)
    dh_ref[...] = grad
    e2[mine, :] = grad.astype(bf16)
    sent_e2 = partner.push(e2.at[mine], e2.at[mine])
    sent_y.wait_recv()
    y = h2_ref[...] + (acc_y[mine, :] + got[1].astype(f32) + vectors[6:7])
    y_ref[...] = y.astype(bf16)
    give_y = give(3, y_ref, y_out)
    spread_n.middle()
    go_ref[...] = mul_nt(e2[mine, :], co_w[...]).astype(bf16)
    attend_back(q2_ref, k2_ref, v2_ref, p2_ref, go_ref, dq2.at[mine], dkv2.at[:, :width], dkv2.at[:, width:])
    sent_dkv2 = partner.push(dkv2, dkv2_got)
    sent_dq2 = partner.push(dq2.at[mine], dq2.at[mine])
    spread_g.last(0)
    spread_n.far()
    spread_n.corner(0)
    grad = mul_nt(dq2[mine, :], cq_w[...])
    grad = norm_back(grad, h1_ref[...], vectors[8:9], sums, 1) + dh_ref[...]
    dh_ref[...] = grad
    e1[mine, :] = grad.astype(bf16)
    sent_e1 = partner.push(e1.at[mine], e1.at[mine])
    go_ref[...] = mul_nt(e1[mine, :], so_w[...]).astype(bf16)
    attend_back(q1_ref, k1_ref, v1_ref, p1_ref, go_ref, dq1.at[mine], dkv1.at[:, :width], dkv1.at[:, width:])
    sent_dkv1 = partner.push(dkv1, dkv1_got)
    sent_dq1 = partner.push(dq1.at[mine], dq1.at[mine])
    spread_g.last(1)
    spread_g.last(3)
    spread_n.corner(2)
    give_y.start()

    sent_dkv2.wait_recv()
    dkv2_got[...] = (dkv2[...].astype(f32) + dkv2_got[...].astype(f32)).astype(bf16)
    dm_ref[...] = mul_nt(dkv2_got[mine, :], ckv_w[...]).astype(bf16)
    give_dm = give(4, dm_ref, dm_out)
    give_dm.start()

    sent = []

    def weight_grad_of(left, right, column):
        index = len(sent)
        slot = index % 2
        if index >= 2:
            sent[index - 2].wait()
        stage[slot] = mul_tn(left, right).astype(bf16)
        copy = pltpu.make_async_copy(
            stage.at[slot], grads_ref.at[:, pl.ds(column, width)], stores.at[index]
        )
        copy.start()
        sent.append(copy)

    for copy in halves:
        copy.wait_recv()
    sent_e2.wait_recv()
    weight_grad_of(o2_half[...], e2[...], 7 * width)
    weight_grad_of(m_ref[:, my_half], dkv2_got[:, :width], 5 * width)
    weight_grad_of(m_ref[:, my_half], dkv2_got[:, width:], 6 * width)
    spread_g.last(2)
    spread_n.corner(1)
    spread_n.corner(3)
    sent_dq2.wait_recv()
    weight_grad_of(n2_half[...], dq2[...], 4 * width)
    sent_e1.wait_recv()
    weight_grad_of(o1_half[...], e1[...], 3 * width)
    sent_dkv1.wait_recv()
    dkv1_got[...] = (dkv1[...].astype(f32) + dkv1_got[...].astype(f32)).astype(bf16)
    grad = mul_nt(dq1[mine, :], qkv_w[:, :width])
    grad += mul_nt(dkv1_got[mine, :width], qkv_w[:, width : 2 * width])
    grad += mul_nt(dkv1_got[mine, width:], qkv_w[:, 2 * width :])
    dx = norm_back(grad, x_ref[mine, :].astype(f32), vectors[7:8], sums, 0) + dh_ref[...]
    dx_ref[...] = dx.astype(bf16)
    give_dx = give(5, dx_ref, dx_out)
    give_dx.start()
    sent_sums = partner.push(sums, sums_got)
    weight_grad_of(n1_ref[:, my_half], dkv1_got[:, :width], width)
    weight_grad_of(n1_ref[:, my_half], dkv1_got[:, width:], 2 * width)
    sent_dq1.wait_recv()
    weight_grad_of(n1_ref[:, my_half], dq1[...], 0)

    def columns(values):
        return jnp.sum(values.astype(f32), axis=0, keepdims=True)

    value_half = pl.ds(pl.multiple_of(width + core * half, half), half)
    sent_sums.wait_recv()
    lines = [
        columns(dq1[:, my_half]),
        columns(dkv1_got[:, value_half]),
        columns(e1[:, my_half]),
        columns(dq2[:, my_half]),
        columns(dkv2_got[:, value_half]),
        columns(e2[:, my_half]),
        columns(g_ref[:, my_half]),
        sums[0:6, my_half] + sums_got[0:6, my_half],
    ]
    lines = jnp.concatenate(lines + [jnp.zeros((128 - 13, half), f32)], axis=0).T
    sent[-1].wait()
    sent[-2].wait()
    stage[0, :, :128] = lines.astype(bf16)
    final = pltpu.make_async_copy(
        stage.at[0, :, pl.ds(0, 128)], grads_ref.at[:, pl.ds(8 * width, 128)], stores.at[8]
    )
    final.start()
    spread_n.last(0)
    spread_n.last(1)
    spread_n.last(3)
    spread_n.last(2)
    final.wait()
    partner.finish()
    for move in (bring_x, bring_m, bring_g, give_y, give_dm, give_dx):
        move.finish()
    spread_g.finish()
    spread_n.finish()


def layer(x, memory, grads, vectors, ids, fc_bias, weights, fc_in, fc_out, devices):
    block, width = x.shape[1:]
    rows = ids.shape[1]
    count = rows // 2
    units = 512
    bf16, f32 = jnp.bfloat16, jnp.float32
    half = width // 2
    vmem = pl.BlockSpec(memory_space=pltpu.VMEM)
    hbm = pl.BlockSpec(memory_space=pl.ANY)
    every = jax.ShapeDtypeStruct((devices * count, width), bf16)
    moved = jax.ShapeDtypeStruct(x.shape, bf16)
    scores = (width // (2 * HEAD), rows, rows)
    kept = [
        ((rows, width), bf16), ((count, width), bf16), ((rows, width), bf16), ((rows, width), bf16),
        (scores, bf16), ((count, width), bf16), ((count, width), f32), ((count, width), bf16),
        ((count, width), bf16), ((rows, width), bf16), ((rows, width), bf16), (scores, bf16),
        ((count, width), bf16), ((count, width), f32), ((count, width), bf16),
    ]
    return pl.pallas_call(
        layer_kernel,
        in_specs=[vmem] * 3 + [hbm] * 10,
        out_specs=[hbm] * 6,
        out_shape=[
            moved, moved, moved, jax.ShapeDtypeStruct((half, 8 * width + 128), bf16), every, every
        ],
        scratch_shapes=[
            *[pltpu.VMEM((rows, width), bf16)] * 3,
            pltpu.VMEM((16, width), f32),
            pltpu.VMEM(ids.shape, jnp.int32),
            pltpu.VMEM(ids.shape, jnp.int32),
            pltpu.VMEM((rows, 128), jnp.int32),
            *[pltpu.VMEM(*shape) for shape in kept],
            *[pltpu.VMEM((count, width), bf16)] * 3,
            *[pltpu.VMEM((2 * w.shape[0], w.shape[1]), bf16) for w in weights],
            pltpu.VMEM((2, width, units), bf16),
            pltpu.VMEM((2, units, width), bf16),
            pltpu.VMEM((rows, width), bf16),
            pltpu.VMEM((rows, width), f32),
            pltpu.VMEM((rows, width), f32),
            pltpu.VMEM((2, count, width), bf16),
            pltpu.VMEM((2, count, width), bf16),
            pltpu.VMEM((count, width), bf16),
            *[pltpu.VMEM((rows, 2 * width), bf16)] * 4,
            *[pltpu.VMEM((rows, width), bf16)] * 4,
            *[pltpu.VMEM((rows, half), bf16)] * 3,
            pltpu.VMEM((count, width), f32),
            pltpu.VMEM((8, width), f32),
            pltpu.VMEM((8, width), f32),
            pltpu.VMEM((2, half, width), bf16),
            pltpu.SemaphoreType.DMA((32,)),
            pltpu.SemaphoreType.DMA((32,)),
            pltpu.SemaphoreType.DMA((5,)),
            pltpu.SemaphoreType.DMA((2, 2)),
            pltpu.SemaphoreType.DMA((9,)),
            pltpu.SemaphoreType.DMA((6, 2)),
            pltpu.SemaphoreType.DMA((6, 2)),
            pltpu.SemaphoreType.DMA((6,)),
            pltpu.SemaphoreType.DMA((2, 43)),
            pltpu.SemaphoreType.DMA((2, 43)),
            pltpu.SemaphoreType.DMA((2,)),
        ],
        compiler_params=pltpu.CompilerParams(
            vmem_limit_bytes=60 * 2**20, collective_id=1, has_side_effects=True
        ),
        cost_estimate=pl.CostEstimate(flops=80 * 10**9, bytes_accessed=64 * 2**20, transcendentals=0),
    )(vectors, ids, fc_bias, x, memory, grads, *weights, fc_in, fc_out)


def widen_kernel(*refs):
    din_part, dout_part, sum_ref, din_ref, dout_ref = refs[:5]
    din_ref[...] = din_part[...].astype(jnp.float32)
    dout_ref[...] = dout_part[...].astype(jnp.float32)
    column = 0
    for shard_ref in refs[5:]:
        shard_ref[...] = sum_ref[:, column : column + shard_ref.shape[1]].astype(jnp.float32)
        column += shard_ref.shape[1]


def widen(din, dout, total, widths):
    width, hidden = din.shape
    steps = 8
    units, height = hidden // steps, total.shape[0] // steps
    wide = pl.BlockSpec((width // steps, hidden), lambda at: (at, 0))
    tall = pl.BlockSpec((units, width), lambda at: (at, 0))
    f32 = jnp.float32
    return pl.pallas_call(
        widen_kernel,
        grid=(steps,),
        in_specs=[wide, tall, pl.BlockSpec((height, total.shape[1]), lambda at: (at, 0))],
        out_specs=[wide, tall] + [pl.BlockSpec((height, w), lambda at: (at, 0)) for w in widths],
        out_shape=[jax.ShapeDtypeStruct(din.shape, f32), jax.ShapeDtypeStruct(dout.shape, f32)]
        + [jax.ShapeDtypeStruct((total.shape[0], w), f32) for w in widths],
        compiler_params=pltpu.CompilerParams(vmem_limit_bytes=56 * 2**20),
        cost_estimate=pl.CostEstimate(flops=0, bytes_accessed=18 * width * hidden, transcendentals=0),
    )(din, dout, total)


def fast_body(
    hidden_in,
    memory,
    segment_ids,
    memory_ids,
    out_grad,
    self_qkv,
    self_out,
    cross_query,
    cross_kv,
    cross_out,
    fc_in,
    fc_out,
    biases,
    fc_in_bias,
    norm_gains,
    norm_shifts,
):
    width = hidden_in.shape[-1]
    f32 = jnp.float32
    ids = jnp.concatenate([segment_ids[:, 0], memory_ids[:, 0]], axis=0)
    vectors = jnp.concatenate([biases, norm_gains, norm_shifts], axis=1).astype(f32).T
    vectors = jnp.pad(vectors, ((0, 16 - vectors.shape[0]), (0, 0)))
    fc_bias = fc_in_bias.astype(f32)[None]
    devices = lax.axis_size("rep") * lax.axis_size("fsdp") * lax.axis_size("seq")
    weights = (self_qkv, self_out, cross_query, cross_kv, cross_out)
    hidden_out, hidden_grad, memory_grad, grads, normed_every, grad_every = layer(
        hidden_in[:, 0], memory[:, 0], out_grad[:, 0], vectors, ids, fc_bias, weights, fc_in, fc_out, devices
    )
    din, dout, grad_fc_bias, total = ffn_grads(
        normed_every, grad_every, fc_in, fc_out, fc_bias, grads
    )
    widths = [weight.shape[1] for weight in weights]
    grad_fc_in, grad_fc_out, *shards = widen(din, dout, total, widths)
    column = total[:, 8 * width :].astype(f32)
    return (
        hidden_out[:, None],
        hidden_grad[:, None],
        memory_grad[:, None],
        *shards,
        grad_fc_in,
        grad_fc_out,
        column[:, :7],
        grad_fc_bias[0],
        column[:, 7:10],
        column[:, 10:13],
    )


def solution(mesh):
    fits = mesh.shape["rep"] == 4 and mesh.shape["fsdp"] == 2 and mesh.shape["seq"] == 4
    chosen = fast_body if fits else body
    return jax.shard_map(
        chosen,
        mesh=mesh,
        in_specs=(
            P(None, ("rep", "fsdp"), "seq", None),
            P(None, ("rep", "fsdp"), "seq", None),
            P(None, ("rep", "fsdp"), None),
            P(None, ("rep", "fsdp"), None),
            P(None, ("rep", "fsdp"), "seq", None),
            P("fsdp", None),
            P("fsdp", None),
            P("fsdp", None),
            P("fsdp", None),
            P("fsdp", None),
            P(None, "fsdp"),
            P("fsdp", None),
            P("fsdp", None),
            P("fsdp"),
            P("fsdp", None),
            P("fsdp", None),
        ),
        out_specs=(
            P(None, ("rep", "fsdp"), "seq", None),
            P(None, ("rep", "fsdp"), "seq", None),
            P(None, ("rep", "fsdp"), "seq", None),
            P("fsdp", None),
            P("fsdp", None),
            P("fsdp", None),
            P("fsdp", None),
            P("fsdp", None),
            P(None, "fsdp"),
            P("fsdp", None),
            P("fsdp", None),
            P("fsdp"),
            P("fsdp", None),
            P("fsdp", None),
        ),
        check_vma=False,
    )
```

```python
import functools
import math

import jax
import jax.numpy as jnp
from jax import lax
from jax.experimental import pallas as pl
from jax.experimental.pallas import tpu as pltpu
from jax.sharding import PartitionSpec as P

HEAD = 64


NORM_EPSILON = 1e-05
MASKED_SCORE = -1e30


def norm_forward(values, norm_gain, norm_shift):
    average = jnp.mean(values, axis=-1, keepdims=True)
    centred = values - average
    inverse = lax.rsqrt(jnp.mean(centred * centred, axis=-1, keepdims=True) + NORM_EPSILON)
    scaled = centred * inverse
    return (scaled * norm_gain + norm_shift, scaled, inverse)


def norm_backward(grad_normed, scaled, inverse, norm_gain):
    grad_scaled = grad_normed * norm_gain
    first_mean = jnp.mean(grad_scaled, axis=-1, keepdims=True)
    second_mean = jnp.mean(grad_scaled * scaled, axis=-1, keepdims=True)
    grad_values = (grad_scaled - first_mean - scaled * second_mean) * inverse
    gain_grad = jnp.sum(grad_normed * scaled, axis=(0, 1))
    shift_grad = jnp.sum(grad_normed, axis=(0, 1))
    return (grad_values, gain_grad, shift_grad)


def split_heads(values):
    return values.reshape(values.shape[:-1] + (values.shape[-1] // HEAD, HEAD))


def join_heads(values):
    return values.reshape(values.shape[:2] + (values.shape[2] * values.shape[3],))


def masked_scores(queries, key_rows, allowed):
    raw_scores = jnp.einsum(
        "mqhe,mkhe->mhqk", queries, key_rows, preferred_element_type=jnp.float32
    )
    return jnp.where(allowed[:, None], raw_scores * HEAD ** (-0.5), MASKED_SCORE)


def attend_forward(queries, key_rows, value_rows, allowed):
    scores = masked_scores(queries, key_rows, allowed)
    highest = jnp.max(scores, axis=-1, keepdims=True)
    exponent = jnp.exp(scores - highest)
    row_totals = jnp.sum(exponent, axis=-1, keepdims=True)
    weights = (exponent / row_totals).astype(jnp.bfloat16)
    joined = jnp.einsum("mhqk,mkhe->mqhe", weights, value_rows, preferred_element_type=jnp.float32)
    return (join_heads(joined).astype(jnp.bfloat16), highest + jnp.log(row_totals))


def attend_backward(queries, key_rows, value_rows, allowed, log_totals, grad_joined):
    scores = masked_scores(queries, key_rows, allowed)
    probability = jnp.exp(scores - log_totals)
    weights = probability.astype(jnp.bfloat16)
    grad_value_rows = jnp.einsum(
        "mhqk,mqhe->mkhe", weights, grad_joined, preferred_element_type=jnp.float32
    )
    grad_weights = jnp.einsum(
        "mqhe,mkhe->mhqk", grad_joined, value_rows, preferred_element_type=jnp.float32
    )
    grad_scores = probability * (
        grad_weights - jnp.sum(grad_weights * probability, axis=-1, keepdims=True)
    )
    grad_scores = grad_scores.astype(jnp.bfloat16)
    grad_queries = jnp.einsum(
        "mhqk,mkhe->mqhe", grad_scores, key_rows, preferred_element_type=jnp.float32
    ) * HEAD ** (-0.5)
    grad_key_rows = jnp.einsum(
        "mhqk,mqhe->mkhe", grad_scores, queries, preferred_element_type=jnp.float32
    ) * HEAD ** (-0.5)
    return (join_heads(grad_queries), join_heads(grad_key_rows), join_heads(grad_value_rows))


def gelu_slope(values):
    cumulative = 0.5 * (1.0 + lax.erf(values * 2.0 ** (-0.5)))
    density = jnp.exp(-0.5 * values * values) / math.sqrt(2.0 * math.pi)
    return cumulative + values * density


def feed_forward(rows, weight_in, bias_in, weight_out):
    pre_active = jnp.einsum(
        "mtd,df->mtf", rows, weight_in, preferred_element_type=jnp.float32
    ) + bias_in.astype(jnp.float32)
    active = jax.nn.gelu(pre_active, approximate=False).astype(jnp.bfloat16)
    partial_out = jnp.einsum("mtf,fd->mtd", active, weight_out, preferred_element_type=jnp.float32)
    return (pre_active, active, partial_out)


def feed_back(rows, grad_rows, pre_active, active, weight_in, weight_out):
    grad_active = jnp.einsum(
        "mtd,fd->mtf", grad_rows, weight_out, preferred_element_type=jnp.float32
    )
    grad_inner = (grad_active * gelu_slope(pre_active)).astype(jnp.bfloat16)
    grad_weight_out = jnp.einsum(
        "mtf,mtd->fd", active, grad_rows, preferred_element_type=jnp.float32
    )
    grad_weight_in = jnp.einsum("mtd,mtf->df", rows, grad_inner, preferred_element_type=jnp.float32)
    grad_bias_in = jnp.sum(grad_inner.astype(jnp.float32), axis=(0, 1))
    grad_rows_in = jnp.einsum(
        "mtf,df->mtd", grad_inner, weight_in, preferred_element_type=jnp.float32
    )
    return (grad_weight_in, grad_weight_out, grad_bias_in, grad_rows_in)


def project(rows, weight):
    return jnp.einsum("mtd,de->mte", rows, weight, preferred_element_type=jnp.float32)


def project_back(grad_rows, weight):
    return jnp.einsum("mte,de->mtd", grad_rows, weight, preferred_element_type=jnp.float32)


def weight_grad(rows, grad_rows):
    return jnp.einsum("mtd,mte->de", rows, grad_rows, preferred_element_type=jnp.float32)


def column_sums(grad_rows):
    return jnp.sum(grad_rows.astype(jnp.float32), axis=(0, 1))


def body(
    hidden_in,
    memory,
    segment_ids,
    memory_ids,
    out_grad,
    self_qkv,
    self_out,
    cross_query,
    cross_kv,
    cross_out,
    fc_in,
    fc_out,
    biases,
    fc_in_bias,
    norm_gains,
    norm_shifts,
):
    micro_count, single, tokens, model_width = hidden_in.shape
    seq_index = lax.axis_index("seq")
    zero_row = jnp.zeros((model_width,), jnp.float32)
    outputs_list = []
    grads_list = []
    memory_list = []
    attn_total = None
    mlp_total = None
    for micro in range(micro_count):
        full_qkv = lax.all_gather(self_qkv, "fsdp", axis=0, tiled=True)
        full_self_out = lax.all_gather(self_out, "fsdp", axis=0, tiled=True)
        full_query = lax.all_gather(cross_query, "fsdp", axis=0, tiled=True)
        full_memory_kv = lax.all_gather(cross_kv, "fsdp", axis=0, tiled=True)
        full_cross_out = lax.all_gather(cross_out, "fsdp", axis=0, tiled=True)
        full_biases = lax.all_gather(biases, "fsdp", axis=0, tiled=True)
        full_gains = lax.all_gather(norm_gains, "fsdp", axis=0, tiled=True)
        full_shifts = lax.all_gather(norm_shifts, "fsdp", axis=0, tiled=True)
        bias_float = full_biases.astype(jnp.float32)
        gain_float = full_gains.astype(jnp.float32)
        shift_float = full_shifts.astype(jnp.float32)
        hidden = hidden_in[micro : micro + 1][:, 0].astype(jnp.float32)
        memory_rows = memory[micro : micro + 1][:, 0]
        token_ids = segment_ids[micro : micro + 1][:, 0]
        source_ids = memory_ids[micro : micro + 1][:, 0]
        query_ids = lax.dynamic_slice_in_dim(token_ids, seq_index * tokens, tokens, 1)
        query_place = seq_index * tokens + jnp.arange(tokens, dtype=jnp.int32)
        key_place = jnp.arange(token_ids.shape[1], dtype=jnp.int32)
        self_allowed = (query_place[:, None] >= key_place[None, :])[None] & (
            query_ids[:, :, None] == token_ids[:, None, :]
        )
        cross_allowed = query_ids[:, :, None] == source_ids[:, None, :]
        normed_one, scaled_one, inverse_one = norm_forward(
            hidden, gain_float[:, 0], shift_float[:, 0]
        )
        normed_one = normed_one.astype(jnp.bfloat16)
        qkv_bias = jnp.concatenate([bias_float[:, 0], zero_row, bias_float[:, 1]])
        projected = (project(normed_one, full_qkv) + qkv_bias).astype(jnp.bfloat16)
        self_queries = split_heads(projected[..., :model_width])
        kv_all = lax.all_gather(projected[..., model_width:], "seq", axis=1, tiled=True)
        self_key_rows = split_heads(kv_all[..., :model_width])
        self_value_rows = split_heads(kv_all[..., model_width:])
        self_mixed, self_totals = attend_forward(
            self_queries, self_key_rows, self_value_rows, self_allowed
        )
        after_self = hidden + project(self_mixed, full_self_out) + bias_float[:, 2]
        normed_two, scaled_two, inverse_two = norm_forward(
            after_self, gain_float[:, 1], shift_float[:, 1]
        )
        normed_two = normed_two.astype(jnp.bfloat16)
        cross_queries = (project(normed_two, full_query) + bias_float[:, 3]).astype(jnp.bfloat16)
        memory_bias = jnp.concatenate([zero_row, bias_float[:, 4]])
        memory_kv = (project(memory_rows, full_memory_kv) + memory_bias).astype(jnp.bfloat16)
        memory_all = lax.all_gather(memory_kv, "seq", axis=1, tiled=True)
        memory_key_rows = split_heads(memory_all[..., :model_width])
        memory_value_rows = split_heads(memory_all[..., model_width:])
        cross_mixed, cross_totals = attend_forward(
            split_heads(cross_queries), memory_key_rows, memory_value_rows, cross_allowed
        )
        after_cross = after_self + project(cross_mixed, full_cross_out) + bias_float[:, 5]
        normed_three, scaled_three, inverse_three = norm_forward(
            after_cross, gain_float[:, 2], shift_float[:, 2]
        )
        normed_three = normed_three.astype(jnp.bfloat16)
        grad_out = out_grad[micro : micro + 1][:, 0]
        mlp_inputs = lax.all_gather(normed_three, "fsdp", axis=0, tiled=True)
        pre_active, active, partial_out = feed_forward(mlp_inputs, fc_in, fc_in_bias, fc_out)
        mlp_branch = lax.psum_scatter(
            partial_out.astype(jnp.bfloat16), "fsdp", scatter_dimension=0, tiled=True
        ).astype(jnp.float32)
        output = after_cross + mlp_branch + bias_float[:, 6]
        hidden_out = output.astype(jnp.bfloat16)[:, None]
        back_qkv = lax.all_gather(self_qkv, "fsdp", axis=0, tiled=True)
        back_self_out = lax.all_gather(self_out, "fsdp", axis=0, tiled=True)
        back_query = lax.all_gather(cross_query, "fsdp", axis=0, tiled=True)
        back_memory_kv = lax.all_gather(cross_kv, "fsdp", axis=0, tiled=True)
        back_cross_out = lax.all_gather(cross_out, "fsdp", axis=0, tiled=True)
        back_gains = lax.all_gather(norm_gains, "fsdp", axis=0, tiled=True)
        back_gain_float = back_gains.astype(jnp.float32)
        grad_gathered = lax.all_gather(grad_out, "fsdp", axis=0, tiled=True)
        one_grad_fc_in, one_grad_fc_out, one_grad_fc_bias, grad_partial = feed_back(
            mlp_inputs, grad_gathered, pre_active, active, fc_in, fc_out
        )
        grad_normed_three = lax.psum_scatter(
            grad_partial.astype(jnp.bfloat16), "fsdp", scatter_dimension=0, tiled=True
        ).astype(jnp.float32)
        grad_three, gain_three, shift_three = norm_backward(
            grad_normed_three, scaled_three, inverse_three, back_gain_float[:, 2]
        )
        grad_after_cross = grad_out.astype(jnp.float32) + grad_three
        grad_cross_branch = grad_after_cross.astype(jnp.bfloat16)
        grad_cross_out = weight_grad(cross_mixed, grad_cross_branch)
        grad_cross_mixed = project_back(grad_cross_branch, back_cross_out).astype(jnp.bfloat16)
        cross_grad_queries, memory_grad_keys, memory_grad_values = attend_backward(
            split_heads(cross_queries),
            memory_key_rows,
            memory_value_rows,
            cross_allowed,
            cross_totals,
            split_heads(grad_cross_mixed),
        )
        own_memory_keys = lax.psum_scatter(
            memory_grad_keys.astype(jnp.bfloat16), "seq", scatter_dimension=1, tiled=True
        )
        own_memory_values = lax.psum_scatter(
            memory_grad_values.astype(jnp.bfloat16), "seq", scatter_dimension=1, tiled=True
        )
        grad_memory_kv = jnp.concatenate([own_memory_keys, own_memory_values], axis=-1)
        grad_memory_weight = weight_grad(memory_rows, grad_memory_kv)
        memory_grad = project_back(grad_memory_kv, back_memory_kv).astype(jnp.bfloat16)[:, None]
        grad_cross_queries = cross_grad_queries.astype(jnp.bfloat16)
        grad_query_weight = weight_grad(normed_two, grad_cross_queries)
        grad_normed_two = project_back(grad_cross_queries, back_query)
        grad_two, gain_two, shift_two = norm_backward(
            grad_normed_two, scaled_two, inverse_two, back_gain_float[:, 1]
        )
        grad_after_self = grad_after_cross + grad_two
        grad_self_branch = grad_after_self.astype(jnp.bfloat16)
        grad_self_out = weight_grad(self_mixed, grad_self_branch)
        grad_self_mixed = project_back(grad_self_branch, back_self_out).astype(jnp.bfloat16)
        self_grad_queries, self_grad_keys, self_grad_values = attend_backward(
            self_queries,
            self_key_rows,
            self_value_rows,
            self_allowed,
            self_totals,
            split_heads(grad_self_mixed),
        )
        own_self_keys = lax.psum_scatter(
            self_grad_keys.astype(jnp.bfloat16), "seq", scatter_dimension=1, tiled=True
        )
        own_self_values = lax.psum_scatter(
            self_grad_values.astype(jnp.bfloat16), "seq", scatter_dimension=1, tiled=True
        )
        grad_projected = jnp.concatenate(
            [self_grad_queries.astype(jnp.bfloat16), own_self_keys, own_self_values], axis=-1
        )
        grad_qkv_weight = weight_grad(normed_one, grad_projected)
        grad_normed_one = project_back(grad_projected, back_qkv)
        grad_one, gain_one, shift_one = norm_backward(
            grad_normed_one, scaled_one, inverse_one, back_gain_float[:, 0]
        )
        hidden_grad = (grad_after_self + grad_one).astype(jnp.bfloat16)[:, None]
        grad_biases = jnp.stack(
            [
                column_sums(grad_projected[..., :model_width]),
                column_sums(grad_projected[..., 2 * model_width :]),
                column_sums(grad_self_branch),
                column_sums(grad_cross_queries),
                column_sums(grad_memory_kv[..., model_width:]),
                column_sums(grad_cross_branch),
                column_sums(grad_out),
            ],
            axis=1,
        )
        grad_gains = jnp.stack([gain_one, gain_two, gain_three], axis=1)
        grad_shifts = jnp.stack([shift_one, shift_two, shift_three], axis=1)
        attn_grads = (
            grad_qkv_weight,
            grad_self_out,
            grad_query_weight,
            grad_memory_weight,
            grad_cross_out,
            grad_biases,
            grad_gains,
            grad_shifts,
        )
        mlp_grads = (one_grad_fc_in, one_grad_fc_out, one_grad_fc_bias)
        hidden_out, hidden_grad, memory_grad, attn_grads, mlp_grads = (
            hidden_out,
            hidden_grad,
            memory_grad,
            attn_grads,
            mlp_grads,
        )
        outputs_list.append(hidden_out)
        grads_list.append(hidden_grad)
        memory_list.append(memory_grad)
        if attn_total is None:
            attn_total = attn_grads
            mlp_total = mlp_grads
        else:
            attn_total = jax.tree.map(jnp.add, attn_total, attn_grads)
            mlp_total = jax.tree.map(jnp.add, mlp_total, mlp_grads)
    grad_fc_in, grad_fc_out, grad_fc_bias = mlp_total
    (
        shard_qkv,
        shard_self_out,
        shard_query,
        shard_memory_kv,
        shard_cross_out,
        shard_biases,
        shard_gains,
        shard_shifts,
    ) = (
        lax.psum_scatter(
            attn_total[0].astype(jnp.bfloat16), "fsdp", scatter_dimension=0, tiled=True
        ).astype(jnp.float32),
        lax.psum_scatter(
            attn_total[1].astype(jnp.bfloat16), "fsdp", scatter_dimension=0, tiled=True
        ).astype(jnp.float32),
        lax.psum_scatter(
            attn_total[2].astype(jnp.bfloat16), "fsdp", scatter_dimension=0, tiled=True
        ).astype(jnp.float32),
        lax.psum_scatter(
            attn_total[3].astype(jnp.bfloat16), "fsdp", scatter_dimension=0, tiled=True
        ).astype(jnp.float32),
        lax.psum_scatter(
            attn_total[4].astype(jnp.bfloat16), "fsdp", scatter_dimension=0, tiled=True
        ).astype(jnp.float32),
        lax.psum_scatter(
            attn_total[5].astype(jnp.bfloat16), "fsdp", scatter_dimension=0, tiled=True
        ).astype(jnp.float32),
        lax.psum_scatter(
            attn_total[6].astype(jnp.bfloat16), "fsdp", scatter_dimension=0, tiled=True
        ).astype(jnp.float32),
        lax.psum_scatter(
            attn_total[7].astype(jnp.bfloat16), "fsdp", scatter_dimension=0, tiled=True
        ).astype(jnp.float32),
    )
    summed = (
        lax.psum(shard_qkv.astype(jnp.bfloat16), ("rep", "seq")).astype(jnp.float32),
        lax.psum(shard_self_out.astype(jnp.bfloat16), ("rep", "seq")).astype(jnp.float32),
        lax.psum(shard_query.astype(jnp.bfloat16), ("rep", "seq")).astype(jnp.float32),
        lax.psum(shard_memory_kv.astype(jnp.bfloat16), ("rep", "seq")).astype(jnp.float32),
        lax.psum(shard_cross_out.astype(jnp.bfloat16), ("rep", "seq")).astype(jnp.float32),
        lax.psum(grad_fc_in.astype(jnp.bfloat16), ("rep", "seq")).astype(jnp.float32),
        lax.psum(grad_fc_out.astype(jnp.bfloat16), ("rep", "seq")).astype(jnp.float32),
        lax.psum(shard_biases.astype(jnp.bfloat16), ("rep", "seq")).astype(jnp.float32),
        lax.psum(grad_fc_bias.astype(jnp.bfloat16), ("rep", "seq")).astype(jnp.float32),
        lax.psum(shard_gains.astype(jnp.bfloat16), ("rep", "seq")).astype(jnp.float32),
        lax.psum(shard_shifts.astype(jnp.bfloat16), ("rep", "seq")).astype(jnp.float32),
    )
    hidden_out = jnp.concatenate(outputs_list, axis=0)
    hidden_grad = jnp.concatenate(grads_list, axis=0)
    memory_grad = jnp.concatenate(memory_list, axis=0)
    return (
        hidden_out,
        hidden_grad,
        memory_grad,
        summed[0],
        summed[1],
        summed[2],
        summed[3],
        summed[4],
        summed[5],
        summed[6],
        summed[7],
        summed[8],
        summed[9],
        summed[10],
    )


def mul(left, right):
    return jnp.dot(left, right, preferred_element_type=jnp.float32)


def mul_nt(left, right):
    return lax.dot_general(left, right, (((1,), (1,)), ((), ())), preferred_element_type=jnp.float32)


def mul_tn(left, right):
    return lax.dot_general(left, right, (((0,), (0,)), ((), ())), preferred_element_type=jnp.float32)


MESH = pl.DeviceIdType.MESH


def gelu_pair(values, refine=False):
    depth = 1.0 + (0.3275911 * 2.0**-0.5) * jnp.abs(values)
    inv = pltpu.reciprocal(depth, approx=True)
    if refine:
        inv = inv * (2.0 - depth * inv)
    bell = jnp.exp(-0.5 * values * values)
    series = 0.7107068705 + inv * (-0.7265760135 + inv * 0.5307027145)
    series = inv * (0.127414796 + inv * (-0.142248368 + inv * series))
    tail = series * bell
    cumulative = jnp.where(values >= 0.0, 1.0 - tail, tail)
    return values * cumulative, cumulative + values * (bell * (1.0 / math.sqrt(2.0 * math.pi)))


def position():
    rep, core, deep = lax.axis_index("rep"), lax.axis_index("fsdp"), lax.axis_index("seq")
    return rep % 2, rep // 2, core, deep


def device(across, up, core, deep):
    return (up * 2 + across, core, deep)


def greet(partners):
    barrier = pltpu.get_barrier_semaphore()
    for partner in partners:
        pl.semaphore_signal(barrier, inc=1, device_id=partner, device_id_type=MESH)
    pl.semaphore_wait(barrier, len(partners))


class ChunkSum:
    def __init__(self, turned, column, width, own_ref, sum_ref, held, first, second, third, done, send, recv, local):
        across, up, core, deep = position()
        self.side, self.next = (up, across) if turned else (across, up)
        one = device(1 - across, up, core, deep)
        two = device(across, 1 - up, core, deep)
        self.one, self.two = (two, one) if turned else (one, two)
        self.deep = deep
        self.others = [(deep + step) % 4 for step in (1, 2, 3)]
        self.third_ids = [device(across, up, core, other) for other in self.others]
        self.columns = pl.ds(column, width)
        self.own, self.sum = own_ref, sum_ref
        self.held, self.first, self.second, self.third, self.done = held, first, second, third, done
        self.send, self.recv, self.local = send, recv, local
        self.quarter = pl.multiple_of(self.next * 128, 128)
        self.start_row = self.side * 256

    def remote(self, index, src, dst, target):
        return pltpu.make_async_remote_copy(
            src_ref=src,
            dst_ref=dst,
            send_sem=self.send.at[index],
            recv_sem=self.recv.at[index],
            device_id=target,
            device_id_type=MESH,
        )

    def rows(self, ref, start, count):
        return ref.at[pl.ds(pl.multiple_of(start, 32), count), self.columns]

    def copy_a(self):
        return self.remote(0, self.rows(self.own, (1 - self.side) * 256, 256), self.first, self.one)

    def load(self):
        return pltpu.make_async_copy(self.rows(self.own, self.start_row, 256), self.held, self.local.at[0])

    def copy_b(self):
        away = pl.multiple_of((1 - self.next) * 128, 128)
        return self.remote(1, self.held.at[pl.ds(away, 128)], self.second, self.two)

    def copy_c(self, turn):
        start = pl.multiple_of(self.quarter + self.others[turn] * 32, 32)
        return self.remote(2 + turn, self.held.at[pl.ds(start, 32)], self.third.at[turn], self.third_ids[turn])

    def place(self):
        return self.rows(self.sum, self.start_row + self.quarter + self.deep * 32, 32)

    def copy_d(self, turn):
        return self.remote(5 + turn, self.done, self.place(), self.third_ids[turn])

    def store(self):
        return pltpu.make_async_copy(self.done, self.place(), self.local.at[1])

    def copy_e(self):
        part = self.rows(self.sum, self.start_row + self.quarter, 128)
        return self.remote(8, part, part, self.two)

    def copy_f(self):
        part = self.rows(self.sum, self.start_row, 256)
        return self.remote(9, part, part, self.one)

    def stage(self, number):
        if number == 0:
            self.copy_a().start()
            self.load().start()
        elif number == 1:
            self.load().wait()
            self.copy_a().wait_recv()
            self.held[...] = self.held[...] + self.first[...]
            self.copy_b().start()
        elif number == 2:
            self.copy_b().wait_recv()
            self.copy_b().wait_send()
            mine = pl.ds(self.quarter, 128)
            self.held[mine] = self.held[mine] + self.second[...]
            for turn in range(3):
                self.copy_c(turn).start()
        elif number == 3:
            for turn in range(3):
                self.copy_c(turn).wait_recv()
            start = pl.multiple_of(self.quarter + self.deep * 32, 32)
            total = self.held[pl.ds(start, 32)].astype(jnp.float32)
            for turn in range(3):
                total += self.third[turn].astype(jnp.float32)
            self.done[...] = total.astype(self.done.dtype)
            self.store().start()
            for turn in range(3):
                self.copy_d(turn).start()
        elif number == 4:
            self.store().wait()
            for turn in range(3):
                self.copy_d(turn).wait_recv()
            self.copy_e().start()
        elif number == 5:
            self.copy_e().wait_recv()
            self.copy_f().start()
        elif number == 6:
            self.copy_f().wait_recv()
            self.copy_a().wait_send()
            for turn in range(3):
                self.copy_c(turn).wait_send()
                self.copy_d(turn).wait_send()
            self.copy_e().wait_send()
            self.copy_f().wait_send()


BEGIN = (0, 3, 6, 9)
AFTER = (0, 2, 3, 4, 5, 6, 8)


def ffn_kernel(
    step, tiles, plan, rows_ref, grads_ref, in_ref, out_ref, bias_ref, own_ref,
    din_ref, dout_ref, dbias_ref, sum_ref, flip, acc_in, acc_out, us, das, actives, inners, sums, *rest
):
    units = flip.shape[0]
    steps = rows_ref.shape[0] // step
    at = pl.program_id(0)
    send, recv, local = rest[-3:]
    buffers = rest[:-3]
    chunks = []
    for index, (turned, column, width, _) in enumerate(plan):
        held, first, second, third, done = buffers[5 * index : 5 * index + 5]
        chunks.append(
            ChunkSum(turned, column, width, own_ref, sum_ref, held, first, second, third, done,
                     send.at[index], recv.at[index], local.at[index])
        )

    @pl.when(at == 0)
    def _():
        across, up, core, deep = position()
        greet(
            [device(1 - across, up, core, deep), device(across, 1 - up, core, deep)]
            + [device(across, up, core, (deep + turn) % 4) for turn in (1, 2, 3)]
        )

    work = {}
    for chunk, (_, _, _, slots) in zip(chunks, plan):
        for number, slot in enumerate(slots):
            work.setdefault(min(slot, tiles), []).append((slot, number, chunk))

    def traffic(slot):
        for _, number, chunk in sorted(work.get(slot, []), key=lambda job: job[:2]):
            chunk.stage(number)

    for slot in range(tiles):
        if slot in work:
            pl.when(at == slot)(functools.partial(traffic, slot))

    flip[...] = in_ref[...].T

    def front(turn):
        part = pl.ds(turn * step, step)
        us[turn % 2] = mul_nt(flip[...], rows_ref[part, :])
        das[turn % 2] = mul_nt(out_ref[...], grads_ref[part, :])

    bias = jnp.broadcast_to(bias_ref[...], (128, units)).T[:, :1]

    def middle(turn):
        active, slope = gelu_pair(us[turn % 2] + bias)
        inner = (das[turn % 2] * slope).astype(jnp.bfloat16)
        actives[turn % 2] = active.astype(jnp.bfloat16)
        inners[turn % 2] = inner
        total = inner[:, :128].astype(jnp.float32)
        for lane in range(1, step // 128):
            total += inner[:, lane * 128 : (lane + 1) * 128].astype(jnp.float32)
        sums[...] = total if turn == 0 else sums[...] + total

    def back(turn):
        part = pl.ds(turn * step, step)
        out_part = mul(actives[turn % 2], grads_ref[part, :])
        in_part = mul(inners[turn % 2], rows_ref[part, :])
        if turn:
            out_part += acc_out[...]
            in_part += acc_in[...]
        if turn < steps - 1:
            acc_out[...] = out_part
            acc_in[...] = in_part
        else:
            dout_ref[...] = out_part.astype(jnp.bfloat16)
            din_ref[...] = in_part.astype(jnp.bfloat16).T

    front(0)
    for turn in range(steps + 1):
        if turn:
            back(turn - 1)
        if turn + 1 < steps:
            front(turn + 1)
        if turn < steps:
            middle(turn)
    dbias_ref[...] = jnp.sum(sums[...].T, axis=0, keepdims=True)
    pl.when(at == tiles - 1)(functools.partial(traffic, tiles))


def ffn_grads(rows, grads, fc_in, fc_out, bias, own):
    count, width = rows.shape
    hidden = fc_in.shape[1]
    units, step = 256, count // 4
    tiles = hidden // units
    plan = [(False, 8 * width, 128, (0, 1, 2, 3, 4, 5, 6))]
    share = 4 * width // len(BEGIN)
    for pair, begin in enumerate(BEGIN):
        slots = [begin + after for after in AFTER]
        plan.append((False, pair * share, share, slots))
        plan.append((True, (len(BEGIN) + pair) * share, share, slots))
    buffers = []
    for _, _, columns, _ in plan:
        buffers += [
            pltpu.VMEM((256, columns), jnp.bfloat16),
            pltpu.VMEM((256, columns), jnp.bfloat16),
            pltpu.VMEM((128, columns), jnp.bfloat16),
            pltpu.VMEM((3, 32, columns), jnp.bfloat16),
            pltpu.VMEM((32, columns), jnp.bfloat16),
        ]
    whole = functools.partial(pl.BlockSpec, pipeline_mode=pl.Buffered(1))
    return pl.pallas_call(
        functools.partial(ffn_kernel, step, tiles, plan),
        grid=(tiles,),
        in_specs=[
            whole((count, width), lambda at: (0, 0)),
            whole((count, width), lambda at: (0, 0)),
            pl.BlockSpec((width, units), lambda at: (0, at)),
            pl.BlockSpec((units, width), lambda at: (at, 0)),
            pl.BlockSpec((1, units), lambda at: (0, at)),
            pl.BlockSpec(memory_space=pl.ANY),
        ],
        out_specs=[
            pl.BlockSpec((width, units), lambda at: (0, at)),
            pl.BlockSpec((units, width), lambda at: (at, 0)),
            pl.BlockSpec((1, units), lambda at: (0, at)),
            pl.BlockSpec(memory_space=pl.ANY),
        ],
        out_shape=[
            jax.ShapeDtypeStruct((width, hidden), jnp.bfloat16),
            jax.ShapeDtypeStruct((hidden, width), jnp.bfloat16),
            jax.ShapeDtypeStruct((1, hidden), jnp.float32),
            jax.ShapeDtypeStruct(own.shape, own.dtype),
        ],
        scratch_shapes=[
            pltpu.VMEM((units, width), jnp.bfloat16),
            pltpu.VMEM((units, width), jnp.float32),
            pltpu.VMEM((units, width), jnp.float32),
            pltpu.VMEM((2, units, step), jnp.float32),
            pltpu.VMEM((2, units, step), jnp.float32),
            pltpu.VMEM((2, units, step), jnp.bfloat16),
            pltpu.VMEM((2, units, step), jnp.bfloat16),
            pltpu.VMEM((units, 128), jnp.float32),
            *buffers,
            pltpu.SemaphoreType.DMA((len(plan), 10)),
            pltpu.SemaphoreType.DMA((len(plan), 10)),
            pltpu.SemaphoreType.DMA((len(plan), 2)),
        ],
        compiler_params=pltpu.CompilerParams(
            vmem_limit_bytes=58 * 2**20, collective_id=0, has_side_effects=True
        ),
        cost_estimate=pl.CostEstimate(
            flops=8 * count * width * hidden,
            bytes_accessed=4 * count * width + 12 * width * hidden,
            transcendentals=count * hidden,
        ),
    )(rows, grads, fc_in, fc_out, bias, own)


def norm_parts(values):
    centred = values - jnp.mean(values, axis=-1, keepdims=True)
    inverse = lax.rsqrt(jnp.mean(centred * centred, axis=-1, keepdims=True) + NORM_EPSILON)
    return centred * inverse, inverse


def normed(values, vectors, which):
    scaled, _ = norm_parts(values)
    return (scaled * vectors[7 + which : 8 + which] + vectors[10 + which : 11 + which]).astype(jnp.bfloat16)


class Partner:
    def __init__(self, send, recv):
        across, up, core, deep = position()
        self.core = core
        self.id = device(across, up, 1 - core, deep)
        self.send, self.recv = send, recv
        self.copies = []

    def push(self, src, dst):
        index = len(self.copies)
        copy = pltpu.make_async_remote_copy(
            src_ref=src,
            dst_ref=dst,
            send_sem=self.send.at[index],
            recv_sem=self.recv.at[index],
            device_id=self.id,
            device_id_type=MESH,
        )
        copy.start()
        self.copies.append(copy)
        return copy

    def finish(self):
        for copy in self.copies:
            copy.wait_send()


class Weights:
    def __init__(self, partner, shard, whole, local):
        half = shard.shape[0]
        mine = whole.at[pl.ds(pl.multiple_of(partner.core * half, half), half)]
        self.remote = partner.push(shard, mine)
        self.near = pltpu.make_async_copy(shard, mine, local)
        self.near.start()
        self.whole = whole

    def get(self):
        self.near.wait()
        self.remote.wait_recv()
        return self.whole


def two_heads(values, lane):
    zero = jnp.zeros_like(values)
    return jnp.concatenate([jnp.where(lane, values, zero), jnp.where(lane, zero, values)], axis=0)


def lane_of():
    return lax.broadcasted_iota(jnp.int32, (1, 2 * HEAD), 1) < HEAD


def attend(q_ref, k_ref, v_ref, p_ref, o_ref, allowed):
    lane = lane_of()
    count = q_ref.shape[0]
    for pair in range(q_ref.shape[1] // (2 * HEAD)):
        columns = pl.ds(pair * 2 * HEAD, 2 * HEAD)
        scores = mul_nt(two_heads(q_ref[:, columns], lane), k_ref[:, columns])
        scores = jnp.where(allowed, scores * HEAD ** (-0.5), MASKED_SCORE)
        exponent = jnp.exp(scores - jnp.max(scores, axis=-1, keepdims=True))
        weights = (exponent / jnp.sum(exponent, axis=-1, keepdims=True)).astype(jnp.bfloat16)
        p_ref[pair] = weights
        mixed = mul(weights, v_ref[:, columns])
        o_ref[:, columns] = jnp.where(lane, mixed[:count], mixed[count:]).astype(jnp.bfloat16)


def attend_back(q_ref, k_ref, v_ref, p_ref, go_ref, dq_ref, dk_ref, dv_ref):
    lane = lane_of()
    count = q_ref.shape[0]
    for pair in range(q_ref.shape[1] // (2 * HEAD)):
        columns = pl.ds(pair * 2 * HEAD, 2 * HEAD)
        grads = two_heads(go_ref[:, columns], lane)
        weights = p_ref[pair]
        dv_ref[:, columns] = mul_tn(weights, grads).astype(jnp.bfloat16)
        grad_weights = mul_nt(grads, v_ref[:, columns])
        exact = weights.astype(jnp.float32)
        inner = jnp.sum(grad_weights * exact, axis=-1, keepdims=True)
        scores = (exact * (grad_weights - inner)).astype(jnp.bfloat16)
        queries = mul(scores, k_ref[:, columns]) * HEAD ** (-0.5)
        dq_ref[:, columns] = jnp.where(lane, queries[:count], queries[count:]).astype(jnp.bfloat16)
        keys = mul_tn(scores, two_heads(q_ref[:, columns], lane)) * HEAD ** (-0.5)
        dk_ref[:, columns] = keys.astype(jnp.bfloat16)


def norm_back(grads, values, gain, sums_ref, row):
    scaled, inverse = norm_parts(values)
    sums_ref[row : row + 1, :] = jnp.sum(grads * scaled, axis=0, keepdims=True)
    sums_ref[row + 3 : row + 4, :] = jnp.sum(grads, axis=0, keepdims=True)
    inner = grads * gain
    first = jnp.mean(inner, axis=-1, keepdims=True)
    second = jnp.mean(inner * scaled, axis=-1, keepdims=True)
    return (inner - first - scaled * second) * inverse


class Bring:
    def __init__(self, src, dst, send, recv, local):
        across, up, core, deep = position()
        self.core, self.deep = core, deep
        self.src, self.dst = src, dst
        self.send, self.recv, self.local = send, recv, local
        self.across, self.up = across, up

    def stays(self, micro):
        return (self.deep // 2 == self.core) & (2 * micro + self.core == self.deep)

    def far(self, micro, index):
        block = self.src.shape[1]
        return pltpu.make_async_remote_copy(
            src_ref=self.src.at[micro],
            dst_ref=self.dst.at[pl.ds(pl.multiple_of(self.deep * block, block), block)],
            send_sem=self.send.at[micro],
            recv_sem=self.recv.at[index],
            device_id=device(self.across, self.up, self.deep // 2, 2 * micro + self.core),
            device_id_type=MESH,
        )

    def near(self, micro):
        block = self.src.shape[1]
        return pltpu.make_async_copy(
            self.src.at[micro],
            self.dst.at[pl.ds(pl.multiple_of(self.deep * block, block), block)],
            self.local,
        )

    def start(self):
        for micro in range(2):
            @pl.when(self.stays(micro))
            def _():
                self.near(micro).start()

            @pl.when(jnp.logical_not(self.stays(micro)))
            def _():
                self.far(micro, self.deep % 2).start()

    def wait(self):
        for block in range(2):
            here = (self.deep % 2 == self.core) & (2 * self.core + block == self.deep)

            @pl.when(here)
            def _():
                self.near(block).wait()

            @pl.when(jnp.logical_not(here))
            def _():
                self.far(block, block).wait_recv()

    def finish(self):
        for micro in range(2):
            @pl.when(jnp.logical_not(self.stays(micro)))
            def _():
                self.far(micro, self.deep % 2).wait_send()


class SendBack:
    def __init__(self, src, dst, send, recv, local):
        self.src, self.dst = src, dst
        self.send, self.recv, self.local = send, recv, local
        self.across, self.up, self.core, self.deep = position()

    def stays(self, block):
        return (self.deep % 2 == self.core) & (2 * self.core + block == self.deep)

    def far(self, block, index):
        count = self.dst.shape[1]
        return pltpu.make_async_remote_copy(
            src_ref=self.src.at[pl.ds(block * count, count)],
            dst_ref=self.dst.at[self.deep // 2],
            send_sem=self.send.at[block],
            recv_sem=self.recv.at[index],
            device_id=device(self.across, self.up, self.deep % 2, 2 * self.core + block),
            device_id_type=MESH,
        )

    def near(self, block):
        count = self.dst.shape[1]
        return pltpu.make_async_copy(
            self.src.at[pl.ds(block * count, count)], self.dst.at[self.deep // 2], self.local
        )

    def start(self):
        for block in range(2):
            @pl.when(self.stays(block))
            def _():
                self.near(block).start()

            @pl.when(jnp.logical_not(self.stays(block)))
            def _():
                self.far(block, self.deep // 2).start()

    def finish(self):
        for micro in range(2):
            here = (self.deep // 2 == self.core) & (2 * micro + self.core == self.deep)

            @pl.when(here)
            def _():
                self.near(micro).wait()

            @pl.when(jnp.logical_not(here))
            def _():
                self.far(micro, micro).wait_recv()
        for block in range(2):
            @pl.when(jnp.logical_not(self.stays(block)))
            def _():
                self.far(block, self.deep // 2).wait_send()


class Spread:
    def __init__(self, own, every, send, recv, local):
        self.own, self.every = own, every
        self.send, self.recv, self.local = send, recv, local
        self.across, self.up, self.core, self.deep = position()
        self.count = own.shape[0]
        self.right = device(1 - self.across, self.up, self.core, self.deep)
        self.above = device(self.across, 1 - self.up, self.core, self.deep)
        self.twin = device(self.across, self.up, 1 - self.core, self.deep)

    def item(self, flip_x, flip_y, step, half=None):
        column = (2 if flip_y else 0) + (1 if flip_x else 0)
        slot = (column * 4 + (self.deep + step) % 4) * 2 + self.core
        start = slot * self.count
        if half is None:
            return self.every.at[pl.ds(pl.multiple_of(start, self.count), self.count)]
        part = self.count // 2
        return self.every.at[pl.ds(pl.multiple_of(start + half * part, part), part)]

    def copy(self, index, src, dst, target):
        return pltpu.make_async_remote_copy(
            src_ref=src,
            dst_ref=dst,
            send_sem=self.send.at[index],
            recv_sem=self.recv.at[index],
            device_id=target,
            device_id_type=MESH,
        )

    def hop(self, step, up):
        there = (step - 1) % 4 if up else (step + 1) % 4
        place = self.item(False, False, step)
        target = device(self.across, self.up, self.core, (self.deep + (1 if up else 3)) % 4)
        return pltpu.make_async_remote_copy(
            src_ref=self.own if step == 0 else place,
            dst_ref=place,
            send_sem=self.send.at[(35 if up else 39) + step],
            recv_sem=self.recv.at[there - 1],
            device_id=target,
            device_id_type=MESH,
        )

    def arrived(self, step):
        place = self.item(False, False, step)
        return pltpu.make_async_remote_copy(
            src_ref=place,
            dst_ref=place,
            send_sem=self.send.at[35],
            recv_sem=self.recv.at[step - 1],
            device_id=self.twin,
            device_id_type=MESH,
        )

    def column(self, step, index, target):
        src = self.own if step == 0 else self.item(False, False, step)
        dst = self.item(index == 3, index == 7, step)
        return self.copy(index + step, src, dst, target)

    def passed(self, step, index, flip_x, flip_y, target, half=None):
        src = self.item(flip_x, flip_y, step, half)
        dst = src if half is None else self.item(True, True, step, half)
        return self.copy(index + step, src, dst, target)

    def store(self):
        return pltpu.make_async_copy(self.own, self.item(False, False, 0), self.local)

    def fan(self, step):
        self.column(step, 3, self.right).start()
        self.column(step, 7, self.above).start()
        self.column(step, 19, self.twin).start()

    def begin(self):
        self.fan(0)
        pl.when(self.deep < 3)(lambda: self.hop(0, True).start())
        pl.when(self.deep > 0)(lambda: self.hop(0, False).start())
        self.store().start()

    def relay(self, step, up):
        self.arrived(step).wait_recv()
        if up and step > 1:
            pl.when(self.deep < 3)(lambda: self.hop(step, True).start())
        if not up and step < 3:
            pl.when(self.deep > 0)(lambda: self.hop(step, False).start())
        self.fan(step)

    def near(self):
        pl.when(self.deep > 0)(lambda: self.relay(3, True))
        pl.when(self.deep < 3)(lambda: self.relay(1, False))

    def middle(self):
        pl.when(self.deep > 1)(lambda: self.relay(2, True))
        pl.when(self.deep < 2)(lambda: self.relay(2, False))

    def far(self):
        pl.when(self.deep == 3)(lambda: self.relay(1, True))
        pl.when(self.deep == 0)(lambda: self.relay(3, False))

    def corner(self, step):
        self.column(step, 3, self.right).wait_recv()
        self.passed(step, 15, True, False, self.above, 0).start()
        self.passed(step, 23, True, False, self.twin).start()
        self.column(step, 7, self.above).wait_recv()
        self.passed(step, 11, False, True, self.right, 1).start()
        self.passed(step, 27, False, True, self.twin).start()

    def last(self, step):
        self.passed(step, 15, True, False, self.above, 0).wait_recv()
        self.passed(step, 11, False, True, self.right, 1).wait_recv()
        self.passed(step, 31, True, True, self.twin).start()

    def finish(self):
        self.store().wait()
        for step in range(4):
            arrivals = [
                self.column(step, 19, self.twin),
                self.passed(step, 23, True, False, self.twin),
                self.passed(step, 27, False, True, self.twin),
                self.passed(step, 31, True, True, self.twin),
            ]
            for copy in arrivals:
                copy.wait_recv()
                copy.wait_send()
            self.column(step, 3, self.right).wait_send()
            self.column(step, 7, self.above).wait_send()
            self.passed(step, 15, True, False, self.above, 0).wait_send()
            self.passed(step, 11, False, True, self.right, 1).wait_send()
        pl.when(self.deep < 3)(lambda: self.hop(0, True).wait_send())
        pl.when((self.deep < 3) & (self.deep > 0))(lambda: self.hop(3, True).wait_send())
        pl.when(self.deep == 2)(lambda: self.hop(2, True).wait_send())
        pl.when(self.deep > 0)(lambda: self.hop(0, False).wait_send())
        pl.when((self.deep < 3) & (self.deep > 0))(lambda: self.hop(1, False).wait_send())
        pl.when(self.deep == 1)(lambda: self.hop(2, False).wait_send())


def layer_kernel(
    vec_half_ref, ids_ref, fcb_ref, x_hbm, m_hbm, g_hbm,
    qkv_hbm, so_hbm, cq_hbm, ckv_hbm, co_hbm, in_hbm, out_hbm,
    y_out, dx_out, dm_out, grads_ref, every_n, every_g,
    x_ref, m_ref, g_ref, vec_ref, ids_got, ids_all, id_rows,
    n1_ref, q1_ref, k1_ref, v1_ref, p1_ref, o1_ref, h1_ref, n2_ref, q2_ref, k2_ref, v2_ref, p2_ref,
    o2_ref, h2_ref, n3_ref, y_ref, dx_ref, dm_ref,
    qkv_w, so_w, cq_w, ckv_w, co_w, in_w, out_w, chip_n, acc_y, acc_n, part, got, go_ref,
    dkv2, dkv2_got, dkv1, dkv1_got, dq1, dq2, e1, e2, n2_half, o1_half, o2_half, dh_ref, sums, sums_got,
    stage, send, recv, local, tiles, stores, move_send, move_recv, move_local,
    spread_send, spread_recv, spread_local,
):
    across, up, core, deep = position()
    column = [device(across, up, 1 - core, deep)]
    for turn in (1, 2, 3):
        for other in (0, 1):
            column.append(device(across, up, other, (deep + turn) % 4))
    greet(column + [device(1 - across, up, core, deep), device(across, 1 - up, core, deep)])
    partner = Partner(send, recv)
    bf16, f32 = jnp.bfloat16, jnp.float32
    count, width = q1_ref.shape
    units = in_w.shape[2]
    half = width // 2
    mine = pl.ds(pl.multiple_of(core * count, count), count)
    theirs = pl.ds(pl.multiple_of((1 - core) * count, count), count)
    my_half = pl.ds(pl.multiple_of(core * half, half), half)
    their_half = pl.ds(pl.multiple_of((1 - core) * half, half), half)

    def bring(index, src, dst):
        return Bring(src, dst, move_send.at[index], move_recv.at[index], move_local.at[index])

    def give(index, src, dst):
        return SendBack(src, dst, move_send.at[index], move_recv.at[index], move_local.at[index])

    bring_x = bring(0, x_hbm, x_ref)
    bring_x.start()
    sent_ids = partner.push(ids_ref, ids_got)
    sent_vec = partner.push(vec_half_ref, vec_ref.at[:, my_half])
    vec_ref[:, my_half] = vec_half_ref[...]
    qkv = Weights(partner, qkv_hbm, qkv_w, local.at[0])
    bring_x.wait()
    sent_x = partner.push(x_ref.at[mine], x_ref.at[mine])
    bring_g, bring_m = bring(1, g_hbm, g_ref), bring(2, m_hbm, m_ref)
    bring_m.start()
    bring_g.start()
    so = Weights(partner, so_hbm, so_w, local.at[2])
    ckv = Weights(partner, ckv_hbm, ckv_w, local.at[1])
    cq = Weights(partner, cq_hbm, cq_w, local.at[3])
    co = Weights(partner, co_hbm, co_w, local.at[4])

    sent_ids.wait_recv()
    ids = jnp.where(deep % 2 == core, ids_ref[...], ids_got[...])
    ids_all[...] = ids
    micro = deep // 2
    token_row = jnp.where(micro == 0, ids[0:1], ids[1:2])
    source_row = jnp.where(micro == 0, ids[2:3], ids[3:4])
    id_rows[...] = jnp.broadcast_to(token_row, (128, token_row.shape[1])).T
    query_ids = id_rows[mine, :][:, :1]
    sent_vec.wait_recv()
    vectors = vec_ref[...]
    sent_x.wait_recv()
    n1_ref[...] = normed(x_ref[...].astype(f32), vectors, 0)
    place = core * count + lax.broadcasted_iota(jnp.int32, (count, 1), 0)
    keys = lax.broadcasted_iota(jnp.int32, (1, token_row.shape[1]), 1)
    allowed = (place >= keys) & (query_ids == token_row)
    allowed = jnp.concatenate([allowed, allowed], axis=0)
    w = qkv.get()
    q1_ref[...] = (mul(n1_ref[mine, :], w[:, :width]) + vectors[0:1]).astype(bf16)
    k1_ref[...] = mul(n1_ref[...], w[:, width : 2 * width]).astype(bf16)
    v1_ref[...] = (mul(n1_ref[...], w[:, 2 * width :]) + vectors[1:2]).astype(bf16)
    attend(q1_ref, k1_ref, v1_ref, p1_ref, o1_ref, allowed)
    bring_m.wait()
    sent_m = partner.push(m_ref.at[mine], m_ref.at[mine])
    bring_g.wait()
    sent_g = partner.push(g_ref.at[mine], g_ref.at[mine])
    spread_g = Spread(g_ref.at[mine], every_g, spread_send.at[0], spread_recv.at[0], spread_local.at[0])
    spread_g.begin()
    w = so.get()
    h1_ref[...] = x_ref[mine, :].astype(f32) + mul(o1_ref[...], w[...]) + vectors[2:3]
    n2_ref[...] = normed(h1_ref[...], vectors, 1)
    w = ckv.get()
    sent_m.wait_recv()
    k2_ref[...] = mul(m_ref[...], w[:, :width]).astype(bf16)
    v2_ref[...] = (mul(m_ref[...], w[:, width:]) + vectors[4:5]).astype(bf16)
    w = cq.get()
    q2_ref[...] = (mul(n2_ref[...], w[...]) + vectors[3:4]).astype(bf16)
    spread_g.near()
    allowed = query_ids == source_row
    allowed = jnp.concatenate([allowed, allowed], axis=0)
    attend(q2_ref, k2_ref, v2_ref, p2_ref, o2_ref, allowed)
    w = co.get()
    h2_ref[...] = h1_ref[...] + mul(o2_ref[...], w[...]) + vectors[5:6]
    n3_ref[...] = normed(h2_ref[...], vectors, 2)
    rows_sent = partner.push(n3_ref, chip_n.at[mine])
    chip_n[mine, :] = n3_ref[...]
    spread_g.middle()
    spread_n = Spread(n3_ref, every_n, spread_send.at[1], spread_recv.at[1], spread_local.at[1])
    spread_n.begin()

    def tile_copies(index):
        slot = index % 2
        where = pl.ds(index * units, units)
        return (
            pltpu.make_async_copy(in_hbm.at[:, where], in_w.at[slot], tiles.at[slot, 0]),
            pltpu.make_async_copy(out_hbm.at[where], out_w.at[slot], tiles.at[slot, 1]),
        )

    steps = in_hbm.shape[1] // units
    for copy in tile_copies(0):
        copy.start()
    halves = [
        partner.push(n2_ref.at[:, their_half], n2_half.at[mine]),
        partner.push(o1_ref.at[:, their_half], o1_half.at[mine]),
        partner.push(o2_ref.at[:, their_half], o2_half.at[mine]),
    ]
    n2_half[mine, :] = n2_ref[:, my_half]
    o1_half[mine, :] = o1_ref[:, my_half]
    o2_half[mine, :] = o2_ref[:, my_half]
    sent_g.wait_recv()
    rows_sent.wait_recv()
    for index in range(steps):
        if index + 1 < steps:
            for copy in tile_copies(index + 1):
                copy.start()
        for copy in tile_copies(index):
            copy.wait()
        slot = index % 2
        inner = mul(chip_n[...], in_w[slot]) + fcb_ref[:, index * units : (index + 1) * units]
        active, slope = gelu_pair(inner, refine=True)
        back = (mul_nt(g_ref[...], out_w[slot]) * slope).astype(bf16)
        if index == 0:
            acc_y[...] = mul(active.astype(bf16), out_w[slot])
            acc_n[...] = mul_nt(back, in_w[slot])
        else:
            acc_y[...] += mul(active.astype(bf16), out_w[slot])
            acc_n[...] += mul_nt(back, in_w[slot])
        if index == 2 * steps // 8:
            spread_g.far()
            spread_g.corner(0)
        if index == 4 * steps // 8:
            spread_n.near()
        if index == 6 * steps // 8:
            spread_g.corner(1)
            spread_g.corner(3)
    part[0] = acc_n[theirs, :].astype(bf16)
    sent_n = partner.push(part.at[0], got.at[0])
    part[1] = acc_y[theirs, :].astype(bf16)
    sent_y = partner.push(part.at[1], got.at[1])
    spread_n.middle()
    spread_g.corner(2)
    sent_n.wait_recv()
    grad = acc_n[mine, :] + got[0].astype(f32)
    grad = norm_back(grad, h2_ref[...], vectors[9:10], sums, 2) + g_ref[mine, :].astype(f32)
    dh_ref[...] = grad
    e2[mine, :] = grad.astype(bf16)
    sent_e2 = partner.push(e2.at[mine], e2.at[mine])
    sent_y.wait_recv()
    y = h2_ref[...] + (acc_y[mine, :] + got[1].astype(f32) + vectors[6:7])
    y_ref[...] = y.astype(bf16)
    give_y = give(3, y_ref, y_out)
    spread_n.far()
    go_ref[...] = mul_nt(e2[mine, :], co_w[...]).astype(bf16)
    attend_back(q2_ref, k2_ref, v2_ref, p2_ref, go_ref, dq2.at[mine], dkv2.at[:, :width], dkv2.at[:, width:])
    sent_dkv2 = partner.push(dkv2, dkv2_got)
    sent_dq2 = partner.push(dq2.at[mine], dq2.at[mine])
    spread_g.last(0)
    spread_n.corner(0)
    grad = mul_nt(dq2[mine, :], cq_w[...])
    grad = norm_back(grad, h1_ref[...], vectors[8:9], sums, 1) + dh_ref[...]
    dh_ref[...] = grad
    e1[mine, :] = grad.astype(bf16)
    sent_e1 = partner.push(e1.at[mine], e1.at[mine])
    go_ref[...] = mul_nt(e1[mine, :], so_w[...]).astype(bf16)
    attend_back(q1_ref, k1_ref, v1_ref, p1_ref, go_ref, dq1.at[mine], dkv1.at[:, :width], dkv1.at[:, width:])
    sent_dkv1 = partner.push(dkv1, dkv1_got)
    sent_dq1 = partner.push(dq1.at[mine], dq1.at[mine])
    spread_g.last(1)
    spread_g.last(3)
    spread_n.corner(1)
    spread_n.corner(3)
    give_y.start()

    sent_dkv2.wait_recv()
    dkv2_got[...] = (dkv2[...].astype(f32) + dkv2_got[...].astype(f32)).astype(bf16)
    dm_ref[...] = mul_nt(dkv2_got[mine, :], ckv_w[...]).astype(bf16)
    give_dm = give(4, dm_ref, dm_out)
    give_dm.start()

    sent = []

    def weight_grad_of(left, right, column):
        index = len(sent)
        slot = index % 2
        if index >= 2:
            sent[index - 2].wait()
        stage[slot] = mul_tn(left, right).astype(bf16)
        copy = pltpu.make_async_copy(
            stage.at[slot], grads_ref.at[:, pl.ds(column, width)], stores.at[index]
        )
        copy.start()
        sent.append(copy)

    for copy in halves:
        copy.wait_recv()
    sent_e2.wait_recv()
    weight_grad_of(o2_half[...], e2[...], 7 * width)
    weight_grad_of(m_ref[:, my_half], dkv2_got[:, :width], 5 * width)
    weight_grad_of(m_ref[:, my_half], dkv2_got[:, width:], 6 * width)
    spread_g.last(2)
    spread_n.corner(2)
    spread_n.last(0)
    sent_dq2.wait_recv()
    weight_grad_of(n2_half[...], dq2[...], 4 * width)
    sent_e1.wait_recv()
    weight_grad_of(o1_half[...], e1[...], 3 * width)
    sent_dkv1.wait_recv()
    dkv1_got[...] = (dkv1[...].astype(f32) + dkv1_got[...].astype(f32)).astype(bf16)
    grad = mul_nt(dq1[mine, :], qkv_w[:, :width])
    grad += mul_nt(dkv1_got[mine, :width], qkv_w[:, width : 2 * width])
    grad += mul_nt(dkv1_got[mine, width:], qkv_w[:, 2 * width :])
    dx = norm_back(grad, x_ref[mine, :].astype(f32), vectors[7:8], sums, 0) + dh_ref[...]
    dx_ref[...] = dx.astype(bf16)
    give_dx = give(5, dx_ref, dx_out)
    give_dx.start()
    sent_sums = partner.push(sums, sums_got)
    weight_grad_of(n1_ref[:, my_half], dkv1_got[:, :width], width)
    weight_grad_of(n1_ref[:, my_half], dkv1_got[:, width:], 2 * width)
    sent_dq1.wait_recv()
    weight_grad_of(n1_ref[:, my_half], dq1[...], 0)

    def columns(values):
        return jnp.sum(values.astype(f32), axis=0, keepdims=True)

    value_half = pl.ds(pl.multiple_of(width + core * half, half), half)
    sent_sums.wait_recv()
    lines = [
        columns(dq1[:, my_half]),
        columns(dkv1_got[:, value_half]),
        columns(e1[:, my_half]),
        columns(dq2[:, my_half]),
        columns(dkv2_got[:, value_half]),
        columns(e2[:, my_half]),
        columns(g_ref[:, my_half]),
        sums[0:6, my_half] + sums_got[0:6, my_half],
    ]
    lines = jnp.concatenate(lines + [jnp.zeros((128 - 13, half), f32)], axis=0).T
    sent[-1].wait()
    sent[-2].wait()
    stage[0, :, :128] = lines.astype(bf16)
    final = pltpu.make_async_copy(
        stage.at[0, :, pl.ds(0, 128)], grads_ref.at[:, pl.ds(8 * width, 128)], stores.at[8]
    )
    final.start()
    spread_n.last(1)
    spread_n.last(3)
    spread_n.last(2)
    final.wait()
    partner.finish()
    for move in (bring_x, bring_m, bring_g, give_y, give_dm, give_dx):
        move.finish()
    spread_g.finish()
    spread_n.finish()


def layer(x, memory, grads, vectors, ids, fc_bias, weights, fc_in, fc_out, devices):
    block, width = x.shape[1:]
    rows = ids.shape[1]
    count = rows // 2
    units = 512
    bf16, f32 = jnp.bfloat16, jnp.float32
    half = width // 2
    vmem = pl.BlockSpec(memory_space=pltpu.VMEM)
    hbm = pl.BlockSpec(memory_space=pl.ANY)
    every = jax.ShapeDtypeStruct((devices * count, width), bf16)
    moved = jax.ShapeDtypeStruct(x.shape, bf16)
    scores = (width // (2 * HEAD), rows, rows)
    kept = [
        ((rows, width), bf16), ((count, width), bf16), ((rows, width), bf16), ((rows, width), bf16),
        (scores, bf16), ((count, width), bf16), ((count, width), f32), ((count, width), bf16),
        ((count, width), bf16), ((rows, width), bf16), ((rows, width), bf16), (scores, bf16),
        ((count, width), bf16), ((count, width), f32), ((count, width), bf16),
    ]
    return pl.pallas_call(
        layer_kernel,
        in_specs=[vmem] * 3 + [hbm] * 10,
        out_specs=[hbm] * 6,
        out_shape=[
            moved, moved, moved, jax.ShapeDtypeStruct((half, 8 * width + 128), bf16), every, every
        ],
        scratch_shapes=[
            *[pltpu.VMEM((rows, width), bf16)] * 3,
            pltpu.VMEM((16, width), f32),
            pltpu.VMEM(ids.shape, jnp.int32),
            pltpu.VMEM(ids.shape, jnp.int32),
            pltpu.VMEM((rows, 128), jnp.int32),
            *[pltpu.VMEM(*shape) for shape in kept],
            *[pltpu.VMEM((count, width), bf16)] * 3,
            *[pltpu.VMEM((2 * w.shape[0], w.shape[1]), bf16) for w in weights],
            pltpu.VMEM((2, width, units), bf16),
            pltpu.VMEM((2, units, width), bf16),
            pltpu.VMEM((rows, width), bf16),
            pltpu.VMEM((rows, width), f32),
            pltpu.VMEM((rows, width), f32),
            pltpu.VMEM((2, count, width), bf16),
            pltpu.VMEM((2, count, width), bf16),
            pltpu.VMEM((count, width), bf16),
            *[pltpu.VMEM((rows, 2 * width), bf16)] * 4,
            *[pltpu.VMEM((rows, width), bf16)] * 4,
            *[pltpu.VMEM((rows, half), bf16)] * 3,
            pltpu.VMEM((count, width), f32),
            pltpu.VMEM((8, width), f32),
            pltpu.VMEM((8, width), f32),
            pltpu.VMEM((2, half, width), bf16),
            pltpu.SemaphoreType.DMA((32,)),
            pltpu.SemaphoreType.DMA((32,)),
            pltpu.SemaphoreType.DMA((5,)),
            pltpu.SemaphoreType.DMA((2, 2)),
            pltpu.SemaphoreType.DMA((9,)),
            pltpu.SemaphoreType.DMA((6, 2)),
            pltpu.SemaphoreType.DMA((6, 2)),
            pltpu.SemaphoreType.DMA((6,)),
            pltpu.SemaphoreType.DMA((2, 43)),
            pltpu.SemaphoreType.DMA((2, 43)),
            pltpu.SemaphoreType.DMA((2,)),
        ],
        compiler_params=pltpu.CompilerParams(
            vmem_limit_bytes=60 * 2**20, collective_id=1, has_side_effects=True
        ),
        cost_estimate=pl.CostEstimate(flops=80 * 10**9, bytes_accessed=64 * 2**20, transcendentals=0),
    )(vectors, ids, fc_bias, x, memory, grads, *weights, fc_in, fc_out)


def widen_kernel(*refs):
    din_part, dout_part, sum_ref, din_ref, dout_ref = refs[:5]
    din_ref[...] = din_part[...].astype(jnp.float32)
    dout_ref[...] = dout_part[...].astype(jnp.float32)
    column = 0
    for shard_ref in refs[5:]:
        shard_ref[...] = sum_ref[:, column : column + shard_ref.shape[1]].astype(jnp.float32)
        column += shard_ref.shape[1]


def widen(din, dout, total, widths):
    width, hidden = din.shape
    steps = 8
    units, height = hidden // steps, total.shape[0] // steps
    wide = pl.BlockSpec((width // steps, hidden), lambda at: (at, 0))
    tall = pl.BlockSpec((units, width), lambda at: (at, 0))
    f32 = jnp.float32
    return pl.pallas_call(
        widen_kernel,
        grid=(steps,),
        in_specs=[wide, tall, pl.BlockSpec((height, total.shape[1]), lambda at: (at, 0))],
        out_specs=[wide, tall] + [pl.BlockSpec((height, w), lambda at: (at, 0)) for w in widths],
        out_shape=[jax.ShapeDtypeStruct(din.shape, f32), jax.ShapeDtypeStruct(dout.shape, f32)]
        + [jax.ShapeDtypeStruct((total.shape[0], w), f32) for w in widths],
        compiler_params=pltpu.CompilerParams(vmem_limit_bytes=56 * 2**20),
        cost_estimate=pl.CostEstimate(flops=0, bytes_accessed=18 * width * hidden, transcendentals=0),
    )(din, dout, total)


def fast_body(
    hidden_in,
    memory,
    segment_ids,
    memory_ids,
    out_grad,
    self_qkv,
    self_out,
    cross_query,
    cross_kv,
    cross_out,
    fc_in,
    fc_out,
    biases,
    fc_in_bias,
    norm_gains,
    norm_shifts,
):
    width = hidden_in.shape[-1]
    f32 = jnp.float32
    ids = jnp.concatenate([segment_ids[:, 0], memory_ids[:, 0]], axis=0)
    vectors = jnp.concatenate([biases, norm_gains, norm_shifts], axis=1).astype(f32).T
    vectors = jnp.pad(vectors, ((0, 16 - vectors.shape[0]), (0, 0)))
    fc_bias = fc_in_bias.astype(f32)[None]
    devices = lax.axis_size("rep") * lax.axis_size("fsdp") * lax.axis_size("seq")
    weights = (self_qkv, self_out, cross_query, cross_kv, cross_out)
    hidden_out, hidden_grad, memory_grad, grads, normed_every, grad_every = layer(
        hidden_in[:, 0], memory[:, 0], out_grad[:, 0], vectors, ids, fc_bias, weights, fc_in, fc_out, devices
    )
    din, dout, grad_fc_bias, total = ffn_grads(
        normed_every, grad_every, fc_in, fc_out, fc_bias, grads
    )
    widths = [weight.shape[1] for weight in weights]
    grad_fc_in, grad_fc_out, *shards = widen(din, dout, total, widths)
    column = total[:, 8 * width :].astype(f32)
    return (
        hidden_out[:, None],
        hidden_grad[:, None],
        memory_grad[:, None],
        *shards,
        grad_fc_in,
        grad_fc_out,
        column[:, :7],
        grad_fc_bias[0],
        column[:, 7:10],
        column[:, 10:13],
    )


def solution(mesh):
    fits = mesh.shape["rep"] == 4 and mesh.shape["fsdp"] == 2 and mesh.shape["seq"] == 4
    chosen = fast_body if fits else body
    return jax.shard_map(
        chosen,
        mesh=mesh,
        in_specs=(
            P(None, ("rep", "fsdp"), "seq", None),
            P(None, ("rep", "fsdp"), "seq", None),
            P(None, ("rep", "fsdp"), None),
            P(None, ("rep", "fsdp"), None),
            P(None, ("rep", "fsdp"), "seq", None),
            P("fsdp", None),
            P("fsdp", None),
            P("fsdp", None),
            P("fsdp", None),
            P("fsdp", None),
            P(None, "fsdp"),
            P("fsdp", None),
            P("fsdp", None),
            P("fsdp"),
            P("fsdp", None),
            P("fsdp", None),
        ),
        out_specs=(
            P(None, ("rep", "fsdp"), "seq", None),
            P(None, ("rep", "fsdp"), "seq", None),
            P(None, ("rep", "fsdp"), "seq", None),
            P("fsdp", None),
            P("fsdp", None),
            P("fsdp", None),
            P("fsdp", None),
            P("fsdp", None),
            P(None, "fsdp"),
            P("fsdp", None),
            P("fsdp", None),
            P("fsdp"),
            P("fsdp", None),
            P("fsdp", None),
        ),
        check_vma=False,
    )
```

```python
import functools
import math

import jax
import jax.numpy as jnp
from jax import lax
from jax.experimental import pallas as pl
from jax.experimental.pallas import tpu as pltpu
from jax.sharding import PartitionSpec as P

HEAD = 64


NORM_EPSILON = 1e-05
MASKED_SCORE = -1e30


def norm_forward(values, norm_gain, norm_shift):
    average = jnp.mean(values, axis=-1, keepdims=True)
    centred = values - average
    inverse = lax.rsqrt(jnp.mean(centred * centred, axis=-1, keepdims=True) + NORM_EPSILON)
    scaled = centred * inverse
    return (scaled * norm_gain + norm_shift, scaled, inverse)


def norm_backward(grad_normed, scaled, inverse, norm_gain):
    grad_scaled = grad_normed * norm_gain
    first_mean = jnp.mean(grad_scaled, axis=-1, keepdims=True)
    second_mean = jnp.mean(grad_scaled * scaled, axis=-1, keepdims=True)
    grad_values = (grad_scaled - first_mean - scaled * second_mean) * inverse
    gain_grad = jnp.sum(grad_normed * scaled, axis=(0, 1))
    shift_grad = jnp.sum(grad_normed, axis=(0, 1))
    return (grad_values, gain_grad, shift_grad)


def split_heads(values):
    return values.reshape(values.shape[:-1] + (values.shape[-1] // HEAD, HEAD))


def join_heads(values):
    return values.reshape(values.shape[:2] + (values.shape[2] * values.shape[3],))


def masked_scores(queries, key_rows, allowed):
    raw_scores = jnp.einsum(
        "mqhe,mkhe->mhqk", queries, key_rows, preferred_element_type=jnp.float32
    )
    return jnp.where(allowed[:, None], raw_scores * HEAD ** (-0.5), MASKED_SCORE)


def attend_forward(queries, key_rows, value_rows, allowed):
    scores = masked_scores(queries, key_rows, allowed)
    highest = jnp.max(scores, axis=-1, keepdims=True)
    exponent = jnp.exp(scores - highest)
    row_totals = jnp.sum(exponent, axis=-1, keepdims=True)
    weights = (exponent / row_totals).astype(jnp.bfloat16)
    joined = jnp.einsum("mhqk,mkhe->mqhe", weights, value_rows, preferred_element_type=jnp.float32)
    return (join_heads(joined).astype(jnp.bfloat16), highest + jnp.log(row_totals))


def attend_backward(queries, key_rows, value_rows, allowed, log_totals, grad_joined):
    scores = masked_scores(queries, key_rows, allowed)
    probability = jnp.exp(scores - log_totals)
    weights = probability.astype(jnp.bfloat16)
    grad_value_rows = jnp.einsum(
        "mhqk,mqhe->mkhe", weights, grad_joined, preferred_element_type=jnp.float32
    )
    grad_weights = jnp.einsum(
        "mqhe,mkhe->mhqk", grad_joined, value_rows, preferred_element_type=jnp.float32
    )
    grad_scores = probability * (
        grad_weights - jnp.sum(grad_weights * probability, axis=-1, keepdims=True)
    )
    grad_scores = grad_scores.astype(jnp.bfloat16)
    grad_queries = jnp.einsum(
        "mhqk,mkhe->mqhe", grad_scores, key_rows, preferred_element_type=jnp.float32
    ) * HEAD ** (-0.5)
    grad_key_rows = jnp.einsum(
        "mhqk,mqhe->mkhe", grad_scores, queries, preferred_element_type=jnp.float32
    ) * HEAD ** (-0.5)
    return (join_heads(grad_queries), join_heads(grad_key_rows), join_heads(grad_value_rows))


def gelu_slope(values):
    cumulative = 0.5 * (1.0 + lax.erf(values * 2.0 ** (-0.5)))
    density = jnp.exp(-0.5 * values * values) / math.sqrt(2.0 * math.pi)
    return cumulative + values * density


def feed_forward(rows, weight_in, bias_in, weight_out):
    pre_active = jnp.einsum(
        "mtd,df->mtf", rows, weight_in, preferred_element_type=jnp.float32
    ) + bias_in.astype(jnp.float32)
    active = jax.nn.gelu(pre_active, approximate=False).astype(jnp.bfloat16)
    partial_out = jnp.einsum("mtf,fd->mtd", active, weight_out, preferred_element_type=jnp.float32)
    return (pre_active, active, partial_out)


def feed_back(rows, grad_rows, pre_active, active, weight_in, weight_out):
    grad_active = jnp.einsum(
        "mtd,fd->mtf", grad_rows, weight_out, preferred_element_type=jnp.float32
    )
    grad_inner = (grad_active * gelu_slope(pre_active)).astype(jnp.bfloat16)
    grad_weight_out = jnp.einsum(
        "mtf,mtd->fd", active, grad_rows, preferred_element_type=jnp.float32
    )
    grad_weight_in = jnp.einsum("mtd,mtf->df", rows, grad_inner, preferred_element_type=jnp.float32)
    grad_bias_in = jnp.sum(grad_inner.astype(jnp.float32), axis=(0, 1))
    grad_rows_in = jnp.einsum(
        "mtf,df->mtd", grad_inner, weight_in, preferred_element_type=jnp.float32
    )
    return (grad_weight_in, grad_weight_out, grad_bias_in, grad_rows_in)


def project(rows, weight):
    return jnp.einsum("mtd,de->mte", rows, weight, preferred_element_type=jnp.float32)


def project_back(grad_rows, weight):
    return jnp.einsum("mte,de->mtd", grad_rows, weight, preferred_element_type=jnp.float32)


def weight_grad(rows, grad_rows):
    return jnp.einsum("mtd,mte->de", rows, grad_rows, preferred_element_type=jnp.float32)


def column_sums(grad_rows):
    return jnp.sum(grad_rows.astype(jnp.float32), axis=(0, 1))


def body(
    hidden_in,
    memory,
    segment_ids,
    memory_ids,
    out_grad,
    self_qkv,
    self_out,
    cross_query,
    cross_kv,
    cross_out,
    fc_in,
    fc_out,
    biases,
    fc_in_bias,
    norm_gains,
    norm_shifts,
):
    micro_count, single, tokens, model_width = hidden_in.shape
    seq_index = lax.axis_index("seq")
    zero_row = jnp.zeros((model_width,), jnp.float32)
    outputs_list = []
    grads_list = []
    memory_list = []
    attn_total = None
    mlp_total = None
    for micro in range(micro_count):
        full_qkv = lax.all_gather(self_qkv, "fsdp", axis=0, tiled=True)
        full_self_out = lax.all_gather(self_out, "fsdp", axis=0, tiled=True)
        full_query = lax.all_gather(cross_query, "fsdp", axis=0, tiled=True)
        full_memory_kv = lax.all_gather(cross_kv, "fsdp", axis=0, tiled=True)
        full_cross_out = lax.all_gather(cross_out, "fsdp", axis=0, tiled=True)
        full_biases = lax.all_gather(biases, "fsdp", axis=0, tiled=True)
        full_gains = lax.all_gather(norm_gains, "fsdp", axis=0, tiled=True)
        full_shifts = lax.all_gather(norm_shifts, "fsdp", axis=0, tiled=True)
        bias_float = full_biases.astype(jnp.float32)
        gain_float = full_gains.astype(jnp.float32)
        shift_float = full_shifts.astype(jnp.float32)
        hidden = hidden_in[micro : micro + 1][:, 0].astype(jnp.float32)
        memory_rows = memory[micro : micro + 1][:, 0]
        token_ids = segment_ids[micro : micro + 1][:, 0]
        source_ids = memory_ids[micro : micro + 1][:, 0]
        query_ids = lax.dynamic_slice_in_dim(token_ids, seq_index * tokens, tokens, 1)
        query_place = seq_index * tokens + jnp.arange(tokens, dtype=jnp.int32)
        key_place = jnp.arange(token_ids.shape[1], dtype=jnp.int32)
        self_allowed = (query_place[:, None] >= key_place[None, :])[None] & (
            query_ids[:, :, None] == token_ids[:, None, :]
        )
        cross_allowed = query_ids[:, :, None] == source_ids[:, None, :]
        normed_one, scaled_one, inverse_one = norm_forward(
            hidden, gain_float[:, 0], shift_float[:, 0]
        )
        normed_one = normed_one.astype(jnp.bfloat16)
        qkv_bias = jnp.concatenate([bias_float[:, 0], zero_row, bias_float[:, 1]])
        projected = (project(normed_one, full_qkv) + qkv_bias).astype(jnp.bfloat16)
        self_queries = split_heads(projected[..., :model_width])
        kv_all = lax.all_gather(projected[..., model_width:], "seq", axis=1, tiled=True)
        self_key_rows = split_heads(kv_all[..., :model_width])
        self_value_rows = split_heads(kv_all[..., model_width:])
        self_mixed, self_totals = attend_forward(
            self_queries, self_key_rows, self_value_rows, self_allowed
        )
        after_self = hidden + project(self_mixed, full_self_out) + bias_float[:, 2]
        normed_two, scaled_two, inverse_two = norm_forward(
            after_self, gain_float[:, 1], shift_float[:, 1]
        )
        normed_two = normed_two.astype(jnp.bfloat16)
        cross_queries = (project(normed_two, full_query) + bias_float[:, 3]).astype(jnp.bfloat16)
        memory_bias = jnp.concatenate([zero_row, bias_float[:, 4]])
        memory_kv = (project(memory_rows, full_memory_kv) + memory_bias).astype(jnp.bfloat16)
        memory_all = lax.all_gather(memory_kv, "seq", axis=1, tiled=True)
        memory_key_rows = split_heads(memory_all[..., :model_width])
        memory_value_rows = split_heads(memory_all[..., model_width:])
        cross_mixed, cross_totals = attend_forward(
            split_heads(cross_queries), memory_key_rows, memory_value_rows, cross_allowed
        )
        after_cross = after_self + project(cross_mixed, full_cross_out) + bias_float[:, 5]
        normed_three, scaled_three, inverse_three = norm_forward(
            after_cross, gain_float[:, 2], shift_float[:, 2]
        )
        normed_three = normed_three.astype(jnp.bfloat16)
        grad_out = out_grad[micro : micro + 1][:, 0]
        mlp_inputs = lax.all_gather(normed_three, "fsdp", axis=0, tiled=True)
        pre_active, active, partial_out = feed_forward(mlp_inputs, fc_in, fc_in_bias, fc_out)
        mlp_branch = lax.psum_scatter(
            partial_out.astype(jnp.bfloat16), "fsdp", scatter_dimension=0, tiled=True
        ).astype(jnp.float32)
        output = after_cross + mlp_branch + bias_float[:, 6]
        hidden_out = output.astype(jnp.bfloat16)[:, None]
        back_qkv = lax.all_gather(self_qkv, "fsdp", axis=0, tiled=True)
        back_self_out = lax.all_gather(self_out, "fsdp", axis=0, tiled=True)
        back_query = lax.all_gather(cross_query, "fsdp", axis=0, tiled=True)
        back_memory_kv = lax.all_gather(cross_kv, "fsdp", axis=0, tiled=True)
        back_cross_out = lax.all_gather(cross_out, "fsdp", axis=0, tiled=True)
        back_gains = lax.all_gather(norm_gains, "fsdp", axis=0, tiled=True)
        back_gain_float = back_gains.astype(jnp.float32)
        grad_gathered = lax.all_gather(grad_out, "fsdp", axis=0, tiled=True)
        one_grad_fc_in, one_grad_fc_out, one_grad_fc_bias, grad_partial = feed_back(
            mlp_inputs, grad_gathered, pre_active, active, fc_in, fc_out
        )
        grad_normed_three = lax.psum_scatter(
            grad_partial.astype(jnp.bfloat16), "fsdp", scatter_dimension=0, tiled=True
        ).astype(jnp.float32)
        grad_three, gain_three, shift_three = norm_backward(
            grad_normed_three, scaled_three, inverse_three, back_gain_float[:, 2]
        )
        grad_after_cross = grad_out.astype(jnp.float32) + grad_three
        grad_cross_branch = grad_after_cross.astype(jnp.bfloat16)
        grad_cross_out = weight_grad(cross_mixed, grad_cross_branch)
        grad_cross_mixed = project_back(grad_cross_branch, back_cross_out).astype(jnp.bfloat16)
        cross_grad_queries, memory_grad_keys, memory_grad_values = attend_backward(
            split_heads(cross_queries),
            memory_key_rows,
            memory_value_rows,
            cross_allowed,
            cross_totals,
            split_heads(grad_cross_mixed),
        )
        own_memory_keys = lax.psum_scatter(
            memory_grad_keys.astype(jnp.bfloat16), "seq", scatter_dimension=1, tiled=True
        )
        own_memory_values = lax.psum_scatter(
            memory_grad_values.astype(jnp.bfloat16), "seq", scatter_dimension=1, tiled=True
        )
        grad_memory_kv = jnp.concatenate([own_memory_keys, own_memory_values], axis=-1)
        grad_memory_weight = weight_grad(memory_rows, grad_memory_kv)
        memory_grad = project_back(grad_memory_kv, back_memory_kv).astype(jnp.bfloat16)[:, None]
        grad_cross_queries = cross_grad_queries.astype(jnp.bfloat16)
        grad_query_weight = weight_grad(normed_two, grad_cross_queries)
        grad_normed_two = project_back(grad_cross_queries, back_query)
        grad_two, gain_two, shift_two = norm_backward(
            grad_normed_two, scaled_two, inverse_two, back_gain_float[:, 1]
        )
        grad_after_self = grad_after_cross + grad_two
        grad_self_branch = grad_after_self.astype(jnp.bfloat16)
        grad_self_out = weight_grad(self_mixed, grad_self_branch)
        grad_self_mixed = project_back(grad_self_branch, back_self_out).astype(jnp.bfloat16)
        self_grad_queries, self_grad_keys, self_grad_values = attend_backward(
            self_queries,
            self_key_rows,
            self_value_rows,
            self_allowed,
            self_totals,
            split_heads(grad_self_mixed),
        )
        own_self_keys = lax.psum_scatter(
            self_grad_keys.astype(jnp.bfloat16), "seq", scatter_dimension=1, tiled=True
        )
        own_self_values = lax.psum_scatter(
            self_grad_values.astype(jnp.bfloat16), "seq", scatter_dimension=1, tiled=True
        )
        grad_projected = jnp.concatenate(
            [self_grad_queries.astype(jnp.bfloat16), own_self_keys, own_self_values], axis=-1
        )
        grad_qkv_weight = weight_grad(normed_one, grad_projected)
        grad_normed_one = project_back(grad_projected, back_qkv)
        grad_one, gain_one, shift_one = norm_backward(
            grad_normed_one, scaled_one, inverse_one, back_gain_float[:, 0]
        )
        hidden_grad = (grad_after_self + grad_one).astype(jnp.bfloat16)[:, None]
        grad_biases = jnp.stack(
            [
                column_sums(grad_projected[..., :model_width]),
                column_sums(grad_projected[..., 2 * model_width :]),
                column_sums(grad_self_branch),
                column_sums(grad_cross_queries),
                column_sums(grad_memory_kv[..., model_width:]),
                column_sums(grad_cross_branch),
                column_sums(grad_out),
            ],
            axis=1,
        )
        grad_gains = jnp.stack([gain_one, gain_two, gain_three], axis=1)
        grad_shifts = jnp.stack([shift_one, shift_two, shift_three], axis=1)
        attn_grads = (
            grad_qkv_weight,
            grad_self_out,
            grad_query_weight,
            grad_memory_weight,
            grad_cross_out,
            grad_biases,
            grad_gains,
            grad_shifts,
        )
        mlp_grads = (one_grad_fc_in, one_grad_fc_out, one_grad_fc_bias)
        hidden_out, hidden_grad, memory_grad, attn_grads, mlp_grads = (
            hidden_out,
            hidden_grad,
            memory_grad,
            attn_grads,
            mlp_grads,
        )
        outputs_list.append(hidden_out)
        grads_list.append(hidden_grad)
        memory_list.append(memory_grad)
        if attn_total is None:
            attn_total = attn_grads
            mlp_total = mlp_grads
        else:
            attn_total = jax.tree.map(jnp.add, attn_total, attn_grads)
            mlp_total = jax.tree.map(jnp.add, mlp_total, mlp_grads)
    grad_fc_in, grad_fc_out, grad_fc_bias = mlp_total
    (
        shard_qkv,
        shard_self_out,
        shard_query,
        shard_memory_kv,
        shard_cross_out,
        shard_biases,
        shard_gains,
        shard_shifts,
    ) = (
        lax.psum_scatter(
            attn_total[0].astype(jnp.bfloat16), "fsdp", scatter_dimension=0, tiled=True
        ).astype(jnp.float32),
        lax.psum_scatter(
            attn_total[1].astype(jnp.bfloat16), "fsdp", scatter_dimension=0, tiled=True
        ).astype(jnp.float32),
        lax.psum_scatter(
            attn_total[2].astype(jnp.bfloat16), "fsdp", scatter_dimension=0, tiled=True
        ).astype(jnp.float32),
        lax.psum_scatter(
            attn_total[3].astype(jnp.bfloat16), "fsdp", scatter_dimension=0, tiled=True
        ).astype(jnp.float32),
        lax.psum_scatter(
            attn_total[4].astype(jnp.bfloat16), "fsdp", scatter_dimension=0, tiled=True
        ).astype(jnp.float32),
        lax.psum_scatter(
            attn_total[5].astype(jnp.bfloat16), "fsdp", scatter_dimension=0, tiled=True
        ).astype(jnp.float32),
        lax.psum_scatter(
            attn_total[6].astype(jnp.bfloat16), "fsdp", scatter_dimension=0, tiled=True
        ).astype(jnp.float32),
        lax.psum_scatter(
            attn_total[7].astype(jnp.bfloat16), "fsdp", scatter_dimension=0, tiled=True
        ).astype(jnp.float32),
    )
    summed = (
        lax.psum(shard_qkv.astype(jnp.bfloat16), ("rep", "seq")).astype(jnp.float32),
        lax.psum(shard_self_out.astype(jnp.bfloat16), ("rep", "seq")).astype(jnp.float32),
        lax.psum(shard_query.astype(jnp.bfloat16), ("rep", "seq")).astype(jnp.float32),
        lax.psum(shard_memory_kv.astype(jnp.bfloat16), ("rep", "seq")).astype(jnp.float32),
        lax.psum(shard_cross_out.astype(jnp.bfloat16), ("rep", "seq")).astype(jnp.float32),
        lax.psum(grad_fc_in.astype(jnp.bfloat16), ("rep", "seq")).astype(jnp.float32),
        lax.psum(grad_fc_out.astype(jnp.bfloat16), ("rep", "seq")).astype(jnp.float32),
        lax.psum(shard_biases.astype(jnp.bfloat16), ("rep", "seq")).astype(jnp.float32),
        lax.psum(grad_fc_bias.astype(jnp.bfloat16), ("rep", "seq")).astype(jnp.float32),
        lax.psum(shard_gains.astype(jnp.bfloat16), ("rep", "seq")).astype(jnp.float32),
        lax.psum(shard_shifts.astype(jnp.bfloat16), ("rep", "seq")).astype(jnp.float32),
    )
    hidden_out = jnp.concatenate(outputs_list, axis=0)
    hidden_grad = jnp.concatenate(grads_list, axis=0)
    memory_grad = jnp.concatenate(memory_list, axis=0)
    return (
        hidden_out,
        hidden_grad,
        memory_grad,
        summed[0],
        summed[1],
        summed[2],
        summed[3],
        summed[4],
        summed[5],
        summed[6],
        summed[7],
        summed[8],
        summed[9],
        summed[10],
    )


def mul(left, right):
    return jnp.dot(left, right, preferred_element_type=jnp.float32)


def mul_nt(left, right):
    return lax.dot_general(left, right, (((1,), (1,)), ((), ())), preferred_element_type=jnp.float32)


def mul_tn(left, right):
    return lax.dot_general(left, right, (((0,), (0,)), ((), ())), preferred_element_type=jnp.float32)


MESH = pl.DeviceIdType.MESH


def gelu_pair(values, refine=False):
    depth = 1.0 + (0.3275911 * 2.0**-0.5) * jnp.abs(values)
    inv = pltpu.reciprocal(depth, approx=True)
    if refine:
        inv = inv * (2.0 - depth * inv)
    bell = jnp.exp(-0.5 * values * values)
    series = 0.7107068705 + inv * (-0.7265760135 + inv * 0.5307027145)
    series = inv * (0.127414796 + inv * (-0.142248368 + inv * series))
    tail = series * bell
    cumulative = jnp.where(values >= 0.0, 1.0 - tail, tail)
    return values * cumulative, cumulative + values * (bell * (1.0 / math.sqrt(2.0 * math.pi)))


def position():
    rep, core, deep = lax.axis_index("rep"), lax.axis_index("fsdp"), lax.axis_index("seq")
    return rep % 2, rep // 2, core, deep


def device(across, up, core, deep):
    return (up * 2 + across, core, deep)


def greet(partners):
    barrier = pltpu.get_barrier_semaphore()
    for partner in partners:
        pl.semaphore_signal(barrier, inc=1, device_id=partner, device_id_type=MESH)
    pl.semaphore_wait(barrier, len(partners))


class ChunkSum:
    def __init__(self, turned, column, width, own_ref, sum_ref, held, first, second, third, done, send, recv, local):
        across, up, core, deep = position()
        self.side, self.next = (up, across) if turned else (across, up)
        one = device(1 - across, up, core, deep)
        two = device(across, 1 - up, core, deep)
        self.one, self.two = (two, one) if turned else (one, two)
        self.deep = deep
        self.others = [(deep + step) % 4 for step in (1, 2, 3)]
        self.third_ids = [device(across, up, core, other) for other in self.others]
        self.columns = pl.ds(column, width)
        self.own, self.sum = own_ref, sum_ref
        self.held, self.first, self.second, self.third, self.done = held, first, second, third, done
        self.send, self.recv, self.local = send, recv, local
        self.quarter = pl.multiple_of(self.next * 128, 128)
        self.start_row = self.side * 256

    def remote(self, index, src, dst, target):
        return pltpu.make_async_remote_copy(
            src_ref=src,
            dst_ref=dst,
            send_sem=self.send.at[index],
            recv_sem=self.recv.at[index],
            device_id=target,
            device_id_type=MESH,
        )

    def rows(self, ref, start, count):
        return ref.at[pl.ds(pl.multiple_of(start, 32), count), self.columns]

    def copy_a(self):
        return self.remote(0, self.rows(self.own, (1 - self.side) * 256, 256), self.first, self.one)

    def load(self):
        return pltpu.make_async_copy(self.rows(self.own, self.start_row, 256), self.held, self.local.at[0])

    def copy_b(self):
        away = pl.multiple_of((1 - self.next) * 128, 128)
        return self.remote(1, self.held.at[pl.ds(away, 128)], self.second, self.two)

    def copy_c(self, turn):
        start = pl.multiple_of(self.quarter + self.others[turn] * 32, 32)
        return self.remote(2 + turn, self.held.at[pl.ds(start, 32)], self.third.at[turn], self.third_ids[turn])

    def place(self):
        return self.rows(self.sum, self.start_row + self.quarter + self.deep * 32, 32)

    def copy_d(self, turn):
        return self.remote(5 + turn, self.done, self.place(), self.third_ids[turn])

    def store(self):
        return pltpu.make_async_copy(self.done, self.place(), self.local.at[1])

    def copy_e(self):
        part = self.rows(self.sum, self.start_row + self.quarter, 128)
        return self.remote(8, part, part, self.two)

    def copy_f(self):
        part = self.rows(self.sum, self.start_row, 256)
        return self.remote(9, part, part, self.one)

    def stage(self, number):
        if number == 0:
            self.copy_a().start()
            self.load().start()
        elif number == 1:
            self.load().wait()
            self.copy_a().wait_recv()
            self.held[...] = self.held[...] + self.first[...]
            self.copy_b().start()
        elif number == 2:
            self.copy_b().wait_recv()
            self.copy_b().wait_send()
            mine = pl.ds(self.quarter, 128)
            self.held[mine] = self.held[mine] + self.second[...]
            for turn in range(3):
                self.copy_c(turn).start()
        elif number == 3:
            for turn in range(3):
                self.copy_c(turn).wait_recv()
            start = pl.multiple_of(self.quarter + self.deep * 32, 32)
            total = self.held[pl.ds(start, 32)].astype(jnp.float32)
            for turn in range(3):
                total += self.third[turn].astype(jnp.float32)
            self.done[...] = total.astype(self.done.dtype)
            self.store().start()
            for turn in range(3):
                self.copy_d(turn).start()
        elif number == 4:
            self.store().wait()
            for turn in range(3):
                self.copy_d(turn).wait_recv()
            self.copy_e().start()
        elif number == 5:
            self.copy_e().wait_recv()
            self.copy_f().start()
        elif number == 6:
            self.copy_f().wait_recv()
            self.copy_a().wait_send()
            for turn in range(3):
                self.copy_c(turn).wait_send()
                self.copy_d(turn).wait_send()
            self.copy_e().wait_send()
            self.copy_f().wait_send()


BEGIN = (0, 3, 6, 9)
AFTER = (0, 2, 3, 4, 5, 7, 8)


def ffn_kernel(
    step, tiles, plan, rows_ref, grads_ref, in_ref, out_ref, bias_ref, own_ref,
    din_ref, dout_ref, dbias_ref, sum_ref, flip, acc_in, acc_out, us, das, actives, inners, sums, *rest
):
    units = flip.shape[0]
    steps = rows_ref.shape[0] // step
    at = pl.program_id(0)
    send, recv, local = rest[-3:]
    buffers = rest[:-3]
    chunks = []
    for index, (turned, column, width, _) in enumerate(plan):
        held, first, second, third, done = buffers[5 * index : 5 * index + 5]
        chunks.append(
            ChunkSum(turned, column, width, own_ref, sum_ref, held, first, second, third, done,
                     send.at[index], recv.at[index], local.at[index])
        )

    @pl.when(at == 0)
    def _():
        across, up, core, deep = position()
        greet(
            [device(1 - across, up, core, deep), device(across, 1 - up, core, deep)]
            + [device(across, up, core, (deep + turn) % 4) for turn in (1, 2, 3)]
        )

    work = {}
    for chunk, (_, _, _, slots) in zip(chunks, plan):
        for number, slot in enumerate(slots):
            work.setdefault(min(slot, tiles), []).append((slot, number, chunk))

    def traffic(slot):
        for _, number, chunk in sorted(work.get(slot, []), key=lambda job: job[:2]):
            chunk.stage(number)

    for slot in range(tiles):
        if slot in work:
            pl.when(at == slot)(functools.partial(traffic, slot))

    flip[...] = in_ref[...].T

    def front(turn):
        part = pl.ds(turn * step, step)
        us[turn % 2] = mul_nt(flip[...], rows_ref[part, :])
        das[turn % 2] = mul_nt(out_ref[...], grads_ref[part, :])

    bias = jnp.broadcast_to(bias_ref[...], (128, units)).T[:, :1]

    def middle(turn):
        active, slope = gelu_pair(us[turn % 2] + bias)
        inner = (das[turn % 2] * slope).astype(jnp.bfloat16)
        actives[turn % 2] = active.astype(jnp.bfloat16)
        inners[turn % 2] = inner
        total = inner[:, :128].astype(jnp.float32)
        for lane in range(1, step // 128):
            total += inner[:, lane * 128 : (lane + 1) * 128].astype(jnp.float32)
        sums[...] = total if turn == 0 else sums[...] + total

    def back(turn):
        part = pl.ds(turn * step, step)
        out_part = mul(actives[turn % 2], grads_ref[part, :])
        in_part = mul(inners[turn % 2], rows_ref[part, :])
        if turn:
            out_part += acc_out[...]
            in_part += acc_in[...]
        if turn < steps - 1:
            acc_out[...] = out_part
            acc_in[...] = in_part
        else:
            dout_ref[...] = out_part.astype(jnp.bfloat16)
            din_ref[...] = in_part.astype(jnp.bfloat16).T

    front(0)
    for turn in range(steps + 1):
        if turn:
            back(turn - 1)
        if turn + 1 < steps:
            front(turn + 1)
        if turn < steps:
            middle(turn)
    dbias_ref[...] = jnp.sum(sums[...].T, axis=0, keepdims=True)
    pl.when(at == tiles - 1)(functools.partial(traffic, tiles))


def ffn_grads(rows, grads, fc_in, fc_out, bias, own):
    count, width = rows.shape
    hidden = fc_in.shape[1]
    units, step = 256, count // 4
    tiles = hidden // units
    plan = [(False, 8 * width, 128, (0, 1, 2, 3, 4, 5, 6))]
    for pair, begin in enumerate(BEGIN):
        slots = [begin + after for after in AFTER]
        plan.append((False, pair * width, width, slots))
        plan.append((True, (len(BEGIN) + pair) * width, width, slots))
    buffers = []
    for _, _, columns, _ in plan:
        buffers += [
            pltpu.VMEM((256, columns), jnp.bfloat16),
            pltpu.VMEM((256, columns), jnp.bfloat16),
            pltpu.VMEM((128, columns), jnp.bfloat16),
            pltpu.VMEM((3, 32, columns), jnp.bfloat16),
            pltpu.VMEM((32, columns), jnp.bfloat16),
        ]
    whole = functools.partial(pl.BlockSpec, pipeline_mode=pl.Buffered(1))
    return pl.pallas_call(
        functools.partial(ffn_kernel, step, tiles, plan),
        grid=(tiles,),
        in_specs=[
            whole((count, width), lambda at: (0, 0)),
            whole((count, width), lambda at: (0, 0)),
            pl.BlockSpec((width, units), lambda at: (0, at)),
            pl.BlockSpec((units, width), lambda at: (at, 0)),
            pl.BlockSpec((1, units), lambda at: (0, at)),
            pl.BlockSpec(memory_space=pl.ANY),
        ],
        out_specs=[
            pl.BlockSpec((width, units), lambda at: (0, at)),
            pl.BlockSpec((units, width), lambda at: (at, 0)),
            pl.BlockSpec((1, units), lambda at: (0, at)),
            pl.BlockSpec(memory_space=pl.ANY),
        ],
        out_shape=[
            jax.ShapeDtypeStruct((width, hidden), jnp.bfloat16),
            jax.ShapeDtypeStruct((hidden, width), jnp.bfloat16),
            jax.ShapeDtypeStruct((1, hidden), jnp.float32),
            jax.ShapeDtypeStruct(own.shape, own.dtype),
        ],
        scratch_shapes=[
            pltpu.VMEM((units, width), jnp.bfloat16),
            pltpu.VMEM((units, width), jnp.float32),
            pltpu.VMEM((units, width), jnp.float32),
            pltpu.VMEM((2, units, step), jnp.float32),
            pltpu.VMEM((2, units, step), jnp.float32),
            pltpu.VMEM((2, units, step), jnp.bfloat16),
            pltpu.VMEM((2, units, step), jnp.bfloat16),
            pltpu.VMEM((units, 128), jnp.float32),
            *buffers,
            pltpu.SemaphoreType.DMA((len(plan), 10)),
            pltpu.SemaphoreType.DMA((len(plan), 10)),
            pltpu.SemaphoreType.DMA((len(plan), 2)),
        ],
        compiler_params=pltpu.CompilerParams(
            vmem_limit_bytes=58 * 2**20, collective_id=0, has_side_effects=True
        ),
        cost_estimate=pl.CostEstimate(
            flops=8 * count * width * hidden,
            bytes_accessed=4 * count * width + 12 * width * hidden,
            transcendentals=count * hidden,
        ),
    )(rows, grads, fc_in, fc_out, bias, own)


def norm_parts(values):
    centred = values - jnp.mean(values, axis=-1, keepdims=True)
    inverse = lax.rsqrt(jnp.mean(centred * centred, axis=-1, keepdims=True) + NORM_EPSILON)
    return centred * inverse, inverse


def normed(values, vectors, which):
    scaled, _ = norm_parts(values)
    return (scaled * vectors[7 + which : 8 + which] + vectors[10 + which : 11 + which]).astype(jnp.bfloat16)


class Partner:
    def __init__(self, send, recv):
        across, up, core, deep = position()
        self.core = core
        self.id = device(across, up, 1 - core, deep)
        self.send, self.recv = send, recv
        self.copies = []

    def push(self, src, dst):
        index = len(self.copies)
        copy = pltpu.make_async_remote_copy(
            src_ref=src,
            dst_ref=dst,
            send_sem=self.send.at[index],
            recv_sem=self.recv.at[index],
            device_id=self.id,
            device_id_type=MESH,
        )
        copy.start()
        self.copies.append(copy)
        return copy

    def finish(self):
        for copy in self.copies:
            copy.wait_send()


class Weights:
    def __init__(self, partner, shard, whole, local):
        half = shard.shape[0]
        mine = whole.at[pl.ds(pl.multiple_of(partner.core * half, half), half)]
        self.remote = partner.push(shard, mine)
        self.near = pltpu.make_async_copy(shard, mine, local)
        self.near.start()
        self.whole = whole

    def get(self):
        self.near.wait()
        self.remote.wait_recv()
        return self.whole


def two_heads(values, lane):
    zero = jnp.zeros_like(values)
    return jnp.concatenate([jnp.where(lane, values, zero), jnp.where(lane, zero, values)], axis=0)


def lane_of():
    return lax.broadcasted_iota(jnp.int32, (1, 2 * HEAD), 1) < HEAD


def attend(q_ref, k_ref, v_ref, p_ref, o_ref, allowed):
    lane = lane_of()
    count = q_ref.shape[0]
    for pair in range(q_ref.shape[1] // (2 * HEAD)):
        columns = pl.ds(pair * 2 * HEAD, 2 * HEAD)
        scores = mul_nt(two_heads(q_ref[:, columns], lane), k_ref[:, columns])
        scores = jnp.where(allowed, scores * HEAD ** (-0.5), MASKED_SCORE)
        exponent = jnp.exp(scores - jnp.max(scores, axis=-1, keepdims=True))
        weights = (exponent / jnp.sum(exponent, axis=-1, keepdims=True)).astype(jnp.bfloat16)
        p_ref[pair] = weights
        mixed = mul(weights, v_ref[:, columns])
        o_ref[:, columns] = jnp.where(lane, mixed[:count], mixed[count:]).astype(jnp.bfloat16)


def attend_back(q_ref, k_ref, v_ref, p_ref, go_ref, dq_ref, dk_ref, dv_ref):
    lane = lane_of()
    count = q_ref.shape[0]
    for pair in range(q_ref.shape[1] // (2 * HEAD)):
        columns = pl.ds(pair * 2 * HEAD, 2 * HEAD)
        grads = two_heads(go_ref[:, columns], lane)
        weights = p_ref[pair]
        dv_ref[:, columns] = mul_tn(weights, grads).astype(jnp.bfloat16)
        grad_weights = mul_nt(grads, v_ref[:, columns])
        exact = weights.astype(jnp.float32)
        inner = jnp.sum(grad_weights * exact, axis=-1, keepdims=True)
        scores = (exact * (grad_weights - inner)).astype(jnp.bfloat16)
        queries = mul(scores, k_ref[:, columns]) * HEAD ** (-0.5)
        dq_ref[:, columns] = jnp.where(lane, queries[:count], queries[count:]).astype(jnp.bfloat16)
        keys = mul_tn(scores, two_heads(q_ref[:, columns], lane)) * HEAD ** (-0.5)
        dk_ref[:, columns] = keys.astype(jnp.bfloat16)


def norm_back(grads, values, gain, sums_ref, row):
    scaled, inverse = norm_parts(values)
    sums_ref[row : row + 1, :] = jnp.sum(grads * scaled, axis=0, keepdims=True)
    sums_ref[row + 3 : row + 4, :] = jnp.sum(grads, axis=0, keepdims=True)
    inner = grads * gain
    first = jnp.mean(inner, axis=-1, keepdims=True)
    second = jnp.mean(inner * scaled, axis=-1, keepdims=True)
    return (inner - first - scaled * second) * inverse


class Bring:
    def __init__(self, src, dst, send, recv, local):
        across, up, core, deep = position()
        self.core, self.deep = core, deep
        self.src, self.dst = src, dst
        self.send, self.recv, self.local = send, recv, local
        self.across, self.up = across, up

    def stays(self, micro):
        return (self.deep // 2 == self.core) & (2 * micro + self.core == self.deep)

    def far(self, micro, index):
        block = self.src.shape[1]
        return pltpu.make_async_remote_copy(
            src_ref=self.src.at[micro],
            dst_ref=self.dst.at[pl.ds(pl.multiple_of(self.deep * block, block), block)],
            send_sem=self.send.at[micro],
            recv_sem=self.recv.at[index],
            device_id=device(self.across, self.up, self.deep // 2, 2 * micro + self.core),
            device_id_type=MESH,
        )

    def near(self, micro):
        block = self.src.shape[1]
        return pltpu.make_async_copy(
            self.src.at[micro],
            self.dst.at[pl.ds(pl.multiple_of(self.deep * block, block), block)],
            self.local,
        )

    def start(self):
        for micro in range(2):
            @pl.when(self.stays(micro))
            def _():
                self.near(micro).start()

            @pl.when(jnp.logical_not(self.stays(micro)))
            def _():
                self.far(micro, self.deep % 2).start()

    def wait(self):
        for block in range(2):
            here = (self.deep % 2 == self.core) & (2 * self.core + block == self.deep)

            @pl.when(here)
            def _():
                self.near(block).wait()

            @pl.when(jnp.logical_not(here))
            def _():
                self.far(block, block).wait_recv()

    def finish(self):
        for micro in range(2):
            @pl.when(jnp.logical_not(self.stays(micro)))
            def _():
                self.far(micro, self.deep % 2).wait_send()


class SendBack:
    def __init__(self, src, dst, send, recv, local):
        self.src, self.dst = src, dst
        self.send, self.recv, self.local = send, recv, local
        self.across, self.up, self.core, self.deep = position()

    def stays(self, block):
        return (self.deep % 2 == self.core) & (2 * self.core + block == self.deep)

    def far(self, block, index):
        count = self.dst.shape[1]
        return pltpu.make_async_remote_copy(
            src_ref=self.src.at[pl.ds(block * count, count)],
            dst_ref=self.dst.at[self.deep // 2],
            send_sem=self.send.at[block],
            recv_sem=self.recv.at[index],
            device_id=device(self.across, self.up, self.deep % 2, 2 * self.core + block),
            device_id_type=MESH,
        )

    def near(self, block):
        count = self.dst.shape[1]
        return pltpu.make_async_copy(
            self.src.at[pl.ds(block * count, count)], self.dst.at[self.deep // 2], self.local
        )

    def start(self):
        for block in range(2):
            @pl.when(self.stays(block))
            def _():
                self.near(block).start()

            @pl.when(jnp.logical_not(self.stays(block)))
            def _():
                self.far(block, self.deep // 2).start()

    def finish(self):
        for micro in range(2):
            here = (self.deep // 2 == self.core) & (2 * micro + self.core == self.deep)

            @pl.when(here)
            def _():
                self.near(micro).wait()

            @pl.when(jnp.logical_not(here))
            def _():
                self.far(micro, micro).wait_recv()
        for block in range(2):
            @pl.when(jnp.logical_not(self.stays(block)))
            def _():
                self.far(block, self.deep // 2).wait_send()


class Spread:
    def __init__(self, own, every, send, recv, local):
        self.own, self.every = own, every
        self.send, self.recv, self.local = send, recv, local
        self.across, self.up, self.core, self.deep = position()
        self.count = own.shape[0]
        self.right = device(1 - self.across, self.up, self.core, self.deep)
        self.above = device(self.across, 1 - self.up, self.core, self.deep)
        self.twin = device(self.across, self.up, 1 - self.core, self.deep)

    def item(self, flip_x, flip_y, step, half=None):
        column = (2 if flip_y else 0) + (1 if flip_x else 0)
        slot = (column * 4 + (self.deep + step) % 4) * 2 + self.core
        start = slot * self.count
        if half is None:
            return self.every.at[pl.ds(pl.multiple_of(start, self.count), self.count)]
        part = self.count // 2
        return self.every.at[pl.ds(pl.multiple_of(start + half * part, part), part)]

    def copy(self, index, src, dst, target):
        return pltpu.make_async_remote_copy(
            src_ref=src,
            dst_ref=dst,
            send_sem=self.send.at[index],
            recv_sem=self.recv.at[index],
            device_id=target,
            device_id_type=MESH,
        )

    def hop(self, step, up):
        there = (step - 1) % 4 if up else (step + 1) % 4
        place = self.item(False, False, step)
        target = device(self.across, self.up, self.core, (self.deep + (1 if up else 3)) % 4)
        return pltpu.make_async_remote_copy(
            src_ref=self.own if step == 0 else place,
            dst_ref=place,
            send_sem=self.send.at[(35 if up else 39) + step],
            recv_sem=self.recv.at[there - 1],
            device_id=target,
            device_id_type=MESH,
        )

    def arrived(self, step):
        place = self.item(False, False, step)
        return pltpu.make_async_remote_copy(
            src_ref=place,
            dst_ref=place,
            send_sem=self.send.at[35],
            recv_sem=self.recv.at[step - 1],
            device_id=self.twin,
            device_id_type=MESH,
        )

    def column(self, step, index, target):
        src = self.own if step == 0 else self.item(False, False, step)
        dst = self.item(index == 3, index == 7, step)
        return self.copy(index + step, src, dst, target)

    def passed(self, step, index, flip_x, flip_y, target, half=None):
        src = self.item(flip_x, flip_y, step, half)
        dst = src if half is None else self.item(True, True, step, half)
        return self.copy(index + step, src, dst, target)

    def store(self):
        return pltpu.make_async_copy(self.own, self.item(False, False, 0), self.local)

    def fan(self, step):
        self.column(step, 3, self.right).start()
        self.column(step, 7, self.above).start()
        self.column(step, 19, self.twin).start()

    def begin(self):
        self.fan(0)
        pl.when(self.deep < 3)(lambda: self.hop(0, True).start())
        pl.when(self.deep > 0)(lambda: self.hop(0, False).start())
        self.store().start()

    def relay(self, step, up):
        self.arrived(step).wait_recv()
        if up and step > 1:
            pl.when(self.deep < 3)(lambda: self.hop(step, True).start())
        if not up and step < 3:
            pl.when(self.deep > 0)(lambda: self.hop(step, False).start())
        self.fan(step)

    def near(self):
        pl.when(self.deep > 0)(lambda: self.relay(3, True))
        pl.when(self.deep < 3)(lambda: self.relay(1, False))

    def middle(self):
        pl.when(self.deep > 1)(lambda: self.relay(2, True))
        pl.when(self.deep < 2)(lambda: self.relay(2, False))

    def far(self):
        pl.when(self.deep == 3)(lambda: self.relay(1, True))
        pl.when(self.deep == 0)(lambda: self.relay(3, False))

    def corner(self, step):
        self.column(step, 3, self.right).wait_recv()
        self.passed(step, 15, True, False, self.above, 0).start()
        self.passed(step, 23, True, False, self.twin).start()
        self.column(step, 7, self.above).wait_recv()
        self.passed(step, 11, False, True, self.right, 1).start()
        self.passed(step, 27, False, True, self.twin).start()

    def last(self, step):
        self.passed(step, 15, True, False, self.above, 0).wait_recv()
        self.passed(step, 11, False, True, self.right, 1).wait_recv()
        self.passed(step, 31, True, True, self.twin).start()

    def finish(self):
        self.store().wait()
        for step in range(4):
            arrivals = [
                self.column(step, 19, self.twin),
                self.passed(step, 23, True, False, self.twin),
                self.passed(step, 27, False, True, self.twin),
                self.passed(step, 31, True, True, self.twin),
            ]
            for copy in arrivals:
                copy.wait_recv()
                copy.wait_send()
            self.column(step, 3, self.right).wait_send()
            self.column(step, 7, self.above).wait_send()
            self.passed(step, 15, True, False, self.above, 0).wait_send()
            self.passed(step, 11, False, True, self.right, 1).wait_send()
        pl.when(self.deep < 3)(lambda: self.hop(0, True).wait_send())
        pl.when((self.deep < 3) & (self.deep > 0))(lambda: self.hop(3, True).wait_send())
        pl.when(self.deep == 2)(lambda: self.hop(2, True).wait_send())
        pl.when(self.deep > 0)(lambda: self.hop(0, False).wait_send())
        pl.when((self.deep < 3) & (self.deep > 0))(lambda: self.hop(1, False).wait_send())
        pl.when(self.deep == 1)(lambda: self.hop(2, False).wait_send())


def layer_kernel(
    vec_half_ref, ids_ref, fcb_ref, x_hbm, m_hbm, g_hbm,
    qkv_hbm, so_hbm, cq_hbm, ckv_hbm, co_hbm, in_hbm, out_hbm,
    y_out, dx_out, dm_out, grads_ref, every_n, every_g,
    x_ref, m_ref, g_ref, vec_ref, ids_got, ids_all, id_rows,
    n1_ref, q1_ref, k1_ref, v1_ref, p1_ref, o1_ref, h1_ref, n2_ref, q2_ref, k2_ref, v2_ref, p2_ref,
    o2_ref, h2_ref, n3_ref, y_ref, dx_ref, dm_ref,
    qkv_w, so_w, cq_w, ckv_w, co_w, in_w, out_w, chip_n, acc_y, acc_n, part, got, go_ref,
    dkv2, dkv2_got, dkv1, dkv1_got, dq1, dq2, e1, e2, n2_half, o1_half, o2_half, dh_ref, sums, sums_got,
    stage, send, recv, local, tiles, stores, move_send, move_recv, move_local,
    spread_send, spread_recv, spread_local,
):
    across, up, core, deep = position()
    column = [device(across, up, 1 - core, deep)]
    for turn in (1, 2, 3):
        for other in (0, 1):
            column.append(device(across, up, other, (deep + turn) % 4))
    greet(column + [device(1 - across, up, core, deep), device(across, 1 - up, core, deep)])
    partner = Partner(send, recv)
    bf16, f32 = jnp.bfloat16, jnp.float32
    count, width = q1_ref.shape
    units = in_w.shape[2]
    half = width // 2
    mine = pl.ds(pl.multiple_of(core * count, count), count)
    theirs = pl.ds(pl.multiple_of((1 - core) * count, count), count)
    my_half = pl.ds(pl.multiple_of(core * half, half), half)
    their_half = pl.ds(pl.multiple_of((1 - core) * half, half), half)

    def bring(index, src, dst):
        return Bring(src, dst, move_send.at[index], move_recv.at[index], move_local.at[index])

    def give(index, src, dst):
        return SendBack(src, dst, move_send.at[index], move_recv.at[index], move_local.at[index])

    bring_x = bring(0, x_hbm, x_ref)
    bring_x.start()
    sent_ids = partner.push(ids_ref, ids_got)
    sent_vec = partner.push(vec_half_ref, vec_ref.at[:, my_half])
    vec_ref[:, my_half] = vec_half_ref[...]
    qkv = Weights(partner, qkv_hbm, qkv_w, local.at[0])
    bring_x.wait()
    sent_x = partner.push(x_ref.at[mine], x_ref.at[mine])
    bring_g, bring_m = bring(1, g_hbm, g_ref), bring(2, m_hbm, m_ref)
    bring_m.start()
    bring_g.start()
    so = Weights(partner, so_hbm, so_w, local.at[2])
    ckv = Weights(partner, ckv_hbm, ckv_w, local.at[1])
    cq = Weights(partner, cq_hbm, cq_w, local.at[3])
    co = Weights(partner, co_hbm, co_w, local.at[4])

    sent_ids.wait_recv()
    ids = jnp.where(deep % 2 == core, ids_ref[...], ids_got[...])
    ids_all[...] = ids
    micro = deep // 2
    token_row = jnp.where(micro == 0, ids[0:1], ids[1:2])
    source_row = jnp.where(micro == 0, ids[2:3], ids[3:4])
    id_rows[...] = jnp.broadcast_to(token_row, (128, token_row.shape[1])).T
    query_ids = id_rows[mine, :][:, :1]
    sent_vec.wait_recv()
    vectors = vec_ref[...]
    sent_x.wait_recv()
    n1_ref[...] = normed(x_ref[...].astype(f32), vectors, 0)
    place = core * count + lax.broadcasted_iota(jnp.int32, (count, 1), 0)
    keys = lax.broadcasted_iota(jnp.int32, (1, token_row.shape[1]), 1)
    allowed = (place >= keys) & (query_ids == token_row)
    allowed = jnp.concatenate([allowed, allowed], axis=0)
    w = qkv.get()
    q1_ref[...] = (mul(n1_ref[mine, :], w[:, :width]) + vectors[0:1]).astype(bf16)
    k1_ref[...] = mul(n1_ref[...], w[:, width : 2 * width]).astype(bf16)
    v1_ref[...] = (mul(n1_ref[...], w[:, 2 * width :]) + vectors[1:2]).astype(bf16)
    attend(q1_ref, k1_ref, v1_ref, p1_ref, o1_ref, allowed)
    bring_m.wait()
    sent_m = partner.push(m_ref.at[mine], m_ref.at[mine])
    bring_g.wait()
    sent_g = partner.push(g_ref.at[mine], g_ref.at[mine])
    spread_g = Spread(g_ref.at[mine], every_g, spread_send.at[0], spread_recv.at[0], spread_local.at[0])
    spread_g.begin()
    w = so.get()
    h1_ref[...] = x_ref[mine, :].astype(f32) + mul(o1_ref[...], w[...]) + vectors[2:3]
    n2_ref[...] = normed(h1_ref[...], vectors, 1)
    w = ckv.get()
    sent_m.wait_recv()
    k2_ref[...] = mul(m_ref[...], w[:, :width]).astype(bf16)
    v2_ref[...] = (mul(m_ref[...], w[:, width:]) + vectors[4:5]).astype(bf16)
    w = cq.get()
    q2_ref[...] = (mul(n2_ref[...], w[...]) + vectors[3:4]).astype(bf16)
    spread_g.near()
    allowed = query_ids == source_row
    allowed = jnp.concatenate([allowed, allowed], axis=0)
    attend(q2_ref, k2_ref, v2_ref, p2_ref, o2_ref, allowed)
    w = co.get()
    h2_ref[...] = h1_ref[...] + mul(o2_ref[...], w[...]) + vectors[5:6]
    n3_ref[...] = normed(h2_ref[...], vectors, 2)
    rows_sent = partner.push(n3_ref, chip_n.at[mine])
    chip_n[mine, :] = n3_ref[...]
    spread_g.middle()
    spread_n = Spread(n3_ref, every_n, spread_send.at[1], spread_recv.at[1], spread_local.at[1])
    spread_n.begin()

    def tile_copies(index):
        slot = index % 2
        where = pl.ds(index * units, units)
        return (
            pltpu.make_async_copy(in_hbm.at[:, where], in_w.at[slot], tiles.at[slot, 0]),
            pltpu.make_async_copy(out_hbm.at[where], out_w.at[slot], tiles.at[slot, 1]),
        )

    steps = in_hbm.shape[1] // units
    for copy in tile_copies(0):
        copy.start()
    halves = [
        partner.push(n2_ref.at[:, their_half], n2_half.at[mine]),
        partner.push(o1_ref.at[:, their_half], o1_half.at[mine]),
        partner.push(o2_ref.at[:, their_half], o2_half.at[mine]),
    ]
    n2_half[mine, :] = n2_ref[:, my_half]
    o1_half[mine, :] = o1_ref[:, my_half]
    o2_half[mine, :] = o2_ref[:, my_half]
    sent_g.wait_recv()
    rows_sent.wait_recv()
    for index in range(steps):
        if index + 1 < steps:
            for copy in tile_copies(index + 1):
                copy.start()
        for copy in tile_copies(index):
            copy.wait()
        slot = index % 2
        inner = mul(chip_n[...], in_w[slot]) + fcb_ref[:, index * units : (index + 1) * units]
        active, slope = gelu_pair(inner, refine=True)
        back = (mul_nt(g_ref[...], out_w[slot]) * slope).astype(bf16)
        if index == 0:
            acc_y[...] = mul(active.astype(bf16), out_w[slot])
            acc_n[...] = mul_nt(back, in_w[slot])
        else:
            acc_y[...] += mul(active.astype(bf16), out_w[slot])
            acc_n[...] += mul_nt(back, in_w[slot])
        if index == 2 * steps // 8:
            spread_g.far()
            spread_g.corner(0)
        if index == 6 * steps // 8:
            spread_n.near()
            spread_g.corner(2)
    part[0] = acc_n[theirs, :].astype(bf16)
    sent_n = partner.push(part.at[0], got.at[0])
    part[1] = acc_y[theirs, :].astype(bf16)
    sent_y = partner.push(part.at[1], got.at[1])
    spread_g.corner(1)
    spread_g.corner(3)
    sent_n.wait_recv()
    grad = acc_n[mine, :] + got[0].astype(f32)
    grad = norm_back(grad, h2_ref[...], vectors[9:10], sums, 2) + g_ref[mine, :].astype(f32)
    dh_ref[...] = grad
    e2[mine, :] = grad.astype(bf16)
    sent_e2 = partner.push(e2.at[mine], e2.at[mine])
    sent_y.wait_recv()
    y = h2_ref[...] + (acc_y[mine, :] + got[1].astype(f32) + vectors[6:7])
    y_ref[...] = y.astype(bf16)
    give_y = give(3, y_ref, y_out)
    spread_n.middle()
    go_ref[...] = mul_nt(e2[mine, :], co_w[...]).astype(bf16)
    attend_back(q2_ref, k2_ref, v2_ref, p2_ref, go_ref, dq2.at[mine], dkv2.at[:, :width], dkv2.at[:, width:])
    sent_dkv2 = partner.push(dkv2, dkv2_got)
    sent_dq2 = partner.push(dq2.at[mine], dq2.at[mine])
    spread_g.last(0)
    spread_n.far()
    spread_n.corner(0)
    grad = mul_nt(dq2[mine, :], cq_w[...])
    grad = norm_back(grad, h1_ref[...], vectors[8:9], sums, 1) + dh_ref[...]
    dh_ref[...] = grad
    e1[mine, :] = grad.astype(bf16)
    sent_e1 = partner.push(e1.at[mine], e1.at[mine])
    go_ref[...] = mul_nt(e1[mine, :], so_w[...]).astype(bf16)
    attend_back(q1_ref, k1_ref, v1_ref, p1_ref, go_ref, dq1.at[mine], dkv1.at[:, :width], dkv1.at[:, width:])
    sent_dkv1 = partner.push(dkv1, dkv1_got)
    sent_dq1 = partner.push(dq1.at[mine], dq1.at[mine])
    spread_g.last(1)
    spread_g.last(3)
    spread_n.corner(2)
    give_y.start()

    sent_dkv2.wait_recv()
    dkv2_got[...] = (dkv2[...].astype(f32) + dkv2_got[...].astype(f32)).astype(bf16)
    dm_ref[...] = mul_nt(dkv2_got[mine, :], ckv_w[...]).astype(bf16)
    give_dm = give(4, dm_ref, dm_out)
    give_dm.start()

    sent = []

    def weight_grad_of(left, right, column):
        index = len(sent)
        slot = index % 2
        if index >= 2:
            sent[index - 2].wait()
        stage[slot] = mul_tn(left, right).astype(bf16)
        copy = pltpu.make_async_copy(
            stage.at[slot], grads_ref.at[:, pl.ds(column, width)], stores.at[index]
        )
        copy.start()
        sent.append(copy)

    for copy in halves:
        copy.wait_recv()
    sent_e2.wait_recv()
    weight_grad_of(o2_half[...], e2[...], 7 * width)
    weight_grad_of(m_ref[:, my_half], dkv2_got[:, :width], 5 * width)
    weight_grad_of(m_ref[:, my_half], dkv2_got[:, width:], 6 * width)
    spread_g.last(2)
    spread_n.corner(1)
    spread_n.corner(3)
    sent_dq2.wait_recv()
    weight_grad_of(n2_half[...], dq2[...], 4 * width)
    sent_e1.wait_recv()
    weight_grad_of(o1_half[...], e1[...], 3 * width)
    sent_dkv1.wait_recv()
    dkv1_got[...] = (dkv1[...].astype(f32) + dkv1_got[...].astype(f32)).astype(bf16)
    grad = mul_nt(dq1[mine, :], qkv_w[:, :width])
    grad += mul_nt(dkv1_got[mine, :width], qkv_w[:, width : 2 * width])
    grad += mul_nt(dkv1_got[mine, width:], qkv_w[:, 2 * width :])
    dx = norm_back(grad, x_ref[mine, :].astype(f32), vectors[7:8], sums, 0) + dh_ref[...]
    dx_ref[...] = dx.astype(bf16)
    give_dx = give(5, dx_ref, dx_out)
    give_dx.start()
    sent_sums = partner.push(sums, sums_got)
    weight_grad_of(n1_ref[:, my_half], dkv1_got[:, :width], width)
    weight_grad_of(n1_ref[:, my_half], dkv1_got[:, width:], 2 * width)
    sent_dq1.wait_recv()
    weight_grad_of(n1_ref[:, my_half], dq1[...], 0)

    def columns(values):
        return jnp.sum(values.astype(f32), axis=0, keepdims=True)

    value_half = pl.ds(pl.multiple_of(width + core * half, half), half)
    sent_sums.wait_recv()
    lines = [
        columns(dq1[:, my_half]),
        columns(dkv1_got[:, value_half]),
        columns(e1[:, my_half]),
        columns(dq2[:, my_half]),
        columns(dkv2_got[:, value_half]),
        columns(e2[:, my_half]),
        columns(g_ref[:, my_half]),
        sums[0:6, my_half] + sums_got[0:6, my_half],
    ]
    lines = jnp.concatenate(lines + [jnp.zeros((128 - 13, half), f32)], axis=0).T
    sent[-1].wait()
    sent[-2].wait()
    stage[0, :, :128] = lines.astype(bf16)
    final = pltpu.make_async_copy(
        stage.at[0, :, pl.ds(0, 128)], grads_ref.at[:, pl.ds(8 * width, 128)], stores.at[8]
    )
    final.start()
    spread_n.last(0)
    spread_n.last(1)
    spread_n.last(3)
    spread_n.last(2)
    final.wait()
    partner.finish()
    for move in (bring_x, bring_m, bring_g, give_y, give_dm, give_dx):
        move.finish()
    spread_g.finish()
    spread_n.finish()


def layer(x, memory, grads, vectors, ids, fc_bias, weights, fc_in, fc_out, devices):
    block, width = x.shape[1:]
    rows = ids.shape[1]
    count = rows // 2
    units = 512
    bf16, f32 = jnp.bfloat16, jnp.float32
    half = width // 2
    vmem = pl.BlockSpec(memory_space=pltpu.VMEM)
    hbm = pl.BlockSpec(memory_space=pl.ANY)
    every = jax.ShapeDtypeStruct((devices * count, width), bf16)
    moved = jax.ShapeDtypeStruct(x.shape, bf16)
    scores = (width // (2 * HEAD), rows, rows)
    kept = [
        ((rows, width), bf16), ((count, width), bf16), ((rows, width), bf16), ((rows, width), bf16),
        (scores, bf16), ((count, width), bf16), ((count, width), f32), ((count, width), bf16),
        ((count, width), bf16), ((rows, width), bf16), ((rows, width), bf16), (scores, bf16),
        ((count, width), bf16), ((count, width), f32), ((count, width), bf16),
    ]
    return pl.pallas_call(
        layer_kernel,
        in_specs=[vmem] * 3 + [hbm] * 10,
        out_specs=[hbm] * 6,
        out_shape=[
            moved, moved, moved, jax.ShapeDtypeStruct((half, 8 * width + 128), bf16), every, every
        ],
        scratch_shapes=[
            *[pltpu.VMEM((rows, width), bf16)] * 3,
            pltpu.VMEM((16, width), f32),
            pltpu.VMEM(ids.shape, jnp.int32),
            pltpu.VMEM(ids.shape, jnp.int32),
            pltpu.VMEM((rows, 128), jnp.int32),
            *[pltpu.VMEM(*shape) for shape in kept],
            *[pltpu.VMEM((count, width), bf16)] * 3,
            *[pltpu.VMEM((2 * w.shape[0], w.shape[1]), bf16) for w in weights],
            pltpu.VMEM((2, width, units), bf16),
            pltpu.VMEM((2, units, width), bf16),
            pltpu.VMEM((rows, width), bf16),
            pltpu.VMEM((rows, width), f32),
            pltpu.VMEM((rows, width), f32),
            pltpu.VMEM((2, count, width), bf16),
            pltpu.VMEM((2, count, width), bf16),
            pltpu.VMEM((count, width), bf16),
            *[pltpu.VMEM((rows, 2 * width), bf16)] * 4,
            *[pltpu.VMEM((rows, width), bf16)] * 4,
            *[pltpu.VMEM((rows, half), bf16)] * 3,
            pltpu.VMEM((count, width), f32),
            pltpu.VMEM((8, width), f32),
            pltpu.VMEM((8, width), f32),
            pltpu.VMEM((2, half, width), bf16),
            pltpu.SemaphoreType.DMA((32,)),
            pltpu.SemaphoreType.DMA((32,)),
            pltpu.SemaphoreType.DMA((5,)),
            pltpu.SemaphoreType.DMA((2, 2)),
            pltpu.SemaphoreType.DMA((9,)),
            pltpu.SemaphoreType.DMA((6, 2)),
            pltpu.SemaphoreType.DMA((6, 2)),
            pltpu.SemaphoreType.DMA((6,)),
            pltpu.SemaphoreType.DMA((2, 43)),
            pltpu.SemaphoreType.DMA((2, 43)),
            pltpu.SemaphoreType.DMA((2,)),
        ],
        compiler_params=pltpu.CompilerParams(
            vmem_limit_bytes=60 * 2**20, collective_id=1, has_side_effects=True
        ),
        cost_estimate=pl.CostEstimate(flops=80 * 10**9, bytes_accessed=64 * 2**20, transcendentals=0),
    )(vectors, ids, fc_bias, x, memory, grads, *weights, fc_in, fc_out)


def widen_kernel(*refs):
    din_part, dout_part, sum_ref, din_ref, dout_ref = refs[:5]
    din_ref[...] = din_part[...].astype(jnp.float32)
    dout_ref[...] = dout_part[...].astype(jnp.float32)
    column = 0
    for shard_ref in refs[5:]:
        shard_ref[...] = sum_ref[:, column : column + shard_ref.shape[1]].astype(jnp.float32)
        column += shard_ref.shape[1]


def widen(din, dout, total, widths):
    width, hidden = din.shape
    steps = 8
    units, height = hidden // steps, total.shape[0] // steps
    wide = pl.BlockSpec((width // steps, hidden), lambda at: (at, 0))
    tall = pl.BlockSpec((units, width), lambda at: (at, 0))
    f32 = jnp.float32
    return pl.pallas_call(
        widen_kernel,
        grid=(steps,),
        in_specs=[wide, tall, pl.BlockSpec((height, total.shape[1]), lambda at: (at, 0))],
        out_specs=[wide, tall] + [pl.BlockSpec((height, w), lambda at: (at, 0)) for w in widths],
        out_shape=[jax.ShapeDtypeStruct(din.shape, f32), jax.ShapeDtypeStruct(dout.shape, f32)]
        + [jax.ShapeDtypeStruct((total.shape[0], w), f32) for w in widths],
        compiler_params=pltpu.CompilerParams(vmem_limit_bytes=56 * 2**20),
        cost_estimate=pl.CostEstimate(flops=0, bytes_accessed=18 * width * hidden, transcendentals=0),
    )(din, dout, total)


def fast_body(
    hidden_in,
    memory,
    segment_ids,
    memory_ids,
    out_grad,
    self_qkv,
    self_out,
    cross_query,
    cross_kv,
    cross_out,
    fc_in,
    fc_out,
    biases,
    fc_in_bias,
    norm_gains,
    norm_shifts,
):
    width = hidden_in.shape[-1]
    f32 = jnp.float32
    ids = jnp.concatenate([segment_ids[:, 0], memory_ids[:, 0]], axis=0)
    vectors = jnp.concatenate([biases, norm_gains, norm_shifts], axis=1).astype(f32).T
    vectors = jnp.pad(vectors, ((0, 16 - vectors.shape[0]), (0, 0)))
    fc_bias = fc_in_bias.astype(f32)[None]
    devices = lax.axis_size("rep") * lax.axis_size("fsdp") * lax.axis_size("seq")
    weights = (self_qkv, self_out, cross_query, cross_kv, cross_out)
    hidden_out, hidden_grad, memory_grad, grads, normed_every, grad_every = layer(
        hidden_in[:, 0], memory[:, 0], out_grad[:, 0], vectors, ids, fc_bias, weights, fc_in, fc_out, devices
    )
    din, dout, grad_fc_bias, total = ffn_grads(
        normed_every, grad_every, fc_in, fc_out, fc_bias, grads
    )
    widths = [weight.shape[1] for weight in weights]
    grad_fc_in, grad_fc_out, *shards = widen(din, dout, total, widths)
    column = total[:, 8 * width :].astype(f32)
    return (
        hidden_out[:, None],
        hidden_grad[:, None],
        memory_grad[:, None],
        *shards,
        grad_fc_in,
        grad_fc_out,
        column[:, :7],
        grad_fc_bias[0],
        column[:, 7:10],
        column[:, 10:13],
    )


def solution(mesh):
    fits = mesh.shape["rep"] == 4 and mesh.shape["fsdp"] == 2 and mesh.shape["seq"] == 4
    chosen = fast_body if fits else body
    return jax.shard_map(
        chosen,
        mesh=mesh,
        in_specs=(
            P(None, ("rep", "fsdp"), "seq", None),
            P(None, ("rep", "fsdp"), "seq", None),
            P(None, ("rep", "fsdp"), None),
            P(None, ("rep", "fsdp"), None),
            P(None, ("rep", "fsdp"), "seq", None),
            P("fsdp", None),
            P("fsdp", None),
            P("fsdp", None),
            P("fsdp", None),
            P("fsdp", None),
            P(None, "fsdp"),
            P("fsdp", None),
            P("fsdp", None),
            P("fsdp"),
            P("fsdp", None),
            P("fsdp", None),
        ),
        out_specs=(
            P(None, ("rep", "fsdp"), "seq", None),
            P(None, ("rep", "fsdp"), "seq", None),
            P(None, ("rep", "fsdp"), "seq", None),
            P("fsdp", None),
            P("fsdp", None),
            P("fsdp", None),
            P("fsdp", None),
            P("fsdp", None),
            P(None, "fsdp"),
            P("fsdp", None),
            P("fsdp", None),
            P("fsdp"),
            P("fsdp", None),
            P("fsdp", None),
        ),
        check_vma=False,
    )
```
